32 devices in a mesh: dp: 4 (over y, x), sp: 8 (over z, core).
Axes of the slice: x: 2, y: 2, z: 4, core: 2. Of those that a mesh axis runs over, the one named last changes fastest.
Arguments:
- tokens: bfloat16 [4, 2048, 1152], P('dp', 'sp'), may hold values from -6 to 6
- image_len: int32 [4, 8], P('dp'), may hold values from 0 to 1024, as said below
- timestep: int32 [4, 8], P('dp'), may hold values from 0 to 63
- caption: bfloat16 [4, 120, 1152], P('dp'), may hold values from -6 to 6
- time_embed: float32 [64, 6912], replicated, may hold values from -6 to 6
- mod_table: float32 [6, 1152], replicated, may hold values from -6 to 6
- w_qkv: bfloat16 [1152, 3456], replicated, may hold values from -0.1875 to 0.1875
- w_out: bfloat16 [1152, 1152], replicated, may hold values from -0.5 to 0.5
- cross_q: bfloat16 [1152, 1152], replicated, may hold values from -0.1875 to 0.1875
- cross_kv: bfloat16 [1152, 2304], replicated, may hold values from -0.1875 to 0.1875
- cross_out: bfloat16 [1152, 1152], replicated, may hold values from -0.375 to 0.375
- w_up: bfloat16 [1152, 4608], replicated, may hold values from -0.1875 to 0.1875
- w_down: bfloat16 [4608, 1152], replicated, may hold values from -0.09375 to 0.09375
- cotangent: bfloat16 [4, 2048, 1152], P('dp', 'sp'), may hold values from -6 to 6
Outputs:
- out_tokens: float32 [4, 2048, 1152], P('dp', 'sp')
- grad_tokens: float32 [4, 2048, 1152], P('dp', 'sp')
- grad_table: float32 [6912], P(('dp', 'sp'))
- grad_qkv: float32 [1152, 3456], P('dp', 'sp')
- grad_out: float32 [1152, 1152], P('dp', 'sp')
- grad_cross_q: float32 [1152, 1152], P('dp', 'sp')
- grad_cross_kv: float32 [1152, 2304], P('dp', 'sp')
- grad_cross_out: float32 [1152, 1152], P('dp', 'sp')
- grad_up: float32 [1152, 4608], P('dp', 'sp')
- grad_down: float32 [4608, 1152], P('dp', 'sp')
The draws below stay inside these ranges and needn't reach their ends.
Inputs may be any that keep to these rules, and one draw needn't show every extreme that they name: `image_len`: each row lists its images' patch counts, each 256 or 1024, followed by zeros; a row's counts sum to 2048, and every row holds at least one image of 1024 patches.
All inputs are finite; a program needn't handle non-finite values.
Results may differ from the reference program's by a relative error of at most 0.02.
Values may be sent and summed in bfloat16 or wider, within the bound.
No kernel may reach another device: no remote copies, remote signals or barrier semaphores. Data moves between devices by JAX's collectives and lax.ppermute only.
A program may use at most 320 MiB of HBM per device.

```python
import math
import jax
import jax.numpy as jnp
from jax import lax

D = 1152
HEADS = 16
FF = 4608
NTEXT = 120
BIG = 1024
SMALL = 256
TSTEPS = 64
LEN = 2048
ROWS = 4
SLOTS = 8


def draw_image_len(key, part):
    key = jax.random.fold_in(key, 11)
    count_key, order_key = jax.random.split(key)
    big_count = jax.random.randint(count_key, (ROWS,), 1, LEN // BIG + 1).astype(jnp.int32)
    small_count = (LEN - big_count * BIG) // SMALL
    live_count = big_count + small_count
    orders = jax.vmap(lambda row_key: jax.random.permutation(row_key, SLOTS))(jax.random.split(order_key, ROWS)).astype(jnp.int32)
    slot_ids = jnp.arange(SLOTS, dtype=jnp.int32)
    live_slot = slot_ids[None, :] < live_count[:, None]
    ranked = jnp.where(live_slot, orders, SLOTS + slot_ids[None, :])
    places = jnp.sum((ranked[:, None, :] < ranked[:, :, None]).astype(jnp.int32), axis=2)
    is_big = places < big_count[:, None]
    return jnp.where(live_slot, jnp.where(is_big, BIG, SMALL), 0).astype(jnp.int32)


def place_ends(entries, rng, smallest, high):
    dims = entries.shape
    spot = [jax.random.randint(jax.random.fold_in(rng, axis), (), 0, dims[axis]) for axis in range(len(dims))]
    entries = entries.at[tuple(spot)].set(smallest)
    longest = dims.index(max(dims))
    spot[longest] = (spot[longest] + 1) % dims[longest]
    return entries.at[tuple(spot)].set(high)


def block_scale(rng, extent, shards, least, high):
    def one(dim, blocks):
        draws = jax.random.uniform(jax.random.fold_in(jax.random.fold_in(rng, 6), dim), (blocks,), jnp.float32, least / len(shards), high / len(shards))
        return jnp.repeat(jnp.exp(draws), extent[dim] // blocks).reshape((-1,) + (1,) * (len(extent) - dim - 1))

    loudness = one(*shards[0])
    for cut in shards[1:]:
        loudness = loudness * one(*cut)
    return loudness


def gaussian(own_key, shape, scale, most, shards=(), kind=jnp.bfloat16):
    array = jax.random.normal(own_key, shape, jnp.float32) * scale
    if len(shards) > 0:
        array = block_scale(own_key, shape, shards, -0.22, 0.18) * array
    return jnp.clip(array, min=-most, max=most).astype(kind)


def setup_inputs(seed: int = 0) -> dict:
    seeds = jax.random.split(jax.random.key(seed), 15)
    return {
        "tokens": gaussian(seeds[0], (ROWS, LEN, D), 1.0, 6.0, ((0, 4), (1, 8))),
        "image_len": draw_image_len(jax.random.fold_in(seeds[14], 71), 0),
        "timestep": place_ends(jax.random.randint(seeds[2], (ROWS, SLOTS), 0, TSTEPS), jax.random.fold_in(seeds[2], 1), 0, TSTEPS - 1).astype(jnp.int32),
        "caption": gaussian(seeds[3], (ROWS, NTEXT, D), 1.0, 6.0, ((0, 4),)),
        "time_embed": gaussian(seeds[4], (TSTEPS, 6 * D), 0.6, 6.0, (), jnp.float32),
        "mod_table": gaussian(seeds[5], (6, D), 0.5, 6.0, (), jnp.float32),
        "w_qkv": gaussian(seeds[6], (D, 3 * D), D ** -0.5, 0.1875),
        "w_out": gaussian(seeds[7], (D, D), (D // 8) ** -0.5, 0.5),
        "cross_q": gaussian(seeds[8], (D, D), D ** -0.5, 0.1875),
        "cross_kv": gaussian(seeds[9], (D, 2 * D), D ** -0.5, 0.1875),
        "cross_out": gaussian(seeds[10], (D, D), (D // 4) ** -0.5, 0.375),
        "w_up": gaussian(seeds[11], (D, FF), D ** -0.5, 0.1875),
        "w_down": gaussian(seeds[12], (FF, D), FF ** -0.5, 0.09375),
        "cotangent": gaussian(seeds[13], (ROWS, LEN, D), 1.0, 6.0, ((0, 4), (1, 8))),
    }


@jax.custom_vjp
def low(v):
    return lax.optimization_barrier(v.astype(jnp.bfloat16)).astype(jnp.float32)

@jax.custom_vjp
def low_back(v):
    return v

def low_keep(v):
    return (low(v), None)

def low_pass(kept, grad):
    return (grad,)

def back_keep(v):
    return (v, None)

def back_low(kept, grad):
    return (low(grad),)
low.defvjp(low_keep, low_pass)
low_back.defvjp(back_keep, back_low)
EPS = 1e-06
BIGNEG = -1e+30
HIGH = lax.Precision.HIGHEST

def normed(stream, shift, scale):
    centred = stream - lax.optimization_barrier(jnp.mean(stream, axis=-1, keepdims=True))
    spread = lax.optimization_barrier(jnp.mean(centred * centred, axis=-1, keepdims=True))
    return centred * lax.rsqrt(spread + EPS) * (1.0 + scale) + shift

def product(left, right):
    return jnp.dot(left, right, precision=HIGH)

def self_attention(queries, key_rows, value_rows, labels, factor):
    total_rows = queries.shape[0]
    block_rows = min(512, total_rows)
    block_count = total_rows // block_rows

    def one_block(items_in):
        query_block, query_label = items_in
        scores = low_back(jnp.einsum('qhd,khd->hqk', query_block, key_rows, precision=HIGH) * factor)
        allowed = (query_label[:, None] == labels[None, :])[None]
        scores = jnp.where(allowed, scores, BIGNEG)
        row_max = lax.optimization_barrier(jnp.max(scores, axis=-1, keepdims=True))
        raised = jnp.exp(scores - row_max)
        weights = low(raised / lax.optimization_barrier(jnp.sum(raised, axis=-1, keepdims=True)))
        return jnp.einsum('hqk,khd->qhd', weights, value_rows, precision=HIGH)
    result = lax.map(jax.checkpoint(one_block), (queries.reshape(block_count, block_rows, queries.shape[1], queries.shape[2]), labels.reshape(block_count, block_rows)))
    return result.reshape(queries.shape)

def row_layer(stream, params, row_lens, row_steps, caption_rows, time_float):
    mod_table, w_qkv, w_out, cross_q, cross_kv, cross_out, w_up, w_down = params
    total_rows = stream.shape[0]
    model_width = stream.shape[1]
    head_size = model_width // HEADS
    factor = 1.0 / math.sqrt(head_size)
    image_ends = jnp.cumsum(row_lens).astype(jnp.int32)
    places = jnp.arange(total_rows, dtype=jnp.int32)
    labels = lax.optimization_barrier(jnp.sum((image_ends[None, :] <= places[:, None]).astype(jnp.int32), axis=1)).astype(jnp.int32)
    step_pick = (row_steps[:, None] == jnp.arange(time_float.shape[0], dtype=jnp.int32)[None, :]).astype(jnp.float32)
    slot_mod = product(step_pick, time_float)
    slot_pick = (labels[:, None] == jnp.arange(row_lens.shape[0], dtype=jnp.int32)[None, :]).astype(jnp.float32)
    modulation = product(slot_pick, slot_mod).reshape(total_rows, 6, model_width) + mod_table[None]
    shift_one = modulation[:, 0]
    scale_one = modulation[:, 1]
    gate_one = modulation[:, 2]
    shift_two = modulation[:, 3]
    scale_two = modulation[:, 4]
    gate_two = modulation[:, 5]
    first_in = low(normed(stream, shift_one, scale_one))
    projected = low(low_back(product(first_in, w_qkv))).reshape(total_rows, 3, HEADS, head_size)
    attended = self_attention(projected[:, 0], projected[:, 1], projected[:, 2], labels, factor)
    attended = low(low_back(attended)).reshape(total_rows, model_width)
    attn_branch = low_back(product(attended, w_out))
    stream_one = stream + gate_one * attn_branch
    cross_in = low(stream_one)
    cross_queries = low(low_back(product(cross_in, cross_q))).reshape(total_rows, HEADS, head_size)
    text_kv = product(caption_rows, cross_kv)
    text_keys = low(text_kv[:, :model_width]).reshape(-1, HEADS, head_size)
    text_values = low(text_kv[:, model_width:]).reshape(-1, HEADS, head_size)
    cross_scores = low_back(jnp.einsum('qhd,khd->hqk', cross_queries, text_keys, precision=HIGH) * factor)
    row_max = lax.optimization_barrier(jnp.max(cross_scores, axis=-1, keepdims=True))
    raised = jnp.exp(cross_scores - row_max)
    cross_weights = low(raised / lax.optimization_barrier(jnp.sum(raised, axis=-1, keepdims=True)))
    cross_mixed = low(low_back(jnp.einsum('hqk,khd->qhd', cross_weights, text_values, precision=HIGH)))
    cross_branch = low_back(product(cross_mixed.reshape(total_rows, model_width), cross_out))
    stream_two = stream_one + cross_branch
    second_in = low(normed(stream_two, shift_two, scale_two))
    hidden_pre = low_back(product(second_in, w_up))
    hidden = low(jax.nn.gelu(hidden_pre, approximate=True))
    mlp_branch = low_back(product(hidden, w_down))
    return stream_two + gate_two * mlp_branch

def reference(tokens, image_len, timestep, caption, time_embed, mod_table, w_qkv, w_out, cross_q, cross_kv, cross_out, w_up, w_down, cotangent):
    params = (mod_table.astype(jnp.float32), w_qkv.astype(jnp.float32), w_out.astype(jnp.float32), cross_q.astype(jnp.float32), cross_kv.astype(jnp.float32), cross_out.astype(jnp.float32), w_up.astype(jnp.float32), w_down.astype(jnp.float32))
    time_float = time_embed.astype(jnp.float32)

    def one_row(running, items_in):
        row_tokens, row_grad, row_lens, row_steps, row_caption = items_in
        caption_rows = row_caption.astype(jnp.float32)

        def layer_fn(stream, weights_in):
            return row_layer(stream, weights_in, row_lens, row_steps, caption_rows, time_float)
        output, pull = jax.vjp(layer_fn, row_tokens.astype(jnp.float32), params)
        grad_stream, grad_params = pull(row_grad.astype(jnp.float32))
        running = jax.tree.map(lambda before, added: before + added, running, grad_params)
        return (running, (output, grad_stream))
    start = jax.tree.map(jnp.zeros_like, params)
    totals, (outputs, grad_rows) = lax.scan(one_row, start, (tokens, cotangent, image_len, timestep, caption))
    return (outputs, grad_rows, totals[0].reshape(-1), totals[1], totals[2], totals[3], totals[4], totals[5], totals[6], totals[7])
```

```python
import functools
import math

import jax
import jax.numpy as jnp
from jax import lax
from jax.experimental import pallas as pl
from jax.experimental.pallas import tpu as pltpu
from jax.sharding import PartitionSpec as P

HEADS = 16
BIG = 1024
EPS = 1e-06
BIGNEG = -1e30
LOG2E = 1.4426950408889634
BF = jnp.bfloat16
F32 = jnp.float32
WIN = 256
VMEM_LIMIT = 48 * 1024 * 1024


def matmul(left, right):
    return jnp.dot(left, right, preferred_element_type=F32)


def matmul_tn(left, right):
    return lax.dot_general(left, right, (((0,), (0,)), ((), ())), preferred_element_type=F32)


def matmul_nt(left, right):
    return lax.dot_general(left, right, (((1,), (1,)), ((), ())), preferred_element_type=F32)


def head_window(head, width):
    size = width // HEADS
    low = head * size
    start = pl.multiple_of(jnp.minimum(low // 128 * 128, width - WIN), 128)
    lane = lax.broadcasted_iota(jnp.int32, (1, WIN), 1) + start
    mask = jnp.logical_and(lane >= low, lane < low + size)
    return pl.ds(start, WIN), mask


def keep_columns(ref, win, mask, value):
    ref[:, win] = jnp.where(mask, value, ref[:, win])


def attend_kernel(big_ref, q_ref, k0_ref, v0_ref, k1_ref, v1_ref, out_ref, lse_ref, *, factor):
    width = q_ref.shape[1]
    scale = factor * LOG2E

    def run(pairs):
        def one_head(head, carry):
            win, mask = head_window(head, width)
            query = q_ref[:, win] * mask.astype(BF)
            scores = [matmul_nt(query, key[:, win]) for key, _ in pairs]
            top = functools.reduce(jnp.maximum, [jnp.max(s, axis=1, keepdims=True) for s in scores])
            raised = [jnp.exp2((s - top) * scale) for s in scores]
            total = sum(jnp.sum(r, axis=1, keepdims=True) for r in raised)
            inverse = 1.0 / total
            result = sum(
                matmul((r * inverse).astype(BF), value[:, win])
                for r, (_, value) in zip(raised, pairs)
            )
            keep_columns(out_ref, win, mask, result.astype(BF))
            lane = lax.broadcasted_iota(jnp.int32, (1, 128), 1)
            lse = top * scale + jnp.log2(total)
            lse_ref[...] = jnp.where(lane == head, lse, lse_ref[...])
            return carry

        lax.fori_loop(0, HEADS, one_head, 0, unroll=2)

    lse_ref[...] = jnp.zeros_like(lse_ref)

    @pl.when(big_ref[0] == 1)
    def _():
        run([(k0_ref, v0_ref), (k1_ref, v1_ref)])

    @pl.when(big_ref[0] == 0)
    def _():
        run([(k0_ref, v0_ref)])


def query_grad_kernel(
    big_ref, q_ref, k0_ref, v0_ref, k1_ref, v1_ref, do_ref, stat_ref, out_ref, *, factor
):
    width = q_ref.shape[1]
    scale = factor * LOG2E

    def run(pairs):
        def one_head(head, carry):
            win, mask = head_window(head, width)
            keep = mask.astype(BF)
            query = q_ref[:, win] * keep
            grad = do_ref[:, win] * keep
            lane = lax.broadcasted_iota(jnp.int32, (1, 128), 1)
            stat = stat_ref[...]
            lse = jnp.sum(jnp.where(lane == head, stat, 0.0), axis=1, keepdims=True)
            delta = jnp.sum(jnp.where(lane == head + HEADS, stat, 0.0), axis=1, keepdims=True)
            total = None
            for key, value in pairs:
                prob = jnp.exp2(matmul_nt(query, key[:, win]) * scale - lse)
                grad_prob = matmul_nt(grad, value[:, win])
                grad_score = (prob * (grad_prob - delta)).astype(BF)
                part = matmul(grad_score, key[:, win])
                total = part if total is None else total + part
            keep_columns(out_ref, win, mask, (total * factor).astype(BF))
            return carry

        lax.fori_loop(0, HEADS, one_head, 0, unroll=2)

    @pl.when(big_ref[0] == 1)
    def _():
        run([(k0_ref, v0_ref), (k1_ref, v1_ref)])

    @pl.when(big_ref[0] == 0)
    def _():
        run([(k0_ref, v0_ref)])


def key_grad_kernel(
    big_ref, k_ref, v_ref, q0_ref, q1_ref, pack0_ref, pack1_ref, dk_ref, dv_ref, stats, *, factor
):
    width = k_ref.shape[1]
    rows = k_ref.shape[0]
    scale = factor * LOG2E
    blocks = 1 + pack1_ref.shape[0]

    def unpack(block, pack):
        both = pack[rows : rows + 16, :].astype(F32)
        joined = both[:8] + both[8:]
        for group in range(4):
            stats[block, 8 * group : 8 * group + 8, :] = joined[:, group * rows : group * rows + rows]

    unpack(0, pack0_ref[...])
    for block in range(1, blocks):
        unpack(block, pack1_ref[block - 1])

    def run(count):
        def one_head(head, carry):
            win, mask = head_window(head, width)
            keep = mask.astype(BF)
            key = k_ref[:, win] * keep
            value = v_ref[:, win] * keep
            grad_key = grad_value = None
            for block in range(count):
                if block == 0:
                    query, grad = q0_ref[:, win], pack0_ref[0:rows, win]
                else:
                    query = q1_ref[(block - 1) * rows : block * rows, win]
                    grad = pack1_ref[block - 1, 0:rows, win]
                lse = stats[block, pl.ds(head, 1), :]
                delta = stats[block, pl.ds(head + HEADS, 1), :]
                prob = jnp.exp2(matmul_nt(key, query) * scale - lse)
                grad_prob = matmul_nt(value, grad)
                grad_score = (prob * (grad_prob - delta)).astype(BF)
                part_value = matmul(prob.astype(BF), grad)
                part_key = matmul(grad_score, query)
                grad_value = part_value if block == 0 else grad_value + part_value
                grad_key = part_key if block == 0 else grad_key + part_key
            keep_columns(dk_ref, win, mask, (grad_key * factor).astype(BF))
            keep_columns(dv_ref, win, mask, grad_value.astype(BF))
            return carry

        lax.fori_loop(0, HEADS, one_head, 0, unroll=2)

    @pl.when(big_ref[0] == 1)
    def _():
        run(blocks)

    @pl.when(big_ref[0] == 0)
    def _():
        run(1)


def text_probs(query, key, scale, live):
    scores = matmul_nt(query, key)
    lane = lax.broadcasted_iota(jnp.int32, (1, scores.shape[1]), 1)
    scores = jnp.where(lane < live, scores, BIGNEG)
    raised = jnp.exp2((scores - jnp.max(scores, axis=1, keepdims=True)) * scale)
    return raised * (1.0 / jnp.sum(raised, axis=1, keepdims=True))


def cross_kernel(q_ref, k_ref, v_ref, out_ref, *, factor, live):
    width = q_ref.shape[1]

    def one_head(head, carry):
        win, mask = head_window(head, width)
        query = q_ref[:, win] * mask.astype(BF)
        probs = text_probs(query, k_ref[:, win], factor * LOG2E, live)
        keep_columns(out_ref, win, mask, matmul(probs.astype(BF), v_ref[:, win]).astype(BF))
        return carry

    lax.fori_loop(0, HEADS, one_head, 0, unroll=4)


def cross_grad_kernel(q_ref, g_ref, k_ref, v_ref, dq_ref, dk_ref, dv_ref, *, factor, live):
    width = q_ref.shape[1]

    def one_head(head, carry):
        win, mask = head_window(head, width)
        keep = mask.astype(BF)
        query = q_ref[:, win]
        grad = g_ref[:, win]
        key = k_ref[:, win]
        probs = text_probs(query * keep, key, factor * LOG2E, live)
        grad_probs = matmul_nt(grad * keep, v_ref[:, win])
        inner = jnp.sum(probs * grad_probs, axis=1, keepdims=True)
        grad_scores = (probs * (grad_probs - inner)).astype(BF)
        keep_columns(dq_ref, win, mask, (matmul(grad_scores, key) * factor).astype(BF))
        keep_columns(dk_ref, win, mask, matmul_tn(grad_scores, query) * factor)
        keep_columns(dv_ref, win, mask, matmul_tn(probs.astype(BF), grad))
        return carry

    lax.fori_loop(0, HEADS, one_head, 0, unroll=4)


def weight_grad_kernel(x0_ref, x1_ref, g0_ref, g1_ref, out_ref, turned):
    rows, width = x0_ref.shape
    step = pl.program_id(0)

    @pl.when(step == 0)
    def _():
        for part, ref in enumerate((x0_ref, x1_ref)):
            for low in range(0, width, 128):
                turned[low : low + 128, part * rows : part * rows + rows] = ref[:, low : low + 128].T

    tall = out_ref.shape[0]
    here = pl.ds(pl.multiple_of(step * tall, 16), tall)
    total = matmul(turned[here, 0:rows], g0_ref[...]) + matmul(turned[here, rows:], g1_ref[...])
    out_ref[...] = total.astype(out_ref.dtype)


def whole(shape):
    return pl.BlockSpec(shape, lambda *_: (0,) * len(shape))


def params():
    return pltpu.CompilerParams(vmem_limit_bytes=VMEM_LIMIT)


def cost(flops, nbytes, exps=0):
    return pl.CostEstimate(flops=int(flops), bytes_accessed=int(nbytes), transcendentals=int(exps))


def part_spec(rows, width, at):
    return pl.BlockSpec((rows, width), lambda i, *_: (0, at))


def attend(big, own, others, factor):
    rows, width = own.shape[0], own.shape[1] // 3
    far = others.shape[0]
    return pl.pallas_call(
        functools.partial(attend_kernel, factor=factor),
        grid_spec=pltpu.PrefetchScalarGridSpec(
            num_scalar_prefetch=1,
            grid=(1,),
            in_specs=[
                part_spec(rows, width, 0),
                part_spec(rows, width, 1),
                part_spec(rows, width, 2),
                part_spec(far, width, 1),
                part_spec(far, width, 2),
            ],
            out_specs=[whole((rows, width)), whole((rows, 128))],
        ),
        out_shape=[
            jax.ShapeDtypeStruct((rows, width), BF),
            jax.ShapeDtypeStruct((rows, 128), F32),
        ],
        compiler_params=params(),
        cost_estimate=cost(4 * HEADS * rows * (rows + far) * WIN, 6 * far * width, HEADS * rows * far),
    )(big, own, own, own, others, others)


def query_grad(big, own, others, grad, stat, factor):
    rows, width = own.shape[0], own.shape[1] // 3
    far = others.shape[0]
    return pl.pallas_call(
        functools.partial(query_grad_kernel, factor=factor),
        grid_spec=pltpu.PrefetchScalarGridSpec(
            num_scalar_prefetch=1,
            grid=(1,),
            in_specs=[
                part_spec(rows, width, 0),
                part_spec(rows, width, 1),
                part_spec(rows, width, 2),
                part_spec(far, width, 1),
                part_spec(far, width, 2),
                whole((rows, width)),
                whole((rows, 128)),
            ],
            out_specs=whole((rows, width)),
        ),
        out_shape=jax.ShapeDtypeStruct((rows, width), BF),
        compiler_params=params(),
        cost_estimate=cost(6 * HEADS * rows * (rows + far) * WIN, 6 * far * width, HEADS * rows * far),
    )(big, own, own, own, others, others, grad, stat)


def key_grad(big, own, others, pack, packs, factor):
    rows, width = own.shape[0], own.shape[1] // 3
    far = others.shape[0]
    return pl.pallas_call(
        functools.partial(key_grad_kernel, factor=factor),
        grid_spec=pltpu.PrefetchScalarGridSpec(
            num_scalar_prefetch=1,
            grid=(1,),
            in_specs=[
                part_spec(rows, width, 1),
                part_spec(rows, width, 2),
                part_spec(rows, width, 0),
                part_spec(far, width, 0),
                whole(pack.shape),
                whole(packs.shape),
            ],
            out_specs=[whole((rows, width))] * 2,
            scratch_shapes=[pltpu.VMEM((1 + packs.shape[0], 2 * HEADS, rows), F32)],
        ),
        out_shape=[jax.ShapeDtypeStruct((rows, width), BF)] * 2,
        compiler_params=params(),
        cost_estimate=cost(8 * HEADS * rows * (rows + far) * WIN, 6 * far * width, HEADS * rows * far),
    )(big, own, own, own, others, pack, packs)


def cross_attend(queries, keys, values, factor, live):
    rows, width = queries.shape
    return pl.pallas_call(
        functools.partial(cross_kernel, factor=factor, live=live),
        out_shape=jax.ShapeDtypeStruct((rows, width), BF),
        compiler_params=params(),
        cost_estimate=cost(4 * HEADS * rows * 128 * WIN, 6 * rows * width, HEADS * rows * 128),
    )(queries, keys, values)


def cross_grad(queries, grad, keys, values, factor, live):
    rows, width = queries.shape
    return pl.pallas_call(
        functools.partial(cross_grad_kernel, factor=factor, live=live),
        out_shape=[
            jax.ShapeDtypeStruct((rows, width), BF),
            jax.ShapeDtypeStruct(keys.shape, F32),
            jax.ShapeDtypeStruct(keys.shape, F32),
        ],
        compiler_params=params(),
        cost_estimate=cost(10 * HEADS * rows * 128 * WIN, 12 * rows * width, HEADS * rows * 128),
    )(queries, grad, keys, values)


def weight_grad(x0, x1, g0, g1):
    rows, width = x0.shape
    depth = g0.shape[1]
    tall = width // 4
    return pl.pallas_call(
        weight_grad_kernel,
        grid=(4,),
        in_specs=[whole((rows, width))] * 2 + [whole((rows, depth))] * 2,
        out_specs=pl.BlockSpec((tall, depth), lambda i: (i, 0)),
        out_shape=jax.ShapeDtypeStruct((width, depth), BF),
        scratch_shapes=[pltpu.VMEM((width, 2 * rows), BF)],
        compiler_params=params(),
        cost_estimate=cost(4 * rows * width * depth, 2 * width * depth + 4 * rows * (width + depth)),
    )(x0, x1, g0, g1)


def normal(stream):
    centred = stream - jnp.mean(stream, axis=-1, keepdims=True)
    spread = lax.rsqrt(jnp.mean(centred * centred, axis=-1, keepdims=True) + EPS)
    return centred * spread, spread


def norm_back(normed, spread, scale, grad):
    scaled = grad * (1.0 + scale)
    back = spread * (
        scaled
        - jnp.mean(scaled, axis=-1, keepdims=True)
        - normed * jnp.mean(scaled * normed, axis=-1, keepdims=True)
    )
    return back, jnp.sum(grad, axis=0), jnp.sum(grad * normed, axis=0)


def local(
    tokens,
    image_len,
    timestep,
    caption,
    time_embed,
    mod_table,
    w_qkv,
    w_out,
    cross_q,
    cross_kv,
    cross_out,
    w_up,
    w_down,
    cotangent,
):
    sp_count = lax.axis_size("sp")
    dp_count = lax.axis_size("dp")
    place = lax.axis_index("sp")
    core = place % 2
    stream_in = tokens[0].astype(F32)
    rows, width = stream_in.shape
    factor = 1.0 / math.sqrt(width // HEADS)
    blocks = BIG // rows

    ends = jnp.cumsum(image_len[0])
    label = jnp.sum((ends <= place * rows).astype(jnp.int32))
    length = image_len[0, label]
    within = place - (ends[label] - length) // rows
    large = (length > rows).astype(jnp.int32)
    big = large.reshape(1)
    modulation = lax.dynamic_slice_in_dim(time_embed, timestep[0, label], 1, axis=0).reshape(6, width) + mod_table
    shift_one, scale_one, gate_one, shift_two, scale_two, gate_two = [modulation[i] for i in range(6)]

    to_right = [(i, i + 1) for i in range(sp_count - 1)]
    to_left = [(i + 1, i) for i in range(sp_count - 1)]
    to_pair = [(i, i ^ 1) for i in range(sp_count)]

    def image_blocks(block):
        from_left, from_right = [block], [block]
        for _ in range(blocks - 1):
            from_left.append(lax.ppermute(from_left[-1], "sp", to_right))
            from_right.append(lax.ppermute(from_right[-1], "sp", to_left))
        return [
            jnp.where(within + i < blocks, from_right[i], from_left[blocks - i])
            for i in range(1, blocks)
        ]

    normed_one, spread_one = normal(stream_in)
    first_in = (normed_one * (1.0 + scale_one) + shift_one).astype(BF)
    other_in = jnp.concatenate(image_blocks(first_in), axis=0)

    def halves(grad):
        count = sp_count
        size = grad.shape[1] // count
        even, odd = [
            jnp.concatenate([grad[:, i * size : (i + 1) * size] for i in range(c, count, 2)], axis=1)
            for c in (0, 1)
        ]
        first = core == 0
        return jnp.where(first, even, odd), jnp.where(first, odd, even)

    def pair_grad(acts, grad):
        keep, send = halves(grad)
        return weight_grad(acts, lax.ppermute(acts, "sp", to_pair), keep, lax.ppermute(send, "sp", to_pair))

    groups = [[c + 2 * z for z in range(sp_count // 2)] for c in (0, 1)]

    def spread_sum(part):
        part = lax.psum_scatter(part, "dp", scatter_dimension=0, tiled=True)
        return lax.psum_scatter(
            part, "sp", scatter_dimension=1, axis_index_groups=groups, tiled=True
        ).astype(F32)

    caption_rows = caption[0]
    live = caption_rows.shape[0]
    padded = -(-live // 128) * 128
    caption_pad = jnp.concatenate([caption_rows, jnp.zeros((padded - live, width), BF)], axis=0)
    text_kv = matmul(caption_pad, cross_kv).astype(BF)
    text_keys, text_values = text_kv[:, :width], text_kv[:, width:]
    own = matmul(first_in, w_qkv).astype(BF)
    others = matmul(other_in, w_qkv).astype(BF)
    attended, logsum = attend(big, own, others, factor)
    attn_branch = matmul(attended, w_out)
    stream_one = stream_in + gate_one * attn_branch
    cross_in = stream_one.astype(BF)
    cross_queries = matmul(cross_in, cross_q).astype(BF)
    cross_mixed = cross_attend(cross_queries, text_keys, text_values, factor, live)
    stream_two = stream_one + matmul(cross_mixed, cross_out)
    normed_two, spread_two = normal(stream_two)
    second_in = (normed_two * (1.0 + scale_two) + shift_two).astype(BF)
    hidden_pre = matmul(second_in, w_up)
    angle = math.sqrt(2.0 / math.pi) * (hidden_pre + 0.044715 * hidden_pre * hidden_pre * hidden_pre)
    bend = jnp.tanh(angle)
    hidden = (0.5 * hidden_pre * (1.0 + bend)).astype(BF)
    mlp_branch = matmul(hidden, w_down)
    stream_three = stream_two + gate_two * mlp_branch

    grad_three = cotangent[0].astype(F32)
    grad_gate_two = jnp.sum(grad_three * mlp_branch, axis=0)
    grad_mlp = (gate_two * grad_three).astype(BF)
    part_down = pair_grad(hidden, grad_mlp)
    slope = 0.5 * (1.0 + bend) + 0.5 * hidden_pre * (1.0 - bend * bend) * math.sqrt(2.0 / math.pi) * (
        1.0 + 3 * 0.044715 * hidden_pre * hidden_pre
    )
    grad_pre = (matmul_nt(grad_mlp, w_down) * slope).astype(BF)
    part_up = pair_grad(second_in, grad_pre)
    grad_second = matmul_nt(grad_pre, w_up)
    back_two, grad_shift_two, grad_scale_two = norm_back(normed_two, spread_two, scale_two, grad_second)
    grad_stream_two = grad_three + back_two
    grad_cross = grad_stream_two.astype(BF)
    part_co = pair_grad(cross_mixed, grad_cross)
    grad_mixed = matmul_nt(grad_cross, cross_out).astype(BF)
    grad_cq_rows, grad_text_keys, grad_text_values = cross_grad(
        cross_queries, grad_mixed, text_keys, text_values, factor, live
    )
    grad_text = jnp.concatenate([grad_text_keys[:live], grad_text_values[:live]], axis=1)
    part_cq = pair_grad(cross_in, grad_cq_rows)
    grad_stream_one = grad_stream_two + matmul_nt(grad_cq_rows, cross_q)
    grad_gate_one = jnp.sum(grad_stream_one * attn_branch, axis=0)
    grad_attn = (gate_one * grad_stream_one).astype(BF)
    part_out = pair_grad(attended, grad_attn)
    grad_back = matmul_nt(grad_attn, w_out).astype(BF)

    column = jnp.arange(width, dtype=jnp.int32)[:, None] // (width // HEADS)
    pick = (column + HEADS == jnp.arange(128, dtype=jnp.int32)[None, :]).astype(F32)
    inner = jnp.dot(
        grad_back.astype(F32) * attended.astype(F32), pick, precision=lax.Precision.HIGHEST
    )
    stat = logsum + inner
    turned = stat.T[: 2 * HEADS].reshape(4, 8, rows).transpose(1, 0, 2).reshape(8, 4 * rows)
    high = lax.reduce_precision(turned, exponent_bits=8, mantissa_bits=7)
    both = jnp.concatenate([high, turned - high], axis=0).astype(BF)
    both = jnp.concatenate([both, jnp.zeros((16, width - 4 * rows), BF)], axis=1)
    pack = jnp.concatenate([grad_back, both], axis=0)
    packs = jnp.stack(image_blocks(pack))
    grad_queries = query_grad(big, own, others, grad_back, stat, factor)
    grad_keys, grad_values = key_grad(big, own, others, pack, packs, factor)
    grad_proj = jnp.concatenate([grad_queries, grad_keys, grad_values], axis=1)
    part_qkv = pair_grad(first_in, grad_proj)
    grad_first = matmul_nt(grad_proj, w_qkv)
    back_one, grad_shift_one, grad_scale_one = norm_back(normed_one, spread_one, scale_one, grad_first)
    grad_tokens = grad_stream_one + back_one

    final_down = spread_sum(part_down)
    final_up = spread_sum(part_up)
    final_co = spread_sum(part_co)
    final_cq = spread_sum(part_cq)
    final_out = spread_sum(part_out)
    final_qkv = spread_sum(part_qkv)
    text_part = lax.psum_scatter(grad_text, "sp", scatter_dimension=1, tiled=True).astype(BF)
    part_ckv = matmul_tn(caption_rows, text_part).astype(BF)
    final_ckv = lax.psum_scatter(part_ckv, "dp", scatter_dimension=0, tiled=True).astype(F32)
    table = jnp.concatenate(
        [grad_shift_one, grad_scale_one, grad_gate_one, grad_shift_two, grad_scale_two, grad_gate_two]
    )
    arranged = table.reshape(dp_count, sp_count, -1).transpose(1, 0, 2).reshape(-1)
    final_table = lax.psum_scatter(
        lax.psum_scatter(arranged, "sp", scatter_dimension=0, tiled=True),
        "dp",
        scatter_dimension=0,
        tiled=True,
    )
    return (
        stream_three[None],
        grad_tokens[None],
        final_table,
        final_qkv,
        final_out,
        final_cq,
        final_ckv,
        final_co,
        final_up,
        final_down,
    )


def solution(mesh):
    return jax.shard_map(
        local,
        mesh=mesh,
        in_specs=(
            P("dp", "sp", None),
            P("dp", None),
            P("dp", None),
            P("dp", None, None),
            P(),
            P(),
            P(),
            P(),
            P(),
            P(),
            P(),
            P(),
            P(),
            P("dp", "sp", None),
        ),
        out_specs=(
            P("dp", "sp", None),
            P("dp", "sp", None),
            P(("dp", "sp")),
            P("dp", "sp"),
            P("dp", "sp"),
            P("dp", "sp"),
            P("dp", "sp"),
            P("dp", "sp"),
            P("dp", "sp"),
            P("dp", "sp"),
        ),
        check_vma=False,
    )
```

```python
import functools
import math

import jax
import jax.numpy as jnp
from jax import lax
from jax.experimental import pallas as pl
from jax.experimental.pallas import tpu as pltpu
from jax.sharding import PartitionSpec as P

HEADS = 16
BIG = 1024
EPS = 1e-06
BIGNEG = -1e30
LOG2E = 1.4426950408889634
BF = jnp.bfloat16
F32 = jnp.float32
WIN = 256
VMEM_LIMIT = 48 * 1024 * 1024


def matmul(left, right):
    return jnp.dot(left, right, preferred_element_type=F32)


def matmul_tn(left, right):
    return lax.dot_general(left, right, (((0,), (0,)), ((), ())), preferred_element_type=F32)


def matmul_nt(left, right):
    return lax.dot_general(left, right, (((1,), (1,)), ((), ())), preferred_element_type=F32)


def head_window(head, width):
    size = width // HEADS
    low = head * size
    start = pl.multiple_of(jnp.minimum(low // 128 * 128, width - WIN), 128)
    lane = lax.broadcasted_iota(jnp.int32, (1, WIN), 1) + start
    mask = jnp.logical_and(lane >= low, lane < low + size)
    return pl.ds(start, WIN), mask


def keep_columns(ref, win, mask, value):
    ref[:, win] = jnp.where(mask, value, ref[:, win])


def attend_kernel(big_ref, q_ref, k0_ref, v0_ref, k1_ref, v1_ref, out_ref, lse_ref, *, factor):
    width = q_ref.shape[1]
    scale = factor * LOG2E

    def run(pairs):
        def one_head(head, carry):
            win, mask = head_window(head, width)
            query = q_ref[:, win] * mask.astype(BF)
            scores = [matmul_nt(query, key[:, win]) for key, _ in pairs]
            top = functools.reduce(jnp.maximum, [jnp.max(s, axis=1, keepdims=True) for s in scores])
            raised = [jnp.exp2((s - top) * scale) for s in scores]
            total = sum(jnp.sum(r, axis=1, keepdims=True) for r in raised)
            inverse = 1.0 / total
            result = sum(
                matmul((r * inverse).astype(BF), value[:, win])
                for r, (_, value) in zip(raised, pairs)
            )
            keep_columns(out_ref, win, mask, result.astype(BF))
            lane = lax.broadcasted_iota(jnp.int32, (1, 128), 1)
            lse = top * scale + jnp.log2(total)
            lse_ref[...] = jnp.where(lane == head, lse, lse_ref[...])
            return carry

        lax.fori_loop(0, HEADS, one_head, 0, unroll=2)

    lse_ref[...] = jnp.zeros_like(lse_ref)

    @pl.when(big_ref[0] == 1)
    def _():
        run([(k0_ref, v0_ref), (k1_ref, v1_ref)])

    @pl.when(big_ref[0] == 0)
    def _():
        run([(k0_ref, v0_ref)])


def query_grad_kernel(
    big_ref, q_ref, k0_ref, v0_ref, k1_ref, v1_ref, do_ref, stat_ref, out_ref, *, factor
):
    width = q_ref.shape[1]
    scale = factor * LOG2E

    def run(pairs):
        def one_head(head, carry):
            win, mask = head_window(head, width)
            keep = mask.astype(BF)
            query = q_ref[:, win] * keep
            grad = do_ref[:, win] * keep
            lane = lax.broadcasted_iota(jnp.int32, (1, 128), 1)
            stat = stat_ref[...]
            lse = jnp.sum(jnp.where(lane == head, stat, 0.0), axis=1, keepdims=True)
            delta = jnp.sum(jnp.where(lane == head + HEADS, stat, 0.0), axis=1, keepdims=True)
            total = None
            for key, value in pairs:
                prob = jnp.exp2(matmul_nt(query, key[:, win]) * scale - lse)
                grad_prob = matmul_nt(grad, value[:, win])
                grad_score = (prob * (grad_prob - delta)).astype(BF)
                part = matmul(grad_score, key[:, win])
                total = part if total is None else total + part
            keep_columns(out_ref, win, mask, (total * factor).astype(BF))
            return carry

        lax.fori_loop(0, HEADS, one_head, 0, unroll=2)

    @pl.when(big_ref[0] == 1)
    def _():
        run([(k0_ref, v0_ref), (k1_ref, v1_ref)])

    @pl.when(big_ref[0] == 0)
    def _():
        run([(k0_ref, v0_ref)])


def key_grad_kernel(
    big_ref, k_ref, v_ref, q0_ref, q1_ref, pack0_ref, pack1_ref, dk_ref, dv_ref, stats, *, factor
):
    width = k_ref.shape[1]
    rows = k_ref.shape[0]
    scale = factor * LOG2E
    blocks = 1 + pack1_ref.shape[0]

    def unpack(block, pack):
        both = pack[rows : rows + 16, :].astype(F32)
        joined = both[:8] + both[8:]
        for group in range(4):
            stats[block, 8 * group : 8 * group + 8, :] = joined[:, group * rows : group * rows + rows]

    unpack(0, pack0_ref[...])
    for block in range(1, blocks):
        unpack(block, pack1_ref[block - 1])

    def run(count):
        def one_head(head, carry):
            win, mask = head_window(head, width)
            keep = mask.astype(BF)
            key = k_ref[:, win] * keep
            value = v_ref[:, win] * keep
            grad_key = grad_value = None
            for block in range(count):
                if block == 0:
                    query, grad = q0_ref[:, win], pack0_ref[0:rows, win]
                else:
                    query = q1_ref[(block - 1) * rows : block * rows, win]
                    grad = pack1_ref[block - 1, 0:rows, win]
                lse = stats[block, pl.ds(head, 1), :]
                delta = stats[block, pl.ds(head + HEADS, 1), :]
                prob = jnp.exp2(matmul_nt(key, query) * scale - lse)
                grad_prob = matmul_nt(value, grad)
                grad_score = (prob * (grad_prob - delta)).astype(BF)
                part_value = matmul(prob.astype(BF), grad)
                part_key = matmul(grad_score, query)
                grad_value = part_value if block == 0 else grad_value + part_value
                grad_key = part_key if block == 0 else grad_key + part_key
            keep_columns(dk_ref, win, mask, (grad_key * factor).astype(BF))
            keep_columns(dv_ref, win, mask, grad_value.astype(BF))
            return carry

        lax.fori_loop(0, HEADS, one_head, 0, unroll=2)

    @pl.when(big_ref[0] == 1)
    def _():
        run(blocks)

    @pl.when(big_ref[0] == 0)
    def _():
        run(1)


def text_probs(query, key, scale, live):
    scores = matmul_nt(query, key)
    lane = lax.broadcasted_iota(jnp.int32, (1, scores.shape[1]), 1)
    scores = jnp.where(lane < live, scores, BIGNEG)
    raised = jnp.exp2((scores - jnp.max(scores, axis=1, keepdims=True)) * scale)
    return raised * (1.0 / jnp.sum(raised, axis=1, keepdims=True))


def cross_kernel(q_ref, k_ref, v_ref, out_ref, *, factor, live):
    width = q_ref.shape[1]

    def one_head(head, carry):
        win, mask = head_window(head, width)
        query = q_ref[:, win] * mask.astype(BF)
        probs = text_probs(query, k_ref[:, win], factor * LOG2E, live)
        keep_columns(out_ref, win, mask, matmul(probs.astype(BF), v_ref[:, win]).astype(BF))
        return carry

    lax.fori_loop(0, HEADS, one_head, 0, unroll=4)


def cross_grad_kernel(q_ref, g_ref, k_ref, v_ref, dq_ref, dk_ref, dv_ref, *, factor, live):
    width = q_ref.shape[1]

    def one_head(head, carry):
        win, mask = head_window(head, width)
        keep = mask.astype(BF)
        query = q_ref[:, win]
        grad = g_ref[:, win]
        key = k_ref[:, win]
        probs = text_probs(query * keep, key, factor * LOG2E, live)
        grad_probs = matmul_nt(grad * keep, v_ref[:, win])
        inner = jnp.sum(probs * grad_probs, axis=1, keepdims=True)
        grad_scores = (probs * (grad_probs - inner)).astype(BF)
        keep_columns(dq_ref, win, mask, (matmul(grad_scores, key) * factor).astype(BF))
        keep_columns(dk_ref, win, mask, matmul_tn(grad_scores, query) * factor)
        keep_columns(dv_ref, win, mask, matmul_tn(probs.astype(BF), grad))
        return carry

    lax.fori_loop(0, HEADS, one_head, 0, unroll=4)


def weight_grad_kernel(order_ref, *refs, count):
    sources, outs, turned = refs[: 4 * count], refs[4 * count : -1], refs[-1]
    step = pl.program_id(1)
    for item in range(count):

        @pl.when(pl.program_id(0) == item)
        def _(item=item):
            x0_ref, x1_ref, g0_ref, g1_ref = sources[4 * item : 4 * item + 4]
            rows, width = x0_ref.shape

            @pl.when(step == 0)
            def _():
                for part, ref in enumerate((x0_ref, x1_ref)):
                    for low in range(0, width, 128):
                        turned[low : low + 128, part * rows : part * rows + rows] = ref[
                            :, low : low + 128
                        ].T

            tall = width // 4
            here = pl.ds(pl.multiple_of(order_ref[step] * tall, 16), tall)
            total = matmul(turned[here, 0:rows], g0_ref[...])
            total = (total + matmul(turned[here, rows:], g1_ref[...])).astype(BF)
            if len(outs) == 1:
                outs[0][0, 0] = total
            else:

                @pl.when(step < 2)
                def _():
                    outs[0][0, 0] = total

                @pl.when(step >= 2)
                def _():
                    outs[1][0, 0] = total


def mlp_kernel(x_ref, g_ref, up_ref, down_ref, hidden_ref, pre_ref, branch_ref, grad_ref):
    step = pl.program_id(0)
    up, down = up_ref[...], down_ref[...]
    pre = matmul(x_ref[...], up)
    root = math.sqrt(2.0 / math.pi)
    square = pre * pre
    bend = jnp.tanh(root * (pre + 0.044715 * square * pre))
    hidden = (0.5 * pre * (1.0 + bend)).astype(BF)
    slope = 0.5 * (1.0 + bend) + 0.5 * pre * (1.0 - bend * bend) * root * (1.0 + 3 * 0.044715 * square)
    grad_pre = (matmul_nt(g_ref[...], down) * slope).astype(BF)
    hidden_ref[...] = hidden
    pre_ref[...] = grad_pre
    branch = matmul(hidden, down)
    grad = matmul_nt(grad_pre, up)

    @pl.when(step == 0)
    def _():
        branch_ref[...] = branch
        grad_ref[...] = grad

    @pl.when(step > 0)
    def _():
        branch_ref[...] += branch
        grad_ref[...] += grad


def whole(shape):
    return pl.BlockSpec(shape, lambda *_: (0,) * len(shape))


def params():
    return pltpu.CompilerParams(vmem_limit_bytes=VMEM_LIMIT)


def cost(flops, nbytes, exps=0):
    return pl.CostEstimate(flops=int(flops), bytes_accessed=int(nbytes), transcendentals=int(exps))


def part_spec(rows, width, at):
    return pl.BlockSpec((rows, width), lambda i, *_: (0, at))


def attend(big, own, others, factor):
    rows, width = own.shape[0], own.shape[1] // 3
    far = others.shape[0]
    return pl.pallas_call(
        functools.partial(attend_kernel, factor=factor),
        grid_spec=pltpu.PrefetchScalarGridSpec(
            num_scalar_prefetch=1,
            grid=(1,),
            in_specs=[
                part_spec(rows, width, 0),
                part_spec(rows, width, 1),
                part_spec(rows, width, 2),
                part_spec(far, width, 1),
                part_spec(far, width, 2),
            ],
            out_specs=[whole((rows, width)), whole((rows, 128))],
        ),
        out_shape=[
            jax.ShapeDtypeStruct((rows, width), BF),
            jax.ShapeDtypeStruct((rows, 128), F32),
        ],
        compiler_params=params(),
        cost_estimate=cost(4 * HEADS * rows * (rows + far) * WIN, 6 * far * width, HEADS * rows * far),
    )(big, own, own, own, others, others)


def query_grad(big, own, others, grad, stat, factor):
    rows, width = own.shape[0], own.shape[1] // 3
    far = others.shape[0]
    return pl.pallas_call(
        functools.partial(query_grad_kernel, factor=factor),
        grid_spec=pltpu.PrefetchScalarGridSpec(
            num_scalar_prefetch=1,
            grid=(1,),
            in_specs=[
                part_spec(rows, width, 0),
                part_spec(rows, width, 1),
                part_spec(rows, width, 2),
                part_spec(far, width, 1),
                part_spec(far, width, 2),
                whole((rows, width)),
                whole((rows, 128)),
            ],
            out_specs=whole((rows, width)),
        ),
        out_shape=jax.ShapeDtypeStruct((rows, width), BF),
        compiler_params=params(),
        cost_estimate=cost(6 * HEADS * rows * (rows + far) * WIN, 6 * far * width, HEADS * rows * far),
    )(big, own, own, own, others, others, grad, stat)


def key_grad(big, own, others, pack, packs, factor):
    rows, width = own.shape[0], own.shape[1] // 3
    far = others.shape[0]
    return pl.pallas_call(
        functools.partial(key_grad_kernel, factor=factor),
        grid_spec=pltpu.PrefetchScalarGridSpec(
            num_scalar_prefetch=1,
            grid=(1,),
            in_specs=[
                part_spec(rows, width, 1),
                part_spec(rows, width, 2),
                part_spec(rows, width, 0),
                part_spec(far, width, 0),
                whole(pack.shape),
                whole(packs.shape),
            ],
            out_specs=[whole((rows, width))] * 2,
            scratch_shapes=[pltpu.VMEM((1 + packs.shape[0], 2 * HEADS, rows), F32)],
        ),
        out_shape=[jax.ShapeDtypeStruct((rows, width), BF)] * 2,
        compiler_params=params(),
        cost_estimate=cost(8 * HEADS * rows * (rows + far) * WIN, 6 * far * width, HEADS * rows * far),
    )(big, own, own, own, others, pack, packs)


def cross_attend(queries, keys, values, factor, live):
    rows, width = queries.shape
    return pl.pallas_call(
        functools.partial(cross_kernel, factor=factor, live=live),
        out_shape=jax.ShapeDtypeStruct((rows, width), BF),
        compiler_params=params(),
        cost_estimate=cost(4 * HEADS * rows * 128 * WIN, 6 * rows * width, HEADS * rows * 128),
    )(queries, keys, values)


def cross_grad(queries, grad, keys, values, factor, live):
    rows, width = queries.shape
    return pl.pallas_call(
        functools.partial(cross_grad_kernel, factor=factor, live=live),
        out_shape=[
            jax.ShapeDtypeStruct((rows, width), BF),
            jax.ShapeDtypeStruct(keys.shape, F32),
            jax.ShapeDtypeStruct(keys.shape, F32),
        ],
        compiler_params=params(),
        cost_estimate=cost(10 * HEADS * rows * 128 * WIN, 12 * rows * width, HEADS * rows * 128),
    )(queries, grad, keys, values)


def weight_grad(order, sources, halved):
    count = len(sources)
    rows, width = sources[0][0].shape
    depth = sources[0][2].shape[1]
    tall = width // 4
    block = (1, 1, tall, depth)
    if halved:
        out_specs = [
            pl.BlockSpec(block, lambda k, s, _: (k, jnp.minimum(s, 1), 0, 0)),
            pl.BlockSpec(block, lambda k, s, _: (k, jnp.maximum(s - 2, 0), 0, 0)),
        ]
        out_shape = [jax.ShapeDtypeStruct((count, 2, tall, depth), BF)] * 2
    else:
        out_specs = [pl.BlockSpec(block, lambda k, s, _: (k, s, 0, 0))]
        out_shape = [jax.ShapeDtypeStruct((count, 4, tall, depth), BF)]
    return pl.pallas_call(
        functools.partial(weight_grad_kernel, count=count),
        grid_spec=pltpu.PrefetchScalarGridSpec(
            num_scalar_prefetch=1,
            grid=(count, 4),
            in_specs=([whole((rows, width))] * 2 + [whole((rows, depth))] * 2) * count,
            out_specs=out_specs,
            scratch_shapes=[pltpu.VMEM((width, 2 * rows), BF)],
        ),
        out_shape=out_shape,
        compiler_params=params(),
        cost_estimate=cost(
            4 * count * rows * width * depth, count * (2 * width * depth + 4 * rows * (width + depth))
        ),
    )(order, *[array for source in sources for array in source])


def mlp(inputs, grad, w_up, w_down):
    rows, width = inputs.shape
    units = w_up.shape[1]
    tile = 512
    return pl.pallas_call(
        mlp_kernel,
        grid=(units // tile,),
        in_specs=[
            whole((rows, width)),
            whole((rows, width)),
            pl.BlockSpec((width, tile), lambda i: (0, i)),
            pl.BlockSpec((tile, width), lambda i: (i, 0)),
        ],
        out_specs=[pl.BlockSpec((rows, tile), lambda i: (0, i))] * 2 + [whole((rows, width))] * 2,
        out_shape=[jax.ShapeDtypeStruct((rows, units), BF)] * 2
        + [jax.ShapeDtypeStruct((rows, width), F32)] * 2,
        compiler_params=params(),
        cost_estimate=cost(8 * rows * width * units, 4 * width * units, rows * units),
    )(inputs, grad, w_up, w_down)


def normal(stream):
    centred = stream - jnp.mean(stream, axis=-1, keepdims=True)
    spread = lax.rsqrt(jnp.mean(centred * centred, axis=-1, keepdims=True) + EPS)
    return centred * spread, spread


def norm_back(normed, spread, scale, grad):
    scaled = grad * (1.0 + scale)
    back = spread * (
        scaled
        - jnp.mean(scaled, axis=-1, keepdims=True)
        - normed * jnp.mean(scaled * normed, axis=-1, keepdims=True)
    )
    return back, jnp.sum(grad, axis=0), jnp.sum(grad * normed, axis=0)


def local(
    tokens,
    image_len,
    timestep,
    caption,
    time_embed,
    mod_table,
    w_qkv,
    w_out,
    cross_q,
    cross_kv,
    cross_out,
    w_up,
    w_down,
    cotangent,
):
    sp_count = lax.axis_size("sp")
    dp_count = lax.axis_size("dp")
    place = lax.axis_index("sp")
    row_place = lax.axis_index("dp")
    core = place % 2
    rows, width = tokens.shape[1:]
    factor = 1.0 / math.sqrt(width // HEADS)
    blocks = BIG // rows
    assert blocks == 4

    lengths = image_len[0]
    slots = jnp.arange(lengths.shape[0], dtype=jnp.int32)
    ends = jnp.sum(jnp.where(slots[None, :] <= slots[:, None], lengths[None, :], 0), axis=1)

    def image_of(at):
        before = ends <= at * rows
        begin = jnp.max(jnp.where(before, ends, 0))
        label = jnp.sum(before.astype(jnp.int32))
        length = jnp.sum(jnp.where(slots == label, lengths, 0))
        return label, at - begin // rows, length > rows

    label, within, large = image_of(place)
    pair_within = image_of(place + 1 - 2 * core)[1]
    big = large.astype(jnp.int32).reshape(1)

    pairs = [(i, i ^ 1) for i in range(sp_count)]
    others = [(i, i + 1) for i in range(1, sp_count - 1, 2)] + [(i + 1, i) for i in range(1, sp_count - 1, 2)]
    ahead = [(i, i + 2) for i in range(sp_count - 2)]
    back = [(i + 2, i) for i in range(sp_count - 2)]

    def image_blocks(block):
        pair = lax.ppermute(block, "sp", pairs)
        from_back = lax.ppermute(block, "sp", ahead)
        from_ahead = lax.ppermute(block, "sp", back)
        wants_ahead = jnp.where(core == 0, pair_within + 1 < blocks, pair_within + 3 < blocks)
        second = lax.ppermute(jnp.where(wants_ahead, from_ahead, from_back), "sp", pairs)
        third = lax.ppermute(jnp.where(core == 1, from_back, from_ahead), "sp", others)
        take_pair = jnp.where(core == 0, within + 1 < blocks, within >= 1)
        return [
            second,
            jnp.where(take_pair, pair, third),
            jnp.where(within + 2 < blocks, from_ahead, from_back),
        ]

    def swap(array):
        return lax.ppermute(array, "sp", pairs)

    token_blocks = image_blocks(tokens[0])

    pick = (jnp.sum(jnp.where(slots == label, timestep[0], 0)) == jnp.arange(time_embed.shape[0])).astype(jnp.int32)
    step = jnp.sum(pick * jnp.arange(time_embed.shape[0], dtype=jnp.int32))
    modulation = lax.dynamic_slice_in_dim(time_embed, step, 1, axis=0).reshape(6, width) + mod_table
    shift_one, scale_one, gate_one, shift_two, scale_two, gate_two = [modulation[i] for i in range(6)]

    def first_norm(block):
        normed, spread = normal(block.astype(F32))
        return normed, spread, (normed * (1.0 + scale_one) + shift_one).astype(BF)

    stream_in = tokens[0].astype(F32)
    normed_one, spread_one, first_in = first_norm(tokens[0])
    other_in = first_norm(jnp.concatenate(token_blocks, axis=0))[2]

    def halves(grad):
        size = grad.shape[1] // sp_count
        even, odd = [
            jnp.concatenate([grad[:, i * size : (i + 1) * size] for i in range(c, sp_count, 2)], axis=1)
            for c in (0, 1)
        ]
        first = core == 0
        return jnp.where(first, even, odd), jnp.where(first, odd, even)

    def add(*terms):
        return sum(term.astype(F32) for term in terms)

    def spread_rows(sources, low_first):
        if dp_count == 4:
            first, second = (0, 1) if low_first else (1, 0)
            mine_first = (row_place >> first) & 1
            mine_second = (row_place >> second) & 1
            order = jnp.stack(
                [
                    ((1 - mine_first if s < 2 else mine_first) << first) + ((s % 2) << second)
                    for s in range(4)
                ]
            )
            send, keep = weight_grad(order, sources, True)
            got = lax.ppermute(send, "dp", [(i, i ^ (1 << first)) for i in range(4)])
            at = lambda array, i: lax.dynamic_index_in_dim(array, i, 1, keepdims=False)
            send = add(at(keep, 1 - mine_second), at(got, 1 - mine_second)).astype(BF)
            more = lax.ppermute(send, "dp", [(i, i ^ (1 << second)) for i in range(4)])
            return add(at(keep, mine_second), at(got, mine_second), more)
        parts = weight_grad(jnp.arange(4, dtype=jnp.int32), sources, False)[0]
        parts = parts.reshape(len(sources), dp_count, -1, parts.shape[-1])
        bit = dp_count // 2
        while bit:
            mine = (row_place // bit) % 2
            parts = parts.reshape(len(sources), 2, bit, -1, parts.shape[-1])
            at = lambda i: lax.dynamic_index_in_dim(parts, i, 1, keepdims=False)
            got = lax.ppermute(at(1 - mine), "dp", [(i, i ^ bit) for i in range(dp_count)])
            parts = add(at(mine), got).astype(BF)
            bit //= 2
        return parts[:, 0]

    def spread_columns(part):
        chips = sp_count // 2
        size = part.shape[-1] // chips
        slices = [part[..., z * size : (z + 1) * size] for z in range(chips)]
        bit = 1
        while bit < chips:
            low = (place // 2 // bit) % 2 == 0
            even = jnp.concatenate(slices[0::2], axis=-1).astype(BF)
            odd = jnp.concatenate(slices[1::2], axis=-1).astype(BF)
            got = lax.ppermute(
                jnp.where(low, odd, even), "sp", [(i, i ^ (2 * bit)) for i in range(sp_count)]
            )
            part = add(jnp.where(low, even, odd), got)
            slices = [part[..., z * size : (z + 1) * size] for z in range(len(slices) // 2)]
            bit *= 2
        return slices[0]

    def spread_vector(vector):
        for axis, name, count, mine in ((1, "sp", sp_count, place), (0, "dp", dp_count, row_place)):
            bit = count // 2
            while bit:
                shape = vector.shape
                split = vector.reshape(shape[:axis] + (2, bit) + shape[axis + 1 :])
                at = lambda i: lax.dynamic_index_in_dim(split, i, axis, keepdims=False)
                own = (mine // bit) % 2
                got = lax.ppermute(at(1 - own), name, [(i, i ^ bit) for i in range(count)])
                vector = at(own) + got
                bit //= 2
        return vector.reshape(-1)

    caption_rows = caption[0]
    live = caption_rows.shape[0]
    padded = -(-live // 128) * 128
    caption_pad = jnp.concatenate([caption_rows, jnp.zeros((padded - live, width), BF)], axis=0)
    text_kv = matmul(caption_pad, cross_kv).astype(BF)
    text_keys, text_values = text_kv[:, :width], text_kv[:, width:]
    grad_three = cotangent[0].astype(F32)
    grad_mlp = (gate_two * grad_three).astype(BF)
    mlp_keep, mlp_send = halves(grad_mlp)
    mlp_got = swap(mlp_send)
    first_pair = swap(first_in)
    own = matmul(first_in, w_qkv).astype(BF)
    others_qkv = matmul(other_in, w_qkv).astype(BF)
    attended, logsum = attend(big, own, others_qkv, factor)
    attn_branch = matmul(attended, w_out)
    stream_one = stream_in + gate_one * attn_branch
    cross_in = stream_one.astype(BF)
    cross_queries = matmul(cross_in, cross_q).astype(BF)
    cross_mixed = cross_attend(cross_queries, text_keys, text_values, factor, live)
    stream_two = stream_one + matmul(cross_mixed, cross_out)
    normed_two, spread_two = normal(stream_two)
    second_in = (normed_two * (1.0 + scale_two) + shift_two).astype(BF)
    second_pair = swap(second_in)
    hidden, grad_pre, mlp_branch, grad_second = mlp(second_in, grad_mlp, w_up, w_down)
    stream_three = stream_two + gate_two * mlp_branch

    grad_gate_two = jnp.sum(grad_three * mlp_branch, axis=0)
    rows_down = spread_rows([(hidden, swap(hidden), mlp_keep, mlp_got)], True)
    pre_keep, pre_send = halves(grad_pre)
    rows_up = spread_rows([(second_in, second_pair, pre_keep, swap(pre_send))], False)
    back_two, grad_shift_two, grad_scale_two = norm_back(normed_two, spread_two, scale_two, grad_second)
    grad_stream_two = grad_three + back_two
    grad_cross = grad_stream_two.astype(BF)
    grad_mixed = matmul_nt(grad_cross, cross_out).astype(BF)
    grad_cq_rows, grad_text_keys, grad_text_values = cross_grad(
        cross_queries, grad_mixed, text_keys, text_values, factor, live
    )
    grad_text = jnp.concatenate([grad_text_keys[:live], grad_text_values[:live]], axis=1)
    grad_stream_one = grad_stream_two + matmul_nt(grad_cq_rows, cross_q)
    grad_gate_one = jnp.sum(grad_stream_one * attn_branch, axis=0)
    grad_attn = (gate_one * grad_stream_one).astype(BF)
    grad_back = matmul_nt(grad_attn, w_out).astype(BF)

    column = jnp.arange(width, dtype=jnp.int32)[:, None] // (width // HEADS)
    pick = (column + HEADS == jnp.arange(128, dtype=jnp.int32)[None, :]).astype(F32)
    inner = jnp.dot(
        grad_back.astype(F32) * attended.astype(F32), pick, precision=lax.Precision.HIGHEST
    )
    stat = logsum + inner
    turned = stat.T[: 2 * HEADS].reshape(4, 8, rows).transpose(1, 0, 2).reshape(8, 4 * rows)
    high = lax.reduce_precision(turned, exponent_bits=8, mantissa_bits=7)
    both = jnp.concatenate([high, turned - high], axis=0).astype(BF)
    both = jnp.concatenate([both, jnp.zeros((16, width - 4 * rows), BF)], axis=1)
    pack = jnp.concatenate([grad_back, both], axis=0)
    packs = jnp.stack(image_blocks(pack))

    small = []
    for acts, grad in ((cross_mixed, grad_cross), (cross_in, grad_cq_rows), (attended, grad_attn)):
        keep, send = halves(grad)
        small.append((acts, swap(acts), keep, swap(send)))
    rows_small = spread_rows(small, True)

    grad_queries = query_grad(big, own, others_qkv, grad_back, stat, factor)
    grad_keys, grad_values = key_grad(big, own, others_qkv, pack, packs, factor)
    grad_proj = jnp.concatenate([grad_queries, grad_keys, grad_values], axis=1)
    proj_keep, proj_send = halves(grad_proj)
    rows_qkv = spread_rows([(first_in, first_pair, proj_keep, swap(proj_send))], False)
    grad_first = matmul_nt(grad_proj, w_qkv)
    back_one, grad_shift_one, grad_scale_one = norm_back(normed_one, spread_one, scale_one, grad_first)
    grad_tokens = grad_stream_one + back_one

    final_down = spread_columns(rows_down)[0]
    final_up = spread_columns(rows_up)[0]
    final_small = spread_columns(rows_small)
    final_qkv = spread_columns(rows_qkv)[0]
    text_part = lax.psum_scatter(grad_text, "sp", scatter_dimension=1, tiled=True).astype(BF)
    part_ckv = matmul_tn(caption_rows, text_part).astype(BF)
    final_ckv = lax.psum_scatter(part_ckv, "dp", scatter_dimension=0, tiled=True).astype(F32)
    table = jnp.concatenate(
        [grad_shift_one, grad_scale_one, grad_gate_one, grad_shift_two, grad_scale_two, grad_gate_two]
    )
    final_table = spread_vector(table.reshape(dp_count, sp_count, -1))
    return (
        stream_three[None],
        grad_tokens[None],
        final_table,
        final_qkv,
        final_small[2],
        final_small[1],
        final_ckv,
        final_small[0],
        final_up,
        final_down,
    )


def solution(mesh):
    return jax.shard_map(
        local,
        mesh=mesh,
        in_specs=(
            P("dp", "sp", None),
            P("dp", None),
            P("dp", None),
            P("dp", None, None),
            P(),
            P(),
            P(),
            P(),
            P(),
            P(),
            P(),
            P(),
            P(),
            P("dp", "sp", None),
        ),
        out_specs=(
            P("dp", "sp", None),
            P("dp", "sp", None),
            P(("dp", "sp")),
            P("dp", "sp"),
            P("dp", "sp"),
            P("dp", "sp"),
            P("dp", "sp"),
            P("dp", "sp"),
            P("dp", "sp"),
            P("dp", "sp"),
        ),
        check_vma=False,
    )
```

```python
import functools
import math

import jax
import jax.numpy as jnp
from jax import lax
from jax.experimental import pallas as pl
from jax.experimental.pallas import tpu as pltpu
from jax.sharding import PartitionSpec as P

HEADS = 16
BIG = 1024
EPS = 1e-06
BIGNEG = -1e30
LOG2E = 1.4426950408889634
BF = jnp.bfloat16
F32 = jnp.float32
WIN = 256
COST_SCALE = 0.1
VMEM_LIMIT = 28 * 1024 * 1024


def matmul(left, right):
    return jnp.dot(left, right, preferred_element_type=F32)


def matmul_tn(left, right):
    return lax.dot_general(left, right, (((0,), (0,)), ((), ())), preferred_element_type=F32)


def matmul_nt(left, right):
    return lax.dot_general(left, right, (((1,), (1,)), ((), ())), preferred_element_type=F32)


def head_window(head, width):
    size = width // HEADS
    low = head * size
    start = pl.multiple_of(jnp.minimum(low // 128 * 128, width - WIN), 128)
    lane = lax.broadcasted_iota(jnp.int32, (1, WIN), 1) + start
    mask = jnp.logical_and(lane >= low, lane < low + size)
    return pl.ds(start, WIN), mask


def keep_columns(ref, win, mask, value):
    ref[:, win] = jnp.where(mask, value, ref[:, win])


def attend_kernel(big_ref, q_ref, k0_ref, v0_ref, k1_ref, v1_ref, out_ref, lse_ref, *, factor):
    width = q_ref.shape[1]
    scale = factor * LOG2E

    def run(pairs):
        def one_head(head, carry):
            win, mask = head_window(head, width)
            query = q_ref[:, win] * mask.astype(BF)
            scores = [matmul_nt(query, key[:, win]) for key, _ in pairs]
            top = functools.reduce(jnp.maximum, [jnp.max(s, axis=1, keepdims=True) for s in scores])
            raised = [jnp.exp2((s - top) * scale) for s in scores]
            total = sum(jnp.sum(r, axis=1, keepdims=True) for r in raised)
            inverse = 1.0 / total
            result = sum(
                matmul((r * inverse).astype(BF), value[:, win])
                for r, (_, value) in zip(raised, pairs)
            )
            keep_columns(out_ref, win, mask, result.astype(BF))
            lane = lax.broadcasted_iota(jnp.int32, (1, 128), 1)
            lse = top * scale + jnp.log2(total)
            lse_ref[...] = jnp.where(lane == head, lse, lse_ref[...])
            return carry

        lax.fori_loop(0, HEADS, one_head, 0, unroll=4)

    lse_ref[...] = jnp.zeros_like(lse_ref)

    @pl.when(big_ref[0] == 1)
    def _():
        run([(k0_ref, v0_ref), (k1_ref, v1_ref)])

    @pl.when(big_ref[0] == 0)
    def _():
        run([(k0_ref, v0_ref)])


def query_grad_kernel(
    big_ref, q_ref, k0_ref, v0_ref, k1_ref, v1_ref, do_ref, stat_ref, out_ref, *, factor
):
    width = q_ref.shape[1]
    scale = factor * LOG2E

    def run(pairs):
        def one_head(head, carry):
            win, mask = head_window(head, width)
            keep = mask.astype(BF)
            query = q_ref[:, win] * keep
            grad = do_ref[:, win] * keep
            lane = lax.broadcasted_iota(jnp.int32, (1, 128), 1)
            stat = stat_ref[...]
            lse = jnp.sum(jnp.where(lane == head, stat, 0.0), axis=1, keepdims=True)
            delta = jnp.sum(jnp.where(lane == head + HEADS, stat, 0.0), axis=1, keepdims=True)
            total = None
            for key, value in pairs:
                prob = jnp.exp2(matmul_nt(query, key[:, win]) * scale - lse)
                grad_prob = matmul_nt(grad, value[:, win])
                grad_score = (prob * (grad_prob - delta)).astype(BF)
                part = matmul(grad_score, key[:, win])
                total = part if total is None else total + part
            keep_columns(out_ref, win, mask, (total * factor).astype(BF))
            return carry

        lax.fori_loop(0, HEADS, one_head, 0, unroll=4)

    @pl.when(big_ref[0] == 1)
    def _():
        run([(k0_ref, v0_ref), (k1_ref, v1_ref)])

    @pl.when(big_ref[0] == 0)
    def _():
        run([(k0_ref, v0_ref)])


def key_grad_kernel(
    big_ref, k_ref, v_ref, q0_ref, q1_ref, pack0_ref, pack1_ref, dk_ref, dv_ref, stats, *, factor
):
    width = k_ref.shape[1]
    rows = k_ref.shape[0]
    scale = factor * LOG2E
    blocks = 1 + pack1_ref.shape[0]

    def unpack(block, pack):
        both = pack[rows : rows + 16, :].astype(F32)
        joined = both[:8] + both[8:]
        for group in range(4):
            stats[block, 8 * group : 8 * group + 8, :] = joined[:, group * rows : group * rows + rows]

    unpack(0, pack0_ref[...])
    for block in range(1, blocks):
        unpack(block, pack1_ref[block - 1])

    def run(count):
        def one_head(head, carry):
            win, mask = head_window(head, width)
            keep = mask.astype(BF)
            key = k_ref[:, win] * keep
            value = v_ref[:, win] * keep
            grad_key = grad_value = None
            for block in range(count):
                if block == 0:
                    query, grad = q0_ref[:, win], pack0_ref[0:rows, win]
                else:
                    query = q1_ref[(block - 1) * rows : block * rows, win]
                    grad = pack1_ref[block - 1, 0:rows, win]
                lse = stats[block, pl.ds(head, 1), :]
                delta = stats[block, pl.ds(head + HEADS, 1), :]
                prob = jnp.exp2(matmul_nt(key, query) * scale - lse)
                grad_prob = matmul_nt(value, grad)
                grad_score = (prob * (grad_prob - delta)).astype(BF)
                part_value = matmul(prob.astype(BF), grad)
                part_key = matmul(grad_score, query)
                grad_value = part_value if block == 0 else grad_value + part_value
                grad_key = part_key if block == 0 else grad_key + part_key
            keep_columns(dk_ref, win, mask, (grad_key * factor).astype(BF))
            keep_columns(dv_ref, win, mask, grad_value.astype(BF))
            return carry

        lax.fori_loop(0, HEADS, one_head, 0, unroll=4)

    @pl.when(big_ref[0] == 1)
    def _():
        run(blocks)

    @pl.when(big_ref[0] == 0)
    def _():
        run(1)


def text_probs(query, key, scale, live):
    scores = matmul_nt(query, key)
    lane = lax.broadcasted_iota(jnp.int32, (1, scores.shape[1]), 1)
    scores = jnp.where(lane < live, scores, BIGNEG)
    raised = jnp.exp2((scores - jnp.max(scores, axis=1, keepdims=True)) * scale)
    return raised * (1.0 / jnp.sum(raised, axis=1, keepdims=True))


def cross_kernel(q_ref, k_ref, v_ref, out_ref, *, factor, live):
    width = q_ref.shape[1]

    def one_head(head, carry):
        win, mask = head_window(head, width)
        query = q_ref[:, win] * mask.astype(BF)
        probs = text_probs(query, k_ref[:, win], factor * LOG2E, live)
        keep_columns(out_ref, win, mask, matmul(probs.astype(BF), v_ref[:, win]).astype(BF))
        return carry

    lax.fori_loop(0, HEADS, one_head, 0, unroll=4)


def cross_grad_kernel(q_ref, g_ref, k_ref, v_ref, dq_ref, dk_ref, dv_ref, *, factor, live):
    width = q_ref.shape[1]

    def one_head(head, carry):
        win, mask = head_window(head, width)
        keep = mask.astype(BF)
        query = q_ref[:, win]
        grad = g_ref[:, win]
        key = k_ref[:, win]
        probs = text_probs(query * keep, key, factor * LOG2E, live)
        grad_probs = matmul_nt(grad * keep, v_ref[:, win])
        inner = jnp.sum(probs * grad_probs, axis=1, keepdims=True)
        grad_scores = (probs * (grad_probs - inner)).astype(BF)
        keep_columns(dq_ref, win, mask, (matmul(grad_scores, key) * factor).astype(BF))
        keep_columns(dk_ref, win, mask, matmul_tn(grad_scores, query) * factor)
        keep_columns(dv_ref, win, mask, matmul_tn(probs.astype(BF), grad))
        return carry

    lax.fori_loop(0, HEADS, one_head, 0, unroll=4)


def side_by_side(pieces, width):
    missing = width - sum(piece.shape[1] for piece in pieces)
    if missing:
        pieces = [*pieces, jnp.zeros((pieces[0].shape[0], missing), pieces[0].dtype)]
    return pieces[0] if len(pieces) == 1 else jnp.concatenate(pieces, axis=1)


def weight_grad_kernel(order_ref, *refs, count, depth, high):
    sources, outs, turned = refs[: 4 * count], refs[4 * count : -1], refs[-1]
    step = pl.program_id(0)
    rows, width = sources[0].shape

    @pl.when(step == 0)
    def _():
        for item in range(count):
            for part, ref in enumerate(sources[4 * item : 4 * item + 2]):
                for low in range(0, width, 128):
                    turned[item, low : low + 128, part * rows : part * rows + rows] = ref[:, low : low + 128].T

    tall = width // 4
    pieces = []
    for item in range(count):
        g0_ref, g1_ref = sources[4 * item + 2 : 4 * item + 4]
        columns = slice(item * depth, item * depth + depth)
        for low in range(0, tall, high):
            here = pl.ds(pl.multiple_of(order_ref[step] * tall + low, 16), high)
            total = matmul(turned[item, here, 0:rows], g0_ref[:, columns])
            pieces.append((total + matmul(turned[item, here, rows:], g1_ref[:, columns])).astype(BF))
    total = side_by_side(pieces, outs[0].shape[-1])
    if len(outs) == 1:
        outs[0][0] = total
    else:

        @pl.when(step < 2)
        def _():
            outs[0][0] = total

        @pl.when(step >= 2)
        def _():
            outs[1][0] = total


def mlp_kernel(x_ref, g_ref, up_ref, down_ref, hidden_ref, pre_ref, branch_ref, grad_ref):
    step = pl.program_id(0)
    up, down = up_ref[...], down_ref[...]
    pre = matmul(x_ref[...], up)
    root = math.sqrt(2.0 / math.pi)
    square = pre * pre
    bend = jnp.tanh(root * (pre + 0.044715 * square * pre))
    hidden = (0.5 * pre * (1.0 + bend)).astype(BF)
    slope = 0.5 * (1.0 + bend) + 0.5 * pre * (1.0 - bend * bend) * root * (1.0 + 3 * 0.044715 * square)
    grad_pre = (matmul_nt(g_ref[...], down) * slope).astype(BF)
    hidden_ref[...] = hidden
    pre_ref[...] = grad_pre
    branch = matmul(hidden, down)
    grad = matmul_nt(grad_pre, up)

    @pl.when(step == 0)
    def _():
        branch_ref[...] = branch
        grad_ref[...] = grad

    @pl.when(step > 0)
    def _():
        branch_ref[...] += branch
        grad_ref[...] += grad


def halves_kernel(core_ref, *refs, count, joined):
    keep_ref, send_ref = refs[-2:]
    grads = [ref[...] for ref in refs[:-2]]
    if joined:
        grads = [jnp.concatenate(grads, axis=1)]
    even, odd = [
        jnp.concatenate(
            [
                grad[:, i * (grad.shape[1] // count) : (i + 1) * (grad.shape[1] // count)]
                for grad in grads
                for i in range(c, count, 2)
            ],
            axis=1,
        )
        for c in (0, 1)
    ]
    even, odd = [side_by_side([half], keep_ref.shape[1]) for half in (even, odd)]

    @pl.when(core_ref[0] == 0)
    def _():
        keep_ref[...] = even
        send_ref[...] = odd

    @pl.when(core_ref[0] == 1)
    def _():
        keep_ref[...] = odd
        send_ref[...] = even


def add_kernel(pick_ref, *refs):
    refs[-1][...] = sum(ref[0].astype(F32) for ref in refs[:-1]).astype(BF)


def split_kernel(flag_ref, *refs, size, slices):
    send_ref, keep_ref = refs[-2:]
    total = sum(ref[...].reshape(ref.shape[-2:]).astype(F32) for ref in refs[:-2])
    even, odd = [
        side_by_side([total[:, i * size : (i + 1) * size] for i in range(c, slices, 2)], keep_ref.shape[1])
        for c in (0, 1)
    ]

    @pl.when(flag_ref[1] == 0)
    def _():
        keep_ref[...] = even
        send_ref[...] = odd.astype(BF)

    @pl.when(flag_ref[1] == 1)
    def _():
        keep_ref[...] = odd
        send_ref[...] = even.astype(BF)


def last_kernel(keep_ref, got_ref, *outs, size):
    total = keep_ref[...] + got_ref[...].astype(F32)
    high = total.shape[0]
    at = 0
    for out in outs:
        for low in range(0, out.shape[0], high):
            out[low : low + high, :] = total[:, at : at + size]
            at += size


def prelude_kernel(place_ref, len_ref, step_ref, embed_ref, table_ref, info_ref, mod_ref, slab, sem, *, rows):
    slots = len_ref.shape[1]
    width = table_ref.shape[1]

    def image_of(at):
        first = at * rows
        end = begin = length = step = jnp.int32(0)
        for slot in range(slots):
            count = len_ref[0, slot]
            inside = jnp.logical_and(end <= first, first < end + count)
            begin = jnp.where(inside, end, begin)
            length = jnp.where(inside, count, length)
            step = jnp.where(inside, step_ref[0, slot], step)
            end = end + count
        return (first - begin) // rows, length, step

    place = place_ref[0]
    core = place % 2
    blocks = BIG // rows
    within, length, step = image_of(place)
    pair_within = image_of(place + 1 - 2 * core)[0]
    flags = (
        length > rows,
        jnp.where(core == 0, pair_within + 1 < blocks, pair_within + 3 < blocks),
        jnp.where(core == 0, within + 1 < blocks, within >= 1),
        within + 2 < blocks,
    )
    for index, flag in enumerate(flags):
        info_ref[index] = flag.astype(jnp.int32)
    copy = pltpu.make_async_copy(embed_ref.at[pl.ds(pl.multiple_of(step // 8 * 8, 8), 8), :], slab, sem)
    copy.start()
    copy.wait()
    row = slab[pl.ds(step % 8, 1), :]
    for index in range(6):
        mod_ref[index : index + 1, :] = (
            row[:, index * width : (index + 1) * width] + table_ref[index : index + 1, :]
        )


def whole(shape):
    return pl.BlockSpec(shape, lambda *_: (0,) * len(shape))


def lanes(width):
    return -(-width // 128) * 128


def params():
    return pltpu.CompilerParams(vmem_limit_bytes=VMEM_LIMIT)


def cost(flops, nbytes, exps=0):
    return pl.CostEstimate(
        flops=int(flops * COST_SCALE),
        bytes_accessed=int(nbytes * COST_SCALE),
        transcendentals=int(exps * COST_SCALE),
    )


def part_spec(rows, width, at):
    return pl.BlockSpec((rows, width), lambda i, *_: (0, at))


def halves(core, grads, count, joined):
    rows, width = grads[0].shape[0], sum(grad.shape[1] for grad in grads)
    return pl.pallas_call(
        functools.partial(halves_kernel, count=count, joined=joined),
        grid_spec=pltpu.PrefetchScalarGridSpec(
            num_scalar_prefetch=1,
            grid=(1,),
            in_specs=[whole(grad.shape) for grad in grads],
            out_specs=[whole((rows, lanes(width // 2)))] * 2,
        ),
        out_shape=[jax.ShapeDtypeStruct((rows, lanes(width // 2)), BF)] * 2,
        compiler_params=params(),
        cost_estimate=cost(0, 4 * rows * width),
    )(core, *grads)


def add_picked(pick, arrays):
    _, high, wide = arrays[0].shape
    return pl.pallas_call(
        add_kernel,
        grid_spec=pltpu.PrefetchScalarGridSpec(
            num_scalar_prefetch=1,
            grid=(2,),
            in_specs=[pl.BlockSpec((1, high // 2, wide), lambda r, p: (p[0], r, 0))] * len(arrays),
            out_specs=pl.BlockSpec((high // 2, wide), lambda r, p: (r, 0)),
        ),
        out_shape=jax.ShapeDtypeStruct((high, wide), BF),
        compiler_params=params(),
        cost_estimate=cost(0, 6 * high * wide),
    )(pick, *arrays)


def add_split(flags, picked, arrays, size, slices):
    high, wide = arrays[0].shape
    half = lanes(size * slices // 2)
    return pl.pallas_call(
        functools.partial(split_kernel, size=size, slices=slices),
        grid_spec=pltpu.PrefetchScalarGridSpec(
            num_scalar_prefetch=1,
            grid=(2,),
            in_specs=[pl.BlockSpec((1, high // 2, wide), lambda r, f: (f[0], r, 0))] * len(picked)
            + [pl.BlockSpec((high // 2, wide), lambda r, f: (r, 0))] * len(arrays),
            out_specs=[pl.BlockSpec((high // 2, half), lambda r, f: (r, 0))] * 2,
        ),
        out_shape=[jax.ShapeDtypeStruct((high, half), BF), jax.ShapeDtypeStruct((high, half), F32)],
        compiler_params=params(),
        cost_estimate=cost(0, 6 * high * wide),
    )(flags, *picked, *arrays)


def add_last(keep, got, size, shapes):
    return pl.pallas_call(
        functools.partial(last_kernel, size=size),
        out_shape=[jax.ShapeDtypeStruct(shape, F32) for shape in shapes],
        compiler_params=params(),
        cost_estimate=cost(0, 10 * keep.size),
    )(keep, got)


def prelude(place, image_len, timestep, time_embed, mod_table, rows):
    smem = pl.BlockSpec(memory_space=pltpu.SMEM)
    return pl.pallas_call(
        functools.partial(prelude_kernel, rows=rows),
        in_specs=[smem, smem, smem, pl.BlockSpec(memory_space=pl.ANY), pl.BlockSpec(memory_space=pltpu.VMEM)],
        out_specs=[smem, pl.BlockSpec(memory_space=pltpu.VMEM)],
        out_shape=[jax.ShapeDtypeStruct((4,), jnp.int32), jax.ShapeDtypeStruct(mod_table.shape, F32)],
        scratch_shapes=[pltpu.VMEM((8, time_embed.shape[1]), F32), pltpu.SemaphoreType.DMA],
        compiler_params=params(),
    )(place.reshape(1), image_len, timestep, time_embed, mod_table)


def attend(big, own, others, factor):
    rows, width = own.shape[0], own.shape[1] // 3
    far = others.shape[0]
    return pl.pallas_call(
        functools.partial(attend_kernel, factor=factor),
        grid_spec=pltpu.PrefetchScalarGridSpec(
            num_scalar_prefetch=1,
            grid=(1,),
            in_specs=[
                part_spec(rows, width, 0),
                part_spec(rows, width, 1),
                part_spec(rows, width, 2),
                part_spec(far, width, 1),
                part_spec(far, width, 2),
            ],
            out_specs=[whole((rows, width)), whole((rows, 128))],
        ),
        out_shape=[
            jax.ShapeDtypeStruct((rows, width), BF),
            jax.ShapeDtypeStruct((rows, 128), F32),
        ],
        compiler_params=params(),
        cost_estimate=cost(4 * HEADS * rows * (rows + far) * WIN, 6 * far * width, HEADS * rows * far),
    )(big, own, own, own, others, others)


def query_grad(big, own, others, grad, stat, factor):
    rows, width = own.shape[0], own.shape[1] // 3
    far = others.shape[0]
    return pl.pallas_call(
        functools.partial(query_grad_kernel, factor=factor),
        grid_spec=pltpu.PrefetchScalarGridSpec(
            num_scalar_prefetch=1,
            grid=(1,),
            in_specs=[
                part_spec(rows, width, 0),
                part_spec(rows, width, 1),
                part_spec(rows, width, 2),
                part_spec(far, width, 1),
                part_spec(far, width, 2),
                whole((rows, width)),
                whole((rows, 128)),
            ],
            out_specs=whole((rows, width)),
        ),
        out_shape=jax.ShapeDtypeStruct((rows, width), BF),
        compiler_params=params(),
        cost_estimate=cost(6 * HEADS * rows * (rows + far) * WIN, 6 * far * width, HEADS * rows * far),
    )(big, own, own, own, others, others, grad, stat)


def key_grad(big, own, others, pack, packs, factor):
    rows, width = own.shape[0], own.shape[1] // 3
    far = others.shape[0]
    return pl.pallas_call(
        functools.partial(key_grad_kernel, factor=factor),
        grid_spec=pltpu.PrefetchScalarGridSpec(
            num_scalar_prefetch=1,
            grid=(1,),
            in_specs=[
                part_spec(rows, width, 1),
                part_spec(rows, width, 2),
                part_spec(rows, width, 0),
                part_spec(far, width, 0),
                whole(pack.shape),
                whole(packs.shape),
            ],
            out_specs=[whole((rows, width))] * 2,
            scratch_shapes=[pltpu.VMEM((1 + packs.shape[0], 2 * HEADS, rows), F32)],
        ),
        out_shape=[jax.ShapeDtypeStruct((rows, width), BF)] * 2,
        compiler_params=params(),
        cost_estimate=cost(8 * HEADS * rows * (rows + far) * WIN, 6 * far * width, HEADS * rows * far),
    )(big, own, own, own, others, pack, packs)


def cross_attend(queries, keys, values, factor, live):
    rows, width = queries.shape
    return pl.pallas_call(
        functools.partial(cross_kernel, factor=factor, live=live),
        out_shape=jax.ShapeDtypeStruct((rows, width), BF),
        compiler_params=params(),
        cost_estimate=cost(4 * HEADS * rows * 128 * WIN, 6 * rows * width, HEADS * rows * 128),
    )(queries, keys, values)


def cross_grad(queries, grad, keys, values, factor, live):
    rows, width = queries.shape
    return pl.pallas_call(
        functools.partial(cross_grad_kernel, factor=factor, live=live),
        out_shape=[
            jax.ShapeDtypeStruct((rows, width), BF),
            jax.ShapeDtypeStruct(keys.shape, F32),
            jax.ShapeDtypeStruct(keys.shape, F32),
        ],
        compiler_params=params(),
        cost_estimate=cost(10 * HEADS * rows * 128 * WIN, 12 * rows * width, HEADS * rows * 128),
    )(queries, grad, keys, values)


def weight_grad(order, sources, depth, high, halved):
    count = len(sources)
    rows, width = sources[0][0].shape
    wide = lanes(count * (width // 4 // high) * depth)
    block = (1, high, wide)
    if halved:
        out_specs = [
            pl.BlockSpec(block, lambda s, _: (jnp.minimum(s, 1), 0, 0)),
            pl.BlockSpec(block, lambda s, _: (jnp.maximum(s - 2, 0), 0, 0)),
        ]
        out_shape = [jax.ShapeDtypeStruct((2, high, wide), BF)] * 2
    else:
        out_specs = [pl.BlockSpec(block, lambda s, _: (s, 0, 0))]
        out_shape = [jax.ShapeDtypeStruct((4, high, wide), BF)]
    return pl.pallas_call(
        functools.partial(weight_grad_kernel, count=count, depth=depth, high=high),
        grid_spec=pltpu.PrefetchScalarGridSpec(
            num_scalar_prefetch=1,
            grid=(4,),
            in_specs=[whole(array.shape) for source in sources for array in source],
            out_specs=out_specs,
            scratch_shapes=[pltpu.VMEM((count, width, 2 * rows), BF)],
        ),
        out_shape=out_shape,
        compiler_params=params(),
        cost_estimate=cost(
            4 * count * rows * width * depth, count * (2 * width * depth + 4 * rows * (width + depth))
        ),
    )(order, *[array for source in sources for array in source])


def mlp(inputs, grad, w_up, w_down):
    rows, width = inputs.shape
    units = w_up.shape[1]
    tile = 512
    return pl.pallas_call(
        mlp_kernel,
        grid=(units // tile,),
        in_specs=[
            whole((rows, width)),
            whole((rows, width)),
            pl.BlockSpec((width, tile), lambda i: (0, i)),
            pl.BlockSpec((tile, width), lambda i: (i, 0)),
        ],
        out_specs=[pl.BlockSpec((rows, tile), lambda i: (0, i))] * 2 + [whole((rows, width))] * 2,
        out_shape=[jax.ShapeDtypeStruct((rows, units), BF)] * 2
        + [jax.ShapeDtypeStruct((rows, width), F32)] * 2,
        compiler_params=params(),
        cost_estimate=cost(8 * rows * width * units, 4 * width * units, rows * units),
    )(inputs, grad, w_up, w_down)


def normal(stream):
    centred = stream - jnp.mean(stream, axis=-1, keepdims=True)
    spread = lax.rsqrt(jnp.mean(centred * centred, axis=-1, keepdims=True) + EPS)
    return centred * spread, spread


def norm_back(normed, spread, scale, grad):
    scaled = grad * (1.0 + scale)
    back = spread * (
        scaled
        - jnp.mean(scaled, axis=-1, keepdims=True)
        - normed * jnp.mean(scaled * normed, axis=-1, keepdims=True)
    )
    return back, jnp.sum(grad, axis=0), jnp.sum(grad * normed, axis=0)


def local(
    tokens,
    image_len,
    timestep,
    caption,
    time_embed,
    mod_table,
    w_qkv,
    w_out,
    cross_q,
    cross_kv,
    cross_out,
    w_up,
    w_down,
    cotangent,
):
    sp_count = lax.axis_size("sp")
    dp_count = lax.axis_size("dp")
    place = lax.axis_index("sp")
    row_place = lax.axis_index("dp")
    core = place % 2
    rows, width = tokens.shape[1:]
    factor = 1.0 / math.sqrt(width // HEADS)
    blocks = BIG // rows
    assert blocks == 4

    big, modulation = prelude(place, image_len, timestep, time_embed, mod_table, rows)
    shift_one, scale_one, gate_one, shift_two, scale_two, gate_two = [modulation[i] for i in range(6)]

    def tie(value, *before):
        return lax.optimization_barrier((value, *[array for array in before if array is not None]))[0]

    pairs = [(i, i ^ 1) for i in range(sp_count)]
    others = [(i, i + 1) for i in range(1, sp_count - 1, 2)] + [(i + 1, i) for i in range(1, sp_count - 1, 2)]
    ahead = [(i, i + 2) for i in range(sp_count - 2)]
    back = [(i + 2, i) for i in range(sp_count - 2)]

    def image_blocks(block):
        pair = lax.ppermute(block, "sp", pairs)
        from_back = lax.ppermute(block, "sp", ahead)
        from_ahead = lax.ppermute(block, "sp", back)
        send_pair = jnp.where(big[1] == 1, from_ahead, from_back)
        send_other = jnp.where(core == 1, from_back, from_ahead)
        second = lax.ppermute(send_pair, "sp", pairs)
        third = lax.ppermute(send_other, "sp", others)
        return (
            [
                second,
                jnp.where(big[2] == 1, pair, third),
                jnp.where(big[3] == 1, from_ahead, from_back),
            ],
            send_pair,
            send_other,
        )

    def swap(array):
        return lax.ppermute(array, "sp", pairs)

    token_blocks, *token_sends = image_blocks(tokens[0])

    def first_norm(block):
        normed, spread = normal(block.astype(F32))
        return normed, spread, (normed * (1.0 + scale_one) + shift_one).astype(BF)

    stream_in = tokens[0].astype(F32)
    normed_one, spread_one, first_in = first_norm(tokens[0])
    other_in = first_norm(jnp.concatenate(token_blocks, axis=0))[2]

    core_flag = core.reshape(1)
    chips = sp_count // 2
    chip_bits = [(place // 2 >> bit) & 1 for bit in range(chips.bit_length() - 1)]

    def own_half(*grads, joined=True):
        return halves(core_flag, grads, sp_count, joined)

    def add(*terms):
        return sum(term.astype(F32) for term in terms)

    def start_sum(sources, size, low_first):
        depth = chips * size
        tall = sources[0][0].shape[1] // dp_count
        if dp_count != 4:
            parts = weight_grad(jnp.arange(4, dtype=jnp.int32), sources, depth, width // 4, False)[0]
            groups = 4 * tall * dp_count // (4 * width)
            return parts, (len(sources), groups, size, tall)
        first, second = (0, 1) if low_first else (1, 0)
        mine = [(row_place >> first) & 1, (row_place >> second) & 1]
        order = jnp.stack(
            [((1 - mine[0] if s < 2 else mine[0]) << first) + ((s % 2) << second) for s in range(4)]
        )
        send, keep = weight_grad(order, sources, depth, width // 4, True)
        got = lax.ppermute(send, "dp", [(i, i ^ (1 << first)) for i in range(4)])
        return send, (keep, got, mine[1], second, size, [(tall, size)] * len(sources))

    def add_rows(state):
        if dp_count != 4:
            return None, state
        keep, got, mine, second, size, shapes = state
        return add_picked((1 - mine).reshape(1), [keep, got]), state

    def add_columns(parts, send, state):
        if dp_count != 4:
            return add_plain(parts, *state)
        keep, got, mine, second, size, shapes = state
        more = lax.ppermute(send, "dp", [(i, i ^ (1 << second)) for i in range(4)])
        picked, arrays = [keep, got], [more]
        slices = more.shape[1] // size
        for bit, flag in enumerate(chip_bits):
            send, keep = add_split(jnp.stack([mine, flag]), picked, arrays, size, slices)
            got = lax.ppermute(send, "sp", [(i, i ^ (2 << bit)) for i in range(sp_count)])
            picked, arrays, slices = [], [keep, got], slices // 2
        return add_last(keep, got, size, shapes)

    def add_plain(parts, count, groups, size, tall):
        parts = parts[:, :, : count * groups * chips * size].reshape(4, -1, count, groups, chips, size)
        parts = parts.transpose(2, 0, 3, 1, 4, 5).reshape(count, dp_count, tall, chips, size)
        bit = dp_count // 2
        while bit:
            mine = (row_place // bit) % 2
            parts = parts.reshape(count, 2, bit, tall, chips, size)
            at = lambda i: lax.dynamic_index_in_dim(parts, i, 1, keepdims=False)
            got = lax.ppermute(at(1 - mine), "dp", [(i, i ^ bit) for i in range(dp_count)])
            parts = add(at(mine), got).astype(BF)
            bit //= 2
        parts = parts[:, 0].transpose(2, 0, 1, 3)
        bit = chips // 2
        while bit:
            mine = (place // 2 // bit) % 2
            parts = parts.reshape(2, bit, count, tall, size)
            got = lax.ppermute(parts[1 - mine], "sp", [(i, i ^ (2 * bit)) for i in range(sp_count)])
            parts = add(parts[mine], got).astype(BF)
            bit //= 2
        return list(parts[0].astype(F32))

    def spread_vector(vector):
        for axis, name, count, mine in ((1, "sp", sp_count, place), (0, "dp", dp_count, row_place)):
            bit = count // 2
            while bit:
                shape = vector.shape
                split = vector.reshape(shape[:axis] + (2, bit) + shape[axis + 1 :])
                at = lambda i: lax.dynamic_index_in_dim(split, i, axis, keepdims=False)
                own = (mine // bit) % 2
                got = lax.ppermute(at(1 - own), name, [(i, i ^ bit) for i in range(count)])
                vector = at(own) + got
                bit //= 2
        return vector.reshape(-1)

    caption_rows = caption[0]
    live = caption_rows.shape[0]
    padded = -(-live // 128) * 128
    caption_pad = jnp.concatenate([caption_rows, jnp.zeros((padded - live, width), BF)], axis=0)
    text_kv = matmul(caption_pad, cross_kv).astype(BF)
    text_keys, text_values = text_kv[:, :width], text_kv[:, width:]
    grad_three = cotangent[0].astype(F32)
    grad_mlp = (gate_two * grad_three).astype(BF)
    mlp_keep, mlp_send = own_half(grad_mlp)
    mlp_got = swap(mlp_send)
    first_pair = swap(first_in)
    own = matmul(tie(first_in, *token_sends), w_qkv).astype(BF)
    others_qkv = matmul(other_in, w_qkv).astype(BF)
    attended, logsum = attend(big, own, others_qkv, factor)
    attn_branch = matmul(attended, w_out)
    stream_one = stream_in + gate_one * attn_branch
    cross_in = stream_one.astype(BF)
    cross_queries = matmul(cross_in, cross_q).astype(BF)
    cross_mixed = cross_attend(cross_queries, text_keys, text_values, factor, live)
    stream_two = stream_one + matmul(cross_mixed, cross_out)
    normed_two, spread_two = normal(stream_two)
    second_in = (normed_two * (1.0 + scale_two) + shift_two).astype(BF)
    second_pair = swap(second_in)
    hidden, grad_pre, mlp_branch, grad_second = mlp(second_in, grad_mlp, w_up, w_down)
    stream_three = stream_two + gate_two * mlp_branch

    grad_gate_two = jnp.sum(grad_three * mlp_branch, axis=0)
    pre_keep, pre_send = own_half(grad_pre)
    slice_of = lambda weight: weight.shape[1] // sp_count
    send_down, state_down = start_sum([(hidden, swap(hidden), mlp_keep, mlp_got)], slice_of(w_down), True)
    send_up, state_up = start_sum([(second_in, second_pair, pre_keep, swap(pre_send))], slice_of(w_up), False)
    back_two, grad_shift_two, grad_scale_two = norm_back(normed_two, spread_two, scale_two, grad_second)
    grad_stream_two = grad_three + back_two
    grad_cross = grad_stream_two.astype(BF)
    small_acts = [(acts, swap(acts)) for acts in (cross_mixed, cross_in, attended)]
    grad_mixed = matmul_nt(grad_cross, cross_out).astype(BF)
    grad_mixed = tie(grad_mixed, send_down, send_up, *[pair for _, pair in small_acts])
    grad_cq_rows, grad_text_keys, grad_text_values = cross_grad(
        cross_queries, grad_mixed, text_keys, text_values, factor, live
    )
    grad_text = jnp.concatenate([grad_text_keys[:live], grad_text_values[:live]], axis=1)
    grad_stream_one = grad_stream_two + matmul_nt(grad_cq_rows, cross_q)
    grad_gate_one = jnp.sum(grad_stream_one * attn_branch, axis=0)
    grad_attn = (gate_one * grad_stream_one).astype(BF)
    grad_back = matmul_nt(grad_attn, w_out).astype(BF)

    column = jnp.arange(width, dtype=jnp.int32)[:, None] // (width // HEADS)
    pick = (column + HEADS == jnp.arange(128, dtype=jnp.int32)[None, :]).astype(F32)
    inner = jnp.dot(
        grad_back.astype(F32) * attended.astype(F32), pick, precision=lax.Precision.HIGHEST
    )
    stat = logsum + inner
    turned = stat.T[: 2 * HEADS].reshape(4, 8, rows).transpose(1, 0, 2).reshape(8, 4 * rows)
    high = lax.reduce_precision(turned, exponent_bits=8, mantissa_bits=7)
    both = jnp.concatenate([high, turned - high], axis=0).astype(BF)
    both = jnp.concatenate([both, jnp.zeros((16, width - 4 * rows), BF)], axis=1)
    pack = jnp.concatenate([grad_back, both], axis=0)
    pack_blocks, *pack_sends = image_blocks(pack)
    packs = jnp.stack(pack_blocks)

    small_keep, small_send = own_half(grad_cross, grad_cq_rows, grad_attn, joined=False)
    small_got = swap(small_send)
    small = [(*acts, small_keep, small_got) for acts in small_acts]
    send_small, state_small = start_sum(small, slice_of(w_out), True)

    grad_queries = query_grad(big, own, others_qkv, tie(grad_back, *pack_sends), stat, factor)
    grad_keys, grad_values = key_grad(big, own, others_qkv, tie(pack, send_small), packs, factor)
    grad_proj = jnp.concatenate([grad_queries, grad_keys, grad_values], axis=1)
    proj_keep, proj_send = own_half(grad_queries, grad_keys, grad_values)
    more_down, more_up = add_rows(state_down), add_rows(state_up)
    send_qkv, state_qkv = start_sum(
        [(first_in, first_pair, proj_keep, swap(proj_send))], slice_of(w_qkv), False
    )
    grad_first = matmul_nt(tie(grad_proj, send_qkv, more_down[0], more_up[0]), w_qkv)
    back_one, grad_shift_one, grad_scale_one = norm_back(normed_one, spread_one, scale_one, grad_first)
    grad_tokens = grad_stream_one + back_one

    (final_down,) = add_columns(send_down, *more_down)
    (final_up,) = add_columns(send_up, *more_up)
    final_small = add_columns(send_small, *add_rows(state_small))
    (final_qkv,) = add_columns(send_qkv, *add_rows(state_qkv))
    text_part = lax.psum_scatter(grad_text, "sp", scatter_dimension=1, tiled=True).astype(BF)
    part_ckv = matmul_tn(caption_rows, text_part).astype(BF)
    final_ckv = lax.psum_scatter(part_ckv, "dp", scatter_dimension=0, tiled=True).astype(F32)
    table = jnp.concatenate(
        [grad_shift_one, grad_scale_one, grad_gate_one, grad_shift_two, grad_scale_two, grad_gate_two]
    )
    final_table = spread_vector(table.reshape(dp_count, sp_count, -1))
    return (
        stream_three[None],
        grad_tokens[None],
        final_table,
        final_qkv,
        final_small[2],
        final_small[1],
        final_ckv,
        final_small[0],
        final_up,
        final_down,
    )


def solution(mesh):
    return jax.shard_map(
        local,
        mesh=mesh,
        in_specs=(
            P("dp", "sp", None),
            P("dp", None),
            P("dp", None),
            P("dp", None, None),
            P(),
            P(),
            P(),
            P(),
            P(),
            P(),
            P(),
            P(),
            P(),
            P("dp", "sp", None),
        ),
        out_specs=(
            P("dp", "sp", None),
            P("dp", "sp", None),
            P(("dp", "sp")),
            P("dp", "sp"),
            P("dp", "sp"),
            P("dp", "sp"),
            P("dp", "sp"),
            P("dp", "sp"),
            P("dp", "sp"),
            P("dp", "sp"),
        ),
        check_vma=False,
    )
```

```python
import functools
import math

import jax
import jax.numpy as jnp
from jax import lax
from jax.experimental import pallas as pl
from jax.experimental.pallas import tpu as pltpu
from jax.sharding import PartitionSpec as P

HEADS = 16
BIG = 1024
EPS = 1e-06
BIGNEG = -1e30
LOG2E = 1.4426950408889634
BF = jnp.bfloat16
F32 = jnp.float32
WIN = 256
COST_SCALE = 0.001
VMEM_LIMIT = 60 * 1024 * 1024


def matmul(left, right):
    return jnp.dot(left, right, preferred_element_type=F32)


def matmul_tn(left, right):
    return lax.dot_general(left, right, (((0,), (0,)), ((), ())), preferred_element_type=F32)


def matmul_nt(left, right):
    return lax.dot_general(left, right, (((1,), (1,)), ((), ())), preferred_element_type=F32)


def head_window(head, width):
    size = width // HEADS
    low = head * size
    start = pl.multiple_of(jnp.minimum(low // 128 * 128, width - WIN), 128)
    lane = lax.broadcasted_iota(jnp.int32, (1, WIN), 1) + start
    mask = jnp.logical_and(lane >= low, lane < low + size)
    return pl.ds(start, WIN), mask


def keep_columns(ref, win, mask, value):
    ref[:, win] = jnp.where(mask, value, ref[:, win])


def attend_kernel(big_ref, q_ref, k0_ref, v0_ref, k1_ref, v1_ref, out_ref, lse_ref, *, factor):
    width = q_ref.shape[1]
    scale = factor * LOG2E

    def run(pairs):
        def one_head(head, carry):
            win, mask = head_window(head, width)
            query = q_ref[:, win] * mask.astype(BF)
            scores = [matmul_nt(query, key[:, win]) for key, _ in pairs]
            top = functools.reduce(jnp.maximum, [jnp.max(s, axis=1, keepdims=True) for s in scores])
            raised = [jnp.exp2((s - top) * scale) for s in scores]
            total = sum(jnp.sum(r, axis=1, keepdims=True) for r in raised)
            inverse = 1.0 / total
            result = sum(
                matmul((r * inverse).astype(BF), value[:, win])
                for r, (_, value) in zip(raised, pairs)
            )
            keep_columns(out_ref, win, mask, result.astype(BF))
            lane = lax.broadcasted_iota(jnp.int32, (1, 128), 1)
            lse = top * scale + jnp.log2(total)
            lse_ref[...] = jnp.where(lane == head, lse, lse_ref[...])
            return carry

        lax.fori_loop(0, HEADS, one_head, 0, unroll=4)

    lse_ref[...] = jnp.zeros_like(lse_ref)

    @pl.when(big_ref[0] == 1)
    def _():
        run([(k0_ref, v0_ref), (k1_ref, v1_ref)])

    @pl.when(big_ref[0] == 0)
    def _():
        run([(k0_ref, v0_ref)])


def query_grad_kernel(
    big_ref, q_ref, k0_ref, v0_ref, k1_ref, v1_ref, do_ref, stat_ref, out_ref, *, factor
):
    width = q_ref.shape[1]
    scale = factor * LOG2E

    def run(pairs):
        def one_head(head, carry):
            win, mask = head_window(head, width)
            keep = mask.astype(BF)
            query = q_ref[:, win] * keep
            grad = do_ref[:, win] * keep
            lane = lax.broadcasted_iota(jnp.int32, (1, 128), 1)
            stat = stat_ref[...]
            lse = jnp.sum(jnp.where(lane == head, stat, 0.0), axis=1, keepdims=True)
            delta = jnp.sum(jnp.where(lane == head + HEADS, stat, 0.0), axis=1, keepdims=True)
            total = None
            for key, value in pairs:
                prob = jnp.exp2(matmul_nt(query, key[:, win]) * scale - lse)
                grad_prob = matmul_nt(grad, value[:, win])
                grad_score = (prob * (grad_prob - delta)).astype(BF)
                part = matmul(grad_score, key[:, win])
                total = part if total is None else total + part
            keep_columns(out_ref, win, mask, (total * factor).astype(BF))
            return carry

        lax.fori_loop(0, HEADS, one_head, 0, unroll=4)

    @pl.when(big_ref[0] == 1)
    def _():
        run([(k0_ref, v0_ref), (k1_ref, v1_ref)])

    @pl.when(big_ref[0] == 0)
    def _():
        run([(k0_ref, v0_ref)])


def key_grad_kernel(
    big_ref, k_ref, v_ref, q0_ref, q1_ref, pack0_ref, pack1_ref, dk_ref, dv_ref, stats, grads, *, factor
):
    width = k_ref.shape[1]
    rows = k_ref.shape[0]
    scale = factor * LOG2E
    blocks = 1 + pack1_ref.shape[0]

    def unpack(block, pack):
        both = pack[rows : rows + 16, :].astype(F32)
        joined = both[:8] + both[8:]
        for group in range(4):
            stats[8 * group : 8 * group + 8, block * rows : block * rows + rows] = joined[
                :, group * rows : group * rows + rows
            ]

    unpack(0, pack0_ref)
    for block in range(1, blocks):
        unpack(block, pack1_ref.at[block - 1])
        grads[(block - 1) * rows : block * rows, :] = pack1_ref[block - 1, 0:rows, :]

    def run(parts):
        def one_head(head, carry):
            win, mask = head_window(head, width)
            keep = mask.astype(BF)
            key = k_ref[:, win] * keep
            value = v_ref[:, win] * keep
            lse = stats[pl.ds(head, 1), :]
            delta = stats[pl.ds(head + HEADS, 1), :]
            grad_key = grad_value = 0.0
            for query_ref, grad_ref, low, high in parts:
                query, grad = query_ref[:, win], grad_ref[0 : high - low, win]
                prob = jnp.exp2(matmul_nt(key, query) * scale - lse[:, low:high])
                grad_prob = matmul_nt(value, grad)
                grad_score = (prob * (grad_prob - delta[:, low:high])).astype(BF)
                grad_value = grad_value + matmul(prob.astype(BF), grad)
                grad_key = grad_key + matmul(grad_score, query)
            keep_columns(dk_ref, win, mask, (grad_key * factor).astype(BF))
            keep_columns(dv_ref, win, mask, grad_value.astype(BF))
            return carry

        lax.fori_loop(0, HEADS, one_head, 0, unroll=4)

    own = (q0_ref, pack0_ref, 0, rows)

    @pl.when(big_ref[0] == 1)
    def _():
        run([own, (q1_ref, grads, rows, blocks * rows)])

    @pl.when(big_ref[0] == 0)
    def _():
        run([own])


def text_probs(query, key, scale, live):
    scores = matmul_nt(query, key)
    lane = lax.broadcasted_iota(jnp.int32, (1, scores.shape[1]), 1)
    scores = jnp.where(lane < live, scores, BIGNEG)
    raised = jnp.exp2((scores - jnp.max(scores, axis=1, keepdims=True)) * scale)
    return raised * (1.0 / jnp.sum(raised, axis=1, keepdims=True))


def cross_kernel(q_ref, k_ref, v_ref, out_ref, *, factor, live):
    width = q_ref.shape[1]

    def one_head(head, carry):
        win, mask = head_window(head, width)
        query = q_ref[:, win] * mask.astype(BF)
        probs = text_probs(query, k_ref[:, win], factor * LOG2E, live)
        keep_columns(out_ref, win, mask, matmul(probs.astype(BF), v_ref[:, win]).astype(BF))
        return carry

    lax.fori_loop(0, HEADS, one_head, 0, unroll=4)


def cross_grad_kernel(q_ref, g_ref, k_ref, v_ref, dq_ref, dk_ref, dv_ref, *, factor, live):
    width = q_ref.shape[1]

    def one_head(head, carry):
        win, mask = head_window(head, width)
        keep = mask.astype(BF)
        query = q_ref[:, win]
        grad = g_ref[:, win]
        key = k_ref[:, win]
        probs = text_probs(query * keep, key, factor * LOG2E, live)
        grad_probs = matmul_nt(grad * keep, v_ref[:, win])
        inner = jnp.sum(probs * grad_probs, axis=1, keepdims=True)
        grad_scores = (probs * (grad_probs - inner)).astype(BF)
        keep_columns(dq_ref, win, mask, (matmul(grad_scores, key) * factor).astype(BF))
        keep_columns(dk_ref, win, mask, matmul_tn(grad_scores, query) * factor)
        keep_columns(dv_ref, win, mask, matmul_tn(probs.astype(BF), grad))
        return carry

    lax.fori_loop(0, HEADS, one_head, 0, unroll=4)


def side_by_side(pieces, width):
    missing = width - sum(piece.shape[1] for piece in pieces)
    if missing:
        pieces = [*pieces, jnp.zeros((pieces[0].shape[0], missing), pieces[0].dtype)]
    return pieces[0] if len(pieces) == 1 else jnp.concatenate(pieces, axis=1)


def weight_grad_kernel(order_ref, *refs, count, size, high, mode, outs):
    sources, out_refs, turned = refs[: 4 * count], refs[4 * count : -1], refs[-1]
    step = pl.program_id(0)
    rows, width = sources[0].shape
    body, tail = slice_parts(size)

    @pl.when(step == 0)
    def _():
        for item in range(count):
            for part, ref in enumerate(sources[4 * item : 4 * item + 2]):
                for low in range(0, width, 128):
                    turned[item, low : low + 128, part * rows : part * rows + rows] = ref[:, low : low + 128].T

    tall = width // 4
    chunk = order_ref[step]
    pieces = []
    for item in range(count):
        g0_ref, g1_ref = sources[4 * item + 2 : 4 * item + 4]
        wide = g0_ref.shape[1] // count
        columns = slice(item * wide, item * wide + wide)
        for low in range(0, tall, high):
            here = pl.ds(pl.multiple_of(chunk * tall + low, 16), high)
            total = matmul(turned[item, here, 0:rows], g0_ref[:, columns])
            pieces.append((total + matmul(turned[item, here, rows:], g1_ref[:, columns])).astype(BF))
    if len(pieces) == 1:
        half = pieces[0].shape[1] // 2
        groups = [pieces[0][:, :half], pieces[0][:, half:]]
    else:
        groups = [
            side_by_side(
                [piece[:, 2 * p * body : 2 * (p + 1) * body] for piece in pieces]
                + [piece[:, 4 * body + 2 * p * tail : 4 * body + 2 * (p + 1) * tail] for piece in pieces],
                out_refs[0].shape[-1] // (2 if mode == "rows" else 1),
            )
            for p in (0, 1)
        ]
    half = groups[0].shape[1]
    if mode == "rows":
        for ref, here in zip(out_refs, (step < 2, step >= 2)):

            @pl.when(here)
            def _(ref=ref):
                ref[0, :, :half] = groups[0]
                ref[0, :, half:] = groups[1]

    elif mode == "chips":
        store_halves(order_ref[4], out_refs, groups)
    else:
        for p in (0, 1):
            first, second = (chunk >> p) & 1, (chunk >> (1 - p)) & 1
            for kept in (0, 1):

                @pl.when((first == order_ref[4 + p]) == (kept == 1))
                def _(p=p, kept=kept, second=second):
                    out_refs[2 * p + kept][second] = groups[p]


def mlp_kernel(x_ref, g_ref, up_ref, down_ref, hidden_ref, pre_ref, branch_ref, grad_ref, *scratch, tile):
    up, down, sems = scratch[:3]
    kept = (scratch[3:5], scratch[5:7])
    tiles = up.shape[0]
    root = math.sqrt(2.0 / math.pi)

    def columns(step):
        return pl.ds(pl.multiple_of(step * tile, 128), tile)

    def copies(step):
        return (
            pltpu.make_async_copy(up_ref.at[:, columns(step)], up.at[step], sems.at[0, step]),
            pltpu.make_async_copy(down_ref.at[columns(step), :], down.at[step], sems.at[1, step]),
        )

    for step in range(tiles):
        for copy in copies(step):
            copy.start()

    def both(step, parity, first, last):
        if not last:
            for copy in copies(step):
                copy.wait()
            pre = matmul(x_ref[...], up[step])
            grad = matmul_nt(g_ref[...], down[step])
        if not first:
            hidden, grad_pre = (ref[...] for ref in kept[1 - parity])
            branch = matmul(hidden, down[step - 1])
            back = matmul_nt(grad_pre, up[step - 1])
        if not last:
            square = pre * pre
            bend = jnp.tanh(pre * (root * 0.044715 * square + root))
            half = 0.5 * bend + 0.5
            rise = (3 * root * 0.044715 * square + root) * pre
            slope = half + 0.5 * rise * (1.0 - bend * bend)
            hidden = (pre * half).astype(BF)
            grad_pre = (grad * slope).astype(BF)
            for ref, value in zip(kept[parity], (hidden, grad_pre)):
                ref[...] = value
            hidden_ref[:, columns(step)] = hidden
            pre_ref[:, columns(step)] = grad_pre
        if not first:
            branch_ref[...] += branch
            grad_ref[...] += back

    branch_ref[...] = jnp.zeros_like(branch_ref)
    grad_ref[...] = jnp.zeros_like(grad_ref)
    both(0, 0, True, False)

    def two(index, carry):
        both(2 * index + 1, 1, False, False)
        both(2 * index + 2, 0, False, False)
        return carry

    lax.fori_loop(0, (tiles - 1) // 2, two, 0)
    if tiles % 2 == 0:
        both(tiles - 1, 1, False, False)
    both(tiles, tiles % 2, False, True)


def slice_parts(size):
    return size // 128 * 128, size % 128


def halves_kernel(core_ref, *refs, count, joined):
    keep_ref, send_ref = refs[-2:]
    grads = [ref[...] for ref in refs[:-2]]
    if joined and len(grads) > 1:
        grads = [jnp.concatenate(grads, axis=1)]
    size = grads[0].shape[1] // count
    body, tail = slice_parts(size)

    def columns(core):
        picked = []
        for grad in grads:
            bodies = [[], []]
            tails = [[], []]
            for chip in range(count // 2):
                low = (2 * chip + core) * size
                bodies[chip % 2].append(grad[:, low : low + body])
                tails[chip % 2].append(grad[:, low + body : low + size])
            if joined:
                for parity in (0, 1):
                    picked += bodies[parity]
                    picked.append(side_by_side(tails[parity], 128))
            else:
                picked += bodies[0] + bodies[1]
                picked.append(side_by_side(tails[0] + tails[1], 128))
        return side_by_side(picked, keep_ref.shape[1])

    for core in (0, 1):

        @pl.when(core_ref[0] == core)
        def _(core=core):
            keep_ref[...] = columns(core)
            send_ref[...] = columns(1 - core)


def store_halves(flag, refs, pieces):
    for value in (0, 1):

        @pl.when(flag == value)
        def _(value=value):
            for ref, piece in zip(refs, (pieces[1 - value], pieces[value])):
                ref[...] = piece.reshape(ref.shape).astype(ref.dtype)


def add_kernel(pick_ref, *refs):
    refs[-1][...] = sum(ref[0].astype(F32) for ref in refs[:-1]).astype(BF)


def split_rows_kernel(flag_ref, *refs):
    half = refs[-1].shape[1]
    total = sum(ref[...].reshape(ref.shape[-2:]).astype(F32) for ref in refs[:-2])
    store_halves(flag_ref[1], refs[-2:], (total[:, :half], total[:, half:]))


def split_pair_kernel(flag_ref, *refs):
    half = len(refs[:-2]) // 2
    totals = [
        sum(ref[...].reshape(ref.shape[-2:]).astype(F32) for ref in part)
        for part in (refs[:half], refs[half:-2])
    ]
    store_halves(flag_ref[2], refs[-2:], totals)


def split_body_kernel(flag_ref, keep_ref, got_ref, send_ref, own_ref, *, body, tail, pieces):
    total = (keep_ref[...].astype(F32) + got_ref[...].astype(F32)).reshape(keep_ref.shape[-2:])
    base = 2 * pieces * body
    parts = [
        side_by_side(
            [total[:, (2 * k + h) * body : (2 * k + h + 1) * body] for k in range(pieces)]
            + [total[:, base + (2 * k + h) * tail : base + (2 * k + h + 1) * tail] for k in range(pieces)],
            send_ref.shape[-1],
        )
        for h in (0, 1)
    ]
    store_halves(flag_ref[0], (send_ref, own_ref), parts)


def pass_rows_kernel(order_ref, *refs, halves):
    send_ref, keep_ref = refs[-2:]
    total = sum(ref[...].astype(F32) for ref in refs[:-2])

    @pl.when(pl.program_id(0) < halves)
    def _():
        send_ref[...] = total.reshape(send_ref.shape).astype(BF)

    @pl.when(pl.program_id(0) >= halves)
    def _():
        keep_ref[...] = total.reshape(keep_ref.shape)


def last_kernel(keep_ref, got_ref, *outs, body, tail, pieces, turned):
    total = (keep_ref[...] + got_ref[...].astype(F32)).reshape(keep_ref.shape[-2:])
    high = total.shape[0]
    whole_rows = outs[0].shape[1 if turned else 0]
    for piece in range(pieces):
        low = pieces * body + piece * tail
        part = jnp.concatenate(
            [total[:, piece * body : (piece + 1) * body], total[:, low : low + tail]], axis=1
        )
        out, at = outs[piece * high // whole_rows], piece * high % whole_rows
        if turned:
            out[:, at : at + high] = part.T
        else:
            out[at : at + high, :] = part


def prelude_kernel(place_ref, len_ref, step_ref, embed_ref, table_ref, info_ref, mod_ref, slab, sem, *, rows):
    slots = len_ref.shape[1]
    width = table_ref.shape[1]

    def image_of(at):
        first = at * rows
        end = begin = length = step = jnp.int32(0)
        for slot in range(slots):
            count = len_ref[0, slot]
            inside = jnp.logical_and(end <= first, first < end + count)
            begin = jnp.where(inside, end, begin)
            length = jnp.where(inside, count, length)
            step = jnp.where(inside, step_ref[0, slot], step)
            end = end + count
        return (first - begin) // rows, length, step

    place = place_ref[0]
    core = place % 2
    blocks = BIG // rows
    within, length, step = image_of(place)
    pair_within = image_of(place + 1 - 2 * core)[0]
    flags = (
        length > rows,
        jnp.where(core == 0, pair_within + 1 < blocks, pair_within + 3 < blocks),
        jnp.where(core == 0, within + 1 < blocks, within >= 1),
        within + 2 < blocks,
    )
    for index, flag in enumerate(flags):
        info_ref[index] = flag.astype(jnp.int32)
    copy = pltpu.make_async_copy(embed_ref.at[pl.ds(pl.multiple_of(step // 8 * 8, 8), 8), :], slab, sem)
    copy.start()
    copy.wait()
    row = slab[pl.ds(step % 8, 1), :]
    for index in range(6):
        mod_ref[index : index + 1, :] = (
            row[:, index * width : (index + 1) * width] + table_ref[index : index + 1, :]
        )


def whole(shape):
    return pl.BlockSpec(shape, lambda *_: (0,) * len(shape))


def lanes(width):
    return -(-width // 128) * 128


def params(limit=VMEM_LIMIT):
    return pltpu.CompilerParams(vmem_limit_bytes=limit)


def cost(flops, nbytes, exps=0):
    return pl.CostEstimate(
        flops=int(flops * COST_SCALE),
        bytes_accessed=int(nbytes * COST_SCALE),
        transcendentals=int(exps * COST_SCALE),
    )


def part_spec(rows, width, at):
    return pl.BlockSpec((rows, width), lambda i, *_: (0, at))


def halves(core, grads, count, joined):
    rows, width = grads[0].shape[0], sum(grad.shape[1] for grad in grads)
    body, tail = slice_parts((width if joined else grads[0].shape[1]) // count)
    if joined:
        wide = 2 * (count // 4 * body + 128)
    else:
        wide = len(grads) * (count // 2 * body + 128)
    return pl.pallas_call(
        functools.partial(halves_kernel, count=count, joined=joined),
        grid_spec=pltpu.PrefetchScalarGridSpec(
            num_scalar_prefetch=1,
            grid=(1,),
            in_specs=[whole(grad.shape) for grad in grads],
            out_specs=[whole((rows, wide))] * 2,
        ),
        out_shape=[jax.ShapeDtypeStruct((rows, wide), BF)] * 2,
        compiler_params=params(),
        cost_estimate=cost(0, 4 * rows * width),
    )(core, *grads)


def blocks_call(kernel, flags, inputs, outs, grid=(1,)):
    return pl.pallas_call(
        kernel,
        grid_spec=pltpu.PrefetchScalarGridSpec(
            num_scalar_prefetch=1,
            grid=grid,
            in_specs=[pl.BlockSpec(block, place) for _, block, place in inputs],
            out_specs=[pl.BlockSpec(block, place) for _, _, block, place in outs],
        ),
        out_shape=[jax.ShapeDtypeStruct(shape, dtype) for shape, dtype, _, _ in outs],
        compiler_params=params(),
        cost_estimate=cost(0, sum(2 * array.size for array, _, _ in inputs)),
    )(flags, *[array for array, _, _ in inputs])


def picked_rows(array, index, steps):
    _, high, wide = array.shape
    return array, (1, high // steps, wide), lambda r, f: (f[index], r, 0)


def plain_rows(array, steps):
    high, wide = array.shape
    return array, (high // steps, wide), lambda r, f: (r, 0)


def rows_out(high, wide, dtype, steps):
    return (high, wide), dtype, (high // steps, wide), lambda r, f: (r, 0)


def add_picked(pick, arrays):
    _, high, wide = arrays[0].shape
    return blocks_call(
        add_kernel,
        pick.reshape(1),
        [picked_rows(array, 0, 3) for array in arrays],
        [rows_out(high, wide, BF, 3)],
        (3,),
    )[0]


def split_rows(flags, picked, more):
    high, wide = more.shape
    return blocks_call(
        split_rows_kernel,
        flags,
        [picked_rows(array, 0, 3) for array in picked] + [plain_rows(more, 3)],
        [rows_out(high, wide // 2, BF, 3), rows_out(high, wide // 2, F32, 3)],
        (3,),
    )


def split_pair(flags, chains):
    inputs = []
    for index, (keep, got, more) in enumerate(chains):
        inputs += [picked_rows(keep, index, 3), picked_rows(got, index, 3), plain_rows(more, 3)]
    high, wide = chains[0][2].shape
    return blocks_call(
        split_pair_kernel,
        flags,
        inputs,
        [rows_out(high, wide, BF, 3), rows_out(high, wide, F32, 3)],
        (3,),
    )


def split_body(flag, keep, got, size, pieces):
    body, tail = slice_parts(size)
    *lead, high, wide = keep.shape
    out = pieces * body + 128
    kernel = functools.partial(split_body_kernel, body=body, tail=tail, pieces=pieces)
    if lead:
        block = lambda width: (1, high, width)
        place = lambda r, f: (r, 0, 0)
    else:
        block = lambda width: (high // 3, width)
        place = lambda r, f: (r, 0)
    return blocks_call(
        kernel,
        flag.reshape(1),
        [(keep, block(wide), place), (got, block(wide), place)],
        [((*lead, high, out), dtype, block(out), place) for dtype in (BF, F32)],
        (lead[0] if lead else 3,),
    )


def pass_rows(order, keep, got, halves):
    count, high, wide = keep.shape
    block = (1, high, wide)
    place = lambda s, f: (f[s], 0, 0)
    return blocks_call(
        functools.partial(pass_rows_kernel, halves=halves),
        order,
        [(keep, block, place), (got, block, place)],
        [
            ((halves, high, wide), BF, block, lambda s, f: (jnp.minimum(s, halves - 1), 0, 0)),
            ((halves, high, wide), F32, block, lambda s, f: (jnp.maximum(s - halves, 0), 0, 0)),
        ],
        (count,),
    )


def add_last(keep, got, size, shapes, turned):
    body, tail = slice_parts(size)
    pieces = sum(shape[0] for shape in shapes) // keep.shape[-2]
    outs = pl.pallas_call(
        functools.partial(last_kernel, body=body, tail=tail, pieces=pieces, turned=turned),
        out_shape=[jax.ShapeDtypeStruct(shape[::-1] if turned else shape, F32) for shape in shapes],
        compiler_params=params(),
        cost_estimate=cost(0, 10 * keep.size),
    )(keep, got)
    return [out.T for out in outs] if turned else outs


def prelude(place, image_len, timestep, time_embed, mod_table, rows):
    smem = pl.BlockSpec(memory_space=pltpu.SMEM)
    return pl.pallas_call(
        functools.partial(prelude_kernel, rows=rows),
        in_specs=[smem, smem, smem, pl.BlockSpec(memory_space=pl.ANY), pl.BlockSpec(memory_space=pltpu.VMEM)],
        out_specs=[smem, pl.BlockSpec(memory_space=pltpu.VMEM)],
        out_shape=[jax.ShapeDtypeStruct((4,), jnp.int32), jax.ShapeDtypeStruct(mod_table.shape, F32)],
        scratch_shapes=[pltpu.VMEM((8, time_embed.shape[1]), F32), pltpu.SemaphoreType.DMA],
        compiler_params=params(),
    )(place.reshape(1), image_len, timestep, time_embed, mod_table)


def attend(big, own, others, factor):
    rows, width = own.shape[0], own.shape[1] // 3
    far = others.shape[0]
    return pl.pallas_call(
        functools.partial(attend_kernel, factor=factor),
        grid_spec=pltpu.PrefetchScalarGridSpec(
            num_scalar_prefetch=1,
            grid=(1,),
            in_specs=[
                part_spec(rows, width, 0),
                part_spec(rows, width, 1),
                part_spec(rows, width, 2),
                part_spec(far, width, 1),
                part_spec(far, width, 2),
            ],
            out_specs=[whole((rows, width)), whole((rows, 128))],
        ),
        out_shape=[
            jax.ShapeDtypeStruct((rows, width), BF),
            jax.ShapeDtypeStruct((rows, 128), F32),
        ],
        compiler_params=params(),
        cost_estimate=cost(4 * HEADS * rows * (rows + far) * WIN, 6 * far * width, HEADS * rows * far),
    )(big, own, own, own, others, others)


def query_grad(big, own, others, grad, stat, factor):
    rows, width = own.shape[0], own.shape[1] // 3
    far = others.shape[0]
    return pl.pallas_call(
        functools.partial(query_grad_kernel, factor=factor),
        grid_spec=pltpu.PrefetchScalarGridSpec(
            num_scalar_prefetch=1,
            grid=(1,),
            in_specs=[
                part_spec(rows, width, 0),
                part_spec(rows, width, 1),
                part_spec(rows, width, 2),
                part_spec(far, width, 1),
                part_spec(far, width, 2),
                whole((rows, width)),
                whole((rows, 128)),
            ],
            out_specs=whole((rows, width)),
        ),
        out_shape=jax.ShapeDtypeStruct((rows, width), BF),
        compiler_params=params(),
        cost_estimate=cost(6 * HEADS * rows * (rows + far) * WIN, 6 * far * width, HEADS * rows * far),
    )(big, own, own, own, others, others, grad, stat)


def key_grad(big, own, others, pack, packs, factor):
    rows, width = own.shape[0], own.shape[1] // 3
    far = others.shape[0]
    return pl.pallas_call(
        functools.partial(key_grad_kernel, factor=factor),
        grid_spec=pltpu.PrefetchScalarGridSpec(
            num_scalar_prefetch=1,
            grid=(1,),
            in_specs=[
                part_spec(rows, width, 1),
                part_spec(rows, width, 2),
                part_spec(rows, width, 0),
                part_spec(far, width, 0),
                whole(pack.shape),
                whole(packs.shape),
            ],
            out_specs=[whole((rows, width))] * 2,
            scratch_shapes=[
                pltpu.VMEM((2 * HEADS, rows + far), F32),
                pltpu.VMEM((far, width), BF),
            ],
        ),
        out_shape=[jax.ShapeDtypeStruct((rows, width), BF)] * 2,
        compiler_params=params(),
        cost_estimate=cost(8 * HEADS * rows * (rows + far) * WIN, 6 * far * width, HEADS * rows * far),
    )(big, own, own, own, others, pack, packs)


def cross_attend(queries, keys, values, factor, live):
    rows, width = queries.shape
    return pl.pallas_call(
        functools.partial(cross_kernel, factor=factor, live=live),
        out_shape=jax.ShapeDtypeStruct((rows, width), BF),
        compiler_params=params(),
        cost_estimate=cost(4 * HEADS * rows * 128 * WIN, 6 * rows * width, HEADS * rows * 128),
    )(queries, keys, values)


def cross_grad(queries, grad, keys, values, factor, live):
    rows, width = queries.shape
    return pl.pallas_call(
        functools.partial(cross_grad_kernel, factor=factor, live=live),
        out_shape=[
            jax.ShapeDtypeStruct((rows, width), BF),
            jax.ShapeDtypeStruct(keys.shape, F32),
            jax.ShapeDtypeStruct(keys.shape, F32),
        ],
        compiler_params=params(),
        cost_estimate=cost(10 * HEADS * rows * 128 * WIN, 12 * rows * width, HEADS * rows * 128),
    )(queries, grad, keys, values)


def weight_grad(order, sources, size, high, mode):
    count = len(sources)
    rows, width = sources[0][0].shape
    body, _ = slice_parts(size)
    pieces = count * (width // 4 // high)
    wide = 2 * pieces * body + 128
    if mode == "rows":
        shape, block, number = (2, high, 2 * wide), (1, high, 2 * wide), 2
        places = [
            lambda s, _: (jnp.minimum(s, 1), 0, 0),
            lambda s, _: (jnp.maximum(s - 2, 0), 0, 0),
        ]
    elif mode == "chips":
        shape, block, number = (4, high, wide), (1, high, wide), 2
        places = [lambda s, _: (s, 0, 0)] * 2
    else:
        shape, block, number = (2, high, wide), (2, high, wide), 4
        places = [lambda s, _: (0, 0, 0)] * 4
    return pl.pallas_call(
        functools.partial(weight_grad_kernel, count=count, size=size, high=high, mode=mode, outs=number),
        grid_spec=pltpu.PrefetchScalarGridSpec(
            num_scalar_prefetch=1,
            grid=(4,),
            in_specs=[whole(array.shape) for source in sources for array in source],
            out_specs=[pl.BlockSpec(block, place) for place in places],
            scratch_shapes=[pltpu.VMEM((count, width, 2 * rows), BF)],
        ),
        out_shape=[jax.ShapeDtypeStruct(shape, BF)] * number,
        compiler_params=params(),
        cost_estimate=cost(8 * pieces * rows * high * wide, 2 * pieces * high * wide),
    )(order, *[array for source in sources for array in source])


def mlp(inputs, grad, w_up, w_down):
    rows, width = inputs.shape
    units = w_up.shape[1]
    tile = 512
    tiles = units // tile
    vmem = pl.BlockSpec(memory_space=pltpu.VMEM)
    hbm = pl.BlockSpec(memory_space=pl.ANY)
    return pl.pallas_call(
        functools.partial(mlp_kernel, tile=tile),
        in_specs=[vmem, vmem, hbm, hbm],
        out_specs=[vmem] * 4,
        out_shape=[jax.ShapeDtypeStruct((rows, units), BF)] * 2
        + [jax.ShapeDtypeStruct((rows, width), F32)] * 2,
        scratch_shapes=[
            pltpu.VMEM((tiles, width, tile), BF),
            pltpu.VMEM((tiles, tile, width), BF),
            pltpu.SemaphoreType.DMA((2, tiles)),
        ]
        + [pltpu.VMEM((rows, tile), BF)] * 4,
        compiler_params=params(),
        cost_estimate=cost(8 * rows * width * units, 4 * width * units, rows * units),
    )(inputs, grad, w_up, w_down)


def normal(stream):
    centred = stream - jnp.mean(stream, axis=-1, keepdims=True)
    spread = lax.rsqrt(jnp.mean(centred * centred, axis=-1, keepdims=True) + EPS)
    return centred * spread, spread


def norm_back(normed, spread, scale, grad):
    scaled = grad * (1.0 + scale)
    back = spread * (
        scaled
        - jnp.mean(scaled, axis=-1, keepdims=True)
        - normed * jnp.mean(scaled * normed, axis=-1, keepdims=True)
    )
    return back, jnp.sum(grad, axis=0), jnp.sum(grad * normed, axis=0)


def local(
    tokens,
    image_len,
    timestep,
    caption,
    time_embed,
    mod_table,
    w_qkv,
    w_out,
    cross_q,
    cross_kv,
    cross_out,
    w_up,
    w_down,
    cotangent,
):
    sp_count = lax.axis_size("sp")
    dp_count = lax.axis_size("dp")
    place = lax.axis_index("sp")
    row_place = lax.axis_index("dp")
    core = place % 2
    rows, width = tokens.shape[1:]
    factor = 1.0 / math.sqrt(width // HEADS)
    blocks = BIG // rows
    assert blocks == 4

    big, modulation = prelude(place, image_len, timestep, time_embed, mod_table, rows)
    shift_one, scale_one, gate_one, shift_two, scale_two, gate_two = [modulation[i] for i in range(6)]

    def tie(value, *before):
        return lax.optimization_barrier((value, *[array for array in before if array is not None]))[0]

    pairs = [(i, i ^ 1) for i in range(sp_count)]
    others = [(i, i + 1) for i in range(1, sp_count - 1, 2)] + [(i + 1, i) for i in range(1, sp_count - 1, 2)]
    ahead = [(i, i + 2) for i in range(sp_count - 2)]
    back = [(i + 2, i) for i in range(sp_count - 2)]

    def image_blocks(block):
        pair = lax.ppermute(block, "sp", pairs)
        from_back = lax.ppermute(block, "sp", ahead)
        from_ahead = lax.ppermute(block, "sp", back)
        send_pair = jnp.where(big[1] == 1, from_ahead, from_back)
        send_other = jnp.where(core == 1, from_back, from_ahead)
        second = lax.ppermute(send_pair, "sp", pairs)
        third = lax.ppermute(send_other, "sp", others)
        return (
            [
                second,
                jnp.where(big[2] == 1, pair, third),
                jnp.where(big[3] == 1, from_ahead, from_back),
            ],
            send_pair,
            send_other,
        )

    def swap(array):
        return lax.ppermute(array, "sp", pairs)

    token_blocks, *token_sends = image_blocks(tokens[0])

    def first_norm(block):
        normed, spread = normal(block.astype(F32))
        return normed, spread, (normed * (1.0 + scale_one) + shift_one).astype(BF)

    stream_in = tokens[0].astype(F32)
    normed_one, spread_one, first_in = first_norm(tokens[0])
    other_in = first_norm(jnp.concatenate(token_blocks, axis=0))[2]

    core_flag = core.reshape(1)
    chips = sp_count // 2
    square = dp_count == 4 and chips == 4

    def own_half(*grads, joined=True):
        if square:
            return halves(core_flag, grads, sp_count, joined)
        grads = [jnp.concatenate(grads, axis=1)] if joined else grads
        size = grads[0].shape[1] // sp_count
        even, odd = [
            jnp.concatenate(
                [g[:, i * size : (i + 1) * size] for g in grads for i in range(c, sp_count, 2)], axis=1
            )
            for c in (0, 1)
        ]
        return jnp.where(core == 0, even, odd), jnp.where(core == 0, odd, even)

    def add(*terms):
        return sum(term.astype(F32) for term in terms)

    near, far = (place // 2) & 1, (place // 4) & 1
    row_bits = [row_place & 1, row_place >> 1]
    high = width // 4

    def to_row(array, bit):
        return lax.ppermute(array, "dp", [(i, i ^ (1 << bit)) for i in range(dp_count)])

    def to_chip(array, bit):
        return lax.ppermute(array, "sp", [(i, i ^ (2 << bit)) for i in range(sp_count)])

    def plain_sum(sources, size):
        finals = []
        for item, (x0, x1, g0, g1) in enumerate(sources):
            columns = slice(item * chips * size, (item + 1) * chips * size)
            part = (matmul_tn(x0, g0[:, columns]) + matmul_tn(x1, g1[:, columns])).astype(BF)
            part = part.reshape(dp_count, -1, chips, size).transpose(0, 2, 1, 3)
            bit = dp_count // 2
            while bit:
                mine = (row_place // bit) % 2
                part = part.reshape(2, bit, chips, -1, size)
                got = lax.ppermute(part[1 - mine], "dp", [(i, i ^ bit) for i in range(dp_count)])
                part = add(part[mine], got).astype(BF)
                bit //= 2
            part = part.reshape(chips, -1, size)
            bit = chips // 2
            while bit:
                mine = (place // 2 // bit) % 2
                part = part.reshape(2, bit, -1, size)
                got = lax.ppermute(part[1 - mine], "sp", [(i, i ^ (2 * bit)) for i in range(sp_count)])
                part = add(part[mine], got).astype(BF)
                bit //= 2
            finals.append(part[0].astype(F32))
        return finals

    def sum_rows_first(source, size, first):
        second = 1 - first
        pieces = source[0].shape[1] // width
        mine = row_bits[first]
        order = jnp.stack(
            [((1 - mine if s < 2 else mine) << first) + ((s % 2) << second) for s in range(4)]
        )
        send, keep = weight_grad(order, [source], size, high, "rows")
        yield send
        got = to_row(send, first)
        mine = row_bits[second]
        send = add_picked(1 - mine, [keep, got])
        yield send
        send, keep = split_rows(jnp.stack([mine, near]), [keep, got], to_row(send, second))
        yield send
        send, keep = split_body(far, keep, to_chip(send, 0), size, pieces)
        yield send
        turned = size < 256
        yield add_last(keep, to_chip(send, 1), size, [(pieces * high, size)], turned)

    def sum_both_first(source, size):
        order = jnp.stack([jnp.int32(i) for i in range(4)] + row_bits)
        outs = weight_grad(order, [source], size, high, "both")
        yield outs
        got = [to_row(outs[0], 0), to_row(outs[2], 1)]
        sends = [add_picked(1 - row_bits[1], [outs[1], got[0]]), add_picked(1 - row_bits[0], [outs[3], got[1]])]
        yield sends
        more = [to_row(sends[0], 1), to_row(sends[1], 0)]
        flags = jnp.stack([row_bits[1], row_bits[0], near])
        send, keep = split_pair(flags, [(outs[1], got[0], more[0]), (outs[3], got[1], more[1])])
        yield send
        send, keep = split_body(far, keep, to_chip(send, 0), size, 1)
        yield send
        yield add_last(keep, to_chip(send, 1), size, [(high, size)], False)

    def sum_chips_first(sources, size):
        order = jnp.stack([jnp.int32(i) for i in range(4)] + [near])
        send, keep = weight_grad(order, sources, size, high, "chips")
        yield send
        send, keep = split_body(far, keep, to_chip(send, 0), size, len(sources))
        yield send
        mine = row_bits[0]
        order = jnp.stack([2 * (s % 2) + (1 - mine if s < 2 else mine) for s in range(4)])
        send, keep = pass_rows(order, keep, to_chip(send, 1), 2)
        yield send
        order = jnp.stack([1 - row_bits[1], row_bits[1]])
        send, keep = pass_rows(order, keep, to_row(send, 0), 1)
        yield send
        yield add_last(keep, to_row(send, 1), size, [(high, size)] * len(sources), True)

    def spread_vector(vector):
        for axis, name, count, mine in ((1, "sp", sp_count, place), (0, "dp", dp_count, row_place)):
            bit = count // 2
            while bit:
                shape = vector.shape
                split = vector.reshape(shape[:axis] + (2, bit) + shape[axis + 1 :])
                at = lambda i: lax.dynamic_index_in_dim(split, i, axis, keepdims=False)
                own = (mine // bit) % 2
                got = lax.ppermute(at(1 - own), name, [(i, i ^ bit) for i in range(count)])
                vector = at(own) + got
                bit //= 2
        return vector.reshape(-1)

    caption_rows = caption[0]
    live = caption_rows.shape[0]
    padded = -(-live // 128) * 128
    caption_pad = jnp.concatenate([caption_rows, jnp.zeros((padded - live, width), BF)], axis=0)
    text_kv = matmul(caption_pad, cross_kv).astype(BF)
    text_keys, text_values = text_kv[:, :width], text_kv[:, width:]
    grad_three = cotangent[0].astype(F32)
    grad_mlp = (gate_two * grad_three).astype(BF)
    mlp_keep, mlp_send = own_half(grad_mlp, joined=False)
    mlp_got = swap(mlp_send)
    first_pair = swap(first_in)
    own = matmul(tie(first_in, *token_sends), w_qkv).astype(BF)
    others_qkv = matmul(other_in, w_qkv).astype(BF)
    attended, logsum = attend(big, own, others_qkv, factor)
    attn_branch = matmul(attended, w_out)
    stream_one = stream_in + gate_one * attn_branch
    cross_in = stream_one.astype(BF)
    cross_queries = matmul(cross_in, cross_q).astype(BF)
    cross_mixed = cross_attend(cross_queries, text_keys, text_values, factor, live)
    stream_two = stream_one + matmul(cross_mixed, cross_out)
    normed_two, spread_two = normal(stream_two)
    second_in = (normed_two * (1.0 + scale_two) + shift_two).astype(BF)
    second_pair = swap(second_in)
    hidden, grad_pre, mlp_branch, grad_second = mlp(second_in, grad_mlp, w_up, w_down)
    stream_three = stream_two + gate_two * mlp_branch

    grad_gate_two = jnp.sum(grad_three * mlp_branch, axis=0)
    pre_keep, pre_send = own_half(grad_pre)
    slice_of = lambda weight: weight.shape[1] // sp_count
    down_source = (hidden, swap(hidden), mlp_keep, mlp_got)
    up_source = (second_in, second_pair, pre_keep, swap(pre_send))
    if square:
        down_sum = sum_rows_first(down_source, slice_of(w_down), 0)
        up_sum = sum_rows_first(up_source, slice_of(w_up), 1)
        send_down, send_up = next(down_sum), next(up_sum)
    else:
        send_down = send_up = None
    back_two, grad_shift_two, grad_scale_two = norm_back(normed_two, spread_two, scale_two, grad_second)
    grad_stream_two = grad_three + back_two
    grad_cross = grad_stream_two.astype(BF)
    small_acts = [(acts, swap(acts)) for acts in (cross_mixed, cross_in, attended)]
    grad_mixed = matmul_nt(grad_cross, cross_out).astype(BF)
    grad_mixed = tie(grad_mixed, send_down, send_up, *[pair for _, pair in small_acts])
    grad_cq_rows, grad_text_keys, grad_text_values = cross_grad(
        cross_queries, grad_mixed, text_keys, text_values, factor, live
    )
    grad_text = jnp.concatenate([grad_text_keys[:live], grad_text_values[:live]], axis=1)
    grad_stream_one = grad_stream_two + matmul_nt(grad_cq_rows, cross_q)
    grad_gate_one = jnp.sum(grad_stream_one * attn_branch, axis=0)
    grad_attn = (gate_one * grad_stream_one).astype(BF)
    grad_back = matmul_nt(grad_attn, w_out).astype(BF)

    column = jnp.arange(width, dtype=jnp.int32)[:, None] // (width // HEADS)
    pick = (column + HEADS == jnp.arange(128, dtype=jnp.int32)[None, :]).astype(F32)
    inner = jnp.dot(
        grad_back.astype(F32) * attended.astype(F32), pick, precision=lax.Precision.HIGHEST
    )
    stat = logsum + inner
    turned = stat.T[: 2 * HEADS].reshape(4, 8, rows).transpose(1, 0, 2).reshape(8, 4 * rows)
    upper = lax.reduce_precision(turned, exponent_bits=8, mantissa_bits=7)
    both = jnp.concatenate([upper, turned - upper], axis=0).astype(BF)
    both = jnp.concatenate([both, jnp.zeros((16, width - 4 * rows), BF)], axis=1)
    pack = jnp.concatenate([grad_back, both], axis=0)
    pack_blocks, *pack_sends = image_blocks(pack)
    packs = jnp.stack(pack_blocks)

    small_keep, small_send = own_half(grad_cross, grad_cq_rows, grad_attn, joined=False)
    small_got = swap(small_send)
    small = [(*acts, small_keep, small_got) for acts in small_acts]
    send_small = None
    if square:
        small_sum = sum_chips_first(small, slice_of(w_out))
        send_small = next(small_sum)

    grad_queries = query_grad(big, own, others_qkv, tie(grad_back, *pack_sends), stat, factor)
    before = [next(down_sum), next(up_sum), send_small] if square else []
    grad_keys, grad_values = key_grad(big, own, others_qkv, tie(pack, *before), packs, factor)
    grad_proj = jnp.concatenate([grad_queries, grad_keys, grad_values], axis=1)
    proj_keep, proj_send = own_half(grad_queries, grad_keys, grad_values)
    qkv_source = (first_in, first_pair, proj_keep, swap(proj_send))
    before = []
    if square:
        qkv_sum = sum_both_first(qkv_source, slice_of(w_qkv))
        before = next(qkv_sum)
    grad_first = matmul_nt(tie(grad_proj, *before), w_qkv)
    back_one, grad_shift_one, grad_scale_one = norm_back(normed_one, spread_one, scale_one, grad_first)
    grad_tokens = grad_stream_one + back_one

    if square:
        sums = [down_sum, up_sum, small_sum, qkv_sum]
        final_down, final_up, final_small, final_qkv = [list(each)[-1] for each in sums]
    else:
        final_down = plain_sum([down_source], slice_of(w_down))
        final_up = plain_sum([up_source], slice_of(w_up))
        final_small = plain_sum(small, slice_of(w_out))
        final_qkv = plain_sum([qkv_source], slice_of(w_qkv))
    (final_down,), (final_up,), (final_qkv,) = final_down, final_up, final_qkv
    text_part = lax.psum_scatter(grad_text, "sp", scatter_dimension=1, tiled=True).astype(BF)
    part_ckv = matmul_tn(caption_rows, text_part).astype(BF)
    final_ckv = lax.psum_scatter(part_ckv, "dp", scatter_dimension=0, tiled=True).astype(F32)
    table = jnp.concatenate(
        [grad_shift_one, grad_scale_one, grad_gate_one, grad_shift_two, grad_scale_two, grad_gate_two]
    )
    final_table = spread_vector(table.reshape(dp_count, sp_count, -1))
    return (
        stream_three[None],
        grad_tokens[None],
        final_table,
        final_qkv,
        final_small[2],
        final_small[1],
        final_ckv,
        final_small[0],
        final_up,
        final_down,
    )


def solution(mesh):
    return jax.shard_map(
        local,
        mesh=mesh,
        in_specs=(
            P("dp", "sp", None),
            P("dp", None),
            P("dp", None),
            P("dp", None, None),
            P(),
            P(),
            P(),
            P(),
            P(),
            P(),
            P(),
            P(),
            P(),
            P("dp", "sp", None),
        ),
        out_specs=(
            P("dp", "sp", None),
            P("dp", "sp", None),
            P(("dp", "sp")),
            P("dp", "sp"),
            P("dp", "sp"),
            P("dp", "sp"),
            P("dp", "sp"),
            P("dp", "sp"),
            P("dp", "sp"),
            P("dp", "sp"),
        ),
        check_vma=False,
    )
```

```python
import functools
import math

import jax
import jax.numpy as jnp
from jax import lax
from jax.experimental import pallas as pl
from jax.experimental.pallas import tpu as pltpu
from jax.sharding import PartitionSpec as P

HEADS = 16
BIG = 1024
EPS = 1e-06
BIGNEG = -1e30
LOG2E = 1.4426950408889634
BF = jnp.bfloat16
F32 = jnp.float32
WIN = 256
COST_SCALE = 0.001
MIB = 1024 * 1024


def matmul(left, right):
    return jnp.dot(left, right, preferred_element_type=F32)


def matmul_tn(left, right):
    return lax.dot_general(left, right, (((0,), (0,)), ((), ())), preferred_element_type=F32)


def matmul_nt(left, right):
    return lax.dot_general(left, right, (((1,), (1,)), ((), ())), preferred_element_type=F32)


def head_window(head, width):
    size = width // HEADS
    low = head * size
    start = pl.multiple_of(jnp.minimum(low // 128 * 128, width - WIN), 128)
    lane = lax.broadcasted_iota(jnp.int32, (1, WIN), 1) + start
    return start, jnp.logical_and(lane >= low, lane < low + size)


def window(ref, start, offset=0):
    return ref[:, pl.ds(pl.multiple_of(start + offset, 128), WIN)]


def keep_columns(ref, start, mask, value):
    win = pl.ds(start, WIN)
    ref[:, win] = jnp.where(mask, value, ref[:, win])


def each_head(body, unroll=4):
    def step(head, carry):
        body(head)
        return carry

    lax.fori_loop(0, HEADS, step, 0, unroll=unroll)


def attend_kernel(big_ref, own_ref, far_ref, out_ref, lse_ref, *, factor):
    width = out_ref.shape[1]
    scale = factor * LOG2E

    def run(sides):
        def one_head(head):
            start, mask = head_window(head, width)
            query = window(own_ref, start) * mask.astype(BF)
            scores = [matmul_nt(query, window(side, start, width)) for side in sides]
            top = functools.reduce(jnp.maximum, [jnp.max(s, axis=1, keepdims=True) for s in scores])
            raised = [jnp.exp2((s - top) * scale) for s in scores]
            total = sum(jnp.sum(r, axis=1, keepdims=True) for r in raised)
            inverse = 1.0 / total
            result = sum(
                matmul((r * inverse).astype(BF), window(side, start, 2 * width))
                for r, side in zip(raised, sides)
            )
            keep_columns(out_ref, start, mask, result.astype(BF))
            lane = lax.broadcasted_iota(jnp.int32, (1, 128), 1)
            lse_ref[...] = jnp.where(lane == head, top * scale + jnp.log2(total), lse_ref[...])

        each_head(one_head)

    lse_ref[...] = jnp.zeros_like(lse_ref)

    @pl.when(big_ref[0] == 1)
    def _():
        run([own_ref, far_ref])

    @pl.when(big_ref[0] == 0)
    def _():
        run([own_ref])


def query_grad_kernel(big_ref, own_ref, far_ref, pack_ref, stat_ref, out_ref, *, factor):
    rows, width = out_ref.shape
    scale = factor * LOG2E

    def run(sides):
        def one_head(head):
            start, mask = head_window(head, width)
            keep = mask.astype(BF)
            query = window(own_ref, start) * keep
            grad = window(pack_ref.at[0:rows, :], start) * keep
            lane = lax.broadcasted_iota(jnp.int32, (1, 128), 1)
            stat = stat_ref[...]
            lse = jnp.sum(jnp.where(lane == head, stat, 0.0), axis=1, keepdims=True)
            delta = jnp.sum(jnp.where(lane == head + HEADS, stat, 0.0), axis=1, keepdims=True)
            total = None
            for side in sides:
                key = window(side, start, width)
                prob = jnp.exp2(matmul_nt(query, key) * scale - lse)
                grad_prob = matmul_nt(grad, window(side, start, 2 * width))
                grad_score = (prob * (grad_prob - delta)).astype(BF)
                part = matmul(grad_score, key)
                total = part if total is None else total + part
            keep_columns(out_ref, start, mask, (total * factor).astype(BF))

        each_head(one_head)

    @pl.when(big_ref[0] == 1)
    def _():
        run([own_ref, far_ref])

    @pl.when(big_ref[0] == 0)
    def _():
        run([own_ref])


def key_grad_kernel(big_ref, own_ref, far_ref, pack_ref, *refs, factor):
    packs, (dk_ref, dv_ref, stats, grads) = refs[:-4], refs[-4:]
    rows, width = dk_ref.shape
    scale = factor * LOG2E
    blocks = 1 + len(packs)

    def unpack(block, pack):
        both = pack[rows : rows + 16, :].astype(F32)
        joined = both[:8] + both[8:]
        for group in range(4):
            stats[8 * group : 8 * group + 8, block * rows : block * rows + rows] = joined[
                :, group * rows : group * rows + rows
            ]

    unpack(0, pack_ref)
    for block, pack in enumerate(packs):
        unpack(block + 1, pack)
        grads[block * rows : (block + 1) * rows, :] = pack[0:rows, :]

    def run(parts):
        def one_head(head):
            start, mask = head_window(head, width)
            keep = mask.astype(BF)
            key = window(own_ref, start, width) * keep
            value = window(own_ref, start, 2 * width) * keep
            lse = stats[pl.ds(head, 1), :]
            delta = stats[pl.ds(head + HEADS, 1), :]
            grad_key = grad_value = 0.0
            for query_ref, grad_ref, low, high in parts:
                query, grad = window(query_ref, start), window(grad_ref.at[0 : high - low, :], start)
                prob = jnp.exp2(matmul_nt(key, query) * scale - lse[:, low:high])
                grad_prob = matmul_nt(value, grad)
                grad_score = (prob * (grad_prob - delta[:, low:high])).astype(BF)
                grad_value = grad_value + matmul(prob.astype(BF), grad)
                grad_key = grad_key + matmul(grad_score, query)
            keep_columns(dk_ref, start, mask, (grad_key * factor).astype(BF))
            keep_columns(dv_ref, start, mask, grad_value.astype(BF))

        each_head(one_head)

    own = (own_ref, pack_ref, 0, rows)

    @pl.when(big_ref[0] == 1)
    def _():
        run([own, (far_ref, grads, rows, blocks * rows)])

    @pl.when(big_ref[0] == 0)
    def _():
        run([own])


def text_probs(query, key, scale, live):
    scores = matmul_nt(query, key)
    lane = lax.broadcasted_iota(jnp.int32, (1, scores.shape[1]), 1)
    scores = jnp.where(lane < live, scores, BIGNEG)
    raised = jnp.exp2((scores - jnp.max(scores, axis=1, keepdims=True)) * scale)
    return raised * (1.0 / jnp.sum(raised, axis=1, keepdims=True))


def normal(stream):
    centred = stream - jnp.mean(stream, axis=-1, keepdims=True)
    spread = lax.rsqrt(jnp.mean(centred * centred, axis=-1, keepdims=True) + EPS)
    return centred * spread, spread


def norm_back(normed, spread, scale, grad):
    scaled = grad * (1.0 + scale)
    back = spread * (
        scaled
        - jnp.mean(scaled, axis=-1, keepdims=True)
        - normed * jnp.mean(scaled * normed, axis=-1, keepdims=True)
    )
    return back, jnp.sum(grad, axis=0, keepdims=True), jnp.sum(grad * normed, axis=0, keepdims=True)


def middle_kernel(
    tokens_ref, mod_ref, att_ref, out_w_ref, query_w_ref, cross_w_ref, text_ref,
    branch_ref, cross_in_ref, queries_ref, mixed_ref, stream_ref, second_ref, *, factor, live
):
    width = tokens_ref.shape[1]
    branch = matmul(att_ref[...], out_w_ref[...])
    branch_ref[...] = branch
    stream = tokens_ref[...].astype(F32) + mod_ref[2:3, :] * branch
    stream_ref[...] = stream
    cross_in = stream.astype(BF)
    cross_in_ref[...] = cross_in
    queries_ref[...] = matmul(cross_in, query_w_ref[...]).astype(BF)

    def one_head(head):
        start, mask = head_window(head, width)
        query = window(queries_ref, start) * mask.astype(BF)
        probs = text_probs(query, window(text_ref, start), factor * LOG2E, live)
        result = matmul(probs.astype(BF), window(text_ref, start, width))
        keep_columns(mixed_ref, start, mask, result.astype(BF))

    each_head(one_head, 8)
    stream = stream_ref[...] + matmul(mixed_ref[...], cross_w_ref[...])
    stream_ref[...] = stream
    second_ref[...] = (normal(stream)[0] * (1.0 + mod_ref[4:5, :]) + mod_ref[3:4, :]).astype(BF)


def middle_grad_kernel(
    core_ref, second_grad_ref, stream_ref, cot_ref, mlp_ref, mod_ref, branch_ref, att_ref, lse_ref,
    queries_ref, text_ref, out_w_ref, query_w_ref, cross_w_ref,
    out_ref, one_ref, keep_ref, send_ref, text_grad_ref, pack_ref, stat_ref, table_ref,
    mixed, grad_queries, text_key, text_value, *, factor, live, count
):
    rows, width = cot_ref.shape
    cot = cot_ref[...].astype(F32)
    stream = stream_ref[...]
    mlp = mlp_ref[...]
    out_ref[...] = stream + mod_ref[5:6, :] * mlp
    normed, spread = normal(stream)
    back, shift, scale = norm_back(normed, spread, mod_ref[4:5, :], second_grad_ref[...])
    table_ref[...] = jnp.zeros_like(table_ref)
    table_ref[3:4, :] = shift
    table_ref[4:5, :] = scale
    table_ref[5:6, :] = jnp.sum(cot * mlp, axis=0, keepdims=True)
    grad_two = cot + back
    one_ref[...] = grad_two
    grad_cross = grad_two.astype(BF)
    mixed[...] = matmul_nt(grad_cross, cross_w_ref[...]).astype(BF)

    def one_head(head):
        start, mask = head_window(head, width)
        keep = mask.astype(BF)
        query = window(queries_ref, start)
        grad = window(mixed, start)
        key = window(text_ref, start)
        probs = text_probs(query * keep, key, factor * LOG2E, live)
        grad_probs = matmul_nt(grad * keep, window(text_ref, start, width))
        inner = jnp.sum(probs * grad_probs, axis=1, keepdims=True)
        grad_scores = (probs * (grad_probs - inner)).astype(BF)
        keep_columns(grad_queries, start, mask, (matmul(grad_scores, key) * factor).astype(BF))
        keep_columns(text_key, start, mask, matmul_tn(grad_scores, query) * factor)
        keep_columns(text_value, start, mask, matmul_tn(probs.astype(BF), grad))

    each_head(one_head)
    text_grad_ref[:, :width] = text_key[0:live, :]
    text_grad_ref[:, width:] = text_value[0:live, :]
    grad_cq = grad_queries[...]
    grad_one = one_ref[...] + matmul_nt(grad_cq, query_w_ref[...])
    one_ref[...] = grad_one
    table_ref[2:3, :] = jnp.sum(grad_one * branch_ref[...], axis=0, keepdims=True)
    grad_attn = (mod_ref[2:3, :] * grad_one).astype(BF)
    grad_att = matmul_nt(grad_attn, out_w_ref[...]).astype(BF)
    pack_ref[0:rows, :] = grad_att

    product = grad_att.astype(F32) * att_ref[...].astype(F32)
    upper = product.astype(BF)
    lower = (product - upper.astype(F32)).astype(BF)
    size = width // HEADS
    column = lax.broadcasted_iota(jnp.int32, (width, 128), 0)
    low = (lax.broadcasted_iota(jnp.int32, (width, 128), 1) - HEADS) * size
    pick = jnp.logical_and(column >= low, column < low + size).astype(BF)
    stat = lse_ref[...] + matmul(upper, pick) + matmul(lower, pick)
    stat_ref[...] = stat
    turned = stat.T
    upper = [turned[8 * g : 8 * g + 8, :].astype(BF).astype(F32) for g in range(4)]
    lower = [turned[8 * g : 8 * g + 8, :] - part for g, part in enumerate(upper)]
    both = [jnp.concatenate(pair, axis=0) for pair in zip(upper, lower)]
    pack_ref[rows : rows + 16, :] = side_by_side(both, width).astype(BF)

    if count:
        for core in (0, 1):

            @pl.when(core_ref[0] == core)
            def _(core=core):
                grads = [grad_cross, grad_cq, grad_attn]
                keep_ref[...] = half_columns(grads, core, count, False, keep_ref.shape[1])
                send_ref[...] = half_columns(grads, 1 - core, count, False, send_ref.shape[1])

    else:
        for index, grad in enumerate((grad_cross, grad_cq, grad_attn)):
            keep_ref[:, index * width : (index + 1) * width] = grad


def last_grad_kernel(
    dq_ref, dk_ref, dv_ref, weight_ref, tokens_ref, mod_ref, one_ref, table_in_ref, out_ref, table_ref
):
    width = tokens_ref.shape[1]
    grad = sum(
        matmul_nt(ref[...], weight_ref[:, part * width : (part + 1) * width])
        for part, ref in enumerate((dq_ref, dk_ref, dv_ref))
    )
    normed, spread = normal(tokens_ref[...].astype(F32))
    back, shift, scale = norm_back(normed, spread, mod_ref[1:2, :], grad)
    out_ref[...] = one_ref[...] + back
    table_ref[...] = table_in_ref[...]
    table_ref[0:1, :] = shift
    table_ref[1:2, :] = scale


def side_by_side(pieces, width):
    missing = width - sum(piece.shape[1] for piece in pieces)
    if missing:
        pieces = [*pieces, jnp.zeros((pieces[0].shape[0], missing), pieces[0].dtype)]
    return pieces[0] if len(pieces) == 1 else jnp.concatenate(pieces, axis=1)


def slice_parts(size):
    return size // 128 * 128, size % 128


def half_columns(grads, core, count, joined, wide):
    if joined and len(grads) > 1:
        grads = [jnp.concatenate(grads, axis=1)]
    size = grads[0].shape[1] // count
    body, _ = slice_parts(size)
    picked = []
    for grad in grads:
        bodies = [[], []]
        tails = [[], []]
        for chip in range(count // 2):
            low = (2 * chip + core) * size
            bodies[chip % 2].append(grad[:, low : low + body])
            tails[chip % 2].append(grad[:, low + body : low + size])
        if joined:
            for parity in (0, 1):
                picked += bodies[parity]
                picked.append(side_by_side(tails[parity], 128))
        else:
            picked += bodies[0] + bodies[1]
            picked.append(side_by_side(tails[0] + tails[1], 128))
    return side_by_side(picked, wide)


def halves_kernel(core_ref, *refs, count, joined):
    keep_ref, send_ref = refs[-2:]
    for core in (0, 1):

        @pl.when(core_ref[0] == core)
        def _(core=core):
            grads = [ref[...] for ref in refs[:-2]]
            keep_ref[...] = half_columns(grads, core, count, joined, keep_ref.shape[1])
            send_ref[...] = half_columns(grads, 1 - core, count, joined, send_ref.shape[1])


def store_halves(flag, stores, pieces):
    for value in (0, 1):

        @pl.when(flag == value)
        def _(value=value):
            for store, piece in zip(stores, (pieces[1 - value], pieces[value])):
                store(piece())


def into(ref, *index):
    def store(value):
        if index:
            ref[index[0]] = value.astype(ref.dtype)
        else:
            ref[...] = value.astype(ref.dtype)

    return store


def add(*terms):
    return sum(term.astype(F32) for term in terms)


def weight_grad_kernel(order_ref, *refs, count, size, high, mode):
    sources, outs, turned = refs[: 4 * count], refs[4 * count : -1], refs[-1]
    rows, width = sources[0].shape
    body, tail = slice_parts(size)
    tall = width // 4
    for item in range(count):
        for part, ref in enumerate(sources[4 * item : 4 * item + 2]):
            for low in range(0, width, 128):
                turned[item, low : low + 128, part * rows : part * rows + rows] = ref[:, low : low + 128].T

    def one_chunk(step, carry):
        chunk = order_ref[step]
        pieces = []
        for item in range(count):
            g0_ref, g1_ref = sources[4 * item + 2 : 4 * item + 4]
            wide = g0_ref.shape[1] // count
            columns = slice(item * wide, item * wide + wide)
            for low in range(0, tall, high):
                here = pl.ds(pl.multiple_of(chunk * tall + low, 16), high)
                total = matmul(turned[item, here, 0:rows], g0_ref[:, columns])
                pieces.append((total + matmul(turned[item, here, rows:], g1_ref[:, columns])).astype(BF))
        if len(pieces) == 1:
            half = pieces[0].shape[1] // 2
            groups = [pieces[0][:, :half], pieces[0][:, half:]]
        else:
            groups = [
                side_by_side(
                    [piece[:, 2 * p * body : 2 * (p + 1) * body] for piece in pieces]
                    + [piece[:, 4 * body + 2 * p * tail : 4 * body + 2 * (p + 1) * tail] for piece in pieces],
                    outs[0].shape[-1] // (2 if mode == "rows" else 1),
                )
                for p in (0, 1)
            ]
        half = groups[0].shape[1]
        if mode == "rows":
            for index, ref in enumerate(outs):

                @pl.when(step // 2 == index)
                def _(ref=ref):
                    ref[step % 2, :, :half] = groups[0]
                    ref[step % 2, :, half:] = groups[1]

        elif mode == "chips":
            store_halves(
                order_ref[4], [into(ref, step) for ref in outs], [lambda: groups[0], lambda: groups[1]]
            )
        else:
            for p in (0, 1):
                first, second = (chunk >> p) & 1, (chunk >> (1 - p)) & 1
                for kept in (0, 1):

                    @pl.when((first == order_ref[4 + p]) == (kept == 1))
                    def _(p=p, kept=kept, second=second):
                        outs[2 * p + kept][second] = groups[p]

        return carry

    lax.fori_loop(0, 4, one_chunk, 0)


def add_kernel(flag_ref, *refs):
    refs[-1][...] = add(*[ref[flag_ref[0]] for ref in refs[:-1]]).astype(BF)


def split_rows_kernel(flag_ref, *refs):
    half = refs[-1].shape[1]
    mine = flag_ref[0]

    def group(p):
        columns = slice(p * half, (p + 1) * half)
        return lambda: add(*[ref[mine, :, columns] for ref in refs[:-3]], refs[-3][:, columns])

    store_halves(flag_ref[1], [into(ref) for ref in refs[-2:]], [group(0), group(1)])


def split_pair_kernel(flag_ref, *refs):
    def group(p):
        keep, got, more = refs[3 * p : 3 * p + 3]
        return lambda: add(keep[flag_ref[p]], got[flag_ref[p]], more[...])

    store_halves(flag_ref[2], [into(ref) for ref in refs[-2:]], [group(0), group(1)])


def split_body_kernel(flag_ref, keep_ref, got_ref, send_ref, own_ref, *, body, tail, pieces):
    base = 2 * pieces * body

    def split(at):
        total = add(at(keep_ref)[...], at(got_ref)[...])

        def half(h):
            return lambda: side_by_side(
                [total[:, (2 * k + h) * body : (2 * k + h + 1) * body] for k in range(pieces)]
                + [total[:, base + (2 * k + h) * tail : base + (2 * k + h + 1) * tail] for k in range(pieces)],
                send_ref.shape[-1],
            )

        store_halves(flag_ref[0], [into(at(send_ref)), into(at(own_ref))], [half(0), half(1)])

    if len(keep_ref.shape) == 2:
        split(lambda ref: ref)
    else:

        def one(index, carry):
            split(lambda ref: ref.at[index])
            return carry

        lax.fori_loop(0, keep_ref.shape[0], one, 0)


def pass_rows_kernel(order_ref, *refs):
    send_ref, keep_ref = refs[-2:]
    count = send_ref.shape[0]
    for index in range(count):
        send_ref[index] = add(*[ref[order_ref[index]] for ref in refs[:-2]]).astype(BF)
        keep_ref[index] = add(*[ref[order_ref[count + index]] for ref in refs[:-2]])


def last_kernel(keep_ref, got_ref, *outs, body, tail, pieces, turned):
    total = add(keep_ref[...], got_ref[...]).reshape(keep_ref.shape[-2:])
    high = total.shape[0]
    whole_rows = outs[0].shape[1 if turned else 0]
    for piece in range(pieces):
        low = pieces * body + piece * tail
        part = jnp.concatenate(
            [total[:, piece * body : (piece + 1) * body], total[:, low : low + tail]], axis=1
        )
        out, at = outs[piece * high // whole_rows], piece * high % whole_rows
        if turned:
            out[:, at : at + high] = part.T
        else:
            out[at : at + high, :] = part


def mlp_kernel(x_ref, g_ref, up_ref, down_ref, hidden_ref, pre_ref, branch_ref, grad_ref, *scratch, tile):
    up, down, sems = scratch[:3]
    kept = (scratch[3:5], scratch[5:7])
    tiles = up.shape[0]
    root = math.sqrt(2.0 / math.pi)

    def columns(step):
        return pl.ds(pl.multiple_of(step * tile, 128), tile)

    def copies(step):
        return (
            pltpu.make_async_copy(up_ref.at[:, columns(step)], up.at[step], sems.at[0, step]),
            pltpu.make_async_copy(down_ref.at[columns(step), :], down.at[step], sems.at[1, step]),
        )

    for step in range(tiles):
        for copy in copies(step):
            copy.start()

    def both(step, parity, first, last):
        if not last:
            for copy in copies(step):
                copy.wait()
            pre = matmul(x_ref[...], up[step])
            grad = matmul_nt(g_ref[...], down[step])
        if not first:
            hidden, grad_pre = (ref[...] for ref in kept[1 - parity])
            branch = matmul(hidden, down[step - 1])
            back = matmul_nt(grad_pre, up[step - 1])
        if not last:
            square = pre * pre
            bend = jnp.tanh(pre * (root * 0.044715 * square + root))
            half = 0.5 * bend + 0.5
            rise = (3 * root * 0.044715 * square + root) * pre
            slope = half + 0.5 * rise * (1.0 - bend * bend)
            hidden = (pre * half).astype(BF)
            grad_pre = (grad * slope).astype(BF)
            for ref, value in zip(kept[parity], (hidden, grad_pre)):
                ref[...] = value
            hidden_ref[:, columns(step)] = hidden
            pre_ref[:, columns(step)] = grad_pre
        if not first:
            branch_ref[...] += branch
            grad_ref[...] += back

    branch_ref[...] = jnp.zeros_like(branch_ref)
    grad_ref[...] = jnp.zeros_like(grad_ref)
    both(0, 0, True, False)

    def two(index, carry):
        both(2 * index + 1, 1, False, False)
        both(2 * index + 2, 0, False, False)
        return carry

    lax.fori_loop(0, (tiles - 1) // 2, two, 0)
    if tiles % 2 == 0:
        both(tiles - 1, 1, False, False)
    both(tiles, tiles % 2, False, True)


def prelude_kernel(place_ref, len_ref, step_ref, embed_ref, table_ref, info_ref, mod_ref, slab, sem, *, rows):
    slots = len_ref.shape[1]
    width = table_ref.shape[1]

    def image_of(at):
        first = at * rows
        end = begin = length = step = jnp.int32(0)
        for slot in range(slots):
            count = len_ref[0, slot]
            inside = jnp.logical_and(end <= first, first < end + count)
            begin = jnp.where(inside, end, begin)
            length = jnp.where(inside, count, length)
            step = jnp.where(inside, step_ref[0, slot], step)
            end = end + count
        return (first - begin) // rows, length, step

    place = place_ref[0]
    core = place % 2
    blocks = BIG // rows
    within, length, step = image_of(place)
    pair_within = image_of(place + 1 - 2 * core)[0]
    flags = (
        length > rows,
        jnp.where(core == 0, pair_within + 1 < blocks, pair_within + 3 < blocks),
        jnp.where(core == 0, within + 1 < blocks, within >= 1),
        within + 2 < blocks,
    )
    for index, flag in enumerate(flags):
        info_ref[index] = flag.astype(jnp.int32)
    copy = pltpu.make_async_copy(embed_ref.at[pl.ds(pl.multiple_of(step // 8 * 8, 8), 8), :], slab, sem)
    copy.start()
    copy.wait()
    row = slab[pl.ds(step % 8, 1), :]
    for index in range(6):
        mod_ref[index : index + 1, :] = (
            row[:, index * width : (index + 1) * width] + table_ref[index : index + 1, :]
        )


def cost(flops, nbytes, exps=0):
    return pl.CostEstimate(
        flops=int(flops * COST_SCALE),
        bytes_accessed=int(nbytes * COST_SCALE),
        transcendentals=int(exps * COST_SCALE),
    )


def call(kernel, inputs, outs, flags=None, hbm=(), scratch=(), limit=8, flops=0):
    vmem = pl.BlockSpec(memory_space=pltpu.VMEM)
    specs = [pl.BlockSpec(memory_space=pl.ANY) if i in hbm else vmem for i in range(len(inputs))]
    arguments = list(inputs)
    if flags is not None:
        specs.insert(0, pl.BlockSpec(memory_space=pltpu.SMEM))
        arguments.insert(0, flags)
    return pl.pallas_call(
        kernel,
        in_specs=specs,
        out_specs=[vmem] * len(outs),
        out_shape=[jax.ShapeDtypeStruct(shape, dtype) for shape, dtype in outs],
        scratch_shapes=list(scratch),
        compiler_params=pltpu.CompilerParams(vmem_limit_bytes=limit * MIB),
        cost_estimate=cost(flops, sum(2 * array.size for array in inputs)),
    )(*arguments)


def prelude(place, image_len, timestep, time_embed, mod_table, rows):
    smem = pl.BlockSpec(memory_space=pltpu.SMEM)
    return pl.pallas_call(
        functools.partial(prelude_kernel, rows=rows),
        in_specs=[smem, smem, smem, pl.BlockSpec(memory_space=pl.ANY), pl.BlockSpec(memory_space=pltpu.VMEM)],
        out_specs=[smem, pl.BlockSpec(memory_space=pltpu.VMEM)],
        out_shape=[jax.ShapeDtypeStruct((4,), jnp.int32), jax.ShapeDtypeStruct(mod_table.shape, F32)],
        scratch_shapes=[pltpu.VMEM((8, time_embed.shape[1]), F32), pltpu.SemaphoreType.DMA],
        compiler_params=pltpu.CompilerParams(vmem_limit_bytes=4 * MIB),
    )(place.reshape(1), image_len, timestep, time_embed, mod_table)


def half_width(grads, count, joined):
    size = (sum(grad.shape[1] for grad in grads) if joined else grads[0].shape[1]) // count
    body, _ = slice_parts(size)
    return 2 * (count // 4 * body + 128) if joined else len(grads) * (count // 2 * body + 128)


def halves(core, grads, count, joined):
    out = ((grads[0].shape[0], half_width(grads, count, joined)), BF)
    return call(functools.partial(halves_kernel, count=count, joined=joined), grads, [out] * 2, flags=core)


def split_body(flag, keep, got, size, pieces):
    body, tail = slice_parts(size)
    shape = (*keep.shape[:-1], pieces * body + 128)
    kernel = functools.partial(split_body_kernel, body=body, tail=tail, pieces=pieces)
    return call(kernel, [keep, got], [(shape, BF), (shape, F32)], flags=flag.reshape(1))


def pass_rows(order, keep, got):
    shape = (keep.shape[0] // 2, *keep.shape[1:])
    return call(pass_rows_kernel, [keep, got], [(shape, BF), (shape, F32)], flags=order)


def add_last(keep, got, size, shapes, turned):
    body, tail = slice_parts(size)
    pieces = sum(shape[0] for shape in shapes) // keep.shape[-2]
    outs = call(
        functools.partial(last_kernel, body=body, tail=tail, pieces=pieces, turned=turned),
        [keep, got],
        [(shape[::-1] if turned else shape, F32) for shape in shapes],
    )
    return [out.T for out in outs] if turned else outs


def weight_grad(order, sources, size, high, mode):
    count = len(sources)
    rows, width = sources[0][0].shape
    body, _ = slice_parts(size)
    pieces = count * (width // 4 // high)
    wide = 2 * pieces * body + 128
    shape, number = {
        "rows": ((2, high, 2 * wide), 2),
        "chips": ((4, high, wide), 2),
        "both": ((2, high, wide), 4),
    }[mode]
    return call(
        functools.partial(weight_grad_kernel, count=count, size=size, high=high, mode=mode),
        [array for source in sources for array in source],
        [(shape, BF)] * number,
        flags=order,
        scratch=[pltpu.VMEM((count, width, 2 * rows), BF)],
        limit=20,
    )


def mlp(inputs, grad, w_up, w_down):
    rows, width = inputs.shape
    units = w_up.shape[1]
    tile = 512
    tiles = units // tile
    return call(
        functools.partial(mlp_kernel, tile=tile),
        [inputs, grad, w_up, w_down],
        [((rows, units), BF)] * 2 + [((rows, width), F32)] * 2,
        hbm=(2, 3),
        scratch=[
            pltpu.VMEM((tiles, width, tile), BF),
            pltpu.VMEM((tiles, tile, width), BF),
            pltpu.SemaphoreType.DMA((2, tiles)),
        ]
        + [pltpu.VMEM((rows, tile), BF)] * 4,
        limit=32,
    )


def local(
    tokens,
    image_len,
    timestep,
    caption,
    time_embed,
    mod_table,
    w_qkv,
    w_out,
    cross_q,
    cross_kv,
    cross_out,
    w_up,
    w_down,
    cotangent,
):
    sp_count = lax.axis_size("sp")
    dp_count = lax.axis_size("dp")
    place = lax.axis_index("sp")
    row_place = lax.axis_index("dp")
    core = place % 2
    rows, width = tokens.shape[1:]
    factor = 1.0 / math.sqrt(width // HEADS)
    blocks = BIG // rows
    assert blocks == 4

    big, modulation = prelude(place, image_len, timestep, time_embed, mod_table, rows)
    shift_one, scale_one, gate_one, shift_two, scale_two, gate_two = [modulation[i] for i in range(6)]

    def tie(value, *before):
        return lax.optimization_barrier((value, *[array for array in before if array is not None]))[0]

    pairs = [(i, i ^ 1) for i in range(sp_count)]
    others = [(i, i + 1) for i in range(1, sp_count - 1, 2)] + [(i + 1, i) for i in range(1, sp_count - 1, 2)]
    ahead = [(i, i + 2) for i in range(sp_count - 2)]
    back = [(i + 2, i) for i in range(sp_count - 2)]

    def image_blocks(block, *before):
        pair = lax.ppermute(block, "sp", pairs)
        from_back = lax.ppermute(block, "sp", ahead)
        from_ahead = lax.ppermute(block, "sp", back)
        from_ahead, from_back = tie(from_ahead, *before), tie(from_back, *before)
        send_pair = jnp.where(big[1] == 1, from_ahead, from_back)
        send_other = jnp.where(core == 1, from_back, from_ahead)
        second = lax.ppermute(send_pair, "sp", pairs)
        third = lax.ppermute(send_other, "sp", others)
        return (
            [
                second,
                jnp.where(big[2] == 1, pair, third),
                jnp.where(big[3] == 1, from_ahead, from_back),
            ],
            send_pair,
            send_other,
        )

    def swap(array):
        return lax.ppermute(array, "sp", pairs)

    token_blocks, *token_sends = image_blocks(tokens[0])

    def first_norm(block):
        return (normal(block.astype(F32))[0] * (1.0 + scale_one) + shift_one).astype(BF)

    first_in = first_norm(tokens[0])
    other_in = first_norm(jnp.concatenate(token_blocks, axis=0))

    core_flag = core.reshape(1)
    chips = sp_count // 2
    square = dp_count == 4 and chips == 4

    def own_half(*grads, joined=True):
        if square:
            return halves(core_flag, grads, sp_count, joined)
        grads = [jnp.concatenate(grads, axis=1)] if joined else grads
        size = grads[0].shape[1] // sp_count
        even, odd = [
            jnp.concatenate(
                [g[:, i * size : (i + 1) * size] for g in grads for i in range(c, sp_count, 2)], axis=1
            )
            for c in (0, 1)
        ]
        return jnp.where(core == 0, even, odd), jnp.where(core == 0, odd, even)

    near, far = (place // 2) & 1, (place // 4) & 1
    row_bits = [row_place & 1, row_place >> 1]
    high = width // 4

    def to_row(array, bit):
        return lax.ppermute(array, "dp", [(i, i ^ (1 << bit)) for i in range(dp_count)])

    def to_chip(array, bit):
        return lax.ppermute(array, "sp", [(i, i ^ (2 << bit)) for i in range(sp_count)])

    def plain_sum(sources, size):
        finals = []
        for item, (x0, x1, g0, g1) in enumerate(sources):
            columns = slice(item * chips * size, (item + 1) * chips * size)
            part = (matmul_tn(x0, g0[:, columns]) + matmul_tn(x1, g1[:, columns])).astype(BF)
            part = part.reshape(dp_count, -1, chips, size).transpose(0, 2, 1, 3)
            bit = dp_count // 2
            while bit:
                mine = (row_place // bit) % 2
                part = part.reshape(2, bit, chips, -1, size)
                got = lax.ppermute(part[1 - mine], "dp", [(i, i ^ bit) for i in range(dp_count)])
                part = add(part[mine], got).astype(BF)
                bit //= 2
            part = part.reshape(chips, -1, size)
            bit = chips // 2
            while bit:
                mine = (place // 2 // bit) % 2
                part = part.reshape(2, bit, -1, size)
                got = lax.ppermute(part[1 - mine], "sp", [(i, i ^ (2 * bit)) for i in range(sp_count)])
                part = add(part[mine], got).astype(BF)
                bit //= 2
            finals.append(part[0].astype(F32))
        return finals

    def add_picked(pick, keep, got):
        return call(add_kernel, [keep, got], [(keep.shape[1:], BF)], flags=pick.reshape(1))

    def sum_rows_first(source, size, first):
        second = 1 - first
        pieces = source[0].shape[1] // width
        mine = row_bits[first]
        order = jnp.stack(
            [((1 - mine if s < 2 else mine) << first) + ((s % 2) << second) for s in range(4)]
        )
        send, keep = weight_grad(order, [source], size, high, "rows")
        yield send
        got = to_row(send, first)
        mine = row_bits[second]
        (send,) = add_picked(1 - mine, keep, got)
        yield send
        shape = (high, keep.shape[-1] // 2)
        send, keep = call(
            split_rows_kernel,
            [keep, got, to_row(send, second)],
            [(shape, BF), (shape, F32)],
            flags=jnp.stack([mine, near]),
        )
        yield send
        send, keep = split_body(far, keep, to_chip(send, 0), size, pieces)
        yield send
        turned = size < 256
        yield add_last(keep, to_chip(send, 1), size, [(pieces * high, size)], turned)

    def sum_both_first(source, size):
        order = jnp.stack([jnp.int32(i) for i in range(4)] + row_bits)
        outs = weight_grad(order, [source], size, high, "both")
        yield outs
        got = [to_row(outs[0], 0), to_row(outs[2], 1)]
        sends = [
            *add_picked(1 - row_bits[1], outs[1], got[0]),
            *add_picked(1 - row_bits[0], outs[3], got[1]),
        ]
        yield sends
        shape = sends[0].shape
        send, keep = call(
            split_pair_kernel,
            [outs[1], got[0], to_row(sends[0], 1), outs[3], got[1], to_row(sends[1], 0)],
            [(shape, BF), (shape, F32)],
            flags=jnp.stack([row_bits[1], row_bits[0], near]),
        )
        yield send
        send, keep = split_body(far, keep, to_chip(send, 0), size, 1)
        yield send
        yield add_last(keep, to_chip(send, 1), size, [(high, size)], False)

    def sum_chips_first(sources, size):
        order = jnp.stack([jnp.int32(i) for i in range(4)] + [near])
        send, keep = weight_grad(order, sources, size, high, "chips")
        yield send
        send, keep = split_body(far, keep, to_chip(send, 0), size, len(sources))
        yield send
        mine = row_bits[0]
        order = jnp.stack([2 * (s % 2) + (1 - mine if s < 2 else mine) for s in range(4)])
        send, keep = pass_rows(order, keep, to_chip(send, 1))
        yield send
        order = jnp.stack([1 - row_bits[1], row_bits[1]])
        send, keep = pass_rows(order, keep, to_row(send, 0))
        yield send
        yield add_last(keep, to_row(send, 1), size, [(high, size)] * len(sources), True)

    def spread_vector(vector):
        for axis, name, count, mine in ((1, "sp", sp_count, place), (0, "dp", dp_count, row_place)):
            bit = count // 2
            while bit:
                shape = vector.shape
                split = vector.reshape(shape[:axis] + (2, bit) + shape[axis + 1 :])
                at = lambda i: lax.dynamic_index_in_dim(split, i, axis, keepdims=False)
                own = (mine // bit) % 2
                got = lax.ppermute(at(1 - own), name, [(i, i ^ bit) for i in range(count)])
                vector = at(own) + got
                bit //= 2
        return vector.reshape(-1)

    caption_rows = caption[0]
    live = caption_rows.shape[0]
    padded = -(-live // 128) * 128
    caption_pad = jnp.concatenate([caption_rows, jnp.zeros((padded - live, width), BF)], axis=0)
    text = matmul(caption_pad, cross_kv).astype(BF)
    grad_mlp = (gate_two * cotangent[0].astype(F32)).astype(BF)
    mlp_keep, mlp_send = own_half(grad_mlp, joined=False)
    mlp_got = swap(mlp_send)
    first_pair = swap(first_in)
    own = matmul(tie(first_in, *token_sends), w_qkv).astype(BF)
    far_qkv = matmul(other_in, w_qkv).astype(BF)
    block = ((rows, width), BF)
    stream = ((rows, width), F32)
    stats = ((rows, 128), F32)
    attended, logsum = call(
        functools.partial(attend_kernel, factor=factor), [own, far_qkv], [block, stats], flags=big, limit=20
    )
    attn_branch, cross_in, cross_queries, cross_mixed, stream_two, second_in = call(
        functools.partial(middle_kernel, factor=factor, live=live),
        [tokens[0], modulation, attended, w_out, cross_q, cross_out, text],
        [stream, block, block, block, stream, block],
        limit=12,
    )
    second_pair = swap(second_in)
    small_acts = [(acts, swap(acts)) for acts in (cross_mixed, cross_in, attended)]
    hidden, grad_pre, mlp_branch, grad_second = mlp(second_in, grad_mlp, w_up, w_down)

    pre_keep, pre_send = own_half(grad_pre)
    hidden_pair, pre_got = swap(hidden), swap(pre_send)
    small_width = half_width([grad_mlp] * 3, sp_count, False) if square else 3 * width
    small_out = ((rows, small_width), BF)
    stream_three, grad_one, small_keep, small_send, grad_text, pack, stat, table = call(
        functools.partial(middle_grad_kernel, factor=factor, live=live, count=sp_count if square else 0),
        [
            tie(grad_second, pre_send), stream_two, cotangent[0], mlp_branch, modulation, attn_branch, attended,
            logsum, cross_queries, text, w_out, cross_q, cross_out,
        ],
        [
            stream, stream, small_out, small_out, ((live, 2 * width), F32), ((rows + 16, width), BF), stats,
            (modulation.shape, F32),
        ],
        flags=core_flag,
        scratch=[pltpu.VMEM((rows, width), BF)] * 2 + [pltpu.VMEM((padded, width), F32)] * 2,
        limit=16,
    )
    if not square:
        small_keep, small_send = own_half(*jnp.split(small_keep, 3, axis=1), joined=False)
    small_got = swap(small_send)
    slice_of = lambda weight: weight.shape[1] // sp_count
    down_source = (hidden, hidden_pair, mlp_keep, mlp_got)
    up_source = (tie(second_in, pack), second_pair, pre_keep, pre_got)
    send_down = send_up = None
    if square:
        down_sum = sum_rows_first(down_source, slice_of(w_down), 0)
        up_sum = sum_rows_first(up_source, slice_of(w_up), 1)
        send_up = next(up_sum)
        send_down = next(down_sum)
    pack_blocks, *pack_sends = image_blocks(pack, send_down, send_up)
    (grad_queries,) = call(
        functools.partial(query_grad_kernel, factor=factor),
        [own, far_qkv, tie(pack, *pack_sends), stat],
        [block],
        flags=big,
        limit=20,
    )
    small = [(*acts, small_keep, small_got) for acts in small_acts]
    send_small = None
    if square:
        small[0] = (tie(small[0][0], grad_queries), *small[0][1:])
        small_sum = sum_chips_first(small, slice_of(w_out))
        send_small = next(small_sum)
    grad_keys, grad_values = call(
        functools.partial(key_grad_kernel, factor=factor),
        [own, far_qkv, tie(pack, send_small), *pack_blocks],
        [block, block],
        flags=big,
        scratch=[
            pltpu.VMEM((2 * HEADS, blocks * rows), F32),
            pltpu.VMEM(((blocks - 1) * rows, width), BF),
        ],
        limit=24,
    )
    proj_keep, proj_send = own_half(grad_queries, grad_keys, grad_values)
    qkv_source = (first_in, first_pair, proj_keep, swap(proj_send))
    sent = []
    if square:
        qkv_sum = sum_both_first(qkv_source, slice_of(w_qkv))
        sent = next(qkv_sum)
    grad_tokens, table = call(
        last_grad_kernel,
        [tie(grad_queries, *sent), grad_keys, grad_values, w_qkv, tokens[0], modulation, grad_one, table],
        [stream, (modulation.shape, F32)],
        limit=12,
    )

    if square:
        sums = [down_sum, up_sum, small_sum, qkv_sum]
        final_down, final_up, final_small, final_qkv = [list(each)[-1] for each in sums]
    else:
        final_down = plain_sum([down_source], slice_of(w_down))
        final_up = plain_sum([up_source], slice_of(w_up))
        final_small = plain_sum(small, slice_of(w_out))
        final_qkv = plain_sum([qkv_source], slice_of(w_qkv))
    (final_down,), (final_up,), (final_qkv,) = final_down, final_up, final_qkv
    text_part = lax.psum_scatter(grad_text, "sp", scatter_dimension=1, tiled=True).astype(BF)
    part_ckv = matmul_tn(caption_rows, text_part).astype(BF)
    final_ckv = lax.psum_scatter(part_ckv, "dp", scatter_dimension=0, tiled=True).astype(F32)
    final_table = spread_vector(table.reshape(dp_count, sp_count, -1))
    return (
        stream_three[None],
        grad_tokens[None],
        final_table,
        final_qkv,
        final_small[2],
        final_small[1],
        final_ckv,
        final_small[0],
        final_up,
        final_down,
    )


def solution(mesh):
    return jax.shard_map(
        local,
        mesh=mesh,
        in_specs=(
            P("dp", "sp", None),
            P("dp", None),
            P("dp", None),
            P("dp", None, None),
            P(),
            P(),
            P(),
            P(),
            P(),
            P(),
            P(),
            P(),
            P(),
            P("dp", "sp", None),
        ),
        out_specs=(
            P("dp", "sp", None),
            P("dp", "sp", None),
            P(("dp", "sp")),
            P("dp", "sp"),
            P("dp", "sp"),
            P("dp", "sp"),
            P("dp", "sp"),
            P("dp", "sp"),
            P("dp", "sp"),
            P("dp", "sp"),
        ),
        check_vma=False,
    )
```

```python
import functools
import math

import jax
import jax.numpy as jnp
from jax import lax
from jax.experimental import pallas as pl
from jax.experimental.pallas import tpu as pltpu
from jax.sharding import PartitionSpec as P

HEADS = 16
BIG = 1024
EPS = 1e-06
BIGNEG = -1e30
LOG2E = 1.4426950408889634
BF = jnp.bfloat16
F32 = jnp.float32
WIN = 256
COST_SCALE = 0.001
MIB = 1024 * 1024


def matmul(left, right):
    return jnp.dot(left, right, preferred_element_type=F32)


def matmul_tn(left, right):
    return lax.dot_general(left, right, (((0,), (0,)), ((), ())), preferred_element_type=F32)


def matmul_nt(left, right):
    return lax.dot_general(left, right, (((1,), (1,)), ((), ())), preferred_element_type=F32)


def head_window(head, width):
    size = width // HEADS
    low = head * size
    start = pl.multiple_of(jnp.minimum(low // 128 * 128, width - WIN), 128)
    lane = lax.broadcasted_iota(jnp.int32, (1, WIN), 1) + start
    return start, jnp.logical_and(lane >= low, lane < low + size)


def window(ref, start, offset=0):
    return ref[:, pl.ds(pl.multiple_of(start + offset, 128), WIN)]


def keep_columns(ref, start, mask, value):
    win = pl.ds(start, WIN)
    ref[:, win] = jnp.where(mask, value, ref[:, win])


def each_head(body, unroll=4):
    def step(head, carry):
        body(head)
        return carry

    lax.fori_loop(0, HEADS, step, 0, unroll=unroll)


def fetch(sems, *pairs):
    copies = [pltpu.make_async_copy(source, target, sems.at[i]) for i, (source, target) in enumerate(pairs)]
    for copy in copies:
        copy.start()
    return [copy.wait for copy in copies]


def attend_kernel(big_ref, own_ref, far_ref, out_ref, lse_ref, *, factor):
    width = out_ref.shape[1]
    scale = factor * LOG2E

    def run(sides):
        def one_head(head):
            start, mask = head_window(head, width)
            query = window(own_ref, start) * mask.astype(BF)
            scores = [matmul_nt(query, window(side, start, width)) for side in sides]
            top = functools.reduce(jnp.maximum, [jnp.max(s, axis=1, keepdims=True) for s in scores])
            raised = [jnp.exp2((s - top) * scale) for s in scores]
            total = sum(jnp.sum(r, axis=1, keepdims=True) for r in raised)
            inverse = 1.0 / total
            result = sum(
                matmul((r * inverse).astype(BF), window(side, start, 2 * width))
                for r, side in zip(raised, sides)
            )
            keep_columns(out_ref, start, mask, result.astype(BF))
            lane = lax.broadcasted_iota(jnp.int32, (1, 128), 1)
            lse_ref[...] = jnp.where(lane == head, top * scale + jnp.log2(total), lse_ref[...])

        each_head(one_head)

    lse_ref[...] = jnp.zeros_like(lse_ref)

    @pl.when(big_ref[0] == 1)
    def _():
        run([own_ref, far_ref])

    @pl.when(big_ref[0] == 0)
    def _():
        run([own_ref])


def query_grad_kernel(big_ref, own_hbm, far_hbm, pack_hbm, stat_ref, out_ref, own_ref, far_ref, pack_ref, sems, *, factor):
    rows, width = out_ref.shape
    waits = fetch(sems, (own_hbm, own_ref), (pack_hbm, pack_ref), (far_hbm, far_ref))
    for wait in waits:
        wait()
    scale = factor * LOG2E

    def run(sides):
        def one_head(head):
            start, mask = head_window(head, width)
            keep = mask.astype(BF)
            query = window(own_ref, start) * keep
            grad = window(pack_ref.at[0:rows, :], start) * keep
            lane = lax.broadcasted_iota(jnp.int32, (1, 128), 1)
            stat = stat_ref[...]
            lse = jnp.sum(jnp.where(lane == head, stat, 0.0), axis=1, keepdims=True)
            delta = jnp.sum(jnp.where(lane == head + HEADS, stat, 0.0), axis=1, keepdims=True)
            total = None
            for side in sides:
                key = window(side, start, width)
                prob = jnp.exp2(matmul_nt(query, key) * scale - lse)
                grad_prob = matmul_nt(grad, window(side, start, 2 * width))
                grad_score = (prob * (grad_prob - delta)).astype(BF)
                part = matmul(grad_score, key)
                total = part if total is None else total + part
            keep_columns(out_ref, start, mask, (total * factor).astype(BF))

        each_head(one_head)

    @pl.when(big_ref[0] == 1)
    def _():
        run([own_ref, far_ref])

    @pl.when(big_ref[0] == 0)
    def _():
        run([own_ref])


def key_grad_kernel(big_ref, own_hbm, far_hbm, pack_hbm, *refs, factor):
    packs, (dk_ref, dv_ref, own_ref, far_ref, pack_ref, stats, grads, tails, sems) = refs[:-9], refs[-9:]
    rows, width = dk_ref.shape
    pairs = [(pack.at[rows : rows + 16, :], tails.at[i]) for i, pack in enumerate(packs)]
    pairs += [(pack.at[0:rows, :], grads.at[i * rows : (i + 1) * rows, :]) for i, pack in enumerate(packs)]
    pairs += [(own_hbm, own_ref), (pack_hbm, pack_ref), (far_hbm.at[:, 0:width], far_ref)]
    for wait in fetch(sems, *pairs):
        wait()
    scale = factor * LOG2E
    blocks = 1 + len(packs)

    def unpack(block, both):
        both = both.astype(F32)
        joined = both[:8] + both[8:]
        for group in range(4):
            stats[8 * group : 8 * group + 8, block * rows : block * rows + rows] = joined[
                :, group * rows : group * rows + rows
            ]

    unpack(0, pack_ref[rows:, :])
    for block in range(len(packs)):
        unpack(block + 1, tails[block])

    def run(parts):
        def one_head(head):
            start, mask = head_window(head, width)
            keep = mask.astype(BF)
            key = window(own_ref, start, width) * keep
            value = window(own_ref, start, 2 * width) * keep
            lse = stats[pl.ds(head, 1), :]
            delta = stats[pl.ds(head + HEADS, 1), :]
            grad_key = grad_value = 0.0
            for query_ref, grad_ref, low, high in parts:
                query, grad = window(query_ref, start), window(grad_ref.at[0 : high - low, :], start)
                prob = jnp.exp2(matmul_nt(key, query) * scale - lse[:, low:high])
                grad_prob = matmul_nt(value, grad)
                grad_score = (prob * (grad_prob - delta[:, low:high])).astype(BF)
                grad_value = grad_value + matmul(prob.astype(BF), grad)
                grad_key = grad_key + matmul(grad_score, query)
            keep_columns(dk_ref, start, mask, (grad_key * factor).astype(BF))
            keep_columns(dv_ref, start, mask, grad_value.astype(BF))

        each_head(one_head)

    own = (own_ref, pack_ref, 0, rows)

    @pl.when(big_ref[0] == 1)
    def _():
        run([own, (far_ref, grads, rows, blocks * rows)])

    @pl.when(big_ref[0] == 0)
    def _():
        run([own])


def text_probs(query, key, scale, live, axis):
    scores = matmul_nt(query, key) if axis else matmul_nt(key, query)
    shape = (1, scores.shape[1]) if axis else (scores.shape[0], 1)
    scores = jnp.where(lax.broadcasted_iota(jnp.int32, shape, axis) < live, scores, BIGNEG)
    raised = jnp.exp2((scores - jnp.max(scores, axis=axis, keepdims=True)) * scale)
    return raised * (1.0 / jnp.sum(raised, axis=axis, keepdims=True))


def normal(stream):
    centred = stream - jnp.mean(stream, axis=-1, keepdims=True)
    spread = lax.rsqrt(jnp.mean(centred * centred, axis=-1, keepdims=True) + EPS)
    return centred * spread, spread


def norm_back(normed, spread, scale, grad):
    scaled = grad * (1.0 + scale)
    back = spread * (
        scaled
        - jnp.mean(scaled, axis=-1, keepdims=True)
        - normed * jnp.mean(scaled * normed, axis=-1, keepdims=True)
    )
    return back, jnp.sum(grad, axis=0, keepdims=True), jnp.sum(grad * normed, axis=0, keepdims=True)


def middle_kernel(
    tokens_ref, mod_ref, att_ref, out_w_ref, query_w_ref, cross_w_ref, text_ref,
    branch_ref, cross_in_ref, queries_ref, mixed_ref, stream_ref, second_ref, *, factor, live
):
    width = tokens_ref.shape[1]
    branch = matmul(att_ref[...], out_w_ref[...])
    branch_ref[...] = branch
    stream = tokens_ref[...].astype(F32) + mod_ref[2:3, :] * branch
    stream_ref[...] = stream
    cross_in = stream.astype(BF)
    cross_in_ref[...] = cross_in
    queries_ref[...] = matmul(cross_in, query_w_ref[...]).astype(BF)

    def one_head(head):
        start, mask = head_window(head, width)
        query = window(queries_ref, start) * mask.astype(BF)
        probs = text_probs(query, window(text_ref, start), factor * LOG2E, live, 1)
        result = matmul(probs.astype(BF), window(text_ref, start, width))
        keep_columns(mixed_ref, start, mask, result.astype(BF))

    each_head(one_head, 8)
    stream = stream_ref[...] + matmul(mixed_ref[...], cross_w_ref[...])
    stream_ref[...] = stream
    second_ref[...] = (normal(stream)[0] * (1.0 + mod_ref[4:5, :]) + mod_ref[3:4, :]).astype(BF)


def middle_grad_kernel(
    core_ref, second_grad_ref, stream_ref, cot_ref, mlp_ref, mod_ref, branch_ref, att_ref, lse_ref,
    queries_ref, text_ref, out_w_ref, query_w_ref, cross_w_ref,
    out_ref, one_ref, keep_ref, send_ref, text_grad_ref, pack_ref, stat_ref, table_ref,
    mixed, grad_queries, text_key, text_value, *, factor, live, count
):
    rows, width = cot_ref.shape
    cot = cot_ref[...].astype(F32)
    stream = stream_ref[...]
    mlp = mlp_ref[...]
    out_ref[...] = stream + mod_ref[5:6, :] * mlp
    normed, spread = normal(stream)
    back, shift, scale = norm_back(normed, spread, mod_ref[4:5, :], second_grad_ref[...])
    table_ref[...] = jnp.zeros_like(table_ref)
    table_ref[3:4, :] = shift
    table_ref[4:5, :] = scale
    table_ref[5:6, :] = jnp.sum(cot * mlp, axis=0, keepdims=True)
    grad_two = cot + back
    one_ref[...] = grad_two
    grad_cross = grad_two.astype(BF)
    mixed[...] = matmul_nt(grad_cross, cross_w_ref[...]).astype(BF)

    def one_head(head):
        start, mask = head_window(head, width)
        keep = mask.astype(BF)
        query = window(queries_ref, start)
        grad = window(mixed, start)
        key = window(text_ref, start) * keep
        probs = text_probs(query, key, factor * LOG2E, live, 0)
        grad_probs = matmul_nt(window(text_ref, start, width) * keep, grad)
        inner = jnp.sum(probs * grad_probs, axis=0, keepdims=True)
        grad_scores = (probs * (grad_probs - inner)).astype(BF)
        keep_columns(grad_queries, start, mask, (matmul_tn(grad_scores, key) * factor).astype(BF))
        keep_columns(text_key, start, mask, matmul(grad_scores, query) * factor)
        keep_columns(text_value, start, mask, matmul(probs.astype(BF), grad))

    each_head(one_head, 8)
    text_grad_ref[:, :width] = text_key[0:live, :]
    text_grad_ref[:, width:] = text_value[0:live, :]
    grad_cq = grad_queries[...]
    grad_one = one_ref[...] + matmul_nt(grad_cq, query_w_ref[...])
    one_ref[...] = grad_one
    table_ref[2:3, :] = jnp.sum(grad_one * branch_ref[...], axis=0, keepdims=True)
    grad_attn = (mod_ref[2:3, :] * grad_one).astype(BF)
    grad_att = matmul_nt(grad_attn, out_w_ref[...]).astype(BF)
    pack_ref[0:rows, :] = grad_att

    product = grad_att.astype(F32) * att_ref[...].astype(F32)
    upper = product.astype(BF)
    lower = (product - upper.astype(F32)).astype(BF)
    size = width // HEADS
    column = lax.broadcasted_iota(jnp.int32, (width, 128), 0)
    low = (lax.broadcasted_iota(jnp.int32, (width, 128), 1) - HEADS) * size
    pick = jnp.logical_and(column >= low, column < low + size).astype(BF)
    stat = lse_ref[...] + matmul(upper, pick) + matmul(lower, pick)
    stat_ref[...] = stat
    turned = stat.T
    upper = [turned[8 * g : 8 * g + 8, :].astype(BF).astype(F32) for g in range(4)]
    lower = [turned[8 * g : 8 * g + 8, :] - part for g, part in enumerate(upper)]
    both = [jnp.concatenate(pair, axis=0) for pair in zip(upper, lower)]
    pack_ref[rows : rows + 16, :] = side_by_side(both, width).astype(BF)

    if count:
        for core in (0, 1):

            @pl.when(core_ref[0] == core)
            def _(core=core):
                grads = [grad_cross, grad_cq, grad_attn]
                keep_ref[...] = half_columns(grads, core, count, False, keep_ref.shape[1])
                send_ref[...] = half_columns(grads, 1 - core, count, False, send_ref.shape[1])

    else:
        for index, grad in enumerate((grad_cross, grad_cq, grad_attn)):
            keep_ref[:, index * width : (index + 1) * width] = grad


def last_grad_kernel(
    dq_ref, dk_ref, dv_ref, weight_ref, tokens_ref, mod_ref, one_ref, table_in_ref, out_ref, table_ref
):
    width = tokens_ref.shape[1]
    grad = sum(
        matmul_nt(ref[...], weight_ref[:, part * width : (part + 1) * width])
        for part, ref in enumerate((dq_ref, dk_ref, dv_ref))
    )
    normed, spread = normal(tokens_ref[...].astype(F32))
    back, shift, scale = norm_back(normed, spread, mod_ref[1:2, :], grad)
    out_ref[...] = one_ref[...] + back
    table_ref[...] = table_in_ref[...]
    table_ref[0:1, :] = shift
    table_ref[1:2, :] = scale


def side_by_side(pieces, width):
    missing = width - sum(piece.shape[1] for piece in pieces)
    if missing:
        pieces = [*pieces, jnp.zeros((pieces[0].shape[0], missing), pieces[0].dtype)]
    return pieces[0] if len(pieces) == 1 else jnp.concatenate(pieces, axis=1)


def lanes(width):
    return -(-width // 128) * 128


def slice_parts(size):
    return size // 128 * 128, size % 128


def half_columns(grads, core, count, joined, wide):
    if not joined:
        picked = []
        for grad in grads:
            size = grad.shape[1] // count
            low = [(2 * chip + core) * size for chip in (*range(0, count // 2, 2), *range(1, count // 2, 2))]
            picked.append(
                side_by_side([grad[:, at : at + size] for at in low], wide // len(grads))
            )
        return side_by_side(picked, wide)
    grad = grads[0] if len(grads) == 1 else jnp.concatenate(grads, axis=1)
    size = grad.shape[1] // count
    body, _ = slice_parts(size)
    picked = []
    for parity in (0, 1):
        low = [(2 * chip + core) * size for chip in range(parity, count // 2, 2)]
        picked += [grad[:, at : at + body] for at in low]
        picked.append(side_by_side([grad[:, at + body : at + size] for at in low], 128))
    return side_by_side(picked, wide)


def halves_kernel(core_ref, *refs, count, joined):
    keep_ref, send_ref = refs[-2:]
    for core in (0, 1):

        @pl.when(core_ref[0] == core)
        def _(core=core):
            grads = [ref[...] for ref in refs[:-2]]
            keep_ref[...] = half_columns(grads, core, count, joined, keep_ref.shape[1])
            send_ref[...] = half_columns(grads, 1 - core, count, joined, send_ref.shape[1])


def store_halves(flag, stores, pieces):
    for value in (0, 1):

        @pl.when(flag == value)
        def _(value=value):
            for store, piece in zip(stores, (pieces[1 - value], pieces[value])):
                store(piece())


def into(ref):
    def store(value):
        ref[:, : value.shape[1]] = value.astype(ref.dtype)

    return store


def add(*terms):
    return sum(term.astype(F32) for term in terms)


def sending(buffers, sems, out):
    state = {"count": 0}

    def wait(slot):
        pltpu.make_async_copy(buffers.at[slot], out, sems.at[slot]).wait()

    def put(pieces, targets):
        slot = state["count"] % 2
        if state["count"] >= 2:
            wait(slot)
        at = 0
        for piece in pieces:
            buffers[slot, at : at + piece.shape[0], : piece.shape[1]] = piece
            at += piece.shape[0]
        for condition, target in targets:
            copy = pltpu.make_async_copy(buffers.at[slot], target, sems.at[slot])
            if condition is None:
                copy.start()
            else:
                pl.when(condition)(copy.start)
        state["count"] += 1

    def done():
        for slot in range(min(2, state["count"])):
            wait(slot)

    return put, done


def wide_grad_kernel(order_ref, x0_hbm, x1_hbm, g0_hbm, g1_hbm, *refs, mode):
    number = 2 if mode == "rows" else 4
    outs, (x_ref, g_ref, turned, buffers, sems, out_sems) = refs[:number], refs[number:]
    rows, width = x0_hbm.shape
    waits = fetch(
        sems,
        (x0_hbm, x_ref.at[0:rows, :]),
        (x1_hbm, x_ref.at[rows : 2 * rows, :]),
        (g0_hbm, g_ref.at[0:rows, :]),
        (g1_hbm, g_ref.at[rows : 2 * rows, :]),
    )
    for part in (0, 1):
        waits[part]()
        for low in range(0, width, 128):
            turned[low : low + 128, part * rows : (part + 1) * rows] = x_ref[
                part * rows : (part + 1) * rows, low : low + 128
            ].T
    waits[2]()
    waits[3]()
    tall = width // 4
    put, done = sending(buffers, out_sems, outs[0].at[0])
    half = g_ref.shape[1] // 2
    for step in range(4):
        here = pl.ds(pl.multiple_of(order_ref[step] * tall, 16), tall)
        if mode == "rows":
            total = matmul(turned[here, :], g_ref[...]).astype(BF)
            put([total], [(None, outs[step // 2].at[step % 2])])
        else:
            for p in (0, 1):
                total = matmul(turned[here, :], g_ref[:, p * half : (p + 1) * half]).astype(BF)
                first, second = (step >> p) & 1, (step >> (1 - p)) & 1
                mine = order_ref[4 + p]
                put(
                    [total],
                    [(mine != first, outs[2 * p].at[second]), (mine == first, outs[2 * p + 1].at[second])],
                )
    done()


def tall_grad_kernel(order_ref, *refs, count, mode):
    sources, g0_hbm, g1_hbm = refs[: 2 * count], refs[2 * count], refs[2 * count + 1]
    outs, (x_ref, g_ref, turned, buffers, sems, out_sems) = refs[2 * count + 2 : 2 * count + 4], refs[2 * count + 4 :]
    rows, width = sources[0].shape
    pairs = [(g0_hbm, g_ref.at[0:rows, :]), (g1_hbm, g_ref.at[rows : 2 * rows, :])]
    for i, source in enumerate(sources):
        pairs.append((source, x_ref.at[i // 2, i % 2 * rows : (i % 2 + 1) * rows, :]))
    waits = fetch(sems, *pairs)
    wide = g_ref.shape[1]
    for part in (0, 1):
        waits[part]()
        for low in range(0, wide, 128):
            turned[low : low + 128, part * rows : (part + 1) * rows] = g_ref[
                part * rows : (part + 1) * rows, low : low + 128
            ].T
    for wait in waits[2:]:
        wait()
    if mode == "rows":
        high, tall = outs[0].shape[1:]
        put, done = sending(buffers, out_sems, outs[0].at[0])
        for step in range(4):
            here = pl.ds(pl.multiple_of(order_ref[step] * tall, 128), tall)
            total = matmul(turned[0:high, :], x_ref[0, :, here]).astype(BF)
            put([total], [(None, outs[step // 2].at[step % 2])])
    else:
        high = outs[0].shape[0] // count
        put, done = sending(buffers, out_sems, outs[0])
        for p in (0, 1):
            total = [
                matmul(turned[pl.ds(k * (wide // count) + p * high, high), :], x_ref[k]).astype(BF)
                for k in range(count)
            ]
            put(total, [(order_ref[4] != p, outs[0]), (order_ref[4] == p, outs[1])])
    done()


def add_kernel(flag_ref, *refs):
    refs[-1][...] = add(*[ref[flag_ref[0]] for ref in refs[:-1]]).astype(BF)


def split_kernel(flag_ref, *refs, picked, parts, axis):
    views = [ref.at[flag_ref[0]] if i < picked else ref for i, ref in enumerate(refs[:-2])]

    def joined(index):
        def piece():
            sums = [add(*[view[part] for view in views]) for part in parts[index]]
            return sums[0] if len(sums) == 1 else jnp.concatenate(sums, axis=axis)

        return piece

    store_halves(flag_ref[1], [into(ref) for ref in refs[-2:]], [joined(0), joined(1)])


def split_pair_kernel(flag_ref, *refs):
    def group(p):
        keep, got, more = refs[3 * p : 3 * p + 3]
        return lambda: add(keep[flag_ref[p]], got[flag_ref[p]], more[...])

    store_halves(flag_ref[2], [into(ref) for ref in refs[-2:]], [group(0), group(1)])


def last_kernel(keep_ref, got_ref, *outs, size):
    if size:
        body, tail = slice_parts(size)
        for part in (slice(0, body), slice(body, size)):
            outs[0][:, part] = add(keep_ref[:, part], got_ref[:, part])
    else:
        high, wide = outs[0].shape
        for index, out in enumerate(outs):
            part = slice(index * high, (index + 1) * high), slice(0, wide)
            out[...] = add(keep_ref[part], got_ref[part])


def mlp_kernel(x_ref, g_ref, up_ref, down_ref, hidden_ref, pre_ref, branch_ref, grad_ref, *scratch, tile):
    up, down, sems = scratch[:3]
    kept = (scratch[3:5], scratch[5:7])
    tiles = up.shape[0]
    root = math.sqrt(2.0 / math.pi)

    def columns(step):
        return pl.ds(pl.multiple_of(step * tile, 128), tile)

    def copies(step):
        return (
            pltpu.make_async_copy(up_ref.at[:, columns(step)], up.at[step], sems.at[0, step]),
            pltpu.make_async_copy(down_ref.at[columns(step), :], down.at[step], sems.at[1, step]),
        )

    for step in range(tiles):
        for copy in copies(step):
            copy.start()

    def both(step, parity, first, last):
        if not last:
            for copy in copies(step):
                copy.wait()
            pre = matmul(x_ref[...], up[step])
            grad = matmul_nt(g_ref[...], down[step])
        if not first:
            hidden, grad_pre = (ref[...] for ref in kept[1 - parity])
            branch = matmul(hidden, down[step - 1])
            back = matmul_nt(grad_pre, up[step - 1])
        if not last:
            square = pre * pre
            bend = jnp.tanh(pre * (root * 0.044715 * square + root))
            half = 0.5 * bend + 0.5
            rise = (3 * root * 0.044715 * square + root) * pre
            slope = half + 0.5 * rise * (1.0 - bend * bend)
            hidden = (pre * half).astype(BF)
            grad_pre = (grad * slope).astype(BF)
            for ref, value in zip(kept[parity], (hidden, grad_pre)):
                ref[...] = value
            hidden_ref[:, columns(step)] = hidden
            pre_ref[:, columns(step)] = grad_pre
        if not first:
            branch_ref[...] += branch
            grad_ref[...] += back

    branch_ref[...] = jnp.zeros_like(branch_ref)
    grad_ref[...] = jnp.zeros_like(grad_ref)
    both(0, 0, True, False)

    def two(index, carry):
        both(2 * index + 1, 1, False, False)
        both(2 * index + 2, 0, False, False)
        return carry

    lax.fori_loop(0, (tiles - 1) // 2, two, 0)
    if tiles % 2 == 0:
        both(tiles - 1, 1, False, False)
    both(tiles, tiles % 2, False, True)


def prelude_kernel(place_ref, len_ref, step_ref, embed_ref, table_ref, info_ref, mod_ref, slab, sem, *, rows):
    slots = len_ref.shape[1]
    width = table_ref.shape[1]

    def image_of(at):
        first = at * rows
        end = begin = length = step = jnp.int32(0)
        for slot in range(slots):
            count = len_ref[0, slot]
            inside = jnp.logical_and(end <= first, first < end + count)
            begin = jnp.where(inside, end, begin)
            length = jnp.where(inside, count, length)
            step = jnp.where(inside, step_ref[0, slot], step)
            end = end + count
        return (first - begin) // rows, length, step

    place = place_ref[0]
    core = place % 2
    blocks = BIG // rows
    within, length, step = image_of(place)
    pair_within = image_of(place + 1 - 2 * core)[0]
    flags = (
        length > rows,
        jnp.where(core == 0, pair_within + 1 < blocks, pair_within + 3 < blocks),
        jnp.where(core == 0, within + 1 < blocks, within >= 1),
        within + 2 < blocks,
    )
    for index, flag in enumerate(flags):
        info_ref[index] = flag.astype(jnp.int32)
    copy = pltpu.make_async_copy(embed_ref.at[pl.ds(pl.multiple_of(step // 8 * 8, 8), 8), :], slab, sem)
    copy.start()
    copy.wait()
    row = slab[pl.ds(step % 8, 1), :]
    for index in range(6):
        mod_ref[index : index + 1, :] = (
            row[:, index * width : (index + 1) * width] + table_ref[index : index + 1, :]
        )


def call(kernel, inputs, outs, flags=None, hbm=(), scratch=(), limit=60, flops=0, scale=COST_SCALE):
    vmem = pl.BlockSpec(memory_space=pltpu.VMEM)
    anywhere = pl.BlockSpec(memory_space=pl.ANY)
    specs = [anywhere if i in hbm else vmem for i in range(len(inputs))]
    arguments = list(inputs)
    if flags is not None:
        specs.insert(0, pl.BlockSpec(memory_space=pltpu.SMEM))
        arguments.insert(0, flags)
    return pl.pallas_call(
        kernel,
        in_specs=specs,
        out_specs=[anywhere if "out" in hbm else vmem] * len(outs),
        out_shape=[jax.ShapeDtypeStruct(shape, dtype) for shape, dtype in outs],
        scratch_shapes=list(scratch),
        compiler_params=pltpu.CompilerParams(vmem_limit_bytes=limit * MIB),
        cost_estimate=pl.CostEstimate(
            flops=int(flops * scale),
            bytes_accessed=int(sum(2 * array.size for array in inputs) * scale),
            transcendentals=0,
        ),
    )(*arguments)


def prelude(place, image_len, timestep, time_embed, mod_table, rows):
    smem = pl.BlockSpec(memory_space=pltpu.SMEM)
    return pl.pallas_call(
        functools.partial(prelude_kernel, rows=rows),
        in_specs=[smem, smem, smem, pl.BlockSpec(memory_space=pl.ANY), pl.BlockSpec(memory_space=pltpu.VMEM)],
        out_specs=[smem, pl.BlockSpec(memory_space=pltpu.VMEM)],
        out_shape=[jax.ShapeDtypeStruct((4,), jnp.int32), jax.ShapeDtypeStruct(mod_table.shape, F32)],
        scratch_shapes=[pltpu.VMEM((8, time_embed.shape[1]), F32), pltpu.SemaphoreType.DMA],
        compiler_params=pltpu.CompilerParams(vmem_limit_bytes=60 * MIB),
    )(place.reshape(1), image_len, timestep, time_embed, mod_table)


def half_width(grads, count, joined):
    size = (sum(grad.shape[1] for grad in grads) if joined else grads[0].shape[1]) // count
    body, _ = slice_parts(size)
    return 2 * (count // 4 * body + 128) if joined else len(grads) * -(-count // 2 * size // 128) * 128


def halves(core, grads, count, joined):
    out = ((grads[0].shape[0], half_width(grads, count, joined)), BF)
    return call(functools.partial(halves_kernel, count=count, joined=joined), grads, [out] * 2, flags=core)


def split(flags, inputs, picked, parts, shape, axis=1):
    return call(
        functools.partial(split_kernel, picked=picked, parts=parts, axis=axis),
        inputs,
        [(shape, BF), (shape, F32)],
        flags=jnp.stack(flags),
    )


def add_last(keep, got, size, shapes):
    return call(functools.partial(last_kernel, size=size), [keep, got], [(shape, F32) for shape in shapes])


def wide_grad(order, source, mode):
    rows, width = source[0].shape
    depth = source[2].shape[1]
    wide, number = (depth, 2) if mode == "rows" else (depth // 2, 4)
    return call(
        functools.partial(wide_grad_kernel, mode=mode),
        source,
        [((2, width // 4, wide), BF)] * number,
        flags=order,
        hbm=(0, 1, 2, 3, "out"),
        scratch=[
            pltpu.VMEM((2 * rows, width), BF),
            pltpu.VMEM((2 * rows, depth), BF),
            pltpu.VMEM((width, 2 * rows), BF),
            pltpu.VMEM((2, width // 4, wide), BF),
            pltpu.SemaphoreType.DMA((4,)),
            pltpu.SemaphoreType.DMA((2,)),
        ],
    )


def tall_grad(order, acts, keep, got, size, mode):
    count = len(acts)
    rows, width = acts[0][0].shape
    wide = keep.shape[1]
    shape = (2, 4 * size, width // 4) if mode == "rows" else (2 * size * count, width)
    return call(
        functools.partial(tall_grad_kernel, count=count, mode=mode),
        [array for pair in acts for array in pair] + [keep, got],
        [(shape, BF)] * 2,
        flags=order,
        hbm=(*range(2 * count + 2), "out"),
        scratch=[
            pltpu.VMEM((count, 2 * rows, width), BF),
            pltpu.VMEM((2 * rows, wide), BF),
            pltpu.VMEM((wide, 2 * rows), BF),
            pltpu.VMEM((2, *shape[-2:]), BF),
            pltpu.SemaphoreType.DMA((2 * count + 2,)),
            pltpu.SemaphoreType.DMA((2,)),
        ],
    )


def mlp(inputs, grad, w_up, w_down):
    rows, width = inputs.shape
    units = w_up.shape[1]
    tile = 1152
    tiles = units // tile
    return call(
        functools.partial(mlp_kernel, tile=tile),
        [inputs, grad, w_up, w_down],
        [((rows, units), BF)] * 2 + [((rows, width), F32)] * 2,
        hbm=(2, 3),
        scratch=[
            pltpu.VMEM((tiles, width, tile), BF),
            pltpu.VMEM((tiles, tile, width), BF),
            pltpu.SemaphoreType.DMA((2, tiles)),
        ]
        + [pltpu.VMEM((rows, tile), BF)] * 4,
        scale=1.0,
        flops=8 * rows * width * units,
    )


def local(
    tokens,
    image_len,
    timestep,
    caption,
    time_embed,
    mod_table,
    w_qkv,
    w_out,
    cross_q,
    cross_kv,
    cross_out,
    w_up,
    w_down,
    cotangent,
):
    sp_count = lax.axis_size("sp")
    dp_count = lax.axis_size("dp")
    place = lax.axis_index("sp")
    row_place = lax.axis_index("dp")
    core = place % 2
    rows, width = tokens.shape[1:]
    factor = 1.0 / math.sqrt(width // HEADS)
    blocks = BIG // rows
    assert blocks == 4

    big, modulation = prelude(place, image_len, timestep, time_embed, mod_table, rows)
    shift_one, scale_one, gate_one, shift_two, scale_two, gate_two = [modulation[i] for i in range(6)]

    def tie(value, *before):
        return lax.optimization_barrier((value, *[array for array in before if array is not None]))[0]

    pairs = [(i, i ^ 1) for i in range(sp_count)]
    others = [(i, i + 1) for i in range(1, sp_count - 1, 2)] + [(i + 1, i) for i in range(1, sp_count - 1, 2)]
    ahead = [(i, i + 2) for i in range(sp_count - 2)]
    back = [(i + 2, i) for i in range(sp_count - 2)]

    def image_blocks(block, *before):
        from_back = lax.ppermute(block, "sp", ahead)
        from_ahead = lax.ppermute(block, "sp", back)
        from_ahead, from_back = tie(from_ahead, *before), tie(from_back, *before)
        send_pair = jnp.concatenate([jnp.where(big[1] == 1, from_ahead, from_back), block], axis=0)
        send_other = jnp.where(core == 1, from_back, from_ahead)
        both = lax.ppermute(send_pair, "sp", pairs)
        third = lax.ppermute(send_other, "sp", others)
        pair = both[block.shape[0] :]
        return (
            [
                both,
                jnp.where(big[2] == 1, pair, third),
                jnp.where(big[3] == 1, from_ahead, from_back),
            ],
            send_pair,
            send_other,
        )

    def swap(array):
        return lax.ppermute(array, "sp", pairs)

    token_blocks, *token_sends = image_blocks(tokens[0])

    def first_norm(block):
        return (normal(block.astype(F32))[0] * (1.0 + scale_one) + shift_one).astype(BF)

    first_in = first_norm(tokens[0])
    other_in = first_norm(jnp.concatenate([block[:rows] for block in token_blocks], axis=0))

    core_flag = core.reshape(1)
    chips = sp_count // 2
    square = dp_count == 4 and chips == 4

    def own_half(*grads, joined=True):
        if square:
            return halves(core_flag, grads, sp_count, joined)
        grads = [jnp.concatenate(grads, axis=1)] if joined else grads
        size = grads[0].shape[1] // sp_count
        even, odd = [
            jnp.concatenate(
                [g[:, i * size : (i + 1) * size] for g in grads for i in range(c, sp_count, 2)], axis=1
            )
            for c in (0, 1)
        ]
        return jnp.where(core == 0, even, odd), jnp.where(core == 0, odd, even)

    near, far = (place // 2) & 1, (place // 4) & 1
    row_bits = [row_place & 1, row_place >> 1]
    high = width // 4

    def to_row(array, bit):
        return lax.ppermute(array, "dp", [(i, i ^ (1 << bit)) for i in range(dp_count)])

    def to_chip(array, bit):
        return lax.ppermute(array, "sp", [(i, i ^ (2 << bit)) for i in range(sp_count)])

    def plain_sum(sources, size):
        finals = []
        for item, (x0, x1, g0, g1) in enumerate(sources):
            columns = slice(item * chips * size, (item + 1) * chips * size)
            part = (matmul_tn(x0, g0[:, columns]) + matmul_tn(x1, g1[:, columns])).astype(BF)
            part = part.reshape(dp_count, -1, chips, size).transpose(0, 2, 1, 3)
            bit = dp_count // 2
            while bit:
                mine = (row_place // bit) % 2
                part = part.reshape(2, bit, chips, -1, size)
                got = lax.ppermute(part[1 - mine], "dp", [(i, i ^ bit) for i in range(dp_count)])
                part = add(part[mine], got).astype(BF)
                bit //= 2
            part = part.reshape(chips, -1, size)
            bit = chips // 2
            while bit:
                mine = (place // 2 // bit) % 2
                part = part.reshape(2, bit, -1, size)
                got = lax.ppermute(part[1 - mine], "sp", [(i, i ^ (2 * bit)) for i in range(sp_count)])
                part = add(part[mine], got).astype(BF)
                bit //= 2
            finals.append(part[0].astype(F32))
        return finals

    def add_picked(pick, keep, got):
        return call(add_kernel, [keep, got], [(keep.shape[1:], BF)], flags=pick.reshape(1))

    everything = slice(None)

    def cut_slices(size):
        body, tail = slice_parts(size)
        return [
            [
                (everything, slice(h * body, (h + 1) * body)),
                (everything, slice(2 * body + h * tail, 2 * body + (h + 1) * tail)),
            ]
            for h in (0, 1)
        ]

    def sum_wide(source, first, size):
        second = 1 - first
        mine = row_bits[first]
        order = jnp.stack(
            [((1 - mine if s < 2 else mine) << first) + ((s % 2) << second) for s in range(4)]
        )
        if size < 256:
            send, keep = tall_grad(order, [source[:2]], *source[2:], size, "rows")
        else:
            send, keep = wide_grad(order, source, "rows")
        yield send
        got = to_row(send, first)
        mine = row_bits[second]
        (send,) = add_picked(1 - mine, keep, got)
        yield send
        tall, wide = send.shape
        more = to_row(send, second)
        if size < 256:
            groups = [[(slice(h * tall // 2, (h + 1) * tall // 2),)] for h in (0, 1)]
            send, keep = split([mine, near], [keep, got, more], 2, groups, (tall // 2, wide), 0)
            yield send
            groups = [[(slice(h * tall // 4, (h + 1) * tall // 4),)] for h in (0, 1)]
            send, keep = split([far, far], [keep, to_chip(send, 0)], 0, groups, (tall // 4, wide), 0)
            yield send
            (final,) = add_last(keep, to_chip(send, 1), 0, [(size, wide)])
            yield final.T
        else:
            groups = [[(everything, slice(h * wide // 2, (h + 1) * wide // 2))] for h in (0, 1)]
            send, keep = split([mine, near], [keep, got, more], 2, groups, (tall, wide // 2))
            yield send
            shape = (tall, size // 128 * 128 + 128)
            send, keep = split([far, far], [keep, to_chip(send, 0)], 0, cut_slices(size), shape)
            yield send
            (final,) = add_last(keep, to_chip(send, 1), size, [(tall, size)])
            yield final

    def sum_both(source, size):
        order = jnp.stack([jnp.int32(i) for i in range(4)] + row_bits)
        outs = wide_grad(order, source, "both")
        yield outs
        got = [to_row(outs[0], 0), to_row(outs[2], 1)]
        sends = [
            *add_picked(1 - row_bits[1], outs[1], got[0]),
            *add_picked(1 - row_bits[0], outs[3], got[1]),
        ]
        yield sends
        shape = sends[0].shape
        send, keep = call(
            split_pair_kernel,
            [outs[1], got[0], to_row(sends[0], 1), outs[3], got[1], to_row(sends[1], 0)],
            [(shape, BF), (shape, F32)],
            flags=jnp.stack([row_bits[1], row_bits[0], near]),
        )
        yield send
        shape = (shape[0], size // 128 * 128 + 128)
        send, keep = split([far, far], [keep, to_chip(send, 0)], 0, cut_slices(size), shape)
        yield send
        (final,) = add_last(keep, to_chip(send, 1), size, [(high, size)])
        yield final

    def sum_chips_first(acts, keep, got, size):
        count = len(acts)
        order = jnp.stack([jnp.int32(i) for i in range(4)] + [near])
        send, keep = tall_grad(order, acts, keep, got, size, "chips")
        late = yield send
        groups = [
            [(slice((2 * k + h) * size, (2 * k + h + 1) * size),) for k in range(count)] for h in (0, 1)
        ]
        got = to_chip(send, 0)
        send, keep = split([far, far], [tie(keep, late), got], 0, groups, (count * size, width), 0)
        yield send
        groups = [
            [(everything, slice(i * high, (i + 1) * high)) for i in (h, h + 2)] for h in (0, 1)
        ]
        shape = (count * size, lanes(2 * high))
        send, keep = split([row_bits[0]] * 2, [keep, to_chip(send, 1)], 0, groups, shape)
        yield send
        groups = [[(everything, slice(h * high, (h + 1) * high))] for h in (0, 1)]
        shape = (count * size, lanes(high))
        send, keep = split([row_bits[1]] * 2, [keep, to_row(send, 0)], 0, groups, shape)
        yield send
        finals = add_last(keep, to_row(send, 1), 0, [(size, high)] * count)
        yield [final.T for final in finals]

    def spread_vector(vector):
        for axis, name, count, mine in ((0, "dp", dp_count, row_place), (1, "sp", sp_count, place)):
            bit = count // 2
            while bit:
                shape = vector.shape
                split = vector.reshape(shape[:axis] + (2, bit) + shape[axis + 1 :])
                at = lambda i: lax.dynamic_index_in_dim(split, i, axis, keepdims=False)
                own = (mine // bit) % 2
                got = lax.ppermute(at(1 - own), name, [(i, i ^ bit) for i in range(count)])
                vector = at(own) + got
                bit //= 2
        return vector.reshape(-1)

    caption_rows = caption[0]
    live = caption_rows.shape[0]
    padded = -(-live // 128) * 128
    caption_pad = jnp.concatenate([caption_rows, jnp.zeros((padded - live, width), BF)], axis=0)
    text = matmul(caption_pad, cross_kv).astype(BF)
    grad_mlp = (gate_two * cotangent[0].astype(F32)).astype(BF)
    mlp_keep, mlp_send = own_half(grad_mlp, joined=False)
    mlp_got = swap(mlp_send)
    first_pair = swap(first_in)
    own = matmul(tie(first_in, *token_sends), w_qkv).astype(BF)
    far_qkv = matmul(other_in, w_qkv).astype(BF)
    block = ((rows, width), BF)
    stream = ((rows, width), F32)
    stats = ((rows, 128), F32)
    attended, logsum = call(
        functools.partial(attend_kernel, factor=factor),
        [own, far_qkv],
        [block, stats],
        flags=big,
        limit=20,
        scale=1.0,
        flops=4 * HEADS * rows * blocks * rows * WIN,
    )
    attn_branch, cross_in, cross_queries, cross_mixed, stream_two, second_in = call(
        functools.partial(middle_kernel, factor=factor, live=live),
        [tokens[0], modulation, attended, w_out, cross_q, cross_out, text],
        [stream, block, block, block, stream, block],
        limit=12,
        scale=1.0,
        flops=6 * rows * width * width,
    )
    second_pair = swap(second_in)
    small_acts = [(acts, swap(acts)) for acts in (cross_mixed, cross_in, attended)]
    hidden, grad_pre, mlp_branch, grad_second = mlp(tie(second_in, mlp_got, first_pair), grad_mlp, w_up, w_down)

    pre_keep, pre_send = own_half(grad_pre)
    hidden_pair, pre_got = swap(hidden), swap(pre_send)
    early = [pair for _, pair in small_acts]
    small_width = half_width([grad_mlp] * 3, sp_count, False) if square else 3 * width
    small_out = ((rows, small_width), BF)
    stream_three, grad_one, small_keep, small_send, grad_text, pack, stat, table = call(
        functools.partial(middle_grad_kernel, factor=factor, live=live, count=sp_count if square else 0),
        [
            tie(grad_second, pre_send, second_pair, *early), stream_two, cotangent[0], mlp_branch, modulation, attn_branch, attended,
            logsum, cross_queries, text, w_out, cross_q, cross_out,
        ],
        [
            stream, stream, small_out, small_out, ((live, 2 * width), F32), ((rows + 16, width), BF), stats,
            (modulation.shape, F32),
        ],
        flags=core_flag,
        scratch=[pltpu.VMEM((rows, width), BF)] * 2 + [pltpu.VMEM((padded, width), F32)] * 2,
        limit=20,
        scale=1.0,
        flops=8 * rows * width * width,
    )
    if not square:
        small_keep, small_send = own_half(*jnp.split(small_keep, 3, axis=1), joined=False)
    small_got = swap(small_send)
    slice_of = lambda weight: weight.shape[1] // sp_count
    down_source = (hidden, hidden_pair, mlp_keep, mlp_got)
    up_source = (second_in, second_pair, pre_keep, pre_got)
    send_down = send_up = send_small = None
    if square:
        small_sum = sum_chips_first(small_acts, tie(small_keep, pack), small_got, slice_of(w_out))
        send_small = next(small_sum)
        up_sum = sum_wide((tie(second_in, send_small), *up_source[1:]), 1, slice_of(w_up))
        send_up = next(up_sum)
        down_sum = sum_wide((tie(hidden, send_up), *down_source[1:]), 0, slice_of(w_down))
        send_down = next(down_sum)
    pack_blocks, *pack_sends = image_blocks(pack, send_down, send_up)
    (grad_queries,) = call(
        functools.partial(query_grad_kernel, factor=factor),
        [own, far_qkv, tie(pack, *pack_sends), stat],
        [block],
        flags=big,
        hbm=(0, 1, 2),
        scratch=[
            pltpu.VMEM(own.shape, BF),
            pltpu.VMEM(far_qkv.shape, BF),
            pltpu.VMEM(pack.shape, BF),
            pltpu.SemaphoreType.DMA((3,)),
        ],
    )
    grad_keys, grad_values = call(
        functools.partial(key_grad_kernel, factor=factor),
        [own, far_qkv, tie(pack, grad_queries), *pack_blocks],
        [block, block],
        flags=big,
        hbm=(0, 1, 2, *range(3, 2 + blocks)),
        scratch=[
            pltpu.VMEM(own.shape, BF),
            pltpu.VMEM(((blocks - 1) * rows, width), BF),
            pltpu.VMEM(pack.shape, BF),
            pltpu.VMEM((2 * HEADS, blocks * rows), F32),
            pltpu.VMEM(((blocks - 1) * rows, width), BF),
            pltpu.VMEM((blocks - 1, 16, width), BF),
            pltpu.SemaphoreType.DMA((2 * blocks + 1,)),
        ],
    )
    proj_keep, proj_send = own_half(
        tie(grad_queries, small_sum.send(grad_keys) if square else None), grad_keys, grad_values
    )
    qkv_source = (first_in, first_pair, proj_keep, swap(proj_send))
    sent = []
    if square:
        qkv_source = (tie(first_in, next(up_sum)), *qkv_source[1:])
        qkv_sum = sum_both(qkv_source, slice_of(w_qkv))
        sent = [*next(qkv_sum), next(down_sum)]
    grad_tokens, table = call(
        last_grad_kernel,
        [tie(grad_queries, *sent), grad_keys, grad_values, w_qkv, tokens[0], modulation, grad_one, table],
        [stream, (modulation.shape, F32)],
    )

    if square:
        next(qkv_sum)
        table = tie(table, next(qkv_sum))
        sums = [down_sum, up_sum, small_sum, qkv_sum]
        final_down, final_up, final_small, final_qkv = [list(each)[-1] for each in sums]
    else:
        small = [(*acts, small_keep, small_got) for acts in small_acts]
        final_small = plain_sum(small, slice_of(w_out))
        (final_down,) = plain_sum([down_source], slice_of(w_down))
        (final_up,) = plain_sum([up_source], slice_of(w_up))
        (final_qkv,) = plain_sum([qkv_source], slice_of(w_qkv))
    text_part = lax.psum_scatter(grad_text, "sp", scatter_dimension=1, tiled=True).astype(BF)
    part_ckv = matmul_tn(caption_rows, text_part).astype(BF)
    final_ckv = lax.psum_scatter(part_ckv, "dp", scatter_dimension=0, tiled=True).astype(F32)
    final_table = spread_vector(table.reshape(dp_count, sp_count, -1))
    return (
        stream_three[None],
        grad_tokens[None],
        final_table,
        final_qkv,
        final_small[2],
        final_small[1],
        final_ckv,
        final_small[0],
        final_up,
        final_down,
    )


def solution(mesh):
    return jax.shard_map(
        local,
        mesh=mesh,
        in_specs=(
            P("dp", "sp", None),
            P("dp", None),
            P("dp", None),
            P("dp", None, None),
            P(),
            P(),
            P(),
            P(),
            P(),
            P(),
            P(),
            P(),
            P(),
            P("dp", "sp", None),
        ),
        out_specs=(
            P("dp", "sp", None),
            P("dp", "sp", None),
            P(("dp", "sp")),
            P("dp", "sp"),
            P("dp", "sp"),
            P("dp", "sp"),
            P("dp", "sp"),
            P("dp", "sp"),
            P("dp", "sp"),
            P("dp", "sp"),
        ),
        check_vma=False,
    )
```

```python
import functools
import math

import jax
import jax.numpy as jnp
from jax import lax
from jax.experimental import pallas as pl
from jax.experimental.pallas import tpu as pltpu
from jax.sharding import PartitionSpec as P

HEADS = 16
BIG = 1024
EPS = 1e-06
BIGNEG = -1e30
LOG2E = 1.4426950408889634
BF = jnp.bfloat16
F32 = jnp.float32
WIN = 256
COST_SCALE = 0.001
MIB = 1024 * 1024


def matmul(left, right):
    return jnp.dot(left, right, preferred_element_type=F32)


def matmul_tn(left, right):
    return lax.dot_general(left, right, (((0,), (0,)), ((), ())), preferred_element_type=F32)


def matmul_nt(left, right):
    return lax.dot_general(left, right, (((1,), (1,)), ((), ())), preferred_element_type=F32)


def head_window(head, width):
    size = width // HEADS
    low = head * size
    start = pl.multiple_of(jnp.minimum(low // 128 * 128, width - WIN), 128)
    lane = lax.broadcasted_iota(jnp.int32, (1, WIN), 1) + start
    return start, jnp.logical_and(lane >= low, lane < low + size)


def window(ref, start, offset=0):
    return ref[:, pl.ds(pl.multiple_of(start + offset, 128), WIN)]


def keep_columns(ref, start, mask, value):
    win = pl.ds(start, WIN)
    ref[:, win] = jnp.where(mask, value, ref[:, win])


def each_head(body, unroll=4):
    def step(head, carry):
        body(head)
        return carry

    lax.fori_loop(0, HEADS, step, 0, unroll=unroll)


def fetch(sems, *pairs):
    copies = [pltpu.make_async_copy(source, target, sems.at[i]) for i, (source, target) in enumerate(pairs)]
    for copy in copies:
        copy.start()
    return [copy.wait for copy in copies]


def attend(big, own_ref, far_ref, out_ref, lse_ref, factor):
    width = out_ref.shape[1]
    scale = factor * LOG2E

    def run(sides):
        def one_head(head):
            start, mask = head_window(head, width)
            query = window(own_ref, start) * mask.astype(BF)
            scores = [matmul_nt(query, window(side, start, key)) for side, key in sides]
            top = functools.reduce(jnp.maximum, [jnp.max(s, axis=1, keepdims=True) for s in scores])
            raised = [jnp.exp2((s - top) * scale) for s in scores]
            total = sum(jnp.sum(r, axis=1, keepdims=True) for r in raised)
            inverse = 1.0 / total
            result = sum(
                matmul((r * inverse).astype(BF), window(side, start, key + width))
                for r, (side, key) in zip(raised, sides)
            )
            keep_columns(out_ref, start, mask, result.astype(BF))
            lane = lax.broadcasted_iota(jnp.int32, (1, 128), 1)
            lse_ref[...] = jnp.where(lane == head, top * scale + jnp.log2(total), lse_ref[...])

        each_head(one_head)

    lse_ref[...] = jnp.zeros_like(lse_ref)

    @pl.when(big)
    def _():
        run([(own_ref, width), (far_ref, 0)])

    @pl.when(jnp.logical_not(big))
    def _():
        run([(own_ref, width)])


def query_grad_kernel(big_ref, own_ref, far_ref, pack_ref, stat_ref, out_ref, *, factor):
    rows, width = out_ref.shape
    scale = factor * LOG2E

    def run(sides):
        def one_head(head):
            start, mask = head_window(head, width)
            keep = mask.astype(BF)
            query = window(own_ref, start) * keep
            grad = window(pack_ref.at[0:rows, :], start) * keep
            lane = lax.broadcasted_iota(jnp.int32, (1, 128), 1)
            stat = stat_ref[...]
            lse = jnp.sum(jnp.where(lane == head, stat, 0.0), axis=1, keepdims=True)
            delta = jnp.sum(jnp.where(lane == head + HEADS, stat, 0.0), axis=1, keepdims=True)
            total = None
            for side, offset in sides:
                key = window(side, start, offset)
                prob = jnp.exp2(matmul_nt(query, key) * scale - lse)
                grad_prob = matmul_nt(grad, window(side, start, offset + width))
                grad_score = (prob * (grad_prob - delta)).astype(BF)
                part = matmul(grad_score, key)
                total = part if total is None else total + part
            keep_columns(out_ref, start, mask, (total * factor).astype(BF))

        each_head(one_head)

    @pl.when(big_ref[0] == 1)
    def _():
        run([(own_ref, width), (far_ref, 0)])

    @pl.when(big_ref[0] == 0)
    def _():
        run([(own_ref, width)])


def key_grad_kernel(flag_ref, own, far, pack, dq, *refs, factor, count):
    packs, (dk, dv, keep_out, send_out, stats, grads, tails, sems) = refs[:-8], refs[-8:]
    own_ref, far_ref, pack_ref, dq_ref = (slot.ref for slot in (own, far, pack, dq))
    dk_ref, dv_ref, keep_ref, send_ref = (slot.ref for slot in (dk, dv, keep_out, send_out))
    rows, width = dk_ref.shape
    pairs = [(other.at[rows : rows + 16, :], tails.at[i]) for i, other in enumerate(packs)]
    pairs += [(other.at[0:rows, :], grads.at[i * rows : (i + 1) * rows, :]) for i, other in enumerate(packs)]
    waits = fetch(sems, *pairs)
    for slot in (own, far, pack, dq):
        slot.start()
    for wait in waits:
        wait()
    for slot in (own, far, pack, dq):
        slot.wait()
    scale = factor * LOG2E
    blocks = 1 + len(packs)

    def unpack(block, both):
        both = both.astype(F32)
        joined = both[:8] + both[8:]
        for group in range(4):
            stats[8 * group : 8 * group + 8, block * rows : block * rows + rows] = joined[
                :, group * rows : group * rows + rows
            ]

    unpack(0, pack_ref[rows:, :])
    for block in range(len(packs)):
        unpack(block + 1, tails[block])

    def run(parts):
        def one_head(head):
            start, mask = head_window(head, width)
            keep = mask.astype(BF)
            key = window(own_ref, start, width) * keep
            value = window(own_ref, start, 2 * width) * keep
            lse = stats[pl.ds(head, 1), :]
            delta = stats[pl.ds(head + HEADS, 1), :]
            grad_key = grad_value = 0.0
            for query_ref, grad_ref, low, high in parts:
                query, grad = window(query_ref, start), window(grad_ref.at[0 : high - low, :], start)
                prob = jnp.exp2(matmul_nt(key, query) * scale - lse[:, low:high])
                grad_prob = matmul_nt(value, grad)
                grad_score = (prob * (grad_prob - delta[:, low:high])).astype(BF)
                grad_value = grad_value + matmul(prob.astype(BF), grad)
                grad_key = grad_key + matmul(grad_score, query)
            keep_columns(dk_ref, start, mask, (grad_key * factor).astype(BF))
            keep_columns(dv_ref, start, mask, grad_value.astype(BF))

        each_head(one_head)

    local = (own_ref, pack_ref, 0, rows)
    @pl.when(flag_ref[0] == 1)
    def _():
        run([local, (far_ref, grads, rows, blocks * rows)])

    @pl.when(flag_ref[0] == 0)
    def _():
        run([local])

    dk.send()
    dv.send()
    if count:
        for core in (0, 1):

            @pl.when(flag_ref[1] == core)
            def _(core=core):
                grads = [ref[...] for ref in (dq_ref, dk_ref, dv_ref)]
                keep_ref[...] = half_columns(grads, core, count, True, keep_ref.shape[1])
                send_ref[...] = half_columns(grads, 1 - core, count, True, send_ref.shape[1])

    else:
        for index, ref in enumerate((dq_ref, dk_ref, dv_ref)):
            keep_ref[:, index * width : (index + 1) * width] = ref[...]


def text_probs(query, key, scale, live, axis):
    scores = matmul_nt(query, key) if axis else matmul_nt(key, query)
    shape = (1, scores.shape[1]) if axis else (scores.shape[0], 1)
    scores = jnp.where(lax.broadcasted_iota(jnp.int32, shape, axis) < live, scores, BIGNEG)
    raised = jnp.exp2((scores - jnp.max(scores, axis=axis, keepdims=True)) * scale)
    return raised * (1.0 / jnp.sum(raised, axis=axis, keepdims=True))


def normal(stream):
    centred = stream - jnp.mean(stream, axis=-1, keepdims=True)
    spread = lax.rsqrt(jnp.mean(centred * centred, axis=-1, keepdims=True) + EPS)
    return centred * spread, spread


def norm_back(normed, spread, scale, grad):
    scaled = grad * (1.0 + scale)
    back = spread * (
        scaled
        - jnp.mean(scaled, axis=-1, keepdims=True)
        - normed * jnp.mean(scaled * normed, axis=-1, keepdims=True)
    )
    return back, jnp.sum(grad, axis=0, keepdims=True), jnp.sum(grad * normed, axis=0, keepdims=True)


def middle(tokens_ref, mod_ref, att_ref, weights, text_ref, refs, factor, live):
    branch_ref, cross_in_ref, queries_ref, mixed_ref, stream_ref, second_ref = refs
    width = tokens_ref.shape[1]
    out_w_ref, query_w_ref, cross_w_ref = weights
    branch = matmul(att_ref[...], out_w_ref[...])
    branch_ref[...] = branch
    stream = tokens_ref[...].astype(F32) + mod_ref[2:3, :] * branch
    stream_ref[...] = stream
    cross_in = stream.astype(BF)
    cross_in_ref[...] = cross_in
    queries_ref[...] = matmul(cross_in, query_w_ref[...]).astype(BF)

    def one_head(head):
        start, mask = head_window(head, width)
        query = window(queries_ref, start) * mask.astype(BF)
        probs = text_probs(query, window(text_ref, start), factor * LOG2E, live, 1)
        result = matmul(probs.astype(BF), window(text_ref, start, width))
        keep_columns(mixed_ref, start, mask, result.astype(BF))

    each_head(one_head, 8)
    stream = stream_ref[...] + matmul(mixed_ref[...], cross_w_ref[...])
    stream_ref[...] = stream
    second_ref[...] = (normal(stream)[0] * (1.0 + mod_ref[4:5, :]) + mod_ref[3:4, :]).astype(BF)


def forward_kernel(
    flag_ref, own, far, tokens, mod, text, out_w, query_w, cross_w, grad, up_hbm, down_hbm,
    att, lse, branch, cross_in, queries, mixed, stream, second, hidden, keep, send, mlp_out, back,
    up, down, *scratch, factor, live, count
):
    own.start()
    far.start()
    own.wait()
    far.wait()
    late = (tokens, mod, text, out_w, query_w, cross_w, grad)
    for slot in late:
        slot.start()
    sems, *kept = scratch
    tile = down.shape[1]
    tiles = down_hbm.shape[0] // tile
    ring = down.shape[0]

    def copies(step):
        half = tile // 2
        slot = step % ring
        pairs = []
        for part in (0, 1):
            rows = slice(part * up_hbm.shape[0] // 2, (part + 1) * up_hbm.shape[0] // 2)
            pairs.append((up_hbm.at[rows, step * tile : (step + 1) * tile], up.at[slot, rows, :]))
            rows = slice(part * half, (part + 1) * half)
            pairs.append((down_hbm.at[step * tile + part * half : step * tile + (part + 1) * half, :], down.at[slot, rows, :]))
        return [pltpu.make_async_copy(a, b, sems.at[slot, i]) for i, (a, b) in enumerate(pairs)]

    for step in range(min(ring, tiles)):
        for copy in copies(step):
            copy.start()
    attend(flag_ref[0] == 1, own.ref, far.ref, att.ref, lse.ref, factor)
    att.send()
    lse.send()
    for slot in late:
        slot.wait()
    outs = (branch, cross_in, queries, mixed, stream, second)
    weights = (out_w.ref, query_w.ref, cross_w.ref)
    middle(tokens.ref, mod.ref, att.ref, weights, text.ref, [out.ref for out in outs], factor, live)
    for out in outs:
        out.send()

    root = math.sqrt(2.0 / math.pi)
    width = second.ref.shape[1]

    def both(step):
        if step < tiles:
            for copy in copies(step):
                copy.wait()
            pre = matmul(second.ref[...], up[step % ring])
            slope = matmul_nt(grad.ref[...], down[step % ring])
        if step > 0:
            before = (step - 1) % ring
            ahead, behind = (ref[...] for ref in kept[(step - 1) % 2 * 2 : (step - 1) % 2 * 2 + 2])
            branch = matmul(ahead, down[before])
            result = matmul_nt(behind, up[before])
        if step < tiles:
            square = pre * pre
            bend = jnp.tanh(pre * (root * 0.044715 * square + root))
            half = 0.5 * bend + 0.5
            rise = (3 * root * 0.044715 * square + root) * pre
            ahead = (pre * half).astype(BF)
            behind = (slope * (half + 0.5 * rise * (1.0 - bend * bend))).astype(BF)
            kept[step % 2 * 2][...] = ahead
            kept[step % 2 * 2 + 1][...] = behind
            hidden.ref[:, step * tile : (step + 1) * tile] = ahead
            if count:
                size = tile // 2
                body, tail = slice_parts(size)
                group = step % 2 * keep.ref.shape[1] // 2
                spots = (
                    (group + step // 2 * body, 0, body),
                    (group + tiles // 2 * body + step // 2 * tail, body, tail),
                )
                for core in (0, 1):

                    @pl.when(flag_ref[4] == core)
                    def _(core=core):
                        for at, low, wide in spots:
                            mine, other = core * size + low, (1 - core) * size + low
                            keep.ref[:, at : at + wide] = behind[:, mine : mine + wide]
                            send.ref[:, at : at + wide] = behind[:, other : other + wide]

            else:
                keep.ref[:, step * tile : (step + 1) * tile] = behind
        if step > 0:
            if step == 1:
                mlp_out.ref[...] = branch
                back.ref[...] = result
            else:
                mlp_out.ref[...] += branch
                back.ref[...] += result
            if step - 1 + ring < tiles:
                for copy in copies(step - 1 + ring):
                    copy.start()

    for step in range(tiles):
        both(step)
    hidden.send()
    keep.send()
    send.send()
    both(tiles)


def middle_grad_kernel(
    core_ref, second_grad, stream_in, cot_in, mlp_in, mod_in, cross_w, queries, text, query_w, branch, out_w, att, lse,
    out, one, keep, send, text_grad, pack, stat_out, table,
    mixed, grad_queries, text_key, text_value, *, factor, live, count
):
    early = (second_grad, stream_in, cot_in, mlp_in, mod_in)
    for slot in early:
        slot.start()
    for slot in early:
        slot.wait()
    late = (cross_w, queries, text, query_w, branch, out_w, att, lse)
    for slot in late:
        slot.start()
    second_grad_ref, stream_ref, cot_ref, mlp_ref, mod_ref = (slot.ref for slot in early)
    cross_w_ref, queries_ref, text_ref, query_w_ref, branch_ref, out_w_ref, att_ref, lse_ref = (
        slot.ref for slot in late
    )
    one_ref, keep_ref, send_ref, text_grad_ref, pack_ref, stat_ref, table_ref = (
        slot.ref for slot in (one, keep, send, text_grad, pack, stat_out, table)
    )
    rows, width = cot_ref.shape
    cot = cot_ref[...].astype(F32)
    stream = stream_ref[...]
    mlp = mlp_ref[...]
    out.ref[...] = stream + mod_ref[5:6, :] * mlp
    out.send()
    normed, spread = normal(stream)
    back, shift, scale = norm_back(normed, spread, mod_ref[4:5, :], second_grad_ref[...])
    table_ref[...] = jnp.zeros_like(table_ref)
    table_ref[3:4, :] = shift
    table_ref[4:5, :] = scale
    table_ref[5:6, :] = jnp.sum(cot * mlp, axis=0, keepdims=True)
    grad_two = cot + back
    one_ref[...] = grad_two
    grad_cross = grad_two.astype(BF)
    for slot in late:
        slot.wait()
    mixed[...] = matmul_nt(grad_cross, cross_w_ref[...]).astype(BF)

    def one_head(head):
        start, mask = head_window(head, width)
        keep = mask.astype(BF)
        query = window(queries_ref, start)
        grad = window(mixed, start)
        key = window(text_ref, start) * keep
        probs = text_probs(query, key, factor * LOG2E, live, 0)
        grad_probs = matmul_nt(window(text_ref, start, width) * keep, grad)
        inner = jnp.sum(probs * grad_probs, axis=0, keepdims=True)
        grad_scores = (probs * (grad_probs - inner)).astype(BF)
        keep_columns(grad_queries, start, mask, (matmul_tn(grad_scores, key) * factor).astype(BF))
        keep_columns(text_key, start, mask, matmul(grad_scores, query) * factor)
        keep_columns(text_value, start, mask, matmul(probs.astype(BF), grad))

    each_head(one_head, 8)
    text_grad_ref[:, :width] = text_key[0:live, :]
    text_grad_ref[:, width:] = text_value[0:live, :]
    text_grad.send()
    grad_cq = grad_queries[...]
    grad_one = one_ref[...] + matmul_nt(grad_cq, query_w_ref[...])
    one_ref[...] = grad_one
    table_ref[2:3, :] = jnp.sum(grad_one * branch_ref[...], axis=0, keepdims=True)
    grad_attn = (mod_ref[2:3, :] * grad_one).astype(BF)
    grad_att = matmul_nt(grad_attn, out_w_ref[...]).astype(BF)
    pack_ref[0:rows, :] = grad_att

    product = grad_att.astype(F32) * att_ref[...].astype(F32)
    upper = product.astype(BF)
    lower = (product - upper.astype(F32)).astype(BF)
    size = width // HEADS
    column = lax.broadcasted_iota(jnp.int32, (width, 128), 0)
    low = (lax.broadcasted_iota(jnp.int32, (width, 128), 1) - HEADS) * size
    pick = jnp.logical_and(column >= low, column < low + size).astype(BF)
    stat = lse_ref[...] + matmul(upper, pick) + matmul(lower, pick)
    stat_ref[...] = stat
    turned = stat.T
    upper = [turned[8 * g : 8 * g + 8, :].astype(BF).astype(F32) for g in range(4)]
    lower = [turned[8 * g : 8 * g + 8, :] - part for g, part in enumerate(upper)]
    both = [jnp.concatenate(pair, axis=0) for pair in zip(upper, lower)]
    pack_ref[rows : rows + 16, :] = side_by_side(both, width).astype(BF)
    for slot in (pack, stat_out, one, table):
        slot.send()

    if count:
        for core in (0, 1):

            @pl.when(core_ref[0] == core)
            def _(core=core):
                grads = [grad_cross, grad_cq, grad_attn]
                keep_ref[...] = half_columns(grads, core, count, False, keep_ref.shape[1])
                send_ref[...] = half_columns(grads, 1 - core, count, False, send_ref.shape[1])

    else:
        for index, grad in enumerate((grad_cross, grad_cq, grad_attn)):
            keep_ref[:, index * width : (index + 1) * width] = grad


def last_grad_kernel(
    dq_ref, dk_ref, dv_ref, weight_ref, tokens_ref, mod_ref, one_ref, table_in_ref, out_ref, table_ref
):
    width = tokens_ref.shape[1]
    grad = sum(
        matmul_nt(ref[...], weight_ref[:, part * width : (part + 1) * width])
        for part, ref in enumerate((dq_ref, dk_ref, dv_ref))
    )
    normed, spread = normal(tokens_ref[...].astype(F32))
    back, shift, scale = norm_back(normed, spread, mod_ref[1:2, :], grad)
    out_ref[...] = one_ref[...] + back
    table_ref[...] = table_in_ref[...]
    table_ref[0:1, :] = shift
    table_ref[1:2, :] = scale


def side_by_side(pieces, width):
    missing = width - sum(piece.shape[1] for piece in pieces)
    if missing:
        pieces = [*pieces, jnp.zeros((pieces[0].shape[0], missing), pieces[0].dtype)]
    return pieces[0] if len(pieces) == 1 else jnp.concatenate(pieces, axis=1)


def lanes(width):
    return -(-width // 128) * 128


def slice_parts(size):
    return size // 128 * 128, size % 128


def half_columns(grads, core, count, joined, wide):
    if not joined:
        picked = []
        for grad in grads:
            size = grad.shape[1] // count
            low = [(2 * chip + core) * size for chip in (*range(0, count // 2, 2), *range(1, count // 2, 2))]
            picked.append(
                side_by_side([grad[:, at : at + size] for at in low], wide // len(grads))
            )
        return side_by_side(picked, wide)
    grad = grads[0] if len(grads) == 1 else jnp.concatenate(grads, axis=1)
    size = grad.shape[1] // count
    body, _ = slice_parts(size)
    picked = []
    for parity in (0, 1):
        low = [(2 * chip + core) * size for chip in range(parity, count // 2, 2)]
        picked += [grad[:, at : at + body] for at in low]
        picked.append(side_by_side([grad[:, at + body : at + size] for at in low], 128))
    return side_by_side(picked, wide)


def halves_kernel(core_ref, *refs, count, joined):
    keep_ref, send_ref = refs[-2:]
    for core in (0, 1):

        @pl.when(core_ref[0] == core)
        def _(core=core):
            grads = [ref[...] for ref in refs[:-2]]
            keep_ref[...] = half_columns(grads, core, count, joined, keep_ref.shape[1])
            send_ref[...] = half_columns(grads, 1 - core, count, joined, send_ref.shape[1])


def store_halves(flag, stores, pieces):
    for value in (0, 1):

        @pl.when(flag == value)
        def _(value=value):
            for store, piece in zip(stores, (pieces[1 - value], pieces[value])):
                store(piece())


def into(ref):
    def store(value):
        ref[:, : value.shape[1]] = value.astype(ref.dtype)

    return store


def add(*terms):
    return sum(term.astype(F32) for term in terms)


def sending(buffers, sems, out):
    state = {"count": 0}

    def wait(slot):
        pltpu.make_async_copy(buffers.at[slot], out, sems.at[slot]).wait()

    def put(pieces, targets):
        slot = state["count"] % 2
        if state["count"] >= 2:
            wait(slot)
        at = 0
        for piece in pieces:
            buffers[slot, at : at + piece.shape[0], : piece.shape[1]] = piece
            at += piece.shape[0]
        for condition, target in targets:
            copy = pltpu.make_async_copy(buffers.at[slot], target, sems.at[slot])
            if condition is None:
                copy.start()
            else:
                pl.when(condition)(copy.start)
        state["count"] += 1

    def done():
        for slot in range(min(2, state["count"])):
            wait(slot)

    return put, done


def wide_grad_kernel(order_ref, x0_hbm, x1_hbm, g0_hbm, g1_hbm, *refs, mode):
    number = 2 if mode == "rows" else 4
    outs, (x_ref, g_ref, turned, buffers, sems, out_sems) = refs[:number], refs[number:]
    rows, width = x0_hbm.shape
    waits = fetch(
        sems,
        (x0_hbm, x_ref.at[0:rows, :]),
        (x1_hbm, x_ref.at[rows : 2 * rows, :]),
        (g0_hbm, g_ref.at[0:rows, :]),
        (g1_hbm, g_ref.at[rows : 2 * rows, :]),
    )
    for part in (0, 1):
        waits[part]()
        for low in range(0, width, 128):
            turned[low : low + 128, part * rows : (part + 1) * rows] = x_ref[
                part * rows : (part + 1) * rows, low : low + 128
            ].T
    waits[2]()
    waits[3]()
    tall = width // 4
    put, done = sending(buffers, out_sems, outs[0].at[0])
    half = g_ref.shape[1] // 2
    for step in range(4):
        here = pl.ds(pl.multiple_of(order_ref[step] * tall, 16), tall)
        if mode == "rows":
            total = matmul(turned[here, :], g_ref[...]).astype(BF)
            put([total], [(None, outs[step // 2].at[step % 2])])
        else:
            for p in (0, 1):
                total = matmul(turned[here, :], g_ref[:, p * half : (p + 1) * half]).astype(BF)
                first, second = (step >> p) & 1, (step >> (1 - p)) & 1
                mine = order_ref[4 + p]
                put(
                    [total],
                    [(mine != first, outs[2 * p].at[second]), (mine == first, outs[2 * p + 1].at[second])],
                )
    done()


def tall_grad_kernel(order_ref, *refs, count, mode):
    sources, g0_hbm, g1_hbm = refs[: 2 * count], refs[2 * count], refs[2 * count + 1]
    outs, (x_ref, g_ref, turned, buffers, sems, out_sems) = refs[2 * count + 2 : 2 * count + 4], refs[2 * count + 4 :]
    rows, width = sources[0].shape
    pairs = [(g0_hbm, g_ref.at[0:rows, :]), (g1_hbm, g_ref.at[rows : 2 * rows, :])]
    for i, source in enumerate(sources):
        pairs.append((source, x_ref.at[i // 2, i % 2 * rows : (i % 2 + 1) * rows, :]))
    waits = fetch(sems, *pairs)
    wide = g_ref.shape[1]
    for part in (0, 1):
        waits[part]()
        for low in range(0, wide, 128):
            turned[low : low + 128, part * rows : (part + 1) * rows] = g_ref[
                part * rows : (part + 1) * rows, low : low + 128
            ].T
    for wait in waits[2:]:
        wait()
    if mode == "rows":
        high, tall = outs[0].shape[1:]
        put, done = sending(buffers, out_sems, outs[0].at[0])
        for step in range(4):
            here = pl.ds(pl.multiple_of(order_ref[step] * tall, 128), tall)
            total = matmul(turned[0:high, :], x_ref[0, :, here]).astype(BF)
            put([total], [(None, outs[step // 2].at[step % 2])])
    else:
        high = outs[0].shape[0] // count
        put, done = sending(buffers, out_sems, outs[0])
        for p in (0, 1):
            total = [
                matmul(turned[pl.ds(k * (wide // count) + p * high, high), :], x_ref[k]).astype(BF)
                for k in range(count)
            ]
            put(total, [(order_ref[4] != p, outs[0]), (order_ref[4] == p, outs[1])])
    done()


def add_kernel(flag_ref, *refs):
    refs[-1][...] = add(*[ref[...] for ref in refs[:-1]]).astype(BF)


def split_kernel(flag_ref, *refs, parts, axis):
    views = refs[:-2]

    def joined(index):
        def piece():
            sums = [add(*[view[part] for view in views]) for part in parts[index]]
            return sums[0] if len(sums) == 1 else jnp.concatenate(sums, axis=axis)

        return piece

    store_halves(flag_ref[1], [into(ref) for ref in refs[-2:]], [joined(0), joined(1)])


def split_pair_kernel(flag_ref, *refs):
    def group(p):
        keep, got, more = refs[3 * p : 3 * p + 3]
        return lambda: add(keep[...], got[...], more[...])

    store_halves(flag_ref[2], [into(ref) for ref in refs[-2:]], [group(0), group(1)])


def last_kernel(keep_ref, got_ref, *outs, size):
    if size:
        body, tail = slice_parts(size)
        for part in (slice(0, body), slice(body, size)):
            outs[0][:, part] = add(keep_ref[:, part], got_ref[:, part])
    else:
        high, wide = outs[0].shape
        for index, out in enumerate(outs):
            part = slice(index * high, (index + 1) * high), slice(0, wide)
            out[...] = add(keep_ref[part], got_ref[part])


def prelude_kernel(place_ref, len_ref, step_ref, embed_ref, table_ref, info_ref, mod_ref, slab, sem, *, rows):
    slots = len_ref.shape[1]
    width = table_ref.shape[1]

    def image_of(at):
        first = at * rows
        end = begin = length = step = jnp.int32(0)
        for slot in range(slots):
            count = len_ref[0, slot]
            inside = jnp.logical_and(end <= first, first < end + count)
            begin = jnp.where(inside, end, begin)
            length = jnp.where(inside, count, length)
            step = jnp.where(inside, step_ref[0, slot], step)
            end = end + count
        return (first - begin) // rows, length, step

    place = place_ref[0]
    core = place % 2
    blocks = BIG // rows
    within, length, step = image_of(place)
    pair_within = image_of(place + 1 - 2 * core)[0]
    flags = (
        length > rows,
        jnp.where(core == 0, pair_within + 1 < blocks, pair_within + 3 < blocks),
        jnp.where(core == 0, within + 1 < blocks, within >= 1),
        within + 2 < blocks,
        core == 1,
    )
    for index, flag in enumerate(flags):
        info_ref[index] = flag.astype(jnp.int32)
    copy = pltpu.make_async_copy(embed_ref.at[pl.ds(pl.multiple_of(step // 8 * 8, 8), 8), :], slab, sem)
    copy.start()
    copy.wait()
    row = slab[pl.ds(step % 8, 1), :]
    for index in range(6):
        mod_ref[index : index + 1, :] = (
            row[:, index * width : (index + 1) * width] + table_ref[index : index + 1, :]
        )


class Slot:
    def __init__(self, hbm, ref, sems, out=False):
        self.hbm, self.ref, self.out = hbm, ref, out
        self.sent = False
        self.copies = []
        for i, rows in enumerate(row_chunks(ref.shape, ref.dtype)):
            pair = (hbm.at[rows], ref.at[rows])
            self.copies.append(pltpu.make_async_copy(*(pair[::-1] if out else pair), sems.at[i]))

    def start(self):
        self.sent = True
        for copy in self.copies:
            copy.start()

    send = start

    def wait(self):
        for copy in self.copies:
            copy.wait()


def row_chunks(shape, dtype):
    if len(shape) > 2:
        return [slice(i, i + 1) for i in range(shape[0])]
    size = shape[0] * shape[1] * jnp.dtype(dtype).itemsize
    count = max([n for n in (1, 2, 3, 4, 6) if shape[0] % (16 * n) == 0 and size >= n * 200_000] or [1])
    high = shape[0] // count
    return [slice(i * high, (i + 1) * high) for i in range(count)]


def call(kernel, inputs, outs, flags=None, scratch=(), raw=(), lazy=False, limit=60):
    anywhere = pl.BlockSpec(memory_space=pl.ANY)
    arrays, views = [], []
    for entry in inputs:
        array, part = entry if isinstance(entry, tuple) else (entry, None)
        arrays.append(array)
        views.append(part)

    def view_shape(array, part):
        if part is None:
            return array.shape
        if isinstance(part, slice):
            return (array.shape[0], part.stop - part.start)
        return array.shape[1:]

    in_shapes = [view_shape(array, part) for array, part in zip(arrays, views)]
    slots = [(shape, array.dtype) for shape, array in zip(in_shapes, arrays)] + list(outs)
    held = [i for i in range(len(arrays)) if i not in raw]
    held += [len(arrays) + i for i in range(len(outs)) if "out" not in raw]
    buffers = [pltpu.VMEM(*slots[i]) for i in held]
    sems = [pltpu.SemaphoreType.DMA((len(row_chunks(*slots[i])),)) for i in held]

    def managed(*refs):
        refs = list(refs)
        flag_refs = [refs.pop(0)] if flags is not None else []
        hbm, rest = refs[: len(slots)], refs[len(slots) :]
        own, rest = rest[: len(scratch)], rest[len(scratch) :]
        views_in = []
        for ref, part in zip(hbm, views):
            if isinstance(part, slice):
                ref = ref.at[:, part]
            elif part is not None:
                ref = ref.at[flag_refs[0][part]]
            views_in.append(ref)
        given = views_in + hbm[len(arrays) :]
        for n, i in enumerate(held):
            given[i] = Slot(given[i], rest[n], rest[len(held) + n], i >= len(arrays))
        slots_in = [slot for slot in given if isinstance(slot, Slot) and not slot.out]
        slots_out = [slot for slot in given if isinstance(slot, Slot) and slot.out]
        if not lazy:
            for slot in slots_in:
                slot.start()
            for slot in slots_in:
                slot.wait()
            kernel(*flag_refs, *[getattr(slot, "ref", slot) if isinstance(slot, Slot) else slot for slot in given], *own)
        else:
            kernel(*flag_refs, *given, *own)
        for slot in slots_out:
            if not slot.sent:
                slot.send()
        for slot in slots_out:
            slot.wait()

    return pl.pallas_call(
        managed,
        in_specs=([pl.BlockSpec(memory_space=pltpu.SMEM)] if flags is not None else []) + [anywhere] * len(arrays),
        out_specs=[anywhere] * len(outs),
        out_shape=[jax.ShapeDtypeStruct(shape, dtype) for shape, dtype in outs],
        scratch_shapes=[*scratch, *buffers, *sems],
        compiler_params=pltpu.CompilerParams(vmem_limit_bytes=limit * MIB),
        cost_estimate=pl.CostEstimate(flops=1000, bytes_accessed=1000, transcendentals=0),
    )(*([] if flags is None else [flags]), *arrays)


def prelude(place, image_len, timestep, time_embed, mod_table, rows):
    smem = pl.BlockSpec(memory_space=pltpu.SMEM)
    return pl.pallas_call(
        functools.partial(prelude_kernel, rows=rows),
        in_specs=[smem, smem, smem, pl.BlockSpec(memory_space=pl.ANY), pl.BlockSpec(memory_space=pltpu.VMEM)],
        out_specs=[smem, pl.BlockSpec(memory_space=pltpu.VMEM)],
        out_shape=[jax.ShapeDtypeStruct((5,), jnp.int32), jax.ShapeDtypeStruct(mod_table.shape, F32)],
        scratch_shapes=[pltpu.VMEM((8, time_embed.shape[1]), F32), pltpu.SemaphoreType.DMA],
        compiler_params=pltpu.CompilerParams(vmem_limit_bytes=60 * MIB),
    )(place.reshape(1), image_len, timestep, time_embed, mod_table)


def half_width(grads, count, joined):
    size = (sum(grad.shape[1] for grad in grads) if joined else grads[0].shape[1]) // count
    body, _ = slice_parts(size)
    return 2 * (count // 4 * body + 128) if joined else len(grads) * -(-count // 2 * size // 128) * 128


def halves(core, grads, count, joined):
    out = ((grads[0].shape[0], half_width(grads, count, joined)), BF)
    return call(functools.partial(halves_kernel, count=count, joined=joined), grads, [out] * 2, flags=core)


def split(flags, inputs, picked, parts, shape, axis=1):
    inputs = [(array, 0) if i < picked else array for i, array in enumerate(inputs)]
    return call(
        functools.partial(split_kernel, parts=parts, axis=axis),
        inputs,
        [(shape, BF), (shape, F32)],
        flags=jnp.stack(flags),
    )


def add_last(keep, got, size, shapes):
    return call(functools.partial(last_kernel, size=size), [keep, got], [(shape, F32) for shape in shapes])


def wide_grad(order, source, mode):
    rows, width = source[0].shape
    depth = source[2].shape[1]
    wide, number = (depth, 2) if mode == "rows" else (depth // 2, 4)
    return call(
        functools.partial(wide_grad_kernel, mode=mode),
        source,
        [((2, width // 4, wide), BF)] * number,
        flags=order,
        raw=(0, 1, 2, 3, "out"),
        scratch=[
            pltpu.VMEM((2 * rows, width), BF),
            pltpu.VMEM((2 * rows, depth), BF),
            pltpu.VMEM((width, 2 * rows), BF),
            pltpu.VMEM((2, width // 4, wide), BF),
            pltpu.SemaphoreType.DMA((4,)),
            pltpu.SemaphoreType.DMA((2,)),
        ],
    )


def tall_grad(order, acts, keep, got, size, mode):
    count = len(acts)
    rows, width = acts[0][0].shape
    wide = keep.shape[1]
    shape = (2, 4 * size, width // 4) if mode == "rows" else (2 * size * count, width)
    return call(
        functools.partial(tall_grad_kernel, count=count, mode=mode),
        [array for pair in acts for array in pair] + [keep, got],
        [(shape, BF)] * 2,
        flags=order,
        raw=(*range(2 * count + 2), "out"),
        scratch=[
            pltpu.VMEM((count, 2 * rows, width), BF),
            pltpu.VMEM((2 * rows, wide), BF),
            pltpu.VMEM((wide, 2 * rows), BF),
            pltpu.VMEM((2, *shape[-2:]), BF),
            pltpu.SemaphoreType.DMA((2 * count + 2,)),
            pltpu.SemaphoreType.DMA((2,)),
        ],
    )


def local(
    tokens,
    image_len,
    timestep,
    caption,
    time_embed,
    mod_table,
    w_qkv,
    w_out,
    cross_q,
    cross_kv,
    cross_out,
    w_up,
    w_down,
    cotangent,
):
    sp_count = lax.axis_size("sp")
    dp_count = lax.axis_size("dp")
    place = lax.axis_index("sp")
    row_place = lax.axis_index("dp")
    core = place % 2
    rows, width = tokens.shape[1:]
    factor = 1.0 / math.sqrt(width // HEADS)
    blocks = BIG // rows
    assert blocks == 4

    big, modulation = prelude(place, image_len, timestep, time_embed, mod_table, rows)
    shift_one, scale_one, gate_one, shift_two, scale_two, gate_two = [modulation[i] for i in range(6)]

    def tie(value, *before):
        return lax.optimization_barrier((value, *[array for array in before if array is not None]))[0]

    pairs = [(i, i ^ 1) for i in range(sp_count)]
    others = [(i, i + 1) for i in range(1, sp_count - 1, 2)] + [(i + 1, i) for i in range(1, sp_count - 1, 2)]
    ahead = [(i, i + 2) for i in range(sp_count - 2)]
    back = [(i + 2, i) for i in range(sp_count - 2)]

    def image_blocks(block, *before):
        from_back = lax.ppermute(block, "sp", ahead)
        from_ahead = lax.ppermute(block, "sp", back)
        from_ahead, from_back = tie(from_ahead, *before), tie(from_back, *before)
        send_pair = jnp.concatenate([jnp.where(big[1] == 1, from_ahead, from_back), block], axis=0)
        send_other = jnp.where(core == 1, from_back, from_ahead)
        both = lax.ppermute(send_pair, "sp", pairs)
        third = lax.ppermute(send_other, "sp", others)
        pair = both[block.shape[0] :]
        return (
            [
                both,
                jnp.where(big[2] == 1, pair, third),
                jnp.where(big[3] == 1, from_ahead, from_back),
            ],
            send_pair,
            send_other,
        )

    def swap(array):
        return lax.ppermute(array, "sp", pairs)

    token_blocks, *token_sends = image_blocks(tokens[0])

    def first_norm(block):
        return (normal(block.astype(F32))[0] * (1.0 + scale_one) + shift_one).astype(BF)

    first_in = first_norm(tokens[0])
    other_in = first_norm(jnp.concatenate([block[:rows] for block in token_blocks], axis=0))

    core_flag = core.reshape(1)
    chips = sp_count // 2
    square = dp_count == 4 and chips == 4

    def own_half(*grads, joined=True):
        if square:
            return halves(core_flag, grads, sp_count, joined)
        grads = [jnp.concatenate(grads, axis=1)] if joined else grads
        size = grads[0].shape[1] // sp_count
        even, odd = [
            jnp.concatenate(
                [g[:, i * size : (i + 1) * size] for g in grads for i in range(c, sp_count, 2)], axis=1
            )
            for c in (0, 1)
        ]
        return jnp.where(core == 0, even, odd), jnp.where(core == 0, odd, even)

    near, far = (place // 2) & 1, (place // 4) & 1
    row_bits = [row_place & 1, row_place >> 1]
    high = width // 4

    def to_row(array, bit):
        return lax.ppermute(array, "dp", [(i, i ^ (1 << bit)) for i in range(dp_count)])

    def to_chip(array, bit):
        return lax.ppermute(array, "sp", [(i, i ^ (2 << bit)) for i in range(sp_count)])

    def plain_sum(sources, size):
        finals = []
        for item, (x0, x1, g0, g1) in enumerate(sources):
            columns = slice(item * chips * size, (item + 1) * chips * size)
            part = (matmul_tn(x0, g0[:, columns]) + matmul_tn(x1, g1[:, columns])).astype(BF)
            part = part.reshape(dp_count, -1, chips, size).transpose(0, 2, 1, 3)
            bit = dp_count // 2
            while bit:
                mine = (row_place // bit) % 2
                part = part.reshape(2, bit, chips, -1, size)
                got = lax.ppermute(part[1 - mine], "dp", [(i, i ^ bit) for i in range(dp_count)])
                part = add(part[mine], got).astype(BF)
                bit //= 2
            part = part.reshape(chips, -1, size)
            bit = chips // 2
            while bit:
                mine = (place // 2 // bit) % 2
                part = part.reshape(2, bit, -1, size)
                got = lax.ppermute(part[1 - mine], "sp", [(i, i ^ (2 * bit)) for i in range(sp_count)])
                part = add(part[mine], got).astype(BF)
                bit //= 2
            finals.append(part[0].astype(F32))
        return finals

    def add_picked(pick, keep, got):
        return call(add_kernel, [(keep, 0), (got, 0)], [(keep.shape[1:], BF)], flags=pick.reshape(1))

    everything = slice(None)

    def cut_slices(size):
        body, tail = slice_parts(size)
        return [
            [
                (everything, slice(h * body, (h + 1) * body)),
                (everything, slice(2 * body + h * tail, 2 * body + (h + 1) * tail)),
            ]
            for h in (0, 1)
        ]

    def sum_wide(source, first, size):
        second = 1 - first
        mine = row_bits[first]
        order = jnp.stack(
            [((1 - mine if s < 2 else mine) << first) + ((s % 2) << second) for s in range(4)]
        )
        if size < 256:
            send, keep = tall_grad(order, [source[:2]], *source[2:], size, "rows")
        else:
            send, keep = wide_grad(order, source, "rows")
        yield send
        got = to_row(send, first)
        mine = row_bits[second]
        (send,) = add_picked(1 - mine, keep, got)
        yield send
        tall, wide = send.shape
        more = to_row(send, second)
        if size < 256:
            groups = [[(slice(h * tall // 2, (h + 1) * tall // 2),)] for h in (0, 1)]
            send, keep = split([mine, near], [keep, got, more], 2, groups, (tall // 2, wide), 0)
            yield send
            groups = [[(slice(h * tall // 4, (h + 1) * tall // 4),)] for h in (0, 1)]
            send, keep = split([far, far], [keep, to_chip(send, 0)], 0, groups, (tall // 4, wide), 0)
            yield send
            (final,) = add_last(keep, to_chip(send, 1), 0, [(size, wide)])
            yield final.T
        else:
            groups = [[(everything, slice(h * wide // 2, (h + 1) * wide // 2))] for h in (0, 1)]
            send, keep = split([mine, near], [keep, got, more], 2, groups, (tall, wide // 2))
            yield send
            shape = (tall, size // 128 * 128 + 128)
            send, keep = split([far, far], [keep, to_chip(send, 0)], 0, cut_slices(size), shape)
            yield send
            (final,) = add_last(keep, to_chip(send, 1), size, [(tall, size)])
            yield final

    def sum_both(source, size):
        order = jnp.stack([jnp.int32(i) for i in range(4)] + row_bits)
        outs = wide_grad(order, source, "both")
        yield outs
        got = [to_row(outs[0], 0), to_row(outs[2], 1)]
        sends = [
            *add_picked(1 - row_bits[1], outs[1], got[0]),
            *add_picked(1 - row_bits[0], outs[3], got[1]),
        ]
        yield sends
        shape = sends[0].shape
        send, keep = call(
            split_pair_kernel,
            [(outs[1], 0), (got[0], 0), to_row(sends[0], 1), (outs[3], 1), (got[1], 1), to_row(sends[1], 0)],
            [(shape, BF), (shape, F32)],
            flags=jnp.stack([row_bits[1], row_bits[0], near]),
        )
        yield send
        shape = (shape[0], size // 128 * 128 + 128)
        send, keep = split([far, far], [keep, to_chip(send, 0)], 0, cut_slices(size), shape)
        yield send
        (final,) = add_last(keep, to_chip(send, 1), size, [(high, size)])
        yield final

    def sum_chips_first(acts, keep, got, size):
        count = len(acts)
        order = jnp.stack([jnp.int32(i) for i in range(4)] + [near])
        send, keep = tall_grad(order, acts, keep, got, size, "chips")
        late = yield send
        groups = [
            [(slice((2 * k + h) * size, (2 * k + h + 1) * size),) for k in range(count)] for h in (0, 1)
        ]
        got = to_chip(send, 0)
        send, keep = split([far, far], [tie(keep, late), got], 0, groups, (count * size, width), 0)
        yield send
        groups = [
            [(everything, slice(i * high, (i + 1) * high)) for i in (h, h + 2)] for h in (0, 1)
        ]
        shape = (count * size, lanes(2 * high))
        send, keep = split([row_bits[0]] * 2, [keep, to_chip(send, 1)], 0, groups, shape)
        yield send
        groups = [[(everything, slice(h * high, (h + 1) * high))] for h in (0, 1)]
        shape = (count * size, lanes(high))
        send, keep = split([row_bits[1]] * 2, [keep, to_row(send, 0)], 0, groups, shape)
        yield send
        finals = add_last(keep, to_row(send, 1), 0, [(size, high)] * count)
        yield [final.T for final in finals]

    caption_rows = caption[0]
    live = caption_rows.shape[0]
    padded = -(-live // 128) * 128
    caption_pad = jnp.concatenate([caption_rows, jnp.zeros((padded - live, width), BF)], axis=0)
    text = matmul(caption_pad, cross_kv).astype(BF)
    grad_mlp = (gate_two * cotangent[0].astype(F32)).astype(BF)
    mlp_keep, mlp_send = own_half(grad_mlp, joined=False)
    mlp_got = swap(mlp_send)
    first_pair = swap(first_in)
    own = matmul(tie(first_in, *token_sends), w_qkv).astype(BF)
    far_qkv = matmul(other_in, w_qkv).astype(BF)
    block = ((rows, width), BF)
    stream = ((rows, width), F32)
    stats = ((rows, 128), F32)
    units = w_up.shape[1]
    tile = units // 4
    half = half_width([w_up], sp_count, True) if square else units
    (
        attended, logsum, attn_branch, cross_in, cross_queries, cross_mixed, stream_two, second_in,
        hidden, pre_keep, pre_send, mlp_branch, grad_second,
    ) = call(
        functools.partial(forward_kernel, factor=factor, live=live, count=sp_count if square else 0),
        [
            own, (tie(far_qkv, mlp_got, first_pair), slice(width, 3 * width)), tokens[0], modulation, text,
            w_out, cross_q, cross_out, grad_mlp, w_up, w_down,
        ],
        [
            block, stats, stream, block, block, block, stream, block,
            ((rows, units), BF), ((rows, half), BF), ((rows, half), BF), stream, stream,
        ],
        flags=big,
        raw=(9, 10),
        lazy=True,
        scratch=[
            pltpu.VMEM((3, width, tile), BF),
            pltpu.VMEM((3, tile, width), BF),
            pltpu.SemaphoreType.DMA((3, 4)),
        ]
        + [pltpu.VMEM((rows, tile), BF)] * 4,
        limit=62,
    )
    second_pair = swap(second_in)
    small_acts = [(acts, swap(acts)) for acts in (cross_mixed, cross_in, attended)]

    if not square:
        pre_keep, pre_send = own_half(pre_keep)
    hidden_pair, pre_got = swap(hidden), swap(pre_send)
    early = [pair for _, pair in small_acts]
    small_width = half_width([grad_mlp] * 3, sp_count, False) if square else 3 * width
    small_out = ((rows, small_width), BF)
    stream_three, grad_one, small_keep, small_send, grad_text, pack, stat, table = call(
        functools.partial(middle_grad_kernel, factor=factor, live=live, count=sp_count if square else 0),
        [
            tie(grad_second, second_pair, *early), stream_two, cotangent[0], mlp_branch, modulation, cross_out,
            cross_queries, text, cross_q, attn_branch, w_out, attended, logsum,
        ],
        [
            stream, stream, small_out, small_out, ((live, 2 * width), F32), ((rows + 16, width), BF), stats,
            (modulation.shape, F32),
        ],
        flags=core_flag,
        scratch=[pltpu.VMEM((rows, width), BF)] * 2 + [pltpu.VMEM((padded, width), F32)] * 2,
        lazy=True,
    )
    if not square:
        small_keep, small_send = own_half(*jnp.split(small_keep, 3, axis=1), joined=False)
    small_got = swap(small_send)
    slice_of = lambda weight: weight.shape[1] // sp_count
    down_source = (hidden, hidden_pair, mlp_keep, mlp_got)
    up_source = (second_in, second_pair, pre_keep, pre_got)
    send_down = send_up = send_small = None
    if square:
        small_sum = sum_chips_first(small_acts, tie(small_keep, pack), small_got, slice_of(w_out))
        send_small = next(small_sum)
        up_sum = sum_wide((tie(second_in, send_small), *up_source[1:]), 1, slice_of(w_up))
        send_up = next(up_sum)
        down_sum = sum_wide((tie(hidden, send_up), *down_source[1:]), 0, slice_of(w_down))
        send_down = next(down_sum)
    pack_blocks, *pack_sends = image_blocks(pack, send_down, send_up)
    (grad_queries,) = call(
        functools.partial(query_grad_kernel, factor=factor),
        [own, (far_qkv, slice(width, 3 * width)), tie(pack, *pack_sends), stat],
        [block],
        flags=big,
    )
    proj_out = ((rows, half_width([w_qkv], sp_count, True) if square else 3 * width), BF)
    grad_keys, grad_values, proj_keep, proj_send = call(
        functools.partial(key_grad_kernel, factor=factor, count=sp_count if square else 0),
        [own, (far_qkv, slice(0, width)), tie(pack, grad_queries), grad_queries, *pack_blocks],
        [block, block, proj_out, proj_out],
        flags=jnp.stack([big[0], core]),
        raw=tuple(range(4, 3 + blocks)),
        lazy=True,
        scratch=[
            pltpu.VMEM((2 * HEADS, blocks * rows), F32),
            pltpu.VMEM(((blocks - 1) * rows, width), BF),
            pltpu.VMEM((blocks - 1, 16, width), BF),
            pltpu.SemaphoreType.DMA((2 * blocks - 2,)),
        ],
    )
    if square:
        proj_send = tie(proj_send, small_sum.send(grad_keys))
    else:
        proj_keep, proj_send = own_half(*jnp.split(proj_keep, 3, axis=1))
    qkv_source = (first_in, first_pair, proj_keep, swap(proj_send))
    sent = []
    if square:
        sent = [next(up_sum)]
    grad_tokens, table = call(
        last_grad_kernel,
        [tie(grad_queries, *sent), grad_keys, grad_values, w_qkv, tokens[0], modulation, grad_one, table],
        [stream, (modulation.shape, F32)],
    )

    if square:
        qkv_sum = sum_both((tie(first_in, table), *qkv_source[1:]), slice_of(w_qkv))
        next(qkv_sum)
        sums = [down_sum, up_sum, small_sum, qkv_sum]
        final_down, final_up, final_small, final_qkv = [list(each)[-1] for each in sums]
    else:
        small = [(*acts, small_keep, small_got) for acts in small_acts]
        final_small = plain_sum(small, slice_of(w_out))
        (final_down,) = plain_sum([down_source], slice_of(w_down))
        (final_up,) = plain_sum([up_source], slice_of(w_up))
        (final_qkv,) = plain_sum([qkv_source], slice_of(w_qkv))
    table_rows = table.reshape(dp_count, sp_count, -1).transpose(1, 0, 2).reshape(sp_count, 3, -1)
    table_rows = table_rows.transpose(1, 0, 2).reshape(3, 2 * width)
    text_part = lax.psum_scatter(
        jnp.concatenate([grad_text, table_rows], axis=0), "sp", scatter_dimension=1, tiled=True
    )
    part_ckv = matmul_tn(caption_rows, text_part[:live].astype(BF)).astype(BF).reshape(dp_count, -1, text_part.shape[1])
    table_part = text_part[live:].reshape(dp_count, 1, -1)
    table_size = table_part.shape[2]
    table_part = jnp.pad(table_part, ((0, 0), (0, 15), (0, part_ckv.shape[2] - table_size))).astype(BF)
    tall = part_ckv.shape[1]
    both = jnp.concatenate([part_ckv, table_part], axis=1).reshape(dp_count * (tall + 16), -1)
    both = lax.psum_scatter(both, "dp", scatter_dimension=0, tiled=True).astype(F32)
    final_ckv, final_table = both[:tall], both[tall, :table_size]
    return (
        stream_three[None],
        grad_tokens[None],
        final_table,
        final_qkv,
        final_small[2],
        final_small[1],
        final_ckv,
        final_small[0],
        final_up,
        final_down,
    )


def solution(mesh):
    return jax.shard_map(
        local,
        mesh=mesh,
        in_specs=(
            P("dp", "sp", None),
            P("dp", None),
            P("dp", None),
            P("dp", None, None),
            P(),
            P(),
            P(),
            P(),
            P(),
            P(),
            P(),
            P(),
            P(),
            P("dp", "sp", None),
        ),
        out_specs=(
            P("dp", "sp", None),
            P("dp", "sp", None),
            P(("dp", "sp")),
            P("dp", "sp"),
            P("dp", "sp"),
            P("dp", "sp"),
            P("dp", "sp"),
            P("dp", "sp"),
            P("dp", "sp"),
            P("dp", "sp"),
        ),
        check_vma=False,
    )
```

```python
import functools
import math

import jax
import jax.numpy as jnp
from jax import lax
from jax.experimental import pallas as pl
from jax.experimental.pallas import tpu as pltpu
from jax.sharding import PartitionSpec as P

HEADS = 16
BIG = 1024
EPS = 1e-06
BIGNEG = -1e30
LOG2E = 1.4426950408889634
BF = jnp.bfloat16
F32 = jnp.float32
LARGE, CORE, NEAR, FAR, ROW, OTHER, ORDERS = 0, 4, 5, 6, 7, 9, 11
WIN = 256
COST_SCALE = 0.001
MIB = 1024 * 1024


def matmul(left, right):
    return jnp.dot(left, right, preferred_element_type=F32)


def matmul_tn(left, right):
    return lax.dot_general(left, right, (((0,), (0,)), ((), ())), preferred_element_type=F32)


def matmul_nt(left, right):
    return lax.dot_general(left, right, (((1,), (1,)), ((), ())), preferred_element_type=F32)


def head_window(head, width):
    size = width // HEADS
    low = head * size
    start = pl.multiple_of(jnp.minimum(low // 128 * 128, width - WIN), 128)
    lane = lax.broadcasted_iota(jnp.int32, (1, WIN), 1) + start
    return start, jnp.logical_and(lane >= low, lane < low + size)


def window(ref, start, offset=0):
    return ref[:, pl.ds(pl.multiple_of(start + offset, 128), WIN)]


def keep_columns(ref, start, mask, value):
    win = pl.ds(start, WIN)
    ref[:, win] = jnp.where(mask, value, ref[:, win])


def each_head(body, unroll=4):
    def step(head, carry):
        body(head)
        return carry

    lax.fori_loop(0, HEADS, step, 0, unroll=unroll)


def fetch(sems, *pairs):
    copies = [pltpu.make_async_copy(source, target, sems.at[i]) for i, (source, target) in enumerate(pairs)]
    for copy in copies:
        copy.start()
    return [copy.wait for copy in copies]


def attend(big, own_ref, far_ref, out_ref, lse_ref, factor):
    width = out_ref.shape[1]
    scale = factor * LOG2E

    def run(sides):
        def one_head(head):
            start, mask = head_window(head, width)
            query = window(own_ref, start) * mask.astype(BF)
            scores = [matmul_nt(query, window(side, start, key)) for side, key in sides]
            top = functools.reduce(jnp.maximum, [jnp.max(s, axis=1, keepdims=True) for s in scores])
            raised = [jnp.exp2((s - top) * scale) for s in scores]
            total = sum(jnp.sum(r, axis=1, keepdims=True) for r in raised)
            inverse = 1.0 / total
            result = sum(
                matmul((r * inverse).astype(BF), window(side, start, key + width))
                for r, (side, key) in zip(raised, sides)
            )
            keep_columns(out_ref, start, mask, result.astype(BF))
            lane = lax.broadcasted_iota(jnp.int32, (1, 128), 1)
            lse_ref[...] = jnp.where(lane == head, top * scale + jnp.log2(total), lse_ref[...])

        each_head(one_head)

    lse_ref[...] = jnp.zeros_like(lse_ref)

    @pl.when(big)
    def _():
        run([(own_ref, width), (far_ref, 0)])

    @pl.when(jnp.logical_not(big))
    def _():
        run([(own_ref, width)])


def query_grad_kernel(big_ref, own_ref, far_ref, pack_ref, stat_ref, out_ref, *, factor):
    rows, width = out_ref.shape
    scale = factor * LOG2E

    def run(sides):
        def one_head(head):
            start, mask = head_window(head, width)
            keep = mask.astype(BF)
            query = window(own_ref, start) * keep
            grad = window(pack_ref.at[0:rows, :], start) * keep
            lane = lax.broadcasted_iota(jnp.int32, (1, 128), 1)
            stat = stat_ref[...]
            lse = jnp.sum(jnp.where(lane == head, stat, 0.0), axis=1, keepdims=True)
            delta = jnp.sum(jnp.where(lane == head + HEADS, stat, 0.0), axis=1, keepdims=True)
            total = None
            for side, offset in sides:
                key = window(side, start, offset)
                prob = jnp.exp2(matmul_nt(query, key) * scale - lse)
                grad_prob = matmul_nt(grad, window(side, start, offset + width))
                grad_score = (prob * (grad_prob - delta)).astype(BF)
                part = matmul(grad_score, key)
                total = part if total is None else total + part
            keep_columns(out_ref, start, mask, (total * factor).astype(BF))

        each_head(one_head)

    @pl.when(big_ref[0] == 1)
    def _():
        run([(own_ref, width), (far_ref, 0)])

    @pl.when(big_ref[0] == 0)
    def _():
        run([(own_ref, width)])


def key_grad_kernel(flag_ref, own, far, pack, dq, *refs, factor, count):
    packs, (dk, dv, keep_out, send_out, stats, grads, tails, sems) = refs[:-8], refs[-8:]
    own_ref, far_ref, pack_ref, dq_ref = (slot.ref for slot in (own, far, pack, dq))
    dk_ref, dv_ref, keep_ref, send_ref = (slot.ref for slot in (dk, dv, keep_out, send_out))
    rows, width = dk_ref.shape
    pairs = [(other.at[rows : rows + 16, :], tails.at[i]) for i, other in enumerate(packs)]
    pairs += [(other.at[0:rows, :], grads.at[i * rows : (i + 1) * rows, :]) for i, other in enumerate(packs)]
    waits = fetch(sems, *pairs)
    for slot in (own, far, pack, dq):
        slot.start()
    for wait in waits:
        wait()
    for slot in (own, far, pack, dq):
        slot.wait()
    scale = factor * LOG2E
    blocks = 1 + len(packs)

    def unpack(block, both):
        both = both.astype(F32)
        joined = both[:8] + both[8:]
        for group in range(4):
            stats[8 * group : 8 * group + 8, block * rows : block * rows + rows] = joined[
                :, group * rows : group * rows + rows
            ]

    unpack(0, pack_ref[rows:, :])
    for block in range(len(packs)):
        unpack(block + 1, tails[block])

    def run(parts):
        def one_head(head):
            start, mask = head_window(head, width)
            keep = mask.astype(BF)
            key = window(own_ref, start, width) * keep
            value = window(own_ref, start, 2 * width) * keep
            lse = stats[pl.ds(head, 1), :]
            delta = stats[pl.ds(head + HEADS, 1), :]
            grad_key = grad_value = 0.0
            for query_ref, grad_ref, low, high in parts:
                query, grad = window(query_ref, start), window(grad_ref.at[0 : high - low, :], start)
                prob = jnp.exp2(matmul_nt(key, query) * scale - lse[:, low:high])
                grad_prob = matmul_nt(value, grad)
                grad_score = (prob * (grad_prob - delta[:, low:high])).astype(BF)
                grad_value = grad_value + matmul(prob.astype(BF), grad)
                grad_key = grad_key + matmul(grad_score, query)
            keep_columns(dk_ref, start, mask, (grad_key * factor).astype(BF))
            keep_columns(dv_ref, start, mask, grad_value.astype(BF))

        each_head(one_head)

    local = (own_ref, pack_ref, 0, rows)
    @pl.when(flag_ref[0] == 1)
    def _():
        run([local, (far_ref, grads, rows, blocks * rows)])

    @pl.when(flag_ref[0] == 0)
    def _():
        run([local])

    dk.send()
    dv.send()
    if count:
        for core in (0, 1):

            @pl.when(flag_ref[CORE] == core)
            def _(core=core):
                grads = [ref[...] for ref in (dq_ref, dk_ref, dv_ref)]
                keep_ref[...] = half_columns(grads, core, count, True, keep_ref.shape[1])
                send_ref[...] = half_columns(grads, 1 - core, count, True, send_ref.shape[1])

    else:
        for index, ref in enumerate((dq_ref, dk_ref, dv_ref)):
            keep_ref[:, index * width : (index + 1) * width] = ref[...]


def text_probs(query, key, scale, live, axis):
    scores = matmul_nt(query, key) if axis else matmul_nt(key, query)
    shape = (1, scores.shape[1]) if axis else (scores.shape[0], 1)
    scores = jnp.where(lax.broadcasted_iota(jnp.int32, shape, axis) < live, scores, BIGNEG)
    raised = jnp.exp2((scores - jnp.max(scores, axis=axis, keepdims=True)) * scale)
    return raised * (1.0 / jnp.sum(raised, axis=axis, keepdims=True))


def normal(stream):
    centred = stream - jnp.mean(stream, axis=-1, keepdims=True)
    spread = lax.rsqrt(jnp.mean(centred * centred, axis=-1, keepdims=True) + EPS)
    return centred * spread, spread


def norm_back(normed, spread, scale, grad):
    scaled = grad * (1.0 + scale)
    back = spread * (
        scaled
        - jnp.mean(scaled, axis=-1, keepdims=True)
        - normed * jnp.mean(scaled * normed, axis=-1, keepdims=True)
    )
    return back, jnp.sum(grad, axis=0, keepdims=True), jnp.sum(grad * normed, axis=0, keepdims=True)


def middle(tokens_ref, mod_ref, att_ref, weights, text_ref, refs, factor, live):
    branch_ref, cross_in_ref, queries_ref, mixed_ref, stream_ref, second_ref = refs
    width = tokens_ref.shape[1]
    out_w_ref, query_w_ref, cross_w_ref = weights
    branch = matmul(att_ref[...], out_w_ref[...])
    branch_ref[...] = branch
    stream = tokens_ref[...].astype(F32) + mod_ref[2:3, :] * branch
    stream_ref[...] = stream
    cross_in = stream.astype(BF)
    cross_in_ref[...] = cross_in
    queries_ref[...] = matmul(cross_in, query_w_ref[...]).astype(BF)

    def one_head(head):
        start, mask = head_window(head, width)
        query = window(queries_ref, start) * mask.astype(BF)
        probs = text_probs(query, window(text_ref, start), factor * LOG2E, live, 1)
        result = matmul(probs.astype(BF), window(text_ref, start, width))
        keep_columns(mixed_ref, start, mask, result.astype(BF))

    each_head(one_head, 8)
    stream = stream_ref[...] + matmul(mixed_ref[...], cross_w_ref[...])
    stream_ref[...] = stream
    second_ref[...] = (normal(stream)[0] * (1.0 + mod_ref[4:5, :]) + mod_ref[3:4, :]).astype(BF)


def forward_kernel(
    flag_ref, own, far, tokens, mod, text, out_w, query_w, cross_w, grad, cot, up_hbm, down_hbm,
    att, cross_in, mixed, second, hidden, keep, send,
    out, one, small_keep, small_send, text_grad, pack, stat, table,
    up, down, sems, kept0, kept1, lse, branch_ref, queries, stream, mlp_out, back,
    grad_mixed, grad_queries, text_key, text_value, *, factor, live, count
):
    kept = (kept0, kept1)
    own.start()
    far.start()
    own.wait()
    far.wait()
    late = (tokens, mod, text, out_w, query_w, cross_w, grad, cot)
    for slot in late:
        slot.start()
    tile = down.shape[1]
    tiles = down_hbm.shape[0] // tile
    ring = down.shape[0]

    def copies(step):
        half = tile // 2
        slot = step % ring
        pairs = []
        for part in (0, 1):
            rows = slice(part * up_hbm.shape[0] // 2, (part + 1) * up_hbm.shape[0] // 2)
            pairs.append((up_hbm.at[rows, step * tile : (step + 1) * tile], up.at[slot, rows, :]))
            rows = slice(part * half, (part + 1) * half)
            pairs.append((down_hbm.at[step * tile + part * half : step * tile + (part + 1) * half, :], down.at[slot, rows, :]))
        return [pltpu.make_async_copy(a, b, sems.at[slot, i]) for i, (a, b) in enumerate(pairs)]

    for step in range(min(ring, tiles)):
        for copy in copies(step):
            copy.start()
    attend(flag_ref[LARGE] == 1, own.ref, far.ref, att.ref, lse, factor)
    att.send()
    for slot in late:
        slot.wait()
    weights = (out_w.ref, query_w.ref, cross_w.ref)
    outs = (branch_ref, cross_in.ref, queries, mixed.ref, stream, second.ref)
    middle(tokens.ref, mod.ref, att.ref, weights, text.ref, outs, factor, live)
    for slot in (cross_in, mixed, second):
        slot.send()

    root = math.sqrt(2.0 / math.pi)

    def both(step):
        if step < tiles:
            for copy in copies(step):
                copy.wait()
            pre = matmul(second.ref[...], up[step % ring])
            slope = matmul_nt(grad.ref[...], down[step % ring])
        if step > 0:
            before = (step - 1) % ring
            ahead = hidden.ref[:, (step - 1) * tile : step * tile]
            behind = kept[(step - 1) % 2][...]
            branch = matmul(ahead, down[before])
            result = matmul_nt(behind, up[before])
        if step < tiles:
            square = pre * pre
            bend = jnp.tanh(pre * (root * 0.044715 * square + root))
            half = 0.5 * bend + 0.5
            rise = (3 * root * 0.044715 * square + root) * pre
            ahead = (pre * half).astype(BF)
            behind = (slope * (half + 0.5 * rise * (1.0 - bend * bend))).astype(BF)
            kept[step % 2][...] = behind
            hidden.ref[:, step * tile : (step + 1) * tile] = ahead
            if count:
                size = tile // 2
                body, tail = slice_parts(size)
                group = step % 2 * keep.ref.shape[1] // 2
                spots = (
                    (group + step // 2 * body, 0, body),
                    (group + tiles // 2 * body + step // 2 * tail, body, tail),
                )
                for core in (0, 1):

                    @pl.when(flag_ref[CORE] == core)
                    def _(core=core):
                        for at, low, wide in spots:
                            mine, other = core * size + low, (1 - core) * size + low
                            keep.ref[:, at : at + wide] = behind[:, mine : mine + wide]
                            send.ref[:, at : at + wide] = behind[:, other : other + wide]

            else:
                keep.ref[:, step * tile : (step + 1) * tile] = behind
        if step > 0:
            if step == 1:
                mlp_out[...] = branch
                back[...] = result
            else:
                mlp_out[...] += branch
                back[...] += result
            if step - 1 + ring < tiles:
                for copy in copies(step - 1 + ring):
                    copy.start()

    for step in range(tiles):
        both(step)
    hidden.send()
    keep.send()
    send.send()
    both(tiles)
    middle_grad(
        flag_ref, back, stream, cot.ref, mlp_out, mod.ref, branch_ref, att.ref, lse, queries, text.ref, weights,
        out, one, small_keep, small_send, text_grad, pack, stat, table,
        grad_mixed, grad_queries, text_key, text_value, factor, live, count,
    )


def middle_grad(
    flag_ref, second_grad_ref, stream_ref, cot_ref, mlp_ref, mod_ref, branch_ref, att_ref, lse_ref, queries_ref, text_ref,
    weights, out, one, keep, send, text_grad, pack, stat_out, table,
    mixed, grad_queries, text_key, text_value, factor, live, count
):
    out_w_ref, query_w_ref, cross_w_ref = weights
    one_ref, keep_ref, send_ref, text_grad_ref, pack_ref, stat_ref, table_ref = (
        slot.ref for slot in (one, keep, send, text_grad, pack, stat_out, table)
    )
    rows, width = cot_ref.shape
    cot = cot_ref[...].astype(F32)
    stream = stream_ref[...]
    mlp = mlp_ref[...]
    out.ref[...] = stream + mod_ref[5:6, :] * mlp
    out.send()
    normed, spread = normal(stream)
    back, shift, scale = norm_back(normed, spread, mod_ref[4:5, :], second_grad_ref[...])
    table_ref[...] = jnp.zeros_like(table_ref)
    table_ref[3:4, :] = shift
    table_ref[4:5, :] = scale
    table_ref[5:6, :] = jnp.sum(cot * mlp, axis=0, keepdims=True)
    grad_two = cot + back
    one_ref[...] = grad_two
    grad_cross = grad_two.astype(BF)
    mixed[...] = matmul_nt(grad_cross, cross_w_ref[...]).astype(BF)

    def one_head(head):
        start, mask = head_window(head, width)
        keep = mask.astype(BF)
        query = window(queries_ref, start)
        grad = window(mixed, start)
        key = window(text_ref, start) * keep
        probs = text_probs(query, key, factor * LOG2E, live, 0)
        grad_probs = matmul_nt(window(text_ref, start, width) * keep, grad)
        inner = jnp.sum(probs * grad_probs, axis=0, keepdims=True)
        grad_scores = (probs * (grad_probs - inner)).astype(BF)
        keep_columns(grad_queries, start, mask, (matmul_tn(grad_scores, key) * factor).astype(BF))
        keep_columns(text_key, start, mask, matmul(grad_scores, query) * factor)
        keep_columns(text_value, start, mask, matmul(probs.astype(BF), grad))

    each_head(one_head, 8)
    text_grad_ref[:, :width] = text_key[0:live, :]
    text_grad_ref[:, width:] = text_value[0:live, :]
    text_grad.send()
    grad_cq = grad_queries[...]
    grad_one = one_ref[...] + matmul_nt(grad_cq, query_w_ref[...])
    one_ref[...] = grad_one
    table_ref[2:3, :] = jnp.sum(grad_one * branch_ref[...], axis=0, keepdims=True)
    grad_attn = (mod_ref[2:3, :] * grad_one).astype(BF)
    grad_att = matmul_nt(grad_attn, out_w_ref[...]).astype(BF)
    pack_ref[0:rows, :] = grad_att

    product = grad_att.astype(F32) * att_ref[...].astype(F32)
    upper = product.astype(BF)
    lower = (product - upper.astype(F32)).astype(BF)
    size = width // HEADS
    column = lax.broadcasted_iota(jnp.int32, (width, 128), 0)
    low = (lax.broadcasted_iota(jnp.int32, (width, 128), 1) - HEADS) * size
    pick = jnp.logical_and(column >= low, column < low + size).astype(BF)
    stat = lse_ref[...] + matmul(upper, pick) + matmul(lower, pick)
    stat_ref[...] = stat
    turned = stat.T
    upper = [turned[8 * g : 8 * g + 8, :].astype(BF).astype(F32) for g in range(4)]
    lower = [turned[8 * g : 8 * g + 8, :] - part for g, part in enumerate(upper)]
    both = [jnp.concatenate(pair, axis=0) for pair in zip(upper, lower)]
    pack_ref[rows : rows + 16, :] = side_by_side(both, width).astype(BF)
    for slot in (pack, stat_out, one, table):
        slot.send()

    if count:
        for core in (0, 1):

            @pl.when(flag_ref[CORE] == core)
            def _(core=core):
                grads = [grad_cross, grad_cq, grad_attn]
                keep_ref[...] = half_columns(grads, core, count, False, keep_ref.shape[1])
                send_ref[...] = half_columns(grads, 1 - core, count, False, send_ref.shape[1])

    else:
        for index, grad in enumerate((grad_cross, grad_cq, grad_attn)):
            keep_ref[:, index * width : (index + 1) * width] = grad


def last_grad_kernel(
    dq_ref, dk_ref, dv_ref, weight_ref, tokens_ref, mod_ref, one_ref, table_in_ref, out_ref, table_ref
):
    width = tokens_ref.shape[1]
    grad = sum(
        matmul_nt(ref[...], weight_ref[:, part * width : (part + 1) * width])
        for part, ref in enumerate((dq_ref, dk_ref, dv_ref))
    )
    normed, spread = normal(tokens_ref[...].astype(F32))
    back, shift, scale = norm_back(normed, spread, mod_ref[1:2, :], grad)
    out_ref[...] = one_ref[...] + back
    table_ref[...] = table_in_ref[...]
    table_ref[0:1, :] = shift
    table_ref[1:2, :] = scale


def side_by_side(pieces, width):
    missing = width - sum(piece.shape[1] for piece in pieces)
    if missing:
        pieces = [*pieces, jnp.zeros((pieces[0].shape[0], missing), pieces[0].dtype)]
    return pieces[0] if len(pieces) == 1 else jnp.concatenate(pieces, axis=1)


def lanes(width):
    return -(-width // 128) * 128


def slice_parts(size):
    return size // 128 * 128, size % 128


def half_columns(grads, core, count, joined, wide):
    if not joined:
        picked = []
        for grad in grads:
            size = grad.shape[1] // count
            low = [(2 * chip + core) * size for chip in (*range(0, count // 2, 2), *range(1, count // 2, 2))]
            picked.append(
                side_by_side([grad[:, at : at + size] for at in low], wide // len(grads))
            )
        return side_by_side(picked, wide)
    grad = grads[0] if len(grads) == 1 else jnp.concatenate(grads, axis=1)
    size = grad.shape[1] // count
    body, _ = slice_parts(size)
    picked = []
    for parity in (0, 1):
        low = [(2 * chip + core) * size for chip in range(parity, count // 2, 2)]
        picked += [grad[:, at : at + body] for at in low]
        picked.append(side_by_side([grad[:, at + body : at + size] for at in low], 128))
    return side_by_side(picked, wide)


def halves_kernel(core_ref, *refs, count, joined):
    keep_ref, send_ref = refs[-2:]
    for core in (0, 1):

        @pl.when(core_ref[CORE] == core)
        def _(core=core):
            grads = [ref[...] for ref in refs[:-2]]
            keep_ref[...] = half_columns(grads, core, count, joined, keep_ref.shape[1])
            send_ref[...] = half_columns(grads, 1 - core, count, joined, send_ref.shape[1])


def store_halves(flag, stores, pieces):
    for value in (0, 1):

        @pl.when(flag == value)
        def _(value=value):
            for store, piece in zip(stores, (pieces[1 - value], pieces[value])):
                store(piece())


def into(ref):
    def store(value):
        ref[:, : value.shape[1]] = value.astype(ref.dtype)

    return store


def add(*terms):
    return sum(term.astype(F32) for term in terms)


def sending(buffers, sems, out):
    state = {"count": 0}

    def wait(slot):
        pltpu.make_async_copy(buffers.at[slot], out, sems.at[slot]).wait()

    def put(pieces, targets):
        slot = state["count"] % 2
        if state["count"] >= 2:
            wait(slot)
        at = 0
        for piece in pieces:
            buffers[slot, at : at + piece.shape[0], : piece.shape[1]] = piece
            at += piece.shape[0]
        for condition, target in targets:
            copy = pltpu.make_async_copy(buffers.at[slot], target, sems.at[slot])
            if condition is None:
                copy.start()
            else:
                pl.when(condition)(copy.start)
        state["count"] += 1

    def done():
        for slot in range(min(2, state["count"])):
            wait(slot)

    return put, done


def wide_grad_kernel(order_ref, x0_hbm, x1_hbm, g0_hbm, g1_hbm, *refs, mode, first):
    number = 2 if mode == "rows" else 4
    outs, (x_ref, g_ref, turned, buffers, sems, out_sems) = refs[:number], refs[number:]
    rows, width = x0_hbm.shape
    waits = fetch(
        sems,
        (x0_hbm, x_ref.at[0:rows, :]),
        (x1_hbm, x_ref.at[rows : 2 * rows, :]),
        (g0_hbm, g_ref.at[0:rows, :]),
        (g1_hbm, g_ref.at[rows : 2 * rows, :]),
    )
    for part in (0, 1):
        waits[part]()
        for low in range(0, width, 128):
            turned[low : low + 128, part * rows : (part + 1) * rows] = x_ref[
                part * rows : (part + 1) * rows, low : low + 128
            ].T
    waits[2]()
    waits[3]()
    tall = width // 4
    put, done = sending(buffers, out_sems, outs[0].at[0])
    half = g_ref.shape[1] // 2
    for step in range(4):
        here = pl.ds(pl.multiple_of((order_ref[ORDERS + 4 * first + step] if mode == "rows" else step) * tall, 16), tall)
        if mode == "rows":
            total = matmul(turned[here, :], g_ref[...]).astype(BF)
            put([total], [(None, outs[step // 2].at[step % 2])])
        else:
            for p in (0, 1):
                total = matmul(turned[here, :], g_ref[:, p * half : (p + 1) * half]).astype(BF)
                place, second = (step >> p) & 1, (step >> (1 - p)) & 1
                mine = order_ref[ROW + p]
                put(
                    [total],
                    [(mine != place, outs[2 * p].at[second]), (mine == place, outs[2 * p + 1].at[second])],
                )
    done()


def tall_grad_kernel(order_ref, *refs, count, mode, first):
    sources, g0_hbm, g1_hbm = refs[: 2 * count], refs[2 * count], refs[2 * count + 1]
    outs, (x_ref, g_ref, turned, buffers, sems, out_sems) = refs[2 * count + 2 : 2 * count + 4], refs[2 * count + 4 :]
    rows, width = sources[0].shape
    pairs = [(g0_hbm, g_ref.at[0:rows, :]), (g1_hbm, g_ref.at[rows : 2 * rows, :])]
    for i, source in enumerate(sources):
        pairs.append((source, x_ref.at[i // 2, i % 2 * rows : (i % 2 + 1) * rows, :]))
    waits = fetch(sems, *pairs)
    wide = g_ref.shape[1]
    for part in (0, 1):
        waits[part]()
        for low in range(0, wide, 128):
            turned[low : low + 128, part * rows : (part + 1) * rows] = g_ref[
                part * rows : (part + 1) * rows, low : low + 128
            ].T
    for wait in waits[2:]:
        wait()
    if mode == "rows":
        high, tall = outs[0].shape[1:]
        put, done = sending(buffers, out_sems, outs[0].at[0])
        for step in range(4):
            here = pl.ds(pl.multiple_of(order_ref[ORDERS + 4 * first + step] * tall, 128), tall)
            total = matmul(turned[0:high, :], x_ref[0, :, here]).astype(BF)
            put([total], [(None, outs[step // 2].at[step % 2])])
    else:
        high = outs[0].shape[0] // count
        put, done = sending(buffers, out_sems, outs[0])
        for p in (0, 1):
            total = [
                matmul(turned[pl.ds(k * (wide // count) + p * high, high), :], x_ref[k]).astype(BF)
                for k in range(count)
            ]
            put(total, [(order_ref[NEAR] != p, outs[0]), (order_ref[NEAR] == p, outs[1])])
    done()


def add_kernel(flag_ref, *refs):
    refs[-1][...] = add(*[ref[...] for ref in refs[:-1]]).astype(BF)


def split_kernel(flag_ref, *refs, parts, axis, bit):
    views = refs[:-2]

    def joined(index):
        def piece():
            sums = [add(*[view[part] for view in views]) for part in parts[index]]
            return sums[0] if len(sums) == 1 else jnp.concatenate(sums, axis=axis)

        return piece

    store_halves(flag_ref[bit], [into(ref) for ref in refs[-2:]], [joined(0), joined(1)])


def split_pair_kernel(flag_ref, *refs):
    def group(p):
        keep, got, more = refs[3 * p : 3 * p + 3]
        return lambda: add(keep[...], got[...], more[...])

    store_halves(flag_ref[NEAR], [into(ref) for ref in refs[-2:]], [group(0), group(1)])


def last_kernel(keep_ref, got_ref, *outs, size):
    if size:
        body, tail = slice_parts(size)
        for part in (slice(0, body), slice(body, size)):
            outs[0][:, part] = add(keep_ref[:, part], got_ref[:, part])
    else:
        high, wide = outs[0].shape
        for index, out in enumerate(outs):
            part = slice(index * high, (index + 1) * high), slice(0, wide)
            out[...] = add(keep_ref[part], got_ref[part])


def prelude_kernel(place_ref, row_ref, len_ref, step_ref, embed_ref, table_ref, info_ref, mod_ref, slab, sem, *, rows):
    slots = len_ref.shape[1]
    width = table_ref.shape[1]

    def image_of(at):
        first = at * rows
        end = begin = length = step = jnp.int32(0)
        for slot in range(slots):
            count = len_ref[0, slot]
            inside = jnp.logical_and(end <= first, first < end + count)
            begin = jnp.where(inside, end, begin)
            length = jnp.where(inside, count, length)
            step = jnp.where(inside, step_ref[0, slot], step)
            end = end + count
        return (first - begin) // rows, length, step

    place = place_ref[0]
    core = place % 2
    blocks = BIG // rows
    within, length, step = image_of(place)
    pair_within = image_of(place + 1 - 2 * core)[0]
    flags = (
        length > rows,
        jnp.where(core == 0, pair_within + 1 < blocks, pair_within + 3 < blocks),
        jnp.where(core == 0, within + 1 < blocks, within >= 1),
        within + 2 < blocks,
        core == 1,
    )
    bits = [(place // 2) & 1, (place // 4) & 1, row_ref[0] & 1, (row_ref[0] >> 1) & 1]
    values = [flag.astype(jnp.int32) for flag in flags] + bits + [1 - bits[2], 1 - bits[3]]
    for first in (0, 1):
        mine = bits[2 + first]
        values += [((1 - mine if s < 2 else mine) << first) + ((s % 2) << (1 - first)) for s in range(4)]
    for index, value in enumerate(values):
        info_ref[index] = value
    copy = pltpu.make_async_copy(embed_ref.at[pl.ds(pl.multiple_of(step // 8 * 8, 8), 8), :], slab, sem)
    copy.start()
    copy.wait()
    row = slab[pl.ds(step % 8, 1), :]
    for index in range(6):
        mod_ref[index : index + 1, :] = (
            row[:, index * width : (index + 1) * width] + table_ref[index : index + 1, :]
        )


class Slot:
    def __init__(self, hbm, ref, sems, out=False):
        self.hbm, self.ref, self.out = hbm, ref, out
        self.sent = False
        self.copies = []
        for i, rows in enumerate(row_chunks(ref.shape, ref.dtype)):
            pair = (hbm.at[rows], ref.at[rows])
            self.copies.append(pltpu.make_async_copy(*(pair[::-1] if out else pair), sems.at[i]))

    def start(self):
        self.sent = True
        for copy in self.copies:
            copy.start()

    send = start

    def wait(self):
        for copy in self.copies:
            copy.wait()


def row_chunks(shape, dtype):
    if len(shape) > 2:
        return [slice(i, i + 1) for i in range(shape[0])]
    size = shape[0] * shape[1] * jnp.dtype(dtype).itemsize
    count = max([n for n in (1, 2, 3, 4, 6) if shape[0] % (16 * n) == 0 and size >= n * 200_000] or [1])
    high = shape[0] // count
    return [slice(i * high, (i + 1) * high) for i in range(count)]


def call(kernel, inputs, outs, flags=None, scratch=(), raw=(), lazy=False, limit=60):
    anywhere = pl.BlockSpec(memory_space=pl.ANY)
    arrays, views = [], []
    for entry in inputs:
        array, part = entry if isinstance(entry, tuple) else (entry, None)
        arrays.append(array)
        views.append(part)

    def view_shape(array, part):
        if part is None:
            return array.shape
        if isinstance(part, slice):
            return (array.shape[0], part.stop - part.start)
        return array.shape[1:]

    in_shapes = [view_shape(array, part) for array, part in zip(arrays, views)]
    slots = [(shape, array.dtype) for shape, array in zip(in_shapes, arrays)] + list(outs)
    held = [i for i in range(len(arrays)) if i not in raw]
    held += [len(arrays) + i for i in range(len(outs)) if "out" not in raw]
    buffers = [pltpu.VMEM(*slots[i]) for i in held]
    sems = [pltpu.SemaphoreType.DMA((len(row_chunks(*slots[i])),)) for i in held]

    def managed(*refs):
        refs = list(refs)
        flag_refs = [refs.pop(0)] if flags is not None else []
        hbm, rest = refs[: len(slots)], refs[len(slots) :]
        own, rest = rest[: len(scratch)], rest[len(scratch) :]
        views_in = []
        for ref, part in zip(hbm, views):
            if isinstance(part, slice):
                ref = ref.at[:, part]
            elif part is not None:
                ref = ref.at[flag_refs[0][part]]
            views_in.append(ref)
        given = views_in + hbm[len(arrays) :]
        for n, i in enumerate(held):
            given[i] = Slot(given[i], rest[n], rest[len(held) + n], i >= len(arrays))
        slots_in = [slot for slot in given if isinstance(slot, Slot) and not slot.out]
        slots_out = [slot for slot in given if isinstance(slot, Slot) and slot.out]
        if not lazy:
            for slot in slots_in:
                slot.start()
            for slot in slots_in:
                slot.wait()
            kernel(*flag_refs, *[getattr(slot, "ref", slot) if isinstance(slot, Slot) else slot for slot in given], *own)
        else:
            kernel(*flag_refs, *given, *own)
        for slot in slots_out:
            if not slot.sent:
                slot.send()
        for slot in slots_out:
            slot.wait()

    return pl.pallas_call(
        managed,
        in_specs=([pl.BlockSpec(memory_space=pltpu.SMEM)] if flags is not None else []) + [anywhere] * len(arrays),
        out_specs=[anywhere] * len(outs),
        out_shape=[jax.ShapeDtypeStruct(shape, dtype) for shape, dtype in outs],
        scratch_shapes=[*scratch, *buffers, *sems],
        compiler_params=pltpu.CompilerParams(vmem_limit_bytes=limit * MIB),
        cost_estimate=pl.CostEstimate(flops=1000, bytes_accessed=1000, transcendentals=0),
    )(*([] if flags is None else [flags]), *arrays)


def prelude(place, row_place, image_len, timestep, time_embed, mod_table, rows):
    smem = pl.BlockSpec(memory_space=pltpu.SMEM)
    return pl.pallas_call(
        functools.partial(prelude_kernel, rows=rows),
        in_specs=[smem] * 4 + [pl.BlockSpec(memory_space=pl.ANY), pl.BlockSpec(memory_space=pltpu.VMEM)],
        out_specs=[smem, pl.BlockSpec(memory_space=pltpu.VMEM)],
        out_shape=[jax.ShapeDtypeStruct((ORDERS + 8,), jnp.int32), jax.ShapeDtypeStruct(mod_table.shape, F32)],
        scratch_shapes=[pltpu.VMEM((8, time_embed.shape[1]), F32), pltpu.SemaphoreType.DMA],
        compiler_params=pltpu.CompilerParams(vmem_limit_bytes=60 * MIB),
    )(place.reshape(1), row_place.reshape(1), image_len, timestep, time_embed, mod_table)


def half_width(grads, count, joined):
    size = (sum(grad.shape[1] for grad in grads) if joined else grads[0].shape[1]) // count
    body, _ = slice_parts(size)
    return 2 * (count // 4 * body + 128) if joined else len(grads) * -(-count // 2 * size // 128) * 128


def halves(core, grads, count, joined):
    out = ((grads[0].shape[0], half_width(grads, count, joined)), BF)
    return call(functools.partial(halves_kernel, count=count, joined=joined), grads, [out] * 2, flags=core)


def split(flags, bit, inputs, parts, shape, axis=1):
    return call(
        functools.partial(split_kernel, parts=parts, axis=axis, bit=bit),
        inputs,
        [(shape, BF), (shape, F32)],
        flags=flags,
    )


def add_last(keep, got, size, shapes):
    return call(functools.partial(last_kernel, size=size), [keep, got], [(shape, F32) for shape in shapes])


def wide_grad(order, source, mode, first=0):
    rows, width = source[0].shape
    depth = source[2].shape[1]
    wide, number = (depth, 2) if mode == "rows" else (depth // 2, 4)
    return call(
        functools.partial(wide_grad_kernel, mode=mode, first=first),
        source,
        [((2, width // 4, wide), BF)] * number,
        flags=order,
        raw=(0, 1, 2, 3, "out"),
        scratch=[
            pltpu.VMEM((2 * rows, width), BF),
            pltpu.VMEM((2 * rows, depth), BF),
            pltpu.VMEM((width, 2 * rows), BF),
            pltpu.VMEM((2, width // 4, wide), BF),
            pltpu.SemaphoreType.DMA((4,)),
            pltpu.SemaphoreType.DMA((2,)),
        ],
    )


def tall_grad(order, acts, keep, got, size, mode, first=0):
    count = len(acts)
    rows, width = acts[0][0].shape
    wide = keep.shape[1]
    shape = (2, 4 * size, width // 4) if mode == "rows" else (2 * size * count, width)
    return call(
        functools.partial(tall_grad_kernel, count=count, mode=mode, first=first),
        [array for pair in acts for array in pair] + [keep, got],
        [(shape, BF)] * 2,
        flags=order,
        raw=(*range(2 * count + 2), "out"),
        scratch=[
            pltpu.VMEM((count, 2 * rows, width), BF),
            pltpu.VMEM((2 * rows, wide), BF),
            pltpu.VMEM((wide, 2 * rows), BF),
            pltpu.VMEM((2, *shape[-2:]), BF),
            pltpu.SemaphoreType.DMA((2 * count + 2,)),
            pltpu.SemaphoreType.DMA((2,)),
        ],
    )


def local(
    tokens,
    image_len,
    timestep,
    caption,
    time_embed,
    mod_table,
    w_qkv,
    w_out,
    cross_q,
    cross_kv,
    cross_out,
    w_up,
    w_down,
    cotangent,
):
    sp_count = lax.axis_size("sp")
    dp_count = lax.axis_size("dp")
    place = lax.axis_index("sp")
    row_place = lax.axis_index("dp")
    core = place % 2
    rows, width = tokens.shape[1:]
    factor = 1.0 / math.sqrt(width // HEADS)
    blocks = BIG // rows
    assert blocks == 4

    big, modulation = prelude(place, row_place, image_len, timestep, time_embed, mod_table, rows)
    shift_one, scale_one, gate_one, shift_two, scale_two, gate_two = [modulation[i] for i in range(6)]

    def tie(value, *before):
        return lax.optimization_barrier((value, *[array for array in before if array is not None]))[0]

    pairs = [(i, i ^ 1) for i in range(sp_count)]
    others = [(i, i + 1) for i in range(1, sp_count - 1, 2)] + [(i + 1, i) for i in range(1, sp_count - 1, 2)]
    ahead = [(i, i + 2) for i in range(sp_count - 2)]
    back = [(i + 2, i) for i in range(sp_count - 2)]

    def image_blocks(block, *before):
        from_back = lax.ppermute(block, "sp", ahead)
        from_ahead = lax.ppermute(block, "sp", back)
        from_ahead, from_back = tie(from_ahead, *before), tie(from_back, *before)
        send_pair = jnp.concatenate([jnp.where(big[1] == 1, from_ahead, from_back), block], axis=0)
        send_other = jnp.where(core == 1, from_back, from_ahead)
        both = lax.ppermute(send_pair, "sp", pairs)
        third = lax.ppermute(send_other, "sp", others)
        pair = both[block.shape[0] :]
        return (
            [
                both,
                jnp.where(big[2] == 1, pair, third),
                jnp.where(big[3] == 1, from_ahead, from_back),
            ],
            send_pair,
            send_other,
        )

    def swap(array):
        return lax.ppermute(array, "sp", pairs)

    token_blocks, *token_sends = image_blocks(tokens[0])

    def first_norm(block):
        return (normal(block.astype(F32))[0] * (1.0 + scale_one) + shift_one).astype(BF)

    first_in = first_norm(tokens[0])
    other_in = first_norm(jnp.concatenate([block[:rows] for block in token_blocks], axis=0))

    chips = sp_count // 2
    square = dp_count == 4 and chips == 4

    def own_half(*grads, joined=True):
        if square:
            return halves(big, grads, sp_count, joined)
        grads = [jnp.concatenate(grads, axis=1)] if joined else grads
        size = grads[0].shape[1] // sp_count
        even, odd = [
            jnp.concatenate(
                [g[:, i * size : (i + 1) * size] for g in grads for i in range(c, sp_count, 2)], axis=1
            )
            for c in (0, 1)
        ]
        return jnp.where(core == 0, even, odd), jnp.where(core == 0, odd, even)

    high = width // 4

    def to_row(array, bit):
        return lax.ppermute(array, "dp", [(i, i ^ (1 << bit)) for i in range(dp_count)])

    def to_chip(array, bit):
        return lax.ppermute(array, "sp", [(i, i ^ (2 << bit)) for i in range(sp_count)])

    def plain_sum(sources, size):
        finals = []
        for item, (x0, x1, g0, g1) in enumerate(sources):
            columns = slice(item * chips * size, (item + 1) * chips * size)
            part = (matmul_tn(x0, g0[:, columns]) + matmul_tn(x1, g1[:, columns])).astype(BF)
            part = part.reshape(dp_count, -1, chips, size).transpose(0, 2, 1, 3)
            bit = dp_count // 2
            while bit:
                mine = (row_place // bit) % 2
                part = part.reshape(2, bit, chips, -1, size)
                got = lax.ppermute(part[1 - mine], "dp", [(i, i ^ bit) for i in range(dp_count)])
                part = add(part[mine], got).astype(BF)
                bit //= 2
            part = part.reshape(chips, -1, size)
            bit = chips // 2
            while bit:
                mine = (place // 2 // bit) % 2
                part = part.reshape(2, bit, -1, size)
                got = lax.ppermute(part[1 - mine], "sp", [(i, i ^ (2 * bit)) for i in range(sp_count)])
                part = add(part[mine], got).astype(BF)
                bit //= 2
            finals.append(part[0].astype(F32))
        return finals

    def add_picked(keep, got, flag):
        return call(add_kernel, [(keep, flag), (got, flag)], [(keep.shape[1:], BF)], flags=big)

    everything = slice(None)

    def cut_slices(size):
        body, tail = slice_parts(size)
        return [
            [
                (everything, slice(h * body, (h + 1) * body)),
                (everything, slice(2 * body + h * tail, 2 * body + (h + 1) * tail)),
            ]
            for h in (0, 1)
        ]

    def sum_wide(source, first, size):
        second = 1 - first
        if size < 256:
            send, keep = tall_grad(big, [source[:2]], *source[2:], size, "rows", first)
        else:
            send, keep = wide_grad(big, source, "rows", first)
        late = yield send
        got = to_row(send, first)
        (send,) = add_picked(tie(keep, late), got, OTHER + second)
        late = yield send
        tall, wide = send.shape
        more = to_row(send, second)
        inputs = [(tie(keep, late), ROW + second), (got, ROW + second), more]
        if size < 256:
            groups = [[(slice(h * tall // 2, (h + 1) * tall // 2),)] for h in (0, 1)]
            send, keep = split(big, NEAR, inputs, groups, (tall // 2, wide), 0)
            late = yield send
            groups = [[(slice(h * tall // 4, (h + 1) * tall // 4),)] for h in (0, 1)]
            send, keep = split(big, FAR, [tie(keep, late), to_chip(send, 0)], groups, (tall // 4, wide), 0)
            late = yield send
            (final,) = add_last(tie(keep, late), to_chip(send, 1), 0, [(size, wide)])
            yield final.T
        else:
            groups = [[(everything, slice(h * wide // 2, (h + 1) * wide // 2))] for h in (0, 1)]
            send, keep = split(big, NEAR, inputs, groups, (tall, wide // 2))
            late = yield send
            shape = (tall, size // 128 * 128 + 128)
            send, keep = split(big, FAR, [tie(keep, late), to_chip(send, 0)], cut_slices(size), shape)
            late = yield send
            (final,) = add_last(tie(keep, late), to_chip(send, 1), size, [(tall, size)])
            yield final

    def sum_both(source, size):
        outs = wide_grad(big, source, "both")
        late = yield outs[0]
        got = [to_row(outs[0], 0), to_row(outs[2], 1)]
        sends = [
            *add_picked(tie(outs[1], late), got[0], OTHER + 1),
            *add_picked(tie(outs[3], late), got[1], OTHER),
        ]
        late = yield sends[1]
        shape = sends[0].shape
        more = [to_row(sends[0], 1), to_row(sends[1], 0)]
        send, keep = call(
            split_pair_kernel,
            [
                (tie(outs[1], late), ROW + 1), (got[0], ROW + 1), more[0],
                (outs[3], ROW), (got[1], ROW), more[1],
            ],
            [(shape, BF), (shape, F32)],
            flags=big,
        )
        late = yield send
        shape = (shape[0], size // 128 * 128 + 128)
        send, keep = split(big, FAR, [tie(keep, late), to_chip(send, 0)], cut_slices(size), shape)
        late = yield send
        (final,) = add_last(tie(keep, late), to_chip(send, 1), size, [(high, size)])
        yield final

    def sum_chips_first(acts, keep, got, size):
        count = len(acts)
        send, keep = tall_grad(big, acts, keep, got, size, "chips")
        late = yield send
        groups = [
            [(slice((2 * k + h) * size, (2 * k + h + 1) * size),) for k in range(count)] for h in (0, 1)
        ]
        inputs = [tie(keep, late), to_chip(send, 0)]
        send, keep = split(big, FAR, inputs, groups, (count * size, width), 0)
        late = yield send
        groups = [
            [(everything, slice(i * high, (i + 1) * high)) for i in (h, h + 2)] for h in (0, 1)
        ]
        shape = (count * size, lanes(2 * high))
        send, keep = split(big, ROW, [tie(keep, late), to_chip(send, 1)], groups, shape)
        late = yield send
        groups = [[(everything, slice(h * high, (h + 1) * high))] for h in (0, 1)]
        shape = (count * size, lanes(high))
        send, keep = split(big, ROW + 1, [tie(keep, late), to_row(send, 0)], groups, shape)
        late = yield send
        finals = add_last(tie(keep, late), to_row(send, 1), 0, [(size, high)] * count)
        yield [final.T for final in finals]

    caption_rows = caption[0]
    live = caption_rows.shape[0]
    padded = -(-live // 128) * 128
    caption_pad = jnp.concatenate([caption_rows, jnp.zeros((padded - live, width), BF)], axis=0)
    text = matmul(caption_pad, cross_kv).astype(BF)
    grad_mlp = (gate_two * cotangent[0].astype(F32)).astype(BF)
    mlp_keep, mlp_send = own_half(grad_mlp, joined=False)
    mlp_got = swap(mlp_send)
    first_pair = swap(first_in)
    own = matmul(tie(first_in, *token_sends), w_qkv).astype(BF)
    far_qkv = matmul(other_in, w_qkv).astype(BF)
    block = ((rows, width), BF)
    stream = ((rows, width), F32)
    stats = ((rows, 128), F32)
    units = w_up.shape[1]
    tile = units // 4
    half = half_width([w_up], sp_count, True) if square else units
    small_width = half_width([grad_mlp] * 3, sp_count, False) if square else 3 * width
    small_out = ((rows, small_width), BF)
    (
        attended, cross_in, cross_mixed, second_in, hidden, pre_keep, pre_send,
        stream_three, grad_one, small_keep, small_send, grad_text, pack, stat, table,
    ) = call(
        functools.partial(forward_kernel, factor=factor, live=live, count=sp_count if square else 0),
        [
            own, (tie(far_qkv, mlp_got, first_pair), slice(width, 3 * width)), tokens[0], modulation, text,
            w_out, cross_q, cross_out, grad_mlp, cotangent[0], w_up, w_down,
        ],
        [
            block, block, block, block, ((rows, units), BF), ((rows, half), BF), ((rows, half), BF),
            stream, stream, small_out, small_out, ((live, 2 * width), F32), ((rows + 16, width), BF), stats,
            (modulation.shape, F32),
        ],
        flags=big,
        raw=(10, 11),
        lazy=True,
        scratch=[
            pltpu.VMEM((3, width, tile), BF),
            pltpu.VMEM((3, tile, width), BF),
            pltpu.SemaphoreType.DMA((3, 4)),
            pltpu.VMEM((rows, tile), BF),
            pltpu.VMEM((rows, tile), BF),
            pltpu.VMEM((rows, 128), F32),
            pltpu.VMEM((rows, width), F32),
            pltpu.VMEM((rows, width), BF),
            *[pltpu.VMEM((rows, width), F32)] * 3,
            *[pltpu.VMEM((rows, width), BF)] * 2,
            *[pltpu.VMEM((padded, width), F32)] * 2,
        ],
        limit=63,
    )
    second_pair = swap(second_in)
    small_acts = [(acts, swap(acts)) for acts in (cross_mixed, cross_in, attended)]

    if not square:
        pre_keep, pre_send = own_half(pre_keep)
    hidden_pair, pre_got = swap(hidden), swap(pre_send)
    if not square:
        small_keep, small_send = own_half(*jnp.split(small_keep, 3, axis=1), joined=False)
    small_got = swap(small_send)
    slice_of = lambda weight: weight.shape[1] // sp_count
    down_source = (hidden, hidden_pair, mlp_keep, mlp_got)
    up_source = (second_in, second_pair, pre_keep, pre_got)
    send_down = send_up = send_small = None
    if square:
        up_sum = sum_wide((tie(second_in, pack), *up_source[1:]), 1, slice_of(w_up))
        send_up = next(up_sum)
        down_sum = sum_wide((tie(hidden, send_up), *down_source[1:]), 0, slice_of(w_down))
        send_down = next(down_sum)
        small_sum = sum_chips_first(small_acts, tie(small_keep, send_down), small_got, slice_of(w_out))
        send_small = next(small_sum)
    pack_blocks, *pack_sends = image_blocks(pack, send_small)
    (grad_queries,) = call(
        functools.partial(query_grad_kernel, factor=factor),
        [own, (far_qkv, slice(width, 3 * width)), tie(pack, *pack_sends), stat],
        [block],
        flags=big,
    )
    proj_out = ((rows, half_width([w_qkv], sp_count, True) if square else 3 * width), BF)
    grad_keys, grad_values, proj_keep, proj_send = call(
        functools.partial(key_grad_kernel, factor=factor, count=sp_count if square else 0),
        [own, (far_qkv, slice(0, width)), tie(pack, grad_queries), grad_queries, *pack_blocks],
        [block, block, proj_out, proj_out],
        flags=big,
        raw=tuple(range(4, 3 + blocks)),
        lazy=True,
        scratch=[
            pltpu.VMEM((2 * HEADS, blocks * rows), F32),
            pltpu.VMEM(((blocks - 1) * rows, width), BF),
            pltpu.VMEM((blocks - 1, 16, width), BF),
            pltpu.SemaphoreType.DMA((2 * blocks - 2,)),
        ],
    )
    if not square:
        proj_keep, proj_send = own_half(*jnp.split(proj_keep, 3, axis=1))
    qkv_source = (first_in, first_pair, proj_keep, swap(proj_send))
    sent = [grad_keys]
    if square:
        sent = [up_sum.send(grad_keys)]
    grad_tokens, table = call(
        last_grad_kernel,
        [tie(grad_queries, *sent), grad_keys, grad_values, w_qkv, tokens[0], modulation, grad_one, table],
        [stream, (modulation.shape, F32)],
    )

    late = None
    if square:
        late = small_sum.send(down_sum.send(table))
        qkv_sum = sum_both((tie(first_in, late), *qkv_source[1:]), slice_of(w_qkv))
        late = next(qkv_sum)
        for step in (small_sum, up_sum, down_sum, qkv_sum, small_sum, up_sum, down_sum, qkv_sum):
            late = step.send(late)
        final_small = small_sum.send(late)
        final_up = up_sum.send(final_small[0])
        final_down = down_sum.send(final_up)
        final_qkv = qkv_sum.send(qkv_sum.send(final_down))
    else:
        small = [(*acts, small_keep, small_got) for acts in small_acts]
        final_small = plain_sum(small, slice_of(w_out))
        (final_down,) = plain_sum([down_source], slice_of(w_down))
        (final_up,) = plain_sum([up_source], slice_of(w_up))
        (final_qkv,) = plain_sum([qkv_source], slice_of(w_qkv))
    table_rows = table.reshape(dp_count, sp_count, -1).transpose(1, 0, 2).reshape(sp_count, 3, -1)
    table_rows = table_rows.transpose(1, 0, 2).reshape(3, 2 * width)
    text_part = lax.psum_scatter(
        jnp.concatenate([grad_text, table_rows], axis=0), "sp", scatter_dimension=1, tiled=True
    )
    text_part = tie(text_part, late)
    part_ckv = matmul_tn(caption_rows, text_part[:live].astype(BF)).astype(BF).reshape(dp_count, -1, text_part.shape[1])
    table_part = text_part[live:].reshape(dp_count, 1, -1)
    table_size = table_part.shape[2]
    table_part = jnp.pad(table_part, ((0, 0), (0, 15), (0, part_ckv.shape[2] - table_size))).astype(BF)
    tall = part_ckv.shape[1]
    both = jnp.concatenate([part_ckv, table_part], axis=1).reshape(dp_count * (tall + 16), -1)
    both = lax.psum_scatter(both, "dp", scatter_dimension=0, tiled=True).astype(F32)
    final_ckv, final_table = both[:tall], both[tall, :table_size]
    return (
        stream_three[None],
        grad_tokens[None],
        final_table,
        final_qkv,
        final_small[2],
        final_small[1],
        final_ckv,
        final_small[0],
        final_up,
        final_down,
    )


def solution(mesh):
    return jax.shard_map(
        local,
        mesh=mesh,
        in_specs=(
            P("dp", "sp", None),
            P("dp", None),
            P("dp", None),
            P("dp", None, None),
            P(),
            P(),
            P(),
            P(),
            P(),
            P(),
            P(),
            P(),
            P(),
            P("dp", "sp", None),
        ),
        out_specs=(
            P("dp", "sp", None),
            P("dp", "sp", None),
            P(("dp", "sp")),
            P("dp", "sp"),
            P("dp", "sp"),
            P("dp", "sp"),
            P("dp", "sp"),
            P("dp", "sp"),
            P("dp", "sp"),
            P("dp", "sp"),
        ),
        check_vma=False,
    )
```

```python
import functools
import math

import jax
import jax.numpy as jnp
from jax import lax
from jax.experimental import pallas as pl
from jax.experimental.pallas import tpu as pltpu
from jax.sharding import PartitionSpec as P

HEADS = 16
BIG = 1024
EPS = 1e-06
BIGNEG = -1e30
LOG2E = 1.4426950408889634
BF = jnp.bfloat16
F32 = jnp.float32
LARGE, CORE, NEAR, FAR, ROW, OTHER, ORDERS = 0, 4, 5, 6, 7, 9, 11
WIN = 256
COST_SCALE = 0.001
MIB = 1024 * 1024


def matmul(left, right):
    return jnp.dot(left, right, preferred_element_type=F32)


def matmul_tn(left, right):
    return lax.dot_general(left, right, (((0,), (0,)), ((), ())), preferred_element_type=F32)


def matmul_nt(left, right):
    return lax.dot_general(left, right, (((1,), (1,)), ((), ())), preferred_element_type=F32)


def head_window(head, width):
    size = width // HEADS
    low = head * size
    start = pl.multiple_of(jnp.minimum(low // 128 * 128, width - WIN), 128)
    lane = lax.broadcasted_iota(jnp.int32, (1, WIN), 1) + start
    return start, jnp.logical_and(lane >= low, lane < low + size)


def window(ref, start, offset=0):
    return ref[:, pl.ds(pl.multiple_of(start + offset, 128), WIN)]


def keep_columns(ref, start, mask, value):
    win = pl.ds(start, WIN)
    ref[:, win] = jnp.where(mask, value, ref[:, win])


def each_head(body, unroll=4):
    def step(head, carry):
        body(head)
        return carry

    lax.fori_loop(0, HEADS, step, 0, unroll=unroll)


def fetch(sems, *pairs):
    copies = [pltpu.make_async_copy(source, target, sems.at[i]) for i, (source, target) in enumerate(pairs)]
    for copy in copies:
        copy.start()
    return [copy.wait for copy in copies]


def attend(big, own_ref, far_ref, out_ref, lse_ref, factor):
    width = out_ref.shape[1]
    scale = factor * LOG2E

    def run(sides):
        def one_head(head):
            start, mask = head_window(head, width)
            query = window(own_ref, start) * mask.astype(BF)
            scores = [matmul_nt(query, window(side, start, key)) for side, key in sides]
            top = functools.reduce(jnp.maximum, [jnp.max(s, axis=1, keepdims=True) for s in scores])
            raised = [jnp.exp2((s - top) * scale) for s in scores]
            total = sum(jnp.sum(r, axis=1, keepdims=True) for r in raised)
            inverse = 1.0 / total
            result = sum(
                matmul((r * inverse).astype(BF), window(side, start, key + width))
                for r, (side, key) in zip(raised, sides)
            )
            keep_columns(out_ref, start, mask, result.astype(BF))
            lane = lax.broadcasted_iota(jnp.int32, (1, 128), 1)
            lse_ref[...] = jnp.where(lane == head, top * scale + jnp.log2(total), lse_ref[...])

        each_head(one_head)

    lse_ref[...] = jnp.zeros_like(lse_ref)

    @pl.when(big)
    def _():
        run([(own_ref, width), (far_ref, 0)])

    @pl.when(jnp.logical_not(big))
    def _():
        run([(own_ref, width)])


def query_grad_kernel(big_ref, own_ref, far_ref, pack_ref, stat_ref, out_ref, *, factor):
    rows, width = out_ref.shape
    scale = factor * LOG2E

    def run(sides):
        def one_head(head):
            start, mask = head_window(head, width)
            keep = mask.astype(BF)
            query = window(own_ref, start) * keep
            grad = window(pack_ref.at[0:rows, :], start) * keep
            lane = lax.broadcasted_iota(jnp.int32, (1, 128), 1)
            stat = stat_ref[...]
            lse = jnp.sum(jnp.where(lane == head, stat, 0.0), axis=1, keepdims=True)
            delta = jnp.sum(jnp.where(lane == head + HEADS, stat, 0.0), axis=1, keepdims=True)
            total = None
            for side, offset in sides:
                key = window(side, start, offset)
                prob = jnp.exp2(matmul_nt(query, key) * scale - lse)
                grad_prob = matmul_nt(grad, window(side, start, offset + width))
                grad_score = (prob * (grad_prob - delta)).astype(BF)
                part = matmul(grad_score, key)
                total = part if total is None else total + part
            keep_columns(out_ref, start, mask, (total * factor).astype(BF))

        each_head(one_head, 8)

    @pl.when(big_ref[0] == 1)
    def _():
        run([(own_ref, width), (far_ref, 0)])

    @pl.when(big_ref[0] == 0)
    def _():
        run([(own_ref, width)])


def key_grad_kernel(flag_ref, own, far, pack, dq, both, third, ahead, back, *refs, factor, count):
    dk, dv, keep_out, send_out, stats, grads, tails, sems = refs
    own_ref, far_ref, pack_ref, dq_ref = (slot.ref for slot in (own, far, pack, dq))
    dk_ref, dv_ref, keep_ref, send_ref = (slot.ref for slot in (dk, dv, keep_out, send_out))
    rows, width = dk_ref.shape
    tall = rows + 16

    def copies(block, source, low):
        return (
            pltpu.make_async_copy(
                source.at[low : low + rows, :], grads.at[block * rows : (block + 1) * rows, :], sems.at[2 * block]
            ),
            pltpu.make_async_copy(source.at[low + rows : low + tall, :], tails.at[block], sems.at[2 * block + 1]),
        )

    def begin(block, flag, first, second):
        for value, (source, low) in ((1, first), (0, second)):

            @pl.when(flag == value)
            def _(source=source, low=low):
                for copy in copies(block, source, low):
                    copy.start()

    for copy in copies(0, both, 0):
        copy.start()
    begin(1, flag_ref[2], (both, tall), (third, 0))
    begin(2, flag_ref[3], (ahead, 0), (back, 0))
    blocks = 4
    for slot in (own, far, pack, dq):
        slot.start()
    for block in range(blocks - 1):
        for copy in copies(block, both, 0):
            copy.wait()
    for slot in (own, far, pack, dq):
        slot.wait()
    scale = factor * LOG2E

    def unpack(block, both):
        both = both.astype(F32)
        joined = both[:8] + both[8:]
        for group in range(4):
            stats[8 * group : 8 * group + 8, block * rows : block * rows + rows] = joined[
                :, group * rows : group * rows + rows
            ]

    unpack(0, pack_ref[rows:, :])
    for block in range(blocks - 1):
        unpack(block + 1, tails[block])

    def run(parts):
        def one_head(head):
            start, mask = head_window(head, width)
            keep = mask.astype(BF)
            key = window(own_ref, start, width) * keep
            value = window(own_ref, start, 2 * width) * keep
            lse = stats[pl.ds(head, 1), :]
            delta = stats[pl.ds(head + HEADS, 1), :]
            grad_key = grad_value = 0.0
            for query_ref, grad_ref, low, high in parts:
                query, grad = window(query_ref, start), window(grad_ref.at[0 : high - low, :], start)
                prob = jnp.exp2(matmul_nt(key, query) * scale - lse[:, low:high])
                grad_prob = matmul_nt(value, grad)
                grad_score = (prob * (grad_prob - delta[:, low:high])).astype(BF)
                grad_value = grad_value + matmul(prob.astype(BF), grad)
                grad_key = grad_key + matmul(grad_score, query)
            keep_columns(dk_ref, start, mask, (grad_key * factor).astype(BF))
            keep_columns(dv_ref, start, mask, grad_value.astype(BF))

        each_head(one_head, 8)

    local = (own_ref, pack_ref, 0, rows)
    @pl.when(flag_ref[0] == 1)
    def _():
        run([local, (far_ref, grads, rows, blocks * rows)])

    @pl.when(flag_ref[0] == 0)
    def _():
        run([local])

    dk.send()
    dv.send()
    if count:
        for core in (0, 1):

            @pl.when(flag_ref[CORE] == core)
            def _(core=core):
                grads = [ref[...] for ref in (dq_ref, dk_ref, dv_ref)]
                keep_ref[...] = half_columns(grads, core, count, True, keep_ref.shape[1])
                send_ref[...] = half_columns(grads, 1 - core, count, True, send_ref.shape[1])

    else:
        for index, ref in enumerate((dq_ref, dk_ref, dv_ref)):
            keep_ref[:, index * width : (index + 1) * width] = ref[...]


def text_probs(query, key, scale, live, axis):
    scores = matmul_nt(query, key) if axis else matmul_nt(key, query)
    shape = (1, scores.shape[1]) if axis else (scores.shape[0], 1)
    scores = jnp.where(lax.broadcasted_iota(jnp.int32, shape, axis) < live, scores, BIGNEG)
    raised = jnp.exp2((scores - jnp.max(scores, axis=axis, keepdims=True)) * scale)
    return raised * (1.0 / jnp.sum(raised, axis=axis, keepdims=True))


def normal(stream):
    centred = stream - jnp.mean(stream, axis=-1, keepdims=True)
    spread = lax.rsqrt(jnp.mean(centred * centred, axis=-1, keepdims=True) + EPS)
    return centred * spread, spread


def norm_back(normed, spread, scale, grad):
    scaled = grad * (1.0 + scale)
    back = spread * (
        scaled
        - jnp.mean(scaled, axis=-1, keepdims=True)
        - normed * jnp.mean(scaled * normed, axis=-1, keepdims=True)
    )
    return back, jnp.sum(grad, axis=0, keepdims=True), jnp.sum(grad * normed, axis=0, keepdims=True)


def middle(tokens_ref, mod_ref, att_ref, weights, text_ref, refs, factor, live):
    branch_ref, cross_in_ref, queries_ref, mixed_ref, stream_ref, second_ref = refs
    width = tokens_ref.shape[1]
    out_w_ref, query_w_ref, cross_w_ref = weights
    branch = matmul(att_ref[...], out_w_ref[...])
    branch_ref[...] = branch
    stream = tokens_ref[...].astype(F32) + mod_ref[2:3, :] * branch
    stream_ref[...] = stream
    cross_in = stream.astype(BF)
    cross_in_ref[...] = cross_in
    queries_ref[...] = matmul(cross_in, query_w_ref[...]).astype(BF)

    def one_head(head):
        start, mask = head_window(head, width)
        query = window(queries_ref, start) * mask.astype(BF)
        probs = text_probs(query, window(text_ref, start), factor * LOG2E, live, 1)
        result = matmul(probs.astype(BF), window(text_ref, start, width))
        keep_columns(mixed_ref, start, mask, result.astype(BF))

    each_head(one_head, 8)
    stream = stream_ref[...] + matmul(mixed_ref[...], cross_w_ref[...])
    stream_ref[...] = stream
    second_ref[...] = (normal(stream)[0] * (1.0 + mod_ref[4:5, :]) + mod_ref[3:4, :]).astype(BF)


def forward_kernel(
    flag_ref, own, far, tokens, mod, text, out_w, query_w, cross_w, grad, cot, up_hbm, down_hbm,
    acts, up_pack, hidden, keep,
    out, one, small_keep, small_send, text_grad, pack, stat, table,
    up, down, sems, kept0, kept1, lse, branch_ref, queries, stream, mlp_out, back,
    grad_mixed, grad_queries, text_key, text_value, *, factor, live, count
):
    kept = (kept0, kept1)
    rows, width = tokens.ref.shape
    mixed, cross_in, att = (acts.ref.at[i * rows : (i + 1) * rows, :] for i in range(3))
    second = up_pack.ref.at[:, 0:width]
    own.start()
    far.start()
    own.wait()
    far.wait()
    late = (tokens, mod, text, out_w, query_w, cross_w, grad, cot)
    for slot in late:
        slot.start()
    tile = down.shape[1]
    tiles = down_hbm.shape[0] // tile
    ring = down.shape[0]

    def copies(step):
        half = tile // 2
        slot = step % ring
        pairs = []
        for part in (0, 1):
            rows = slice(part * up_hbm.shape[0] // 2, (part + 1) * up_hbm.shape[0] // 2)
            pairs.append((up_hbm.at[rows, step * tile : (step + 1) * tile], up.at[slot, rows, :]))
            rows = slice(part * half, (part + 1) * half)
            pairs.append((down_hbm.at[step * tile + part * half : step * tile + (part + 1) * half, :], down.at[slot, rows, :]))
        return [pltpu.make_async_copy(a, b, sems.at[slot, i]) for i, (a, b) in enumerate(pairs)]

    for step in range(min(ring, tiles)):
        for copy in copies(step):
            copy.start()
    attend(flag_ref[LARGE] == 1, own.ref, far.ref, att, lse, factor)
    for slot in late:
        slot.wait()
    weights = (out_w.ref, query_w.ref, cross_w.ref)
    outs = (branch_ref, cross_in, queries, mixed, stream, second)
    middle(tokens.ref, mod.ref, att, weights, text.ref, outs, factor, live)
    acts.send()

    root = math.sqrt(2.0 / math.pi)

    def both(step):
        if step < tiles:
            for copy in copies(step):
                copy.wait()
            pre = matmul(second[...], up[step % ring])
            slope = matmul_nt(grad.ref[...], down[step % ring])
        if step > 0:
            before = (step - 1) % ring
            ahead = hidden.ref[:, (step - 1) * tile : step * tile]
            behind = kept[(step - 1) % 2][...]
            branch = matmul(ahead, down[before])
            result = matmul_nt(behind, up[before])
        if step < tiles:
            square = pre * pre
            bend = jnp.tanh(pre * (root * 0.044715 * square + root))
            half = 0.5 * bend + 0.5
            rise = (3 * root * 0.044715 * square + root) * pre
            ahead = (pre * half).astype(BF)
            behind = (slope * (half + 0.5 * rise * (1.0 - bend * bend))).astype(BF)
            kept[step % 2][...] = behind
            hidden.ref[:, step * tile : (step + 1) * tile] = ahead
            if count:
                size = tile // 2
                body, tail = slice_parts(size)
                group = step % 2 * keep.ref.shape[1] // 2
                spots = (
                    (group + step // 2 * body, 0, body),
                    (group + tiles // 2 * body + step // 2 * tail, body, tail),
                )
                for core in (0, 1):

                    @pl.when(flag_ref[CORE] == core)
                    def _(core=core):
                        for at, low, wide in spots:
                            mine, other = core * size + low, (1 - core) * size + low
                            keep.ref[:, at : at + wide] = behind[:, mine : mine + wide]
                            up_pack.ref[:, width + at : width + at + wide] = behind[:, other : other + wide]

            else:
                keep.ref[:, step * tile : (step + 1) * tile] = behind
        if step > 0:
            if step == 1:
                mlp_out[...] = branch
                back[...] = result
            else:
                mlp_out[...] += branch
                back[...] += result
            if step - 1 + ring < tiles:
                for copy in copies(step - 1 + ring):
                    copy.start()

    for step in range(tiles):
        both(step)
    hidden.send()
    keep.send()
    up_pack.send()
    both(tiles)
    middle_grad(
        flag_ref, back, stream, cot.ref, mlp_out, mod.ref, branch_ref, att, lse, queries, text.ref, weights,
        out, one, small_keep, small_send, text_grad, pack, stat, table,
        grad_mixed, grad_queries, text_key, text_value, factor, live, count,
    )


def middle_grad(
    flag_ref, second_grad_ref, stream_ref, cot_ref, mlp_ref, mod_ref, branch_ref, att_ref, lse_ref, queries_ref, text_ref,
    weights, out, one, keep, send, text_grad, pack, stat_out, table,
    mixed, grad_queries, text_key, text_value, factor, live, count
):
    out_w_ref, query_w_ref, cross_w_ref = weights
    one_ref, keep_ref, send_ref, text_grad_ref, pack_ref, stat_ref, table_ref = (
        slot.ref for slot in (one, keep, send, text_grad, pack, stat_out, table)
    )
    rows, width = cot_ref.shape
    cot = cot_ref[...].astype(F32)
    stream = stream_ref[...]
    mlp = mlp_ref[...]
    out.ref[...] = stream + mod_ref[5:6, :] * mlp
    out.send()
    normed, spread = normal(stream)
    back, shift, scale = norm_back(normed, spread, mod_ref[4:5, :], second_grad_ref[...])
    table_ref[...] = jnp.zeros_like(table_ref)
    table_ref[3:4, :] = shift
    table_ref[4:5, :] = scale
    table_ref[5:6, :] = jnp.sum(cot * mlp, axis=0, keepdims=True)
    grad_two = cot + back
    one_ref[...] = grad_two
    grad_cross = grad_two.astype(BF)
    mixed[...] = matmul_nt(grad_cross, cross_w_ref[...]).astype(BF)

    def one_head(head):
        start, mask = head_window(head, width)
        keep = mask.astype(BF)
        query = window(queries_ref, start)
        grad = window(mixed, start)
        key = window(text_ref, start) * keep
        probs = text_probs(query, key, factor * LOG2E, live, 0)
        grad_probs = matmul_nt(window(text_ref, start, width) * keep, grad)
        inner = jnp.sum(probs * grad_probs, axis=0, keepdims=True)
        grad_scores = (probs * (grad_probs - inner)).astype(BF)
        keep_columns(grad_queries, start, mask, (matmul_tn(grad_scores, key) * factor).astype(BF))
        keep_columns(text_key, start, mask, matmul(grad_scores, query) * factor)
        keep_columns(text_value, start, mask, matmul(probs.astype(BF), grad))

    each_head(one_head, 8)
    text_grad_ref[:, :width] = text_key[0:live, :]
    text_grad_ref[:, width:] = text_value[0:live, :]
    text_grad.send()
    grad_cq = grad_queries[...]
    grad_one = one_ref[...] + matmul_nt(grad_cq, query_w_ref[...])
    one_ref[...] = grad_one
    table_ref[2:3, :] = jnp.sum(grad_one * branch_ref[...], axis=0, keepdims=True)
    grad_attn = (mod_ref[2:3, :] * grad_one).astype(BF)
    grad_att = matmul_nt(grad_attn, out_w_ref[...]).astype(BF)
    pack_ref[0:rows, :] = grad_att

    product = grad_att.astype(F32) * att_ref[...].astype(F32)
    upper = product.astype(BF)
    lower = (product - upper.astype(F32)).astype(BF)
    size = width // HEADS
    column = lax.broadcasted_iota(jnp.int32, (width, 128), 0)
    low = (lax.broadcasted_iota(jnp.int32, (width, 128), 1) - HEADS) * size
    pick = jnp.logical_and(column >= low, column < low + size).astype(BF)
    stat = lse_ref[...] + matmul(upper, pick) + matmul(lower, pick)
    stat_ref[...] = stat
    turned = stat.T
    upper = [turned[8 * g : 8 * g + 8, :].astype(BF).astype(F32) for g in range(4)]
    lower = [turned[8 * g : 8 * g + 8, :] - part for g, part in enumerate(upper)]
    both = [jnp.concatenate(pair, axis=0) for pair in zip(upper, lower)]
    pack_ref[rows : rows + 16, :] = side_by_side(both, width).astype(BF)
    for slot in (pack, stat_out, one, table):
        slot.send()

    if count:
        for core in (0, 1):

            @pl.when(flag_ref[CORE] == core)
            def _(core=core):
                grads = [grad_cross, grad_cq, grad_attn]
                keep_ref[...] = half_columns(grads, core, count, False, keep_ref.shape[1])
                send_ref[...] = half_columns(grads, 1 - core, count, False, send_ref.shape[1])

    else:
        for index, grad in enumerate((grad_cross, grad_cq, grad_attn)):
            keep_ref[:, index * width : (index + 1) * width] = grad


def last_grad_kernel(
    dq_ref, dk_ref, dv_ref, weight_ref, tokens_ref, mod_ref, one_ref, table_in_ref, out_ref, table_ref
):
    width = tokens_ref.shape[1]
    grad = sum(
        matmul_nt(ref[...], weight_ref[:, part * width : (part + 1) * width])
        for part, ref in enumerate((dq_ref, dk_ref, dv_ref))
    )
    normed, spread = normal(tokens_ref[...].astype(F32))
    back, shift, scale = norm_back(normed, spread, mod_ref[1:2, :], grad)
    out_ref[...] = one_ref[...] + back
    table_ref[...] = table_in_ref[...]
    table_ref[0:1, :] = shift
    table_ref[1:2, :] = scale


def side_by_side(pieces, width):
    missing = width - sum(piece.shape[1] for piece in pieces)
    if missing:
        pieces = [*pieces, jnp.zeros((pieces[0].shape[0], missing), pieces[0].dtype)]
    return pieces[0] if len(pieces) == 1 else jnp.concatenate(pieces, axis=1)


def lanes(width):
    return -(-width // 128) * 128


def slice_parts(size):
    return size // 128 * 128, size % 128


def half_columns(grads, core, count, joined, wide):
    if not joined:
        picked = []
        for grad in grads:
            size = grad.shape[1] // count
            low = [(2 * chip + core) * size for chip in (*range(0, count // 2, 2), *range(1, count // 2, 2))]
            picked.append(
                side_by_side([grad[:, at : at + size] for at in low], wide // len(grads))
            )
        return side_by_side(picked, wide)
    grad = grads[0] if len(grads) == 1 else jnp.concatenate(grads, axis=1)
    size = grad.shape[1] // count
    body, _ = slice_parts(size)
    picked = []
    for parity in (0, 1):
        low = [(2 * chip + core) * size for chip in range(parity, count // 2, 2)]
        picked += [grad[:, at : at + body] for at in low]
        picked.append(side_by_side([grad[:, at + body : at + size] for at in low], 128))
    return side_by_side(picked, wide)


def halves_kernel(core_ref, *refs, count, joined):
    keep_ref, send_ref = refs[-2:]
    for core in (0, 1):

        @pl.when(core_ref[CORE] == core)
        def _(core=core):
            grads = [ref[...] for ref in refs[:-2]]
            keep_ref[...] = half_columns(grads, core, count, joined, keep_ref.shape[1])
            send_ref[...] = half_columns(grads, 1 - core, count, joined, send_ref.shape[1])


def store_halves(flag, stores, pieces):
    for value in (0, 1):

        @pl.when(flag == value)
        def _(value=value):
            for store, piece in zip(stores, (pieces[1 - value], pieces[value])):
                store(piece())


def into(ref):
    def store(value):
        ref[:, : value.shape[1]] = value.astype(ref.dtype)

    return store


def add(*terms):
    return sum(term.astype(F32) for term in terms)


def sending(buffers, sems, out):
    state = {"count": 0}

    def wait(slot):
        pltpu.make_async_copy(buffers.at[slot], out, sems.at[slot]).wait()

    def put(pieces, targets):
        slot = state["count"] % 2
        if state["count"] >= 2:
            wait(slot)
        at = 0
        for piece in pieces:
            buffers[slot, at : at + piece.shape[0], : piece.shape[1]] = piece
            at += piece.shape[0]
        for condition, target in targets:
            copy = pltpu.make_async_copy(buffers.at[slot], target, sems.at[slot])
            if condition is None:
                copy.start()
            else:
                pl.when(condition)(copy.start)
        state["count"] += 1

    def done():
        for slot in range(min(2, state["count"])):
            wait(slot)

    return put, done


def wide_grad_kernel(order_ref, x0_hbm, x1_hbm, g0_hbm, g1_hbm, *refs, mode, first, columns):
    number = 2 if mode == "rows" else 4
    outs, (x_ref, g_ref, turned, buffers, sems, out_sems) = refs[:number], refs[number:]
    rows, width = x0_hbm.shape[0], x_ref.shape[1]
    x0_hbm, x1_hbm, g0_hbm, g1_hbm = (
        hbm if part is None else hbm.at[:, part] for hbm, part in zip((x0_hbm, x1_hbm, g0_hbm, g1_hbm), columns)
    )
    waits = fetch(
        sems,
        (x0_hbm, x_ref.at[0:rows, :]),
        (x1_hbm, x_ref.at[rows : 2 * rows, :]),
        (g0_hbm, g_ref.at[0:rows, :]),
        (g1_hbm, g_ref.at[rows : 2 * rows, :]),
    )
    for part in (0, 1):
        waits[part]()
        for low in range(0, width, 128):
            turned[low : low + 128, part * rows : (part + 1) * rows] = x_ref[
                part * rows : (part + 1) * rows, low : low + 128
            ].T
    waits[2]()
    waits[3]()
    tall = width // 4
    put, done = sending(buffers, out_sems, outs[0].at[0])
    half = g_ref.shape[1] // 2
    for step in range(4):
        here = pl.ds(pl.multiple_of((order_ref[ORDERS + 4 * first + step] if mode == "rows" else step) * tall, 16), tall)
        if mode == "rows":
            total = matmul(turned[here, :], g_ref[...]).astype(BF)
            put([total], [(None, outs[step // 2].at[step % 2])])
        else:
            for p in (0, 1):
                total = matmul(turned[here, :], g_ref[:, p * half : (p + 1) * half]).astype(BF)
                place, second = (step >> p) & 1, (step >> (1 - p)) & 1
                mine = order_ref[ROW + p]
                put(
                    [total],
                    [(mine != place, outs[2 * p].at[second]), (mine == place, outs[2 * p + 1].at[second])],
                )
    done()


def tall_grad_kernel(order_ref, *refs, count, mode, first, columns):
    sources, g0_hbm, g1_hbm = refs[: 2 * count], refs[2 * count], refs[2 * count + 1]
    outs, (x_ref, g_ref, turned, buffers, sems, out_sems) = refs[2 * count + 2 : 2 * count + 4], refs[2 * count + 4 :]
    rows = g0_hbm.shape[0]
    sources = [hbm if part is None else hbm.at[part, :] for hbm, part in zip(sources, columns)]
    pairs = [(g0_hbm, g_ref.at[0:rows, :]), (g1_hbm, g_ref.at[rows : 2 * rows, :])]
    for i, source in enumerate(sources):
        pairs.append((source, x_ref.at[i // 2, i % 2 * rows : (i % 2 + 1) * rows, :]))
    waits = fetch(sems, *pairs)
    wide = g_ref.shape[1]
    for part in (0, 1):
        waits[part]()
        for low in range(0, wide, 128):
            turned[low : low + 128, part * rows : (part + 1) * rows] = g_ref[
                part * rows : (part + 1) * rows, low : low + 128
            ].T
    for wait in waits[2:]:
        wait()
    if mode == "rows":
        high, tall = outs[0].shape[1:]
        put, done = sending(buffers, out_sems, outs[0].at[0])
        for step in range(4):
            here = pl.ds(pl.multiple_of(order_ref[ORDERS + 4 * first + step] * tall, 128), tall)
            total = matmul(turned[0:high, :], x_ref[0, :, here]).astype(BF)
            put([total], [(None, outs[step // 2].at[step % 2])])
    else:
        high = outs[0].shape[0] // count
        put, done = sending(buffers, out_sems, outs[0])
        for p in (0, 1):
            total = [
                matmul(turned[pl.ds(k * (wide // count) + p * high, high), :], x_ref[k]).astype(BF)
                for k in range(count)
            ]
            put(total, [(order_ref[NEAR] != p, outs[0]), (order_ref[NEAR] == p, outs[1])])
    done()


def add_kernel(flag_ref, *refs):
    refs[-1][...] = add(*[ref[...] for ref in refs[:-1]]).astype(BF)


def split_kernel(flag_ref, *refs, parts, axis, bit):
    views = refs[:-2]

    def joined(index):
        def piece():
            sums = [add(*[view[part] for view in views]) for part in parts[index]]
            return sums[0] if len(sums) == 1 else jnp.concatenate(sums, axis=axis)

        return piece

    store_halves(flag_ref[bit], [into(ref) for ref in refs[-2:]], [joined(0), joined(1)])


def split_pair_kernel(flag_ref, *refs):
    def group(p):
        keep, got, more = refs[3 * p : 3 * p + 3]
        return lambda: add(keep[...], got[...], more[...])

    store_halves(flag_ref[NEAR], [into(ref) for ref in refs[-2:]], [group(0), group(1)])


def last_kernel(keep_ref, got_ref, *outs, size):
    if size:
        body, tail = slice_parts(size)
        for part in (slice(0, body), slice(body, size)):
            outs[0][:, part] = add(keep_ref[:, part], got_ref[:, part])
    else:
        high, wide = outs[0].shape
        for index, out in enumerate(outs):
            part = slice(index * high, (index + 1) * high), slice(0, wide)
            out[...] = add(keep_ref[part], got_ref[part])


def prelude_kernel(place_ref, row_ref, len_ref, step_ref, embed_ref, table_ref, info_ref, mod_ref, slab, sem, *, rows):
    slots = len_ref.shape[1]
    width = table_ref.shape[1]

    def image_of(at):
        first = at * rows
        end = begin = length = step = jnp.int32(0)
        for slot in range(slots):
            count = len_ref[0, slot]
            inside = jnp.logical_and(end <= first, first < end + count)
            begin = jnp.where(inside, end, begin)
            length = jnp.where(inside, count, length)
            step = jnp.where(inside, step_ref[0, slot], step)
            end = end + count
        return (first - begin) // rows, length, step

    place = place_ref[0]
    core = place % 2
    blocks = BIG // rows
    within, length, step = image_of(place)
    pair_within = image_of(place + 1 - 2 * core)[0]
    flags = (
        length > rows,
        jnp.where(core == 0, pair_within + 1 < blocks, pair_within + 3 < blocks),
        jnp.where(core == 0, within + 1 < blocks, within >= 1),
        within + 2 < blocks,
        core == 1,
    )
    bits = [(place // 2) & 1, (place // 4) & 1, row_ref[0] & 1, (row_ref[0] >> 1) & 1]
    values = [flag.astype(jnp.int32) for flag in flags] + bits + [1 - bits[2], 1 - bits[3]]
    for first in (0, 1):
        mine = bits[2 + first]
        values += [((1 - mine if s < 2 else mine) << first) + ((s % 2) << (1 - first)) for s in range(4)]
    for index, value in enumerate(values):
        info_ref[index] = value
    copy = pltpu.make_async_copy(embed_ref.at[pl.ds(pl.multiple_of(step // 8 * 8, 8), 8), :], slab, sem)
    copy.start()
    copy.wait()
    row = slab[pl.ds(step % 8, 1), :]
    for index in range(6):
        mod_ref[index : index + 1, :] = (
            row[:, index * width : (index + 1) * width] + table_ref[index : index + 1, :]
        )


class Slot:
    def __init__(self, hbm, ref, sems, out=False):
        self.hbm, self.ref, self.out = hbm, ref, out
        self.sent = False
        self.copies = []
        for i, rows in enumerate(row_chunks(ref.shape, ref.dtype)):
            pair = (hbm.at[rows], ref.at[rows])
            self.copies.append(pltpu.make_async_copy(*(pair[::-1] if out else pair), sems.at[i]))

    def start(self):
        self.sent = True
        for copy in self.copies:
            copy.start()

    send = start

    def wait(self):
        for copy in self.copies:
            copy.wait()


def row_chunks(shape, dtype):
    if len(shape) > 2:
        return [slice(i, i + 1) for i in range(shape[0])]
    size = shape[0] * shape[1] * jnp.dtype(dtype).itemsize
    count = max([n for n in (1, 2, 3, 4, 6) if shape[0] % (16 * n) == 0 and size >= n * 200_000] or [1])
    high = shape[0] // count
    return [slice(i * high, (i + 1) * high) for i in range(count)]


def call(kernel, inputs, outs, flags=None, scratch=(), raw=(), lazy=False, limit=60):
    anywhere = pl.BlockSpec(memory_space=pl.ANY)
    arrays, views = [], []
    for entry in inputs:
        array, part = entry if isinstance(entry, tuple) else (entry, None)
        arrays.append(array)
        views.append(part)

    def view_shape(array, part):
        if part is None:
            return array.shape
        if isinstance(part, slice):
            return (array.shape[0], part.stop - part.start)
        return array.shape[1:]

    in_shapes = [view_shape(array, part) for array, part in zip(arrays, views)]
    slots = [(shape, array.dtype) for shape, array in zip(in_shapes, arrays)] + list(outs)
    held = [i for i in range(len(arrays)) if i not in raw]
    held += [len(arrays) + i for i in range(len(outs)) if "out" not in raw]
    buffers = [pltpu.VMEM(*slots[i]) for i in held]
    sems = [pltpu.SemaphoreType.DMA((len(row_chunks(*slots[i])),)) for i in held]

    def managed(*refs):
        refs = list(refs)
        flag_refs = [refs.pop(0)] if flags is not None else []
        hbm, rest = refs[: len(slots)], refs[len(slots) :]
        own, rest = rest[: len(scratch)], rest[len(scratch) :]
        views_in = []
        for ref, part in zip(hbm, views):
            if isinstance(part, slice):
                ref = ref.at[:, part]
            elif part is not None:
                ref = ref.at[flag_refs[0][part]]
            views_in.append(ref)
        given = views_in + hbm[len(arrays) :]
        for n, i in enumerate(held):
            given[i] = Slot(given[i], rest[n], rest[len(held) + n], i >= len(arrays))
        slots_in = [slot for slot in given if isinstance(slot, Slot) and not slot.out]
        slots_out = [slot for slot in given if isinstance(slot, Slot) and slot.out]
        if not lazy:
            for slot in slots_in:
                slot.start()
            for slot in slots_in:
                slot.wait()
            kernel(*flag_refs, *[getattr(slot, "ref", slot) if isinstance(slot, Slot) else slot for slot in given], *own)
        else:
            kernel(*flag_refs, *given, *own)
        for slot in slots_out:
            if not slot.sent:
                slot.send()
        for slot in slots_out:
            slot.wait()

    return pl.pallas_call(
        managed,
        in_specs=([pl.BlockSpec(memory_space=pltpu.SMEM)] if flags is not None else []) + [anywhere] * len(arrays),
        out_specs=[anywhere] * len(outs),
        out_shape=[jax.ShapeDtypeStruct(shape, dtype) for shape, dtype in outs],
        scratch_shapes=[*scratch, *buffers, *sems],
        compiler_params=pltpu.CompilerParams(vmem_limit_bytes=limit * MIB),
        cost_estimate=pl.CostEstimate(flops=1000, bytes_accessed=1000, transcendentals=0),
    )(*([] if flags is None else [flags]), *arrays)


def prelude(place, row_place, image_len, timestep, time_embed, mod_table, rows):
    smem = pl.BlockSpec(memory_space=pltpu.SMEM)
    return pl.pallas_call(
        functools.partial(prelude_kernel, rows=rows),
        in_specs=[smem] * 4 + [pl.BlockSpec(memory_space=pl.ANY), pl.BlockSpec(memory_space=pltpu.VMEM)],
        out_specs=[smem, pl.BlockSpec(memory_space=pltpu.VMEM)],
        out_shape=[jax.ShapeDtypeStruct((ORDERS + 8,), jnp.int32), jax.ShapeDtypeStruct(mod_table.shape, F32)],
        scratch_shapes=[pltpu.VMEM((8, time_embed.shape[1]), F32), pltpu.SemaphoreType.DMA],
        compiler_params=pltpu.CompilerParams(vmem_limit_bytes=60 * MIB),
    )(place.reshape(1), row_place.reshape(1), image_len, timestep, time_embed, mod_table)


def half_width(grads, count, joined):
    size = (sum(grad.shape[1] for grad in grads) if joined else grads[0].shape[1]) // count
    body, _ = slice_parts(size)
    return 2 * (count // 4 * body + 128) if joined else len(grads) * -(-count // 2 * size // 128) * 128


def halves(core, grads, count, joined):
    out = ((grads[0].shape[0], half_width(grads, count, joined)), BF)
    return call(functools.partial(halves_kernel, count=count, joined=joined), grads, [out] * 2, flags=core)


def split(flags, bit, inputs, parts, shape, axis=1):
    return call(
        functools.partial(split_kernel, parts=parts, axis=axis, bit=bit),
        inputs,
        [(shape, BF), (shape, F32)],
        flags=flags,
    )


def add_last(keep, got, size, shapes):
    return call(functools.partial(last_kernel, size=size), [keep, got], [(shape, F32) for shape in shapes])


def wide_grad(order, source, mode, first=0):
    entries = [entry if isinstance(entry, tuple) else (entry, None) for entry in source]
    source = [array for array, _ in entries]
    columns = [part and slice(part.start, part.stop or array.shape[1]) for array, part in entries]
    rows, width = source[0].shape[0], columns[0].stop if columns[0] else source[0].shape[1]
    depth = source[2].shape[1]
    wide, number = (depth, 2) if mode == "rows" else (depth // 2, 4)
    return call(
        functools.partial(wide_grad_kernel, mode=mode, first=first, columns=columns),
        source,
        [((2, width // 4, wide), BF)] * number,
        flags=order,
        raw=(0, 1, 2, 3, "out"),
        scratch=[
            pltpu.VMEM((2 * rows, width), BF),
            pltpu.VMEM((2 * rows, depth), BF),
            pltpu.VMEM((width, 2 * rows), BF),
            pltpu.VMEM((2, width // 4, wide), BF),
            pltpu.SemaphoreType.DMA((4,)),
            pltpu.SemaphoreType.DMA((2,)),
        ],
    )


def tall_grad(order, acts, keep, got, size, mode, first=0):
    count = len(acts)
    entries = [entry if isinstance(entry, tuple) else (entry, None) for pair in acts for entry in pair]
    rows, wide = keep.shape
    width = entries[0][0].shape[1]
    shape = (2, 4 * size, width // 4) if mode == "rows" else (2 * size * count, width)
    return call(
        functools.partial(
            tall_grad_kernel, count=count, mode=mode, first=first, columns=[part for _, part in entries]
        ),
        [array for array, _ in entries] + [keep, got],
        [(shape, BF)] * 2,
        flags=order,
        raw=(*range(2 * count + 2), "out"),
        scratch=[
            pltpu.VMEM((count, 2 * rows, width), BF),
            pltpu.VMEM((2 * rows, wide), BF),
            pltpu.VMEM((wide, 2 * rows), BF),
            pltpu.VMEM((2, *shape[-2:]), BF),
            pltpu.SemaphoreType.DMA((2 * count + 2,)),
            pltpu.SemaphoreType.DMA((2,)),
        ],
    )


def local(
    tokens,
    image_len,
    timestep,
    caption,
    time_embed,
    mod_table,
    w_qkv,
    w_out,
    cross_q,
    cross_kv,
    cross_out,
    w_up,
    w_down,
    cotangent,
):
    sp_count = lax.axis_size("sp")
    dp_count = lax.axis_size("dp")
    place = lax.axis_index("sp")
    row_place = lax.axis_index("dp")
    core = place % 2
    rows, width = tokens.shape[1:]
    factor = 1.0 / math.sqrt(width // HEADS)
    blocks = BIG // rows
    assert blocks == 4

    big, modulation = prelude(place, row_place, image_len, timestep, time_embed, mod_table, rows)
    shift_one, scale_one, gate_one, shift_two, scale_two, gate_two = [modulation[i] for i in range(6)]

    def tie(value, *before):
        return lax.optimization_barrier((value, *[array for array in before if array is not None]))[0]

    pairs = [(i, i ^ 1) for i in range(sp_count)]
    others = [(i, i + 1) for i in range(1, sp_count - 1, 2)] + [(i + 1, i) for i in range(1, sp_count - 1, 2)]
    ahead = [(i, i + 2) for i in range(sp_count - 2)]
    back = [(i + 2, i) for i in range(sp_count - 2)]

    def image_blocks(block, *before):
        from_back = lax.ppermute(block, "sp", ahead)
        from_ahead = lax.ppermute(block, "sp", back)
        from_ahead, from_back = tie(from_ahead, *before), tie(from_back, *before)
        send_pair = jnp.concatenate([jnp.where(big[1] == 1, from_ahead, from_back), block], axis=0)
        send_other = jnp.where(core == 1, from_back, from_ahead)
        both = lax.ppermute(send_pair, "sp", pairs)
        third = lax.ppermute(send_other, "sp", others)
        return [both, third, from_ahead, from_back], (send_pair, send_other)

    def chosen(both, third, from_ahead, from_back):
        high = both.shape[0] // 2
        return [
            both[:high],
            jnp.where(big[2] == 1, both[high:], third),
            jnp.where(big[3] == 1, from_ahead, from_back),
        ]

    def swap(array):
        return lax.ppermute(array, "sp", pairs)

    token_blocks, token_sends = image_blocks(tokens[0])

    def first_norm(block):
        return (normal(block.astype(F32))[0] * (1.0 + scale_one) + shift_one).astype(BF)

    first_in = first_norm(tokens[0])
    other_in = first_norm(jnp.concatenate(chosen(*token_blocks), axis=0))

    chips = sp_count // 2
    square = dp_count == 4 and chips == 4

    def own_half(*grads, joined=True):
        if square:
            return halves(big, grads, sp_count, joined)
        grads = [jnp.concatenate(grads, axis=1)] if joined else grads
        size = grads[0].shape[1] // sp_count
        even, odd = [
            jnp.concatenate(
                [g[:, i * size : (i + 1) * size] for g in grads for i in range(c, sp_count, 2)], axis=1
            )
            for c in (0, 1)
        ]
        return jnp.where(core == 0, even, odd), jnp.where(core == 0, odd, even)

    high = width // 4

    def to_row(array, bit):
        return lax.ppermute(array, "dp", [(i, i ^ (1 << bit)) for i in range(dp_count)])

    def to_chip(array, bit):
        return lax.ppermute(array, "sp", [(i, i ^ (2 << bit)) for i in range(sp_count)])

    def plain_sum(sources, size):
        finals = []
        for item, (x0, x1, g0, g1) in enumerate(sources):
            columns = slice(item * chips * size, (item + 1) * chips * size)
            part = (matmul_tn(x0, g0[:, columns]) + matmul_tn(x1, g1[:, columns])).astype(BF)
            part = part.reshape(dp_count, -1, chips, size).transpose(0, 2, 1, 3)
            bit = dp_count // 2
            while bit:
                mine = (row_place // bit) % 2
                part = part.reshape(2, bit, chips, -1, size)
                got = lax.ppermute(part[1 - mine], "dp", [(i, i ^ bit) for i in range(dp_count)])
                part = add(part[mine], got).astype(BF)
                bit //= 2
            part = part.reshape(chips, -1, size)
            bit = chips // 2
            while bit:
                mine = (place // 2 // bit) % 2
                part = part.reshape(2, bit, -1, size)
                got = lax.ppermute(part[1 - mine], "sp", [(i, i ^ (2 * bit)) for i in range(sp_count)])
                part = add(part[mine], got).astype(BF)
                bit //= 2
            finals.append(part[0].astype(F32))
        return finals

    def add_picked(keep, got, flag):
        return call(add_kernel, [(keep, flag), (got, flag)], [(keep.shape[1:], BF)], flags=big)

    everything = slice(None)

    def cut_slices(size):
        body, tail = slice_parts(size)
        return [
            [
                (everything, slice(h * body, (h + 1) * body)),
                (everything, slice(2 * body + h * tail, 2 * body + (h + 1) * tail)),
            ]
            for h in (0, 1)
        ]

    def sum_wide(source, first, size):
        second = 1 - first
        if size < 256:
            send, keep = tall_grad(big, [source[:2]], *source[2:], size, "rows", first)
        else:
            send, keep = wide_grad(big, source, "rows", first)
        late = yield send
        got = to_row(send, first)
        (send,) = add_picked(tie(keep, late), got, OTHER + second)
        late = yield send
        tall, wide = send.shape
        more = to_row(send, second)
        inputs = [(tie(keep, late), ROW + second), (got, ROW + second), more]
        if size < 256:
            groups = [[(slice(h * tall // 2, (h + 1) * tall // 2),)] for h in (0, 1)]
            send, keep = split(big, NEAR, inputs, groups, (tall // 2, wide), 0)
            late = yield send
            groups = [[(slice(h * tall // 4, (h + 1) * tall // 4),)] for h in (0, 1)]
            send, keep = split(big, FAR, [tie(keep, late), to_chip(send, 0)], groups, (tall // 4, wide), 0)
            late = yield send
            (final,) = add_last(tie(keep, late), to_chip(send, 1), 0, [(size, wide)])
            yield final.T
        else:
            groups = [[(everything, slice(h * wide // 2, (h + 1) * wide // 2))] for h in (0, 1)]
            send, keep = split(big, NEAR, inputs, groups, (tall, wide // 2))
            late = yield send
            shape = (tall, size // 128 * 128 + 128)
            send, keep = split(big, FAR, [tie(keep, late), to_chip(send, 0)], cut_slices(size), shape)
            late = yield send
            (final,) = add_last(tie(keep, late), to_chip(send, 1), size, [(tall, size)])
            yield final

    def sum_both(source, size):
        outs = wide_grad(big, source, "both")
        late = yield outs[0]
        got = [to_row(outs[0], 0), to_row(outs[2], 1)]
        sends = [
            *add_picked(tie(outs[1], late), got[0], OTHER + 1),
            *add_picked(tie(outs[3], late), got[1], OTHER),
        ]
        late = yield sends[1]
        shape = sends[0].shape
        more = [to_row(sends[0], 1), to_row(sends[1], 0)]
        send, keep = call(
            split_pair_kernel,
            [
                (tie(outs[1], late), ROW + 1), (got[0], ROW + 1), more[0],
                (outs[3], ROW), (got[1], ROW), more[1],
            ],
            [(shape, BF), (shape, F32)],
            flags=big,
        )
        late = yield send
        shape = (shape[0], size // 128 * 128 + 128)
        send, keep = split(big, FAR, [tie(keep, late), to_chip(send, 0)], cut_slices(size), shape)
        late = yield send
        (final,) = add_last(tie(keep, late), to_chip(send, 1), size, [(high, size)])
        yield final

    def sum_chips_first(acts, keep, got, size):
        count = len(acts)
        send, keep = tall_grad(big, acts, keep, got, size, "chips")
        late = yield send
        got = to_chip(send, 0)
        groups = [
            [(everything, slice(i * high, (i + 1) * high)) for i in (h, h + 2)] for h in (0, 1)
        ]
        shape = (2 * count * size, lanes(2 * high))
        send, keep = split(big, ROW, [tie(keep, late), got], groups, shape)
        late = yield send
        got = to_row(send, 0)
        groups = [[(everything, slice(h * high, (h + 1) * high))] for h in (0, 1)]
        shape = (2 * count * size, lanes(high))
        send, keep = split(big, ROW + 1, [tie(keep, late), got], groups, shape)
        late = yield send
        got = to_row(send, 1)
        groups = [
            [(slice((2 * k + h) * size, (2 * k + h + 1) * size),) for k in range(count)] for h in (0, 1)
        ]
        shape = (count * size, lanes(high))
        send, keep = split(big, FAR, [tie(keep, late), got], groups, shape, 0)
        late = yield send
        finals = add_last(tie(keep, late), to_chip(send, 1), 0, [(size, high)] * count)
        yield [final.T for final in finals]

    caption_rows = caption[0]
    live = caption_rows.shape[0]
    padded = -(-live // 128) * 128
    caption_pad = jnp.concatenate([caption_rows, jnp.zeros((padded - live, width), BF)], axis=0)
    text = matmul(caption_pad, cross_kv).astype(BF)
    grad_mlp = (gate_two * cotangent[0].astype(F32)).astype(BF)
    mlp_keep, mlp_send = own_half(grad_mlp, joined=False)
    mlp_got = swap(mlp_send)
    first_pair = swap(first_in)
    own = matmul(tie(first_in, *token_sends), w_qkv).astype(BF)
    far_qkv = matmul(other_in, w_qkv).astype(BF)
    block = ((rows, width), BF)
    stream = ((rows, width), F32)
    stats = ((rows, 128), F32)
    units = w_up.shape[1]
    tile = units // 4
    half = half_width([w_up], sp_count, True) if square else units
    small_width = half_width([grad_mlp] * 3, sp_count, False) if square else 3 * width
    small_out = ((rows, small_width), BF)
    (
        acts, up_pack, hidden, pre_keep,
        stream_three, grad_one, small_keep, small_send, grad_text, pack, stat, table,
    ) = call(
        functools.partial(forward_kernel, factor=factor, live=live, count=sp_count if square else 0),
        [
            own, (tie(far_qkv, mlp_got, first_pair), slice(width, 3 * width)), tokens[0], modulation, text,
            w_out, cross_q, cross_out, grad_mlp, cotangent[0], w_up, w_down,
        ],
        [
            ((3 * rows, width), BF), ((rows, width + (half if square else 0)), BF), ((rows, units), BF),
            ((rows, half), BF),
            stream, stream, small_out, small_out, ((live, 2 * width), F32), ((rows + 16, width), BF), stats,
            (modulation.shape, F32),
        ],
        flags=big,
        raw=(10, 11),
        lazy=True,
        scratch=[
            pltpu.VMEM((3, width, tile), BF),
            pltpu.VMEM((3, tile, width), BF),
            pltpu.SemaphoreType.DMA((3, 4)),
            pltpu.VMEM((rows, tile), BF),
            pltpu.VMEM((rows, tile), BF),
            pltpu.VMEM((rows, 128), F32),
            pltpu.VMEM((rows, width), F32),
            pltpu.VMEM((rows, width), BF),
            *[pltpu.VMEM((rows, width), F32)] * 3,
            *[pltpu.VMEM((rows, width), BF)] * 2,
            *[pltpu.VMEM((padded, width), F32)] * 2,
        ],
        limit=63,
    )

    if not square:
        pre_keep, pre_send = own_half(pre_keep)
        up_pack = jnp.concatenate([up_pack, pre_send], axis=1)
    hidden_pair, up_pair = swap(hidden), swap(up_pack)
    if not square:
        small_keep, small_send = own_half(*jnp.split(small_keep, 3, axis=1), joined=False)
    slice_of = lambda weight: weight.shape[1] // sp_count
    down_source = (hidden, hidden_pair, mlp_keep, mlp_got)
    up_source = ((up_pack, slice(0, width)), (up_pair, slice(0, width)), pre_keep, (up_pair, slice(width, None)))
    send_down = send_up = send_small = None
    if square:
        up_sum = sum_wide((up_source[0], up_source[1], tie(pre_keep, pack), up_source[3]), 1, slice_of(w_up))
        send_up = next(up_sum)
        down_sum = sum_wide((tie(hidden, send_up), *down_source[1:]), 0, slice_of(w_down))
        send_down = next(down_sum)
        small_got = swap(tie(small_send, send_up))
        small_acts = tie(acts, send_up)
        small_acts = [small_acts, swap(small_acts)]
        small_acts = [[(part, slice(i * rows, (i + 1) * rows)) for part in small_acts] for i in range(3)]
        small_sum = sum_chips_first(small_acts, tie(small_keep, send_down), small_got, slice_of(w_out))
        send_small = next(small_sum)
    pack_blocks, pack_sends = image_blocks(pack, send_small)
    (grad_queries,) = call(
        functools.partial(query_grad_kernel, factor=factor),
        [own, (far_qkv, slice(width, 3 * width)), tie(pack, *pack_sends), stat],
        [block],
        flags=big,
    )
    proj_out = ((rows, half_width([w_qkv], sp_count, True) if square else 3 * width), BF)
    grad_keys, grad_values, proj_keep, proj_send = call(
        functools.partial(key_grad_kernel, factor=factor, count=sp_count if square else 0),
        [own, (far_qkv, slice(0, width)), tie(pack, grad_queries), grad_queries, *pack_blocks],
        [block, block, proj_out, proj_out],
        flags=big,
        raw=(4, 5, 6, 7),
        lazy=True,
        scratch=[
            pltpu.VMEM((2 * HEADS, blocks * rows), F32),
            pltpu.VMEM(((blocks - 1) * rows, width), BF),
            pltpu.VMEM((blocks - 1, 16, width), BF),
            pltpu.SemaphoreType.DMA((2 * blocks - 2,)),
        ],
    )
    if not square:
        proj_keep, proj_send = own_half(*jnp.split(proj_keep, 3, axis=1))
    qkv_source = (first_in, first_pair, proj_keep, swap(proj_send))
    grad_tokens, table = call(
        last_grad_kernel,
        [grad_queries, tie(grad_keys, proj_send), grad_values, w_qkv, tokens[0], modulation, grad_one, table],
        [stream, (modulation.shape, F32)],
    )

    table_rows = table.reshape(dp_count, sp_count, -1).transpose(1, 0, 2).reshape(sp_count, 3, -1)
    table_rows = table_rows.transpose(1, 0, 2).reshape(3, 2 * width)
    text_part = lax.psum_scatter(
        jnp.concatenate([grad_text, table_rows], axis=0), "sp", scatter_dimension=1, tiled=True
    )

    def caption_sum(late):
        part = tie(text_part, late)
        part_ckv = matmul_tn(caption_rows, part[:live].astype(BF)).astype(BF).reshape(dp_count, -1, part.shape[1])
        table_part = part[live:].reshape(dp_count, 1, -1)
        table_size = table_part.shape[2]
        table_part = jnp.pad(table_part, ((0, 0), (0, 15), (0, part.shape[1] - table_size))).astype(BF)
        tall = part_ckv.shape[1]
        both = jnp.concatenate([part_ckv, table_part], axis=1).reshape(dp_count * (tall + 16), -1)
        both = lax.psum_scatter(both, "dp", scatter_dimension=0, tiled=True)
        both = both.astype(F32)
        return both[:tall], both[tall, :table_size]

    late = None
    if square:
        late = down_sum.send(up_sum.send(table))
        qkv_sum = sum_both((tie(first_in, late), *qkv_source[1:]), slice_of(w_qkv))
        late = next(qkv_sum)
        for step in (up_sum, down_sum, small_sum, qkv_sum):
            late = step.send(late)
        final_ckv, final_table = caption_sum(late)
        for step in (small_sum, up_sum, down_sum, qkv_sum, small_sum):
            late = step.send(late)
        final_up = up_sum.send(late)
        final_down = down_sum.send(final_up)
        late = qkv_sum.send(tie(final_down, final_ckv))
        final_small = small_sum.send(late)
        final_qkv = qkv_sum.send(final_small[0])
    else:
        final_ckv, final_table = caption_sum(table)
        small_pair, small_got = swap(acts), swap(small_send)
        small = [
            (acts[i * rows : (i + 1) * rows], small_pair[i * rows : (i + 1) * rows], small_keep, small_got)
            for i in range(3)
        ]
        up_source = (up_pack[:, :width], up_pair[:, :width], pre_keep, up_pair[:, width:])
        final_small = plain_sum(small, slice_of(w_out))
        (final_down,) = plain_sum([down_source], slice_of(w_down))
        (final_up,) = plain_sum([up_source], slice_of(w_up))
        (final_qkv,) = plain_sum([qkv_source], slice_of(w_qkv))
    return (
        stream_three[None],
        grad_tokens[None],
        final_table,
        final_qkv,
        final_small[2],
        final_small[1],
        final_ckv,
        final_small[0],
        final_up,
        final_down,
    )


def solution(mesh):
    return jax.shard_map(
        local,
        mesh=mesh,
        in_specs=(
            P("dp", "sp", None),
            P("dp", None),
            P("dp", None),
            P("dp", None, None),
            P(),
            P(),
            P(),
            P(),
            P(),
            P(),
            P(),
            P(),
            P(),
            P("dp", "sp", None),
        ),
        out_specs=(
            P("dp", "sp", None),
            P("dp", "sp", None),
            P(("dp", "sp")),
            P("dp", "sp"),
            P("dp", "sp"),
            P("dp", "sp"),
            P("dp", "sp"),
            P("dp", "sp"),
            P("dp", "sp"),
            P("dp", "sp"),
        ),
        check_vma=False,
    )
```

```python
import functools
import math

import jax
import jax.numpy as jnp
from jax import lax
from jax.experimental import pallas as pl
from jax.experimental.pallas import tpu as pltpu
from jax.sharding import PartitionSpec as P

HEADS = 16
BIG = 1024
EPS = 1e-06
BIGNEG = -1e30
LOG2E = 1.4426950408889634
BF = jnp.bfloat16
F32 = jnp.float32
LARGE, CORE, NEAR, FAR, ROW, OTHER, ORDERS = 0, 4, 5, 6, 7, 9, 11
WIN = 256
COST_SCALE = 0.001
MIB = 1024 * 1024


def matmul(left, right):
    return jnp.dot(left, right, preferred_element_type=F32)


def matmul_tn(left, right):
    return lax.dot_general(left, right, (((0,), (0,)), ((), ())), preferred_element_type=F32)


def matmul_nt(left, right):
    return lax.dot_general(left, right, (((1,), (1,)), ((), ())), preferred_element_type=F32)


def head_window(head, width):
    size = width // HEADS
    low = head * size
    start = pl.multiple_of(jnp.minimum(low // 128 * 128, width - WIN), 128)
    lane = lax.broadcasted_iota(jnp.int32, (1, WIN), 1) + start
    return start, jnp.logical_and(lane >= low, lane < low + size)


def window(ref, start, offset=0):
    return ref[:, pl.ds(pl.multiple_of(start + offset, 128), WIN)]


def keep_columns(ref, start, mask, value):
    win = pl.ds(start, WIN)
    ref[:, win] = jnp.where(mask, value, ref[:, win])


def blockwise(function, arrays, high, wide=None):
    rows, columns = arrays[0].shape
    strips = []
    for low in range(0, rows, high):
        pieces = []
        for left in range(0, columns, wide or columns):
            block = [
                array[
                    slice(low, low + high) if array.shape[0] > 1 else slice(None),
                    slice(left, left + wide) if wide and array.shape[1] > 1 else slice(None),
                ]
                for array in arrays
            ]
            pieces.append(function(*block))
        strips.append([jnp.concatenate(parts, axis=1) if len(parts) > 1 else parts[0] for parts in zip(*pieces)])
    return [jnp.concatenate(parts, axis=0) for parts in zip(*strips)]


def each_head(body, unroll=4):
    def step(head, carry):
        body(head)
        return carry

    lax.fori_loop(0, HEADS, step, 0, unroll=unroll)


def fetch(sems, *pairs):
    copies = [pltpu.make_async_copy(source, target, sems.at[i]) for i, (source, target) in enumerate(pairs)]
    for copy in copies:
        copy.start()
    return [copy.wait for copy in copies]


def attend(big, own_ref, far_ref, out_ref, lse_ref, factor):
    width = out_ref.shape[1]
    scale = factor * LOG2E

    def run(sides):
        def one_head(head):
            start, mask = head_window(head, width)
            query = window(own_ref, start) * mask.astype(BF)
            scores = [matmul_nt(query, window(side, start, key)) for side, key in sides]

            def soften(*scores):
                top = functools.reduce(jnp.maximum, [jnp.max(s, axis=1, keepdims=True) for s in scores])
                raised = [jnp.exp2((s - top) * scale) for s in scores]
                total = sum(jnp.sum(r, axis=1, keepdims=True) for r in raised)
                inverse = 1.0 / total
                return (*[(r * inverse).astype(BF) for r in raised], top * scale + jnp.log2(total))

            *weights, lse = blockwise(soften, scores, 32)
            result = sum(
                matmul(weight, window(side, start, key + width)) for weight, (side, key) in zip(weights, sides)
            )
            keep_columns(out_ref, start, mask, result.astype(BF))
            lane = lax.broadcasted_iota(jnp.int32, (1, 128), 1)
            lse_ref[...] = jnp.where(lane == head, lse, lse_ref[...])

        each_head(one_head)

    lse_ref[...] = jnp.zeros_like(lse_ref)

    @pl.when(big)
    def _():
        run([(own_ref, width), (far_ref, 0)])

    @pl.when(jnp.logical_not(big))
    def _():
        run([(own_ref, width)])


def query_grad_kernel(big_ref, own_ref, far_ref, pack_ref, stat_ref, out_ref, *, factor):
    rows, width = out_ref.shape
    scale = factor * LOG2E

    def run(sides):
        def one_head(head):
            start, mask = head_window(head, width)
            keep = mask.astype(BF)
            query = window(own_ref, start) * keep
            grad = window(pack_ref.at[0:rows, :], start) * keep
            lane = lax.broadcasted_iota(jnp.int32, (1, 128), 1)
            stat = stat_ref[...]
            lse = jnp.sum(jnp.where(lane == head, stat, 0.0), axis=1, keepdims=True)
            delta = jnp.sum(jnp.where(lane == head + HEADS, stat, 0.0), axis=1, keepdims=True)
            total = None
            for side, offset in sides:
                key = window(side, start, offset)
                scores = matmul_nt(query, key)
                grad_prob = matmul_nt(grad, window(side, start, offset + width))
                (grad_score,) = blockwise(
                    lambda s, g, lse, delta: ((jnp.exp2(s * scale - lse) * (g - delta)).astype(BF),),
                    [scores, grad_prob, lse, delta],
                    64,
                    256,
                )
                part = matmul(grad_score, key)
                total = part if total is None else total + part
            keep_columns(out_ref, start, mask, (total * factor).astype(BF))

        each_head(one_head, 8)

    @pl.when(big_ref[0] == 1)
    def _():
        run([(own_ref, width), (far_ref, 0)])

    @pl.when(big_ref[0] == 0)
    def _():
        run([(own_ref, width)])


def key_grad_kernel(flag_ref, own, far, pack, dq, both, third, ahead, back, *refs, factor, count):
    dk, dv, keep_out, send_out, stats, grads, tails, sems = refs
    own_ref, far_ref, pack_ref, dq_ref = (slot.ref for slot in (own, far, pack, dq))
    dk_ref, dv_ref, keep_ref, send_ref = (slot.ref for slot in (dk, dv, keep_out, send_out))
    rows, width = dk_ref.shape
    tall = rows + 16

    def copies(block, source, low):
        return (
            pltpu.make_async_copy(
                source.at[low : low + rows, :], grads.at[block * rows : (block + 1) * rows, :], sems.at[2 * block]
            ),
            pltpu.make_async_copy(source.at[low + rows : low + tall, :], tails.at[block], sems.at[2 * block + 1]),
        )

    def begin(block, flag, first, second):
        for value, (source, low) in ((1, first), (0, second)):

            @pl.when(flag == value)
            def _(source=source, low=low):
                for copy in copies(block, source, low):
                    copy.start()

    for copy in copies(0, both, 0):
        copy.start()
    begin(1, flag_ref[2], (both, tall), (third, 0))
    begin(2, flag_ref[3], (ahead, 0), (back, 0))
    blocks = 4
    for slot in (own, far, pack, dq):
        slot.start()
    for block in range(blocks - 1):
        for copy in copies(block, both, 0):
            copy.wait()
    for slot in (own, far, pack, dq):
        slot.wait()
    scale = factor * LOG2E

    def unpack(block, both):
        both = both.astype(F32)
        joined = both[:8] + both[8:]
        for group in range(4):
            stats[8 * group : 8 * group + 8, block * rows : block * rows + rows] = joined[
                :, group * rows : group * rows + rows
            ]

    unpack(0, pack_ref[rows:, :])
    for block in range(blocks - 1):
        unpack(block + 1, tails[block])

    def run(parts):
        def one_head(head):
            start, mask = head_window(head, width)
            keep = mask.astype(BF)
            key = window(own_ref, start, width) * keep
            value = window(own_ref, start, 2 * width) * keep
            lse = stats[pl.ds(head, 1), :]
            delta = stats[pl.ds(head + HEADS, 1), :]
            grad_key = grad_value = 0.0
            for query_ref, grad_ref, low, high in parts:
                query, grad = window(query_ref, start), window(grad_ref.at[0 : high - low, :], start)
                scores = matmul_nt(key, query)
                grad_prob = matmul_nt(value, grad)

                def score_grad(s, g, lse, delta):
                    prob = jnp.exp2(s * scale - lse)
                    return prob.astype(BF), (prob * (g - delta)).astype(BF)

                prob, grad_score = blockwise(
                    score_grad, [scores, grad_prob, lse[:, low:high], delta[:, low:high]], 64, 256
                )
                grad_value = grad_value + matmul(prob, grad)
                grad_key = grad_key + matmul(grad_score, query)
            keep_columns(dk_ref, start, mask, (grad_key * factor).astype(BF))
            keep_columns(dv_ref, start, mask, grad_value.astype(BF))

        each_head(one_head, 8)

    local = (own_ref, pack_ref, 0, rows)
    @pl.when(flag_ref[0] == 1)
    def _():
        run([local, (far_ref, grads, rows, blocks * rows)])

    @pl.when(flag_ref[0] == 0)
    def _():
        run([local])

    dk.send()
    dv.send()
    if count:
        for core in (0, 1):

            @pl.when(flag_ref[CORE] == core)
            def _(core=core):
                grads = [ref[...] for ref in (dq_ref, dk_ref, dv_ref)]
                keep_ref[...] = half_columns(grads, core, count, True, keep_ref.shape[1])
                send_ref[...] = half_columns(grads, 1 - core, count, True, send_ref.shape[1])

    else:
        for index, ref in enumerate((dq_ref, dk_ref, dv_ref)):
            keep_ref[:, index * width : (index + 1) * width] = ref[...]


def text_probs(query, key, scale, live, axis):
    scores = matmul_nt(query, key) if axis else matmul_nt(key, query)
    shape = (1, scores.shape[1]) if axis else (scores.shape[0], 1)
    scores = jnp.where(lax.broadcasted_iota(jnp.int32, shape, axis) < live, scores, BIGNEG)
    raised = jnp.exp2((scores - jnp.max(scores, axis=axis, keepdims=True)) * scale)
    return raised * (1.0 / jnp.sum(raised, axis=axis, keepdims=True))


def normal(stream):
    centred = stream - jnp.mean(stream, axis=-1, keepdims=True)
    spread = lax.rsqrt(jnp.mean(centred * centred, axis=-1, keepdims=True) + EPS)
    return centred * spread, spread


def norm_back(normed, spread, scale, grad):
    scaled = grad * (1.0 + scale)
    back = spread * (
        scaled
        - jnp.mean(scaled, axis=-1, keepdims=True)
        - normed * jnp.mean(scaled * normed, axis=-1, keepdims=True)
    )
    return back, jnp.sum(grad, axis=0, keepdims=True), jnp.sum(grad * normed, axis=0, keepdims=True)


def middle(tokens_ref, mod_ref, att_ref, weights, text_ref, refs, factor, live):
    branch_ref, cross_in_ref, queries_ref, mixed_ref, stream_ref, second_ref = refs
    width = tokens_ref.shape[1]
    out_w_ref, query_w_ref, cross_w_ref = weights
    branch = matmul(att_ref[...], out_w_ref[...])
    branch_ref[...] = branch
    stream = tokens_ref[...].astype(F32) + mod_ref[2:3, :] * branch
    stream_ref[...] = stream
    cross_in = stream.astype(BF)
    cross_in_ref[...] = cross_in
    queries_ref[...] = matmul(cross_in, query_w_ref[...]).astype(BF)

    def one_head(head):
        start, mask = head_window(head, width)
        query = window(queries_ref, start) * mask.astype(BF)
        probs = text_probs(query, window(text_ref, start), factor * LOG2E, live, 1)
        result = matmul(probs.astype(BF), window(text_ref, start, width))
        keep_columns(mixed_ref, start, mask, result.astype(BF))

    each_head(one_head, 8)
    stream = stream_ref[...] + matmul(mixed_ref[...], cross_w_ref[...])
    stream_ref[...] = stream
    scale, shift = 1.0 + mod_ref[4:5, :], mod_ref[3:4, :]
    for low in range(0, stream.shape[0], 16):
        part = stream_ref[low : low + 16, :]
        second_ref[low : low + 16, :] = (normal(part)[0] * scale + shift).astype(BF)


def forward_kernel(
    flag_ref, own, far, tokens, mod, text, out_w, query_w, cross_w, grad, cot, up_hbm, down_hbm,
    acts, up_pack, hidden, keep,
    out, one, small_keep, small_send, text_grad, pack, stat, table,
    up, down, sems, kept0, kept1, lse, branch_ref, queries, stream, mlp_out, back,
    grad_mixed, grad_queries, text_key, text_value, *, factor, live, count
):
    kept = (kept0, kept1)
    rows, width = tokens.ref.shape
    mixed, cross_in, att = (acts.ref.at[i * rows : (i + 1) * rows, :] for i in range(3))
    second = up_pack.ref.at[:, 0:width]
    own.start()
    far.start()
    own.wait()
    far.wait()
    late = (tokens, mod, text, out_w, query_w, cross_w, grad, cot)
    for slot in late:
        slot.start()
    tile = down.shape[1]
    tiles = down_hbm.shape[0] // tile
    ring = down.shape[0]

    def copies(step):
        half = tile // 2
        slot = step % ring
        pairs = []
        for part in (0, 1):
            rows = slice(part * up_hbm.shape[0] // 2, (part + 1) * up_hbm.shape[0] // 2)
            pairs.append((up_hbm.at[rows, step * tile : (step + 1) * tile], up.at[slot, rows, :]))
            rows = slice(part * half, (part + 1) * half)
            pairs.append((down_hbm.at[step * tile + part * half : step * tile + (part + 1) * half, :], down.at[slot, rows, :]))
        return [pltpu.make_async_copy(a, b, sems.at[slot, i]) for i, (a, b) in enumerate(pairs)]

    for step in range(min(ring, tiles)):
        for copy in copies(step):
            copy.start()
    attend(flag_ref[LARGE] == 1, own.ref, far.ref, att, lse, factor)
    for slot in late:
        slot.wait()
    weights = (out_w.ref, query_w.ref, cross_w.ref)
    outs = (branch_ref, cross_in, queries, mixed, stream, second)
    middle(tokens.ref, mod.ref, att, weights, text.ref, outs, factor, live)
    acts.send()

    root = math.sqrt(2.0 / math.pi)

    def both(step):
        if step < tiles:
            for copy in copies(step):
                copy.wait()
            pre = matmul(second[...], up[step % ring])
            slope = matmul_nt(grad.ref[...], down[step % ring])
        if step > 0:
            before = (step - 1) % ring
            ahead = hidden.ref[:, (step - 1) * tile : step * tile]
            behind = kept[(step - 1) % 2][...]
            branch = matmul(ahead, down[before])
            result = matmul_nt(behind, up[before])
        if step < tiles:

            def bent(pre, grad):
                square = pre * pre
                bend = jnp.tanh(pre * (root * 0.044715 * square + root))
                half = 0.5 * bend + 0.5
                rise = (3 * root * 0.044715 * square + root) * pre
                slope = half + 0.5 * rise * (1.0 - bend * bend)
                return (pre * half).astype(BF), (grad * slope).astype(BF)

            ahead, behind = blockwise(bent, [pre, slope], 64, 128)
            kept[step % 2][...] = behind
            hidden.ref[:, step * tile : (step + 1) * tile] = ahead
            if count:
                size = tile // 2
                body, tail = slice_parts(size)
                group = step % 2 * keep.ref.shape[1] // 2
                spots = (
                    (group + step // 2 * body, 0, body),
                    (group + tiles // 2 * body + step // 2 * tail, body, tail),
                )
                for core in (0, 1):

                    @pl.when(flag_ref[CORE] == core)
                    def _(core=core):
                        for at, low, wide in spots:
                            mine, other = core * size + low, (1 - core) * size + low
                            keep.ref[:, at : at + wide] = behind[:, mine : mine + wide]
                            up_pack.ref[:, width + at : width + at + wide] = behind[:, other : other + wide]

            else:
                keep.ref[:, step * tile : (step + 1) * tile] = behind
        if step > 0:
            if step == 1:
                mlp_out[...] = branch
                back[...] = result
            else:
                mlp_out[...] += branch
                back[...] += result
            if step - 1 + ring < tiles:
                for copy in copies(step - 1 + ring):
                    copy.start()

    for step in range(tiles):
        both(step)
    hidden.send()
    keep.send()
    up_pack.send()
    both(tiles)
    middle_grad(
        flag_ref, back, stream, cot.ref, mlp_out, mod.ref, branch_ref, att, lse, queries, text.ref, weights,
        out, one, small_keep, small_send, text_grad, pack, stat, table,
        grad_mixed, grad_queries, text_key, text_value, factor, live, count,
    )


def middle_grad(
    flag_ref, second_grad_ref, stream_ref, cot_ref, mlp_ref, mod_ref, branch_ref, att_ref, lse_ref, queries_ref, text_ref,
    weights, out, one, keep, send, text_grad, pack, stat_out, table,
    mixed, grad_queries, text_key, text_value, factor, live, count
):
    out_w_ref, query_w_ref, cross_w_ref = weights
    one_ref, keep_ref, send_ref, text_grad_ref, pack_ref, stat_ref, table_ref = (
        slot.ref for slot in (one, keep, send, text_grad, pack, stat_out, table)
    )
    rows, width = cot_ref.shape
    gate, scale = mod_ref[5:6, :], 1.0 + mod_ref[4:5, :]
    sums = [0.0] * 3
    for low in range(0, rows, 16):
        part = slice(low, low + 16)
        cot, stream, mlp, grad = cot_ref[part, :].astype(F32), stream_ref[part, :], mlp_ref[part, :], second_grad_ref[part, :]
        out.ref[part, :] = stream + gate * mlp
        normed, spread = normal(stream)
        scaled = grad * scale
        back = spread * (
            scaled
            - jnp.mean(scaled, axis=-1, keepdims=True)
            - normed * jnp.mean(scaled * normed, axis=-1, keepdims=True)
        )
        one_ref[part, :] = cot + back
        sums = [total + term for total, term in zip(sums, (grad, grad * normed, cot * mlp))]
    out.send()
    table_ref[...] = jnp.zeros_like(table_ref)
    for index, total in enumerate(sums):
        table_ref[3 + index : 4 + index, :] = jnp.sum(total, axis=0, keepdims=True)
    grad_cross = one_ref[...].astype(BF)
    mixed[...] = matmul_nt(grad_cross, cross_w_ref[...]).astype(BF)

    def one_head(head):
        start, mask = head_window(head, width)
        keep = mask.astype(BF)
        query = window(queries_ref, start)
        grad = window(mixed, start)
        key = window(text_ref, start) * keep
        probs = text_probs(query, key, factor * LOG2E, live, 0)
        grad_probs = matmul_nt(window(text_ref, start, width) * keep, grad)
        inner = jnp.sum(probs * grad_probs, axis=0, keepdims=True)
        grad_scores = (probs * (grad_probs - inner)).astype(BF)
        keep_columns(grad_queries, start, mask, (matmul_tn(grad_scores, key) * factor).astype(BF))
        keep_columns(text_key, start, mask, matmul(grad_scores, query) * factor)
        keep_columns(text_value, start, mask, matmul(probs.astype(BF), grad))

    each_head(one_head, 8)
    text_grad_ref[:, :width] = text_key[0:live, :]
    text_grad_ref[:, width:] = text_value[0:live, :]
    text_grad.send()
    grad_cq = grad_queries[...]
    grad_one = one_ref[...] + matmul_nt(grad_cq, query_w_ref[...])
    one_ref[...] = grad_one
    table_ref[2:3, :] = jnp.sum(grad_one * branch_ref[...], axis=0, keepdims=True)
    grad_attn = (mod_ref[2:3, :] * grad_one).astype(BF)
    grad_att = matmul_nt(grad_attn, out_w_ref[...]).astype(BF)
    pack_ref[0:rows, :] = grad_att

    product = grad_att.astype(F32) * att_ref[...].astype(F32)
    upper = product.astype(BF)
    lower = (product - upper.astype(F32)).astype(BF)
    size = width // HEADS
    column = lax.broadcasted_iota(jnp.int32, (width, 128), 0)
    low = (lax.broadcasted_iota(jnp.int32, (width, 128), 1) - HEADS) * size
    pick = jnp.logical_and(column >= low, column < low + size).astype(BF)
    stat = lse_ref[...] + matmul(upper, pick) + matmul(lower, pick)
    stat_ref[...] = stat
    turned = stat.T
    upper = [turned[8 * g : 8 * g + 8, :].astype(BF).astype(F32) for g in range(4)]
    lower = [turned[8 * g : 8 * g + 8, :] - part for g, part in enumerate(upper)]
    both = [jnp.concatenate(pair, axis=0) for pair in zip(upper, lower)]
    pack_ref[rows : rows + 16, :] = side_by_side(both, width).astype(BF)
    for slot in (pack, stat_out, one, table):
        slot.send()

    if count:
        for core in (0, 1):

            @pl.when(flag_ref[CORE] == core)
            def _(core=core):
                grads = [grad_cross, grad_cq, grad_attn]
                keep_ref[...] = half_columns(grads, core, count, False, keep_ref.shape[1])
                send_ref[...] = half_columns(grads, 1 - core, count, False, send_ref.shape[1])

    else:
        for index, grad in enumerate((grad_cross, grad_cq, grad_attn)):
            keep_ref[:, index * width : (index + 1) * width] = grad


def last_grad_kernel(
    dq_ref, dk_ref, dv_ref, weight_ref, tokens_ref, mod_ref, one_ref, table_in_ref, out_ref, table_ref
):
    width = tokens_ref.shape[1]
    grad = sum(
        matmul_nt(ref[...], weight_ref[:, part * width : (part + 1) * width])
        for part, ref in enumerate((dq_ref, dk_ref, dv_ref))
    )
    normed, spread = normal(tokens_ref[...].astype(F32))
    back, shift, scale = norm_back(normed, spread, mod_ref[1:2, :], grad)
    out_ref[...] = one_ref[...] + back
    table_ref[...] = table_in_ref[...]
    table_ref[0:1, :] = shift
    table_ref[1:2, :] = scale


def side_by_side(pieces, width):
    missing = width - sum(piece.shape[1] for piece in pieces)
    if missing:
        pieces = [*pieces, jnp.zeros((pieces[0].shape[0], missing), pieces[0].dtype)]
    return pieces[0] if len(pieces) == 1 else jnp.concatenate(pieces, axis=1)


def lanes(width):
    return -(-width // 128) * 128


def slice_parts(size):
    return size // 128 * 128, size % 128


def half_columns(grads, core, count, joined, wide):
    if not joined:
        picked = []
        for grad in grads:
            size = grad.shape[1] // count
            low = [(2 * chip + core) * size for chip in (*range(0, count // 2, 2), *range(1, count // 2, 2))]
            picked.append(
                side_by_side([grad[:, at : at + size] for at in low], wide // len(grads))
            )
        return side_by_side(picked, wide)
    grad = grads[0] if len(grads) == 1 else jnp.concatenate(grads, axis=1)
    size = grad.shape[1] // count
    body, _ = slice_parts(size)
    picked = []
    for parity in (0, 1):
        low = [(2 * chip + core) * size for chip in range(parity, count // 2, 2)]
        picked += [grad[:, at : at + body] for at in low]
        picked.append(side_by_side([grad[:, at + body : at + size] for at in low], 128))
    return side_by_side(picked, wide)


def halves_kernel(core_ref, *refs, count, joined):
    keep_ref, send_ref = refs[-2:]
    for core in (0, 1):

        @pl.when(core_ref[CORE] == core)
        def _(core=core):
            grads = [ref[...] for ref in refs[:-2]]
            keep_ref[...] = half_columns(grads, core, count, joined, keep_ref.shape[1])
            send_ref[...] = half_columns(grads, 1 - core, count, joined, send_ref.shape[1])


def store_halves(flag, stores, pieces):
    for value in (0, 1):

        @pl.when(flag == value)
        def _(value=value):
            for store, piece in zip(stores, (pieces[1 - value], pieces[value])):
                store(piece())


def into(ref):
    def store(value):
        ref[:, : value.shape[1]] = value.astype(ref.dtype)

    return store


def add(*terms):
    return sum(term.astype(F32) for term in terms)


def sending(buffers, sems, out):
    state = {"count": 0}

    def wait(slot):
        pltpu.make_async_copy(buffers.at[slot], out, sems.at[slot]).wait()

    def put(pieces, targets):
        slot = state["count"] % 2
        if state["count"] >= 2:
            wait(slot)
        at = 0
        for piece in pieces:
            buffers[slot, at : at + piece.shape[0], : piece.shape[1]] = piece
            at += piece.shape[0]
        for condition, target in targets:
            copy = pltpu.make_async_copy(buffers.at[slot], target, sems.at[slot])
            if condition is None:
                copy.start()
            else:
                pl.when(condition)(copy.start)
        state["count"] += 1

    def done():
        for slot in range(min(2, state["count"])):
            wait(slot)

    return put, done


def wide_grad_kernel(order_ref, x0_hbm, x1_hbm, g0_hbm, g1_hbm, *refs, mode, first, columns):
    number = 2 if mode == "rows" else 4
    outs, (x_ref, g_ref, turned, buffers, sems, out_sems) = refs[:number], refs[number:]
    rows, width = x0_hbm.shape[0], x_ref.shape[1]
    x0_hbm, x1_hbm, g0_hbm, g1_hbm = (
        hbm if part is None else hbm.at[:, part] for hbm, part in zip((x0_hbm, x1_hbm, g0_hbm, g1_hbm), columns)
    )
    waits = fetch(
        sems,
        (x0_hbm, x_ref.at[0:rows, :]),
        (x1_hbm, x_ref.at[rows : 2 * rows, :]),
        (g0_hbm, g_ref.at[0:rows, :]),
        (g1_hbm, g_ref.at[rows : 2 * rows, :]),
    )
    for part in (0, 1):
        waits[part]()
        for low in range(0, width, 128):
            turned[low : low + 128, part * rows : (part + 1) * rows] = x_ref[
                part * rows : (part + 1) * rows, low : low + 128
            ].T
    waits[2]()
    waits[3]()
    tall = width // 4
    put, done = sending(buffers, out_sems, outs[0].at[0])
    half = g_ref.shape[1] // 2
    for step in range(4):
        here = pl.ds(pl.multiple_of((order_ref[ORDERS + 4 * first + step] if mode == "rows" else step) * tall, 16), tall)
        if mode == "rows":
            total = matmul(turned[here, :], g_ref[...]).astype(BF)
            put([total], [(None, outs[step // 2].at[step % 2])])
        else:
            for p in (0, 1):
                total = matmul(turned[here, :], g_ref[:, p * half : (p + 1) * half]).astype(BF)
                place, second = (step >> p) & 1, (step >> (1 - p)) & 1
                mine = order_ref[ROW + p]
                put(
                    [total],
                    [(mine != place, outs[2 * p].at[second]), (mine == place, outs[2 * p + 1].at[second])],
                )
    done()


def tall_grad_kernel(order_ref, *refs, count, mode, first, columns):
    sources, g0_hbm, g1_hbm = refs[: 2 * count], refs[2 * count], refs[2 * count + 1]
    outs, (x_ref, g_ref, turned, buffers, sems, out_sems) = refs[2 * count + 2 : 2 * count + 4], refs[2 * count + 4 :]
    rows = g0_hbm.shape[0]
    sources = [hbm if part is None else hbm.at[part, :] for hbm, part in zip(sources, columns)]
    pairs = [(g0_hbm, g_ref.at[0:rows, :]), (g1_hbm, g_ref.at[rows : 2 * rows, :])]
    for i, source in enumerate(sources):
        pairs.append((source, x_ref.at[i // 2, i % 2 * rows : (i % 2 + 1) * rows, :]))
    waits = fetch(sems, *pairs)
    wide = g_ref.shape[1]
    for part in (0, 1):
        waits[part]()
        for low in range(0, wide, 128):
            turned[low : low + 128, part * rows : (part + 1) * rows] = g_ref[
                part * rows : (part + 1) * rows, low : low + 128
            ].T
    for wait in waits[2:]:
        wait()
    if mode == "rows":
        high, tall = outs[0].shape[1:]
        put, done = sending(buffers, out_sems, outs[0].at[0])
        for step in range(4):
            here = pl.ds(pl.multiple_of(order_ref[ORDERS + 4 * first + step] * tall, 128), tall)
            total = matmul(turned[0:high, :], x_ref[0, :, here]).astype(BF)
            put([total], [(None, outs[step // 2].at[step % 2])])
    else:
        high = outs[0].shape[0] // count
        put, done = sending(buffers, out_sems, outs[0])
        for p in (0, 1):
            total = [
                matmul(turned[pl.ds(k * (wide // count) + p * high, high), :], x_ref[k]).astype(BF)
                for k in range(count)
            ]
            put(total, [(order_ref[NEAR] != p, outs[0]), (order_ref[NEAR] == p, outs[1])])
    done()


def add_kernel(flag_ref, *refs):
    refs[-1][...] = add(*[ref[...] for ref in refs[:-1]]).astype(BF)


def split_kernel(flag_ref, *refs, parts, axis, bit):
    views = refs[:-2]

    def joined(index):
        def piece():
            sums = [add(*[view[part] for view in views]) for part in parts[index]]
            return sums[0] if len(sums) == 1 else jnp.concatenate(sums, axis=axis)

        return piece

    store_halves(flag_ref[bit], [into(ref) for ref in refs[-2:]], [joined(0), joined(1)])


def split_pair_kernel(flag_ref, *refs):
    def group(p):
        keep, got, more = refs[3 * p : 3 * p + 3]
        return lambda: add(keep[...], got[...], more[...])

    store_halves(flag_ref[NEAR], [into(ref) for ref in refs[-2:]], [group(0), group(1)])


def last_kernel(keep_ref, got_ref, *outs, size):
    if size:
        body, tail = slice_parts(size)
        for part in (slice(0, body), slice(body, size)):
            outs[0][:, part] = add(keep_ref[:, part], got_ref[:, part])
    else:
        high, wide = outs[0].shape
        for index, out in enumerate(outs):
            part = slice(index * high, (index + 1) * high), slice(0, wide)
            out[...] = add(keep_ref[part], got_ref[part])


def prelude_kernel(place_ref, row_ref, len_ref, step_ref, embed_ref, table_ref, info_ref, mod_ref, slab, sem, *, rows):
    slots = len_ref.shape[1]
    width = table_ref.shape[1]

    def image_of(at):
        first = at * rows
        end = begin = length = step = jnp.int32(0)
        for slot in range(slots):
            count = len_ref[0, slot]
            inside = jnp.logical_and(end <= first, first < end + count)
            begin = jnp.where(inside, end, begin)
            length = jnp.where(inside, count, length)
            step = jnp.where(inside, step_ref[0, slot], step)
            end = end + count
        return (first - begin) // rows, length, step

    place = place_ref[0]
    core = place % 2
    blocks = BIG // rows
    within, length, step = image_of(place)
    pair_within = image_of(place + 1 - 2 * core)[0]
    flags = (
        length > rows,
        jnp.where(core == 0, pair_within + 1 < blocks, pair_within + 3 < blocks),
        jnp.where(core == 0, within + 1 < blocks, within >= 1),
        within + 2 < blocks,
        core == 1,
    )
    bits = [(place // 2) & 1, (place // 4) & 1, row_ref[0] & 1, (row_ref[0] >> 1) & 1]
    values = [flag.astype(jnp.int32) for flag in flags] + bits + [1 - bits[2], 1 - bits[3]]
    for first in (0, 1):
        mine = bits[2 + first]
        values += [((1 - mine if s < 2 else mine) << first) + ((s % 2) << (1 - first)) for s in range(4)]
    for index, value in enumerate(values):
        info_ref[index] = value
    copy = pltpu.make_async_copy(embed_ref.at[pl.ds(pl.multiple_of(step // 8 * 8, 8), 8), :], slab, sem)
    copy.start()
    copy.wait()
    row = slab[pl.ds(step % 8, 1), :]
    for index in range(6):
        mod_ref[index : index + 1, :] = (
            row[:, index * width : (index + 1) * width] + table_ref[index : index + 1, :]
        )


class Slot:
    def __init__(self, hbm, ref, sems, out=False):
        self.hbm, self.ref, self.out = hbm, ref, out
        self.sent = False
        self.copies = []
        for i, rows in enumerate(row_chunks(ref.shape, ref.dtype)):
            pair = (hbm.at[rows], ref.at[rows])
            self.copies.append(pltpu.make_async_copy(*(pair[::-1] if out else pair), sems.at[i]))

    def start(self):
        self.sent = True
        for copy in self.copies:
            copy.start()

    send = start

    def wait(self):
        for copy in self.copies:
            copy.wait()


def row_chunks(shape, dtype):
    if len(shape) > 2:
        return [slice(i, i + 1) for i in range(shape[0])]
    size = shape[0] * shape[1] * jnp.dtype(dtype).itemsize
    count = max([n for n in (1, 2, 3, 4, 6) if shape[0] % (16 * n) == 0 and size >= n * 200_000] or [1])
    high = shape[0] // count
    return [slice(i * high, (i + 1) * high) for i in range(count)]


def call(kernel, inputs, outs, flags=None, scratch=(), raw=(), lazy=False, limit=60):
    anywhere = pl.BlockSpec(memory_space=pl.ANY)
    arrays, views = [], []
    for entry in inputs:
        array, part = entry if isinstance(entry, tuple) else (entry, None)
        arrays.append(array)
        views.append(part)

    def view_shape(array, part):
        if part is None:
            return array.shape
        if isinstance(part, slice):
            return (array.shape[0], part.stop - part.start)
        return array.shape[1:]

    in_shapes = [view_shape(array, part) for array, part in zip(arrays, views)]
    slots = [(shape, array.dtype) for shape, array in zip(in_shapes, arrays)] + list(outs)
    held = [i for i in range(len(arrays)) if i not in raw]
    held += [len(arrays) + i for i in range(len(outs)) if "out" not in raw]
    buffers = [pltpu.VMEM(*slots[i]) for i in held]
    sems = [pltpu.SemaphoreType.DMA((len(row_chunks(*slots[i])),)) for i in held]

    def managed(*refs):
        refs = list(refs)
        flag_refs = [refs.pop(0)] if flags is not None else []
        hbm, rest = refs[: len(slots)], refs[len(slots) :]
        own, rest = rest[: len(scratch)], rest[len(scratch) :]
        views_in = []
        for ref, part in zip(hbm, views):
            if isinstance(part, slice):
                ref = ref.at[:, part]
            elif part is not None:
                ref = ref.at[flag_refs[0][part]]
            views_in.append(ref)
        given = views_in + hbm[len(arrays) :]
        for n, i in enumerate(held):
            given[i] = Slot(given[i], rest[n], rest[len(held) + n], i >= len(arrays))
        slots_in = [slot for slot in given if isinstance(slot, Slot) and not slot.out]
        slots_out = [slot for slot in given if isinstance(slot, Slot) and slot.out]
        if not lazy:
            for slot in slots_in:
                slot.start()
            for slot in slots_in:
                slot.wait()
            kernel(*flag_refs, *[getattr(slot, "ref", slot) if isinstance(slot, Slot) else slot for slot in given], *own)
        else:
            kernel(*flag_refs, *given, *own)
        for slot in slots_out:
            if not slot.sent:
                slot.send()
        for slot in slots_out:
            slot.wait()

    return pl.pallas_call(
        managed,
        in_specs=([pl.BlockSpec(memory_space=pltpu.SMEM)] if flags is not None else []) + [anywhere] * len(arrays),
        out_specs=[anywhere] * len(outs),
        out_shape=[jax.ShapeDtypeStruct(shape, dtype) for shape, dtype in outs],
        scratch_shapes=[*scratch, *buffers, *sems],
        compiler_params=pltpu.CompilerParams(vmem_limit_bytes=limit * MIB),
        cost_estimate=pl.CostEstimate(flops=1000, bytes_accessed=1000, transcendentals=0),
    )(*([] if flags is None else [flags]), *arrays)


def prelude(place, row_place, image_len, timestep, time_embed, mod_table, rows):
    smem = pl.BlockSpec(memory_space=pltpu.SMEM)
    return pl.pallas_call(
        functools.partial(prelude_kernel, rows=rows),
        in_specs=[smem] * 4 + [pl.BlockSpec(memory_space=pl.ANY), pl.BlockSpec(memory_space=pltpu.VMEM)],
        out_specs=[smem, pl.BlockSpec(memory_space=pltpu.VMEM)],
        out_shape=[jax.ShapeDtypeStruct((ORDERS + 8,), jnp.int32), jax.ShapeDtypeStruct(mod_table.shape, F32)],
        scratch_shapes=[pltpu.VMEM((8, time_embed.shape[1]), F32), pltpu.SemaphoreType.DMA],
        compiler_params=pltpu.CompilerParams(vmem_limit_bytes=60 * MIB),
    )(place.reshape(1), row_place.reshape(1), image_len, timestep, time_embed, mod_table)


def half_width(grads, count, joined):
    size = (sum(grad.shape[1] for grad in grads) if joined else grads[0].shape[1]) // count
    body, _ = slice_parts(size)
    return 2 * (count // 4 * body + 128) if joined else len(grads) * -(-count // 2 * size // 128) * 128


def halves(core, grads, count, joined):
    out = ((grads[0].shape[0], half_width(grads, count, joined)), BF)
    return call(functools.partial(halves_kernel, count=count, joined=joined), grads, [out] * 2, flags=core)


def split(flags, bit, inputs, parts, shape, axis=1):
    return call(
        functools.partial(split_kernel, parts=parts, axis=axis, bit=bit),
        inputs,
        [(shape, BF), (shape, F32)],
        flags=flags,
    )


def add_last(keep, got, size, shapes):
    return call(functools.partial(last_kernel, size=size), [keep, got], [(shape, F32) for shape in shapes])


def wide_grad(order, source, mode, first=0):
    entries = [entry if isinstance(entry, tuple) else (entry, None) for entry in source]
    source = [array for array, _ in entries]
    columns = [part and slice(part.start, part.stop or array.shape[1]) for array, part in entries]
    rows, width = source[0].shape[0], columns[0].stop if columns[0] else source[0].shape[1]
    depth = source[2].shape[1]
    wide, number = (depth, 2) if mode == "rows" else (depth // 2, 4)
    return call(
        functools.partial(wide_grad_kernel, mode=mode, first=first, columns=columns),
        source,
        [((2, width // 4, wide), BF)] * number,
        flags=order,
        raw=(0, 1, 2, 3, "out"),
        scratch=[
            pltpu.VMEM((2 * rows, width), BF),
            pltpu.VMEM((2 * rows, depth), BF),
            pltpu.VMEM((width, 2 * rows), BF),
            pltpu.VMEM((2, width // 4, wide), BF),
            pltpu.SemaphoreType.DMA((4,)),
            pltpu.SemaphoreType.DMA((2,)),
        ],
    )


def tall_grad(order, acts, keep, got, size, mode, first=0):
    count = len(acts)
    entries = [entry if isinstance(entry, tuple) else (entry, None) for pair in acts for entry in pair]
    rows, wide = keep.shape
    width = entries[0][0].shape[1]
    shape = (2, 4 * size, width // 4) if mode == "rows" else (2 * size * count, width)
    return call(
        functools.partial(
            tall_grad_kernel, count=count, mode=mode, first=first, columns=[part for _, part in entries]
        ),
        [array for array, _ in entries] + [keep, got],
        [(shape, BF)] * 2,
        flags=order,
        raw=(*range(2 * count + 2), "out"),
        scratch=[
            pltpu.VMEM((count, 2 * rows, width), BF),
            pltpu.VMEM((2 * rows, wide), BF),
            pltpu.VMEM((wide, 2 * rows), BF),
            pltpu.VMEM((2, *shape[-2:]), BF),
            pltpu.SemaphoreType.DMA((2 * count + 2,)),
            pltpu.SemaphoreType.DMA((2,)),
        ],
    )


def local(
    tokens,
    image_len,
    timestep,
    caption,
    time_embed,
    mod_table,
    w_qkv,
    w_out,
    cross_q,
    cross_kv,
    cross_out,
    w_up,
    w_down,
    cotangent,
):
    sp_count = lax.axis_size("sp")
    dp_count = lax.axis_size("dp")
    place = lax.axis_index("sp")
    row_place = lax.axis_index("dp")
    core = place % 2
    rows, width = tokens.shape[1:]
    factor = 1.0 / math.sqrt(width // HEADS)
    blocks = BIG // rows
    assert blocks == 4

    big, modulation = prelude(place, row_place, image_len, timestep, time_embed, mod_table, rows)
    shift_one, scale_one, gate_one, shift_two, scale_two, gate_two = [modulation[i] for i in range(6)]

    def tie(value, *before):
        return lax.optimization_barrier((value, *[array for array in before if array is not None]))[0]

    pairs = [(i, i ^ 1) for i in range(sp_count)]
    others = [(i, i + 1) for i in range(1, sp_count - 1, 2)] + [(i + 1, i) for i in range(1, sp_count - 1, 2)]
    ahead = [(i, i + 2) for i in range(sp_count - 2)]
    back = [(i + 2, i) for i in range(sp_count - 2)]

    def image_blocks(block, *before):
        from_back = lax.ppermute(block, "sp", ahead)
        from_ahead = lax.ppermute(block, "sp", back)
        from_ahead, from_back = tie(from_ahead, *before), tie(from_back, *before)
        send_pair = jnp.concatenate([jnp.where(big[1] == 1, from_ahead, from_back), block], axis=0)
        send_other = jnp.where(core == 1, from_back, from_ahead)
        both = lax.ppermute(send_pair, "sp", pairs)
        third = lax.ppermute(send_other, "sp", others)
        return [both, third, from_ahead, from_back], (send_pair, send_other)

    def chosen(both, third, from_ahead, from_back):
        high = both.shape[0] // 2
        return [
            both[:high],
            jnp.where(big[2] == 1, both[high:], third),
            jnp.where(big[3] == 1, from_ahead, from_back),
        ]

    def swap(array):
        return lax.ppermute(array, "sp", pairs)

    token_blocks, token_sends = image_blocks(tokens[0])

    def first_norm(block):
        return (normal(block.astype(F32))[0] * (1.0 + scale_one) + shift_one).astype(BF)

    first_in = first_norm(tokens[0])
    other_in = first_norm(jnp.concatenate(chosen(*token_blocks), axis=0))

    chips = sp_count // 2
    square = dp_count == 4 and chips == 4

    def own_half(*grads, joined=True):
        if square:
            return halves(big, grads, sp_count, joined)
        grads = [jnp.concatenate(grads, axis=1)] if joined else grads
        size = grads[0].shape[1] // sp_count
        even, odd = [
            jnp.concatenate(
                [g[:, i * size : (i + 1) * size] for g in grads for i in range(c, sp_count, 2)], axis=1
            )
            for c in (0, 1)
        ]
        return jnp.where(core == 0, even, odd), jnp.where(core == 0, odd, even)

    high = width // 4

    def to_row(array, bit):
        return lax.ppermute(array, "dp", [(i, i ^ (1 << bit)) for i in range(dp_count)])

    def to_chip(array, bit):
        return lax.ppermute(array, "sp", [(i, i ^ (2 << bit)) for i in range(sp_count)])

    def plain_sum(sources, size):
        finals = []
        for item, (x0, x1, g0, g1) in enumerate(sources):
            columns = slice(item * chips * size, (item + 1) * chips * size)
            part = (matmul_tn(x0, g0[:, columns]) + matmul_tn(x1, g1[:, columns])).astype(BF)
            part = part.reshape(dp_count, -1, chips, size).transpose(0, 2, 1, 3)
            bit = dp_count // 2
            while bit:
                mine = (row_place // bit) % 2
                part = part.reshape(2, bit, chips, -1, size)
                got = lax.ppermute(part[1 - mine], "dp", [(i, i ^ bit) for i in range(dp_count)])
                part = add(part[mine], got).astype(BF)
                bit //= 2
            part = part.reshape(chips, -1, size)
            bit = chips // 2
            while bit:
                mine = (place // 2 // bit) % 2
                part = part.reshape(2, bit, -1, size)
                got = lax.ppermute(part[1 - mine], "sp", [(i, i ^ (2 * bit)) for i in range(sp_count)])
                part = add(part[mine], got).astype(BF)
                bit //= 2
            finals.append(part[0].astype(F32))
        return finals

    def add_picked(keep, got, flag):
        return call(add_kernel, [(keep, flag), (got, flag)], [(keep.shape[1:], BF)], flags=big)

    everything = slice(None)

    def cut_slices(size):
        body, tail = slice_parts(size)
        return [
            [
                (everything, slice(h * body, (h + 1) * body)),
                (everything, slice(2 * body + h * tail, 2 * body + (h + 1) * tail)),
            ]
            for h in (0, 1)
        ]

    def sum_wide(source, first, size):
        second = 1 - first
        if size < 256:
            send, keep = tall_grad(big, [source[:2]], *source[2:], size, "rows", first)
        else:
            send, keep = wide_grad(big, source, "rows", first)
        late = yield send
        got = to_row(send, first)
        if size < 256:
            _, tall, wide = keep.shape
            flat = lambda array: array.reshape(2 * tall, wide)
            rows_at = lambda low, high: (slice(low, high),)
            groups = [
                [rows_at(y * tall + h * tall // 2, y * tall + (h + 1) * tall // 2) for y in (0, 1)]
                for h in (0, 1)
            ]
            send, keep = split(big, NEAR, [flat(tie(keep, late)), flat(got)], groups, (tall, wide), 0)
            late = yield send
            groups = [[rows_at(h * tall // 2, (h + 1) * tall // 2)] for h in (0, 1)]
            inputs = [tie(keep, late), to_chip(send, 0)]
            send, keep = split(big, ROW + second, inputs, groups, (tall // 2, wide), 0)
            late = yield send
            groups = [[rows_at(h * tall // 4, (h + 1) * tall // 4)] for h in (0, 1)]
            inputs = [tie(keep, late), to_row(send, second)]
            send, keep = split(big, FAR, inputs, groups, (tall // 4, wide), 0)
            late = yield send
            (final,) = add_last(tie(keep, late), to_chip(send, 1), 0, [(size, wide)])
            yield final.T
        else:
            (send,) = add_picked(tie(keep, late), got, OTHER + second)
            late = yield send
            tall, wide = send.shape
            more = to_row(send, second)
            inputs = [(tie(keep, late), ROW + second), (got, ROW + second), more]
            groups = [[(everything, slice(h * wide // 2, (h + 1) * wide // 2))] for h in (0, 1)]
            send, keep = split(big, NEAR, inputs, groups, (tall, wide // 2))
            late = yield send
            shape = (tall, size // 128 * 128 + 128)
            send, keep = split(big, FAR, [tie(keep, late), to_chip(send, 0)], cut_slices(size), shape)
            late = yield send
            (final,) = add_last(tie(keep, late), to_chip(send, 1), size, [(tall, size)])
            yield final

    def sum_both(source, size):
        outs = wide_grad(big, source, "both")
        late = yield outs[0]
        got = [to_row(outs[0], 0), to_row(outs[2], 1)]
        sends = [
            *add_picked(tie(outs[1], late), got[0], OTHER + 1),
            *add_picked(tie(outs[3], late), got[1], OTHER),
        ]
        late = yield sends[1]
        shape = sends[0].shape
        more = [to_row(sends[0], 1), to_row(sends[1], 0)]
        send, keep = call(
            split_pair_kernel,
            [
                (tie(outs[1], late), ROW + 1), (got[0], ROW + 1), more[0],
                (outs[3], ROW), (got[1], ROW), more[1],
            ],
            [(shape, BF), (shape, F32)],
            flags=big,
        )
        late = yield send
        shape = (shape[0], size // 128 * 128 + 128)
        send, keep = split(big, FAR, [tie(keep, late), to_chip(send, 0)], cut_slices(size), shape)
        late = yield send
        (final,) = add_last(tie(keep, late), to_chip(send, 1), size, [(high, size)])
        yield final

    def sum_chips_first(acts, keep, got, size):
        count = len(acts)
        send, keep = tall_grad(big, acts, keep, got, size, "chips")
        late = yield send
        got = to_chip(send, 0)
        groups = [
            [(everything, slice(i * high, (i + 1) * high)) for i in (h, h + 2)] for h in (0, 1)
        ]
        shape = (2 * count * size, lanes(2 * high))
        send, keep = split(big, ROW, [tie(keep, late), got], groups, shape)
        late = yield send
        got = to_row(send, 0)
        groups = [[(everything, slice(h * high, (h + 1) * high))] for h in (0, 1)]
        shape = (2 * count * size, lanes(high))
        send, keep = split(big, ROW + 1, [tie(keep, late), got], groups, shape)
        late = yield send
        got = to_row(send, 1)
        groups = [
            [(slice((2 * k + h) * size, (2 * k + h + 1) * size),) for k in range(count)] for h in (0, 1)
        ]
        shape = (count * size, lanes(high))
        send, keep = split(big, FAR, [tie(keep, late), got], groups, shape, 0)
        late = yield send
        finals = add_last(tie(keep, late), to_chip(send, 1), 0, [(size, high)] * count)
        yield [final.T for final in finals]

    caption_rows = caption[0]
    live = caption_rows.shape[0]
    padded = -(-live // 128) * 128
    caption_pad = jnp.concatenate([caption_rows, jnp.zeros((padded - live, width), BF)], axis=0)
    text = matmul(caption_pad, cross_kv).astype(BF)
    grad_mlp = (gate_two * cotangent[0].astype(F32)).astype(BF)
    mlp_keep, mlp_send = own_half(grad_mlp, joined=False)
    mlp_got = swap(mlp_send)
    first_pair = swap(first_in)
    own = matmul(tie(first_in, *token_sends), w_qkv).astype(BF)
    far_qkv = matmul(other_in, w_qkv).astype(BF)
    block = ((rows, width), BF)
    stream = ((rows, width), F32)
    stats = ((rows, 128), F32)
    units = w_up.shape[1]
    tile = units // 4
    half = half_width([w_up], sp_count, True) if square else units
    small_width = half_width([grad_mlp] * 3, sp_count, False) if square else 3 * width
    small_out = ((rows, small_width), BF)
    (
        acts, up_pack, hidden, pre_keep,
        stream_three, grad_one, small_keep, small_send, grad_text, pack, stat, table,
    ) = call(
        functools.partial(forward_kernel, factor=factor, live=live, count=sp_count if square else 0),
        [
            own, (tie(far_qkv, mlp_got, first_pair), slice(width, 3 * width)), tokens[0], modulation, text,
            w_out, cross_q, cross_out, grad_mlp, cotangent[0], w_up, w_down,
        ],
        [
            ((3 * rows, width), BF), ((rows, width + (half if square else 0)), BF), ((rows, units), BF),
            ((rows, half), BF),
            stream, stream, small_out, small_out, ((live, 2 * width), F32), ((rows + 16, width), BF), stats,
            (modulation.shape, F32),
        ],
        flags=big,
        raw=(10, 11),
        lazy=True,
        scratch=[
            pltpu.VMEM((3, width, tile), BF),
            pltpu.VMEM((3, tile, width), BF),
            pltpu.SemaphoreType.DMA((3, 4)),
            pltpu.VMEM((rows, tile), BF),
            pltpu.VMEM((rows, tile), BF),
            pltpu.VMEM((rows, 128), F32),
            pltpu.VMEM((rows, width), F32),
            pltpu.VMEM((rows, width), BF),
            *[pltpu.VMEM((rows, width), F32)] * 3,
            *[pltpu.VMEM((rows, width), BF)] * 2,
            *[pltpu.VMEM((padded, width), F32)] * 2,
        ],
        limit=63,
    )

    if not square:
        pre_keep, pre_send = own_half(pre_keep)
        up_pack = jnp.concatenate([up_pack, pre_send], axis=1)
    hidden_pair, up_pair = swap(hidden), swap(up_pack)
    if not square:
        small_keep, small_send = own_half(*jnp.split(small_keep, 3, axis=1), joined=False)
    slice_of = lambda weight: weight.shape[1] // sp_count
    down_source = (hidden, hidden_pair, mlp_keep, mlp_got)
    up_source = ((up_pack, slice(0, width)), (up_pair, slice(0, width)), pre_keep, (up_pair, slice(width, None)))
    send_down = send_up = send_small = None
    if square:
        up_sum = sum_wide((up_source[0], up_source[1], tie(pre_keep, pack), up_source[3]), 1, slice_of(w_up))
        send_up = next(up_sum)
        down_sum = sum_wide((tie(hidden, send_up), *down_source[1:]), 0, slice_of(w_down))
        send_down = next(down_sum)
        small_got = swap(tie(small_send, send_up))
        small_acts = tie(acts, send_up)
        small_acts = [small_acts, swap(small_acts)]
        small_acts = [[(part, slice(i * rows, (i + 1) * rows)) for part in small_acts] for i in range(3)]
        small_sum = sum_chips_first(small_acts, tie(small_keep, send_down), small_got, slice_of(w_out))
        send_small = next(small_sum)
    pack_blocks, pack_sends = image_blocks(pack, send_small)
    (grad_queries,) = call(
        functools.partial(query_grad_kernel, factor=factor),
        [own, (far_qkv, slice(width, 3 * width)), tie(pack, *pack_sends), stat],
        [block],
        flags=big,
    )
    proj_out = ((rows, half_width([w_qkv], sp_count, True) if square else 3 * width), BF)
    grad_keys, grad_values, proj_keep, proj_send = call(
        functools.partial(key_grad_kernel, factor=factor, count=sp_count if square else 0),
        [own, (far_qkv, slice(0, width)), tie(pack, grad_queries), grad_queries, *pack_blocks],
        [block, block, proj_out, proj_out],
        flags=big,
        raw=(4, 5, 6, 7),
        lazy=True,
        scratch=[
            pltpu.VMEM((2 * HEADS, blocks * rows), F32),
            pltpu.VMEM(((blocks - 1) * rows, width), BF),
            pltpu.VMEM((blocks - 1, 16, width), BF),
            pltpu.SemaphoreType.DMA((2 * blocks - 2,)),
        ],
    )
    if not square:
        proj_keep, proj_send = own_half(*jnp.split(proj_keep, 3, axis=1))
    qkv_source = (first_in, first_pair, proj_keep, swap(proj_send))
    grad_tokens, table = call(
        last_grad_kernel,
        [grad_queries, tie(grad_keys, proj_send), grad_values, w_qkv, tokens[0], modulation, grad_one, table],
        [stream, (modulation.shape, F32)],
    )

    table_rows = table.reshape(dp_count, sp_count, -1).transpose(1, 0, 2).reshape(sp_count, 3, -1)
    table_rows = table_rows.transpose(1, 0, 2).reshape(3, 2 * width)
    text_part = lax.psum_scatter(
        jnp.concatenate([grad_text, table_rows], axis=0), "sp", scatter_dimension=1, tiled=True
    )

    def caption_sum(late):
        part = tie(text_part, late)
        part_ckv = matmul_tn(caption_rows, part[:live].astype(BF)).astype(BF).reshape(dp_count, -1, part.shape[1])
        table_part = part[live:].reshape(dp_count, 1, -1)
        table_size = table_part.shape[2]
        table_part = jnp.pad(table_part, ((0, 0), (0, 15), (0, part.shape[1] - table_size))).astype(BF)
        tall = part_ckv.shape[1]
        both = jnp.concatenate([part_ckv, table_part], axis=1).reshape(dp_count * (tall + 16), -1)
        both = lax.psum_scatter(both, "dp", scatter_dimension=0, tiled=True)
        both = both.astype(F32)
        return both[:tall], both[tall, :table_size]

    late = None
    if square:
        late = down_sum.send(up_sum.send(table))
        qkv_sum = sum_both((tie(first_in, late), *qkv_source[1:]), slice_of(w_qkv))
        late = next(qkv_sum)
        for step in (up_sum, down_sum, small_sum, qkv_sum):
            late = step.send(late)
        final_ckv, final_table = caption_sum(late)
        for step in (up_sum, down_sum, small_sum, qkv_sum, small_sum):
            late = step.send(late)
        final_up = up_sum.send(late)
        final_down = down_sum.send(final_up)
        late = qkv_sum.send(tie(final_down, final_ckv))
        final_small = small_sum.send(late)
        final_qkv = qkv_sum.send(final_small[0])
    else:
        final_ckv, final_table = caption_sum(table)
        small_pair, small_got = swap(acts), swap(small_send)
        small = [
            (acts[i * rows : (i + 1) * rows], small_pair[i * rows : (i + 1) * rows], small_keep, small_got)
            for i in range(3)
        ]
        up_source = (up_pack[:, :width], up_pair[:, :width], pre_keep, up_pair[:, width:])
        final_small = plain_sum(small, slice_of(w_out))
        (final_down,) = plain_sum([down_source], slice_of(w_down))
        (final_up,) = plain_sum([up_source], slice_of(w_up))
        (final_qkv,) = plain_sum([qkv_source], slice_of(w_qkv))
    return (
        stream_three[None],
        grad_tokens[None],
        final_table,
        final_qkv,
        final_small[2],
        final_small[1],
        final_ckv,
        final_small[0],
        final_up,
        final_down,
    )


def solution(mesh):
    return jax.shard_map(
        local,
        mesh=mesh,
        in_specs=(
            P("dp", "sp", None),
            P("dp", None),
            P("dp", None),
            P("dp", None, None),
            P(),
            P(),
            P(),
            P(),
            P(),
            P(),
            P(),
            P(),
            P(),
            P("dp", "sp", None),
        ),
        out_specs=(
            P("dp", "sp", None),
            P("dp", "sp", None),
            P(("dp", "sp")),
            P("dp", "sp"),
            P("dp", "sp"),
            P("dp", "sp"),
            P("dp", "sp"),
            P("dp", "sp"),
            P("dp", "sp"),
            P("dp", "sp"),
        ),
        check_vma=False,
    )
```

```python
import functools
import math

import jax
import jax.numpy as jnp
from jax import lax
from jax.experimental import pallas as pl
from jax.experimental.pallas import tpu as pltpu
from jax.sharding import PartitionSpec as P

HEADS = 16
BIG = 1024
EPS = 1e-06
BIGNEG = -1e30
LOG2E = 1.4426950408889634
BF = jnp.bfloat16
F32 = jnp.float32
LARGE, CORE, NEAR, FAR, ROW, OTHER, ORDERS = 0, 4, 5, 6, 7, 9, 11
WIN = 256
COST_SCALE = 0.001
MIB = 1024 * 1024


def matmul(left, right):
    return jnp.dot(left, right, preferred_element_type=F32)


def matmul_tn(left, right):
    return lax.dot_general(left, right, (((0,), (0,)), ((), ())), preferred_element_type=F32)


def matmul_nt(left, right):
    return lax.dot_general(left, right, (((1,), (1,)), ((), ())), preferred_element_type=F32)


def head_window(head, width):
    size = width // HEADS
    low = head * size
    start = pl.multiple_of(jnp.minimum(low // 128 * 128, width - WIN), 128)
    lane = lax.broadcasted_iota(jnp.int32, (1, WIN), 1) + start
    return start, jnp.logical_and(lane >= low, lane < low + size)


def pair_window(pair, width):
    size = width // HEADS
    low = 2 * pair * size
    start = pl.multiple_of(low // 128 * 128, 128)
    lane = lax.broadcasted_iota(jnp.int32, (1, WIN), 1) + start
    return start, [
        jnp.logical_and(lane >= low + i * size, lane < low + (i + 1) * size) for i in (0, 1)
    ]


def stacked(block, masks):
    return jnp.concatenate([block * mask.astype(block.dtype) for mask in masks], axis=0)


def keep_pair(ref, start, masks, value):
    rows = ref.shape[0]
    win = pl.ds(start, WIN)
    picked = jnp.where(masks[1], value[rows:], ref[:, win])
    ref[:, win] = jnp.where(masks[0], value[:rows], picked)


def each_pair(body, unroll=2):
    def step(pair, carry):
        body(pair)
        return carry

    lax.fori_loop(0, HEADS // 2, step, 0, unroll=unroll)


def window(ref, start, offset=0):
    return ref[:, pl.ds(pl.multiple_of(start + offset, 128), WIN)]


def keep_columns(ref, start, mask, value):
    win = pl.ds(start, WIN)
    ref[:, win] = jnp.where(mask, value, ref[:, win])


def blockwise(function, arrays, high, wide=None):
    rows, columns = arrays[0].shape
    strips = []
    for low in range(0, rows, high):
        pieces = []
        for left in range(0, columns, wide or columns):
            block = [
                array[
                    slice(low, low + high) if array.shape[0] > 1 else slice(None),
                    slice(left, left + wide) if wide and array.shape[1] > 1 else slice(None),
                ]
                for array in arrays
            ]
            pieces.append(function(*block))
        strips.append([jnp.concatenate(parts, axis=1) if len(parts) > 1 else parts[0] for parts in zip(*pieces)])
    return [jnp.concatenate(parts, axis=0) for parts in zip(*strips)]


def each_head(body, unroll=4):
    def step(head, carry):
        body(head)
        return carry

    lax.fori_loop(0, HEADS, step, 0, unroll=unroll)


def fetch(sems, *pairs):
    copies = [pltpu.make_async_copy(source, target, sems.at[i]) for i, (source, target) in enumerate(pairs)]
    for copy in copies:
        copy.start()
    return [copy.wait for copy in copies]


def attend(big, own_ref, far_ref, out_ref, lse_ref, factor):
    width = out_ref.shape[1]
    scale = factor * LOG2E

    def run(sides):
        def one_pair(pair):
            start, masks = pair_window(pair, width)
            query = stacked(window(own_ref, start), masks)
            scores = [matmul_nt(query, window(side, start, key)) for side, key in sides]
            top = functools.reduce(jnp.maximum, [jnp.max(s, axis=1, keepdims=True) for s in scores])
            raised = [jnp.exp2((s - top) * scale) for s in scores]
            total = sum(jnp.sum(r, axis=1, keepdims=True) for r in raised)
            inverse = 1.0 / total
            result = sum(
                matmul((r * inverse).astype(BF), window(side, start, key + width))
                for r, (side, key) in zip(raised, sides)
            )
            keep_pair(out_ref, start, masks, result.astype(BF))
            lse = top * scale + jnp.log2(total)
            rows = out_ref.shape[0]
            lane = lax.broadcasted_iota(jnp.int32, (1, 128), 1)
            kept = jnp.where(lane == 2 * pair + 1, lse[rows:], lse_ref[...])
            lse_ref[...] = jnp.where(lane == 2 * pair, lse[:rows], kept)

        each_pair(one_pair)

    lse_ref[...] = jnp.zeros_like(lse_ref)

    @pl.when(big)
    def _():
        run([(own_ref, width), (far_ref, 0)])

    @pl.when(jnp.logical_not(big))
    def _():
        run([(own_ref, width)])


def query_grad_kernel(big_ref, own_ref, far_ref, pack_ref, stat_ref, out_ref, *, factor):
    rows, width = out_ref.shape
    scale = factor * LOG2E

    def run(sides):
        def one_pair(pair):
            start, masks = pair_window(pair, width)
            query = stacked(window(own_ref, start), masks)
            grad = stacked(window(pack_ref.at[0:rows, :], start), masks)
            lane = lax.broadcasted_iota(jnp.int32, (1, 128), 1)
            stat = stat_ref[...]

            def column(low):
                return jnp.concatenate(
                    [
                        jnp.sum(jnp.where(lane == low + 2 * pair + i, stat, 0.0), axis=1, keepdims=True)
                        for i in (0, 1)
                    ],
                    axis=0,
                )

            lse, delta = column(0), column(HEADS)
            total = None
            for side, offset in sides:
                key = window(side, start, offset)
                prob = jnp.exp2(matmul_nt(query, key) * scale - lse)
                grad_prob = matmul_nt(grad, window(side, start, offset + width))
                grad_score = (prob * (grad_prob - delta)).astype(BF)
                part = matmul(grad_score, key)
                total = part if total is None else total + part
            keep_pair(out_ref, start, masks, (total * factor).astype(BF))

        each_pair(one_pair, 4)

    @pl.when(big_ref[0] == 1)
    def _():
        run([(own_ref, width), (far_ref, 0)])

    @pl.when(big_ref[0] == 0)
    def _():
        run([(own_ref, width)])


def key_grad_kernel(flag_ref, own, far, pack, dq, both, third, ahead, back, *refs, factor, count):
    dk, dv, keep_out, send_out, stats, grads, tails, sems = refs
    own_ref, far_ref, pack_ref, dq_ref = (slot.ref for slot in (own, far, pack, dq))
    dk_ref, dv_ref, keep_ref, send_ref = (slot.ref for slot in (dk, dv, keep_out, send_out))
    rows, width = dk_ref.shape
    tall = rows + 16

    def copies(block, source, low):
        return (
            pltpu.make_async_copy(
                source.at[low : low + rows, :], grads.at[block * rows : (block + 1) * rows, :], sems.at[2 * block]
            ),
            pltpu.make_async_copy(source.at[low + rows : low + tall, :], tails.at[block], sems.at[2 * block + 1]),
        )

    def begin(block, flag, first, second):
        for value, (source, low) in ((1, first), (0, second)):

            @pl.when(flag == value)
            def _(source=source, low=low):
                for copy in copies(block, source, low):
                    copy.start()

    for copy in copies(0, both, 0):
        copy.start()
    begin(1, flag_ref[2], (both, tall), (third, 0))
    begin(2, flag_ref[3], (ahead, 0), (back, 0))
    blocks = 4
    for slot in (own, far, pack, dq):
        slot.start()
    for block in range(blocks - 1):
        for copy in copies(block, both, 0):
            copy.wait()
    for slot in (own, far, pack, dq):
        slot.wait()
    scale = factor * LOG2E

    def unpack(block, both):
        both = both.astype(F32)
        joined = both[:8] + both[8:]
        for group in range(4):
            stats[8 * group : 8 * group + 8, block * rows : block * rows + rows] = joined[
                :, group * rows : group * rows + rows
            ]

    unpack(0, pack_ref[rows:, :])
    for block in range(blocks - 1):
        unpack(block + 1, tails[block])

    def run(parts):
        def one_pair(pair):
            start, masks = pair_window(pair, width)
            key = stacked(window(own_ref, start, width), masks)
            value = stacked(window(own_ref, start, 2 * width), masks)

            def line(at, low, high):
                return jnp.concatenate(
                    [
                        jnp.broadcast_to(stats[pl.ds(at + 2 * pair + i, 1), low:high], (rows, high - low))
                        for i in (0, 1)
                    ],
                    axis=0,
                )

            grad_key = grad_value = 0.0
            for query_ref, grad_ref, low, high in parts:
                query, grad = window(query_ref, start), window(grad_ref.at[0 : high - low, :], start)
                prob = jnp.exp2(matmul_nt(key, query) * scale - line(0, low, high))
                grad_prob = matmul_nt(value, grad)
                grad_score = (prob * (grad_prob - line(HEADS, low, high))).astype(BF)
                grad_value = grad_value + matmul(prob.astype(BF), grad)
                grad_key = grad_key + matmul(grad_score, query)
            keep_pair(dk_ref, start, masks, (grad_key * factor).astype(BF))
            keep_pair(dv_ref, start, masks, grad_value.astype(BF))

        each_pair(one_pair, 4)

    local = (own_ref, pack_ref, 0, rows)
    @pl.when(flag_ref[0] == 1)
    def _():
        run([local, (far_ref, grads, rows, blocks * rows)])

    @pl.when(flag_ref[0] == 0)
    def _():
        run([local])

    dk.send()
    dv.send()
    if count:
        for core in (0, 1):

            @pl.when(flag_ref[CORE] == core)
            def _(core=core):
                grads = [ref[...] for ref in (dq_ref, dk_ref, dv_ref)]
                keep_ref[...] = half_columns(grads, core, count, True, keep_ref.shape[1])
                send_ref[...] = half_columns(grads, 1 - core, count, True, send_ref.shape[1])

    else:
        for index, ref in enumerate((dq_ref, dk_ref, dv_ref)):
            keep_ref[:, index * width : (index + 1) * width] = ref[...]


def text_probs(query, key, scale, live, axis):
    scores = matmul_nt(query, key) if axis else matmul_nt(key, query)
    shape = (1, scores.shape[1]) if axis else (scores.shape[0], 1)
    scores = jnp.where(lax.broadcasted_iota(jnp.int32, shape, axis) < live, scores, BIGNEG)
    raised = jnp.exp2((scores - jnp.max(scores, axis=axis, keepdims=True)) * scale)
    return raised * (1.0 / jnp.sum(raised, axis=axis, keepdims=True))


def normal(stream):
    centred = stream - jnp.mean(stream, axis=-1, keepdims=True)
    spread = lax.rsqrt(jnp.mean(centred * centred, axis=-1, keepdims=True) + EPS)
    return centred * spread, spread


def norm_back(normed, spread, scale, grad):
    scaled = grad * (1.0 + scale)
    back = spread * (
        scaled
        - jnp.mean(scaled, axis=-1, keepdims=True)
        - normed * jnp.mean(scaled * normed, axis=-1, keepdims=True)
    )
    return back, jnp.sum(grad, axis=0, keepdims=True), jnp.sum(grad * normed, axis=0, keepdims=True)


def middle(tokens_ref, mod_ref, att_ref, weights, text_ref, refs, factor, live):
    branch_ref, cross_in_ref, queries_ref, mixed_ref, stream_ref, second_ref = refs
    width = tokens_ref.shape[1]
    out_w_ref, query_w_ref, cross_w_ref = weights
    branch = matmul(att_ref[...], out_w_ref[...])
    branch_ref[...] = branch
    stream = tokens_ref[...].astype(F32) + mod_ref[2:3, :] * branch
    stream_ref[...] = stream
    cross_in = stream.astype(BF)
    cross_in_ref[...] = cross_in
    queries_ref[...] = matmul(cross_in, query_w_ref[...]).astype(BF)

    def one_head(head):
        start, mask = head_window(head, width)
        query = window(queries_ref, start) * mask.astype(BF)
        probs = text_probs(query, window(text_ref, start), factor * LOG2E, live, 1)
        result = matmul(probs.astype(BF), window(text_ref, start, width))
        keep_columns(mixed_ref, start, mask, result.astype(BF))

    each_head(one_head, 8)
    stream = stream_ref[...] + matmul(mixed_ref[...], cross_w_ref[...])
    stream_ref[...] = stream
    scale, shift = 1.0 + mod_ref[4:5, :], mod_ref[3:4, :]
    for low in range(0, stream.shape[0], 16):
        part = stream_ref[low : low + 16, :]
        second_ref[low : low + 16, :] = (normal(part)[0] * scale + shift).astype(BF)


def forward_kernel(
    flag_ref, own, far, tokens, mod, text, out_w, query_w, cross_w, grad, cot, up_hbm, down_hbm,
    acts, up_pack, hidden, keep,
    out, one, small_keep, small_send, text_grad, pack, stat, table,
    up, down, sems, kept0, kept1, lse, branch_ref, queries, stream, mlp_out, back,
    grad_mixed, grad_queries, text_key, text_value, *, factor, live, count
):
    kept = (kept0, kept1)
    rows, width = tokens.ref.shape
    mixed, cross_in, att = (acts.ref.at[i * rows : (i + 1) * rows, :] for i in range(3))
    second = up_pack.ref.at[:, 0:width]
    own.start()
    far.start()
    own.wait()
    far.wait()
    late = (tokens, mod, text, out_w, query_w, cross_w, grad, cot)
    for slot in late:
        slot.start()
    tile = down.shape[1]
    tiles = down_hbm.shape[0] // tile
    ring = down.shape[0]

    def copies(step):
        half = tile // 2
        slot = step % ring
        pairs = []
        for part in (0, 1):
            rows = slice(part * up_hbm.shape[0] // 2, (part + 1) * up_hbm.shape[0] // 2)
            pairs.append((up_hbm.at[rows, step * tile : (step + 1) * tile], up.at[slot, rows, :]))
            rows = slice(part * half, (part + 1) * half)
            pairs.append((down_hbm.at[step * tile + part * half : step * tile + (part + 1) * half, :], down.at[slot, rows, :]))
        return [pltpu.make_async_copy(a, b, sems.at[slot, i]) for i, (a, b) in enumerate(pairs)]

    for step in range(min(ring, tiles)):
        for copy in copies(step):
            copy.start()
    attend(flag_ref[LARGE] == 1, own.ref, far.ref, att, lse, factor)
    for slot in late:
        slot.wait()
    weights = (out_w.ref, query_w.ref, cross_w.ref)
    outs = (branch_ref, cross_in, queries, mixed, stream, second)
    middle(tokens.ref, mod.ref, att, weights, text.ref, outs, factor, live)
    acts.send()

    root = math.sqrt(2.0 / math.pi)

    def both(step):
        if step < tiles:
            for copy in copies(step):
                copy.wait()
            pre = matmul(second[...], up[step % ring])
            slope = matmul_nt(grad.ref[...], down[step % ring])
        if step > 0:
            before = (step - 1) % ring
            ahead = hidden.ref[:, (step - 1) * tile : step * tile]
            behind = kept[(step - 1) % 2][...]
            branch = matmul(ahead, down[before])
            result = matmul_nt(behind, up[before])
        if step < tiles:

            def bent(pre, grad):
                square = pre * pre
                bend = jnp.tanh(pre * (root * 0.044715 * square + root))
                half = 0.5 * bend + 0.5
                rise = (3 * root * 0.044715 * square + root) * pre
                slope = half + 0.5 * rise * (1.0 - bend * bend)
                return (pre * half).astype(BF), (grad * slope).astype(BF)

            ahead, behind = blockwise(bent, [pre, slope], 64, 128)
            kept[step % 2][...] = behind
            hidden.ref[:, step * tile : (step + 1) * tile] = ahead
            if count:
                size = tile // 2
                body, tail = slice_parts(size)
                group = step % 2 * keep.ref.shape[1] // 2
                spots = (
                    (group + step // 2 * body, 0, body),
                    (group + tiles // 2 * body + step // 2 * tail, body, tail),
                )
                for core in (0, 1):

                    @pl.when(flag_ref[CORE] == core)
                    def _(core=core):
                        for at, low, wide in spots:
                            mine, other = core * size + low, (1 - core) * size + low
                            keep.ref[:, at : at + wide] = behind[:, mine : mine + wide]
                            up_pack.ref[:, width + at : width + at + wide] = behind[:, other : other + wide]

            else:
                keep.ref[:, step * tile : (step + 1) * tile] = behind
        if step > 0:
            if step == 1:
                mlp_out[...] = branch
                back[...] = result
            else:
                mlp_out[...] += branch
                back[...] += result
            if step - 1 + ring < tiles:
                for copy in copies(step - 1 + ring):
                    copy.start()

    for step in range(tiles):
        both(step)
    hidden.send()
    keep.send()
    up_pack.send()
    both(tiles)
    middle_grad(
        flag_ref, back, stream, cot.ref, mlp_out, mod.ref, branch_ref, att, lse, queries, text.ref, weights,
        out, one, small_keep, small_send, text_grad, pack, stat, table,
        grad_mixed, grad_queries, text_key, text_value, factor, live, count,
    )


def middle_grad(
    flag_ref, second_grad_ref, stream_ref, cot_ref, mlp_ref, mod_ref, branch_ref, att_ref, lse_ref, queries_ref, text_ref,
    weights, out, one, keep, send, text_grad, pack, stat_out, table,
    mixed, grad_queries, text_key, text_value, factor, live, count
):
    out_w_ref, query_w_ref, cross_w_ref = weights
    one_ref, keep_ref, send_ref, text_grad_ref, pack_ref, stat_ref, table_ref = (
        slot.ref for slot in (one, keep, send, text_grad, pack, stat_out, table)
    )
    rows, width = cot_ref.shape
    gate, scale = mod_ref[5:6, :], 1.0 + mod_ref[4:5, :]
    sums = [0.0] * 3
    for low in range(0, rows, 16):
        part = slice(low, low + 16)
        cot, stream, mlp, grad = cot_ref[part, :].astype(F32), stream_ref[part, :], mlp_ref[part, :], second_grad_ref[part, :]
        out.ref[part, :] = stream + gate * mlp
        normed, spread = normal(stream)
        scaled = grad * scale
        back = spread * (
            scaled
            - jnp.mean(scaled, axis=-1, keepdims=True)
            - normed * jnp.mean(scaled * normed, axis=-1, keepdims=True)
        )
        one_ref[part, :] = cot + back
        sums = [total + term for total, term in zip(sums, (grad, grad * normed, cot * mlp))]
    out.send()
    table_ref[...] = jnp.zeros_like(table_ref)
    for index, total in enumerate(sums):
        table_ref[3 + index : 4 + index, :] = jnp.sum(total, axis=0, keepdims=True)
    grad_cross = one_ref[...].astype(BF)
    mixed[...] = matmul_nt(grad_cross, cross_w_ref[...]).astype(BF)

    def one_head(head):
        start, mask = head_window(head, width)
        keep = mask.astype(BF)
        query = window(queries_ref, start)
        grad = window(mixed, start)
        key = window(text_ref, start) * keep
        probs = text_probs(query, key, factor * LOG2E, live, 0)
        grad_probs = matmul_nt(window(text_ref, start, width) * keep, grad)
        inner = jnp.sum(probs * grad_probs, axis=0, keepdims=True)
        grad_scores = (probs * (grad_probs - inner)).astype(BF)
        keep_columns(grad_queries, start, mask, (matmul_tn(grad_scores, key) * factor).astype(BF))
        keep_columns(text_key, start, mask, matmul(grad_scores, query) * factor)
        keep_columns(text_value, start, mask, matmul(probs.astype(BF), grad))

    each_head(one_head, 8)
    text_grad_ref[:, :width] = text_key[0:live, :]
    text_grad_ref[:, width:] = text_value[0:live, :]
    text_grad.send()
    grad_cq = grad_queries[...]
    grad_one = one_ref[...] + matmul_nt(grad_cq, query_w_ref[...])
    one_ref[...] = grad_one
    table_ref[2:3, :] = jnp.sum(grad_one * branch_ref[...], axis=0, keepdims=True)
    grad_attn = (mod_ref[2:3, :] * grad_one).astype(BF)
    grad_att = matmul_nt(grad_attn, out_w_ref[...]).astype(BF)
    pack_ref[0:rows, :] = grad_att

    product = grad_att.astype(F32) * att_ref[...].astype(F32)
    upper = product.astype(BF)
    lower = (product - upper.astype(F32)).astype(BF)
    size = width // HEADS
    column = lax.broadcasted_iota(jnp.int32, (width, 128), 0)
    low = (lax.broadcasted_iota(jnp.int32, (width, 128), 1) - HEADS) * size
    pick = jnp.logical_and(column >= low, column < low + size).astype(BF)
    stat = lse_ref[...] + matmul(upper, pick) + matmul(lower, pick)
    stat_ref[...] = stat
    turned = stat.T
    upper = [turned[8 * g : 8 * g + 8, :].astype(BF).astype(F32) for g in range(4)]
    lower = [turned[8 * g : 8 * g + 8, :] - part for g, part in enumerate(upper)]
    both = [jnp.concatenate(pair, axis=0) for pair in zip(upper, lower)]
    pack_ref[rows : rows + 16, :] = side_by_side(both, width).astype(BF)
    for slot in (pack, stat_out, one, table):
        slot.send()

    if count:
        for core in (0, 1):

            @pl.when(flag_ref[CORE] == core)
            def _(core=core):
                grads = [grad_cross, grad_cq, grad_attn]
                keep_ref[...] = half_columns(grads, core, count, False, keep_ref.shape[1])
                send_ref[...] = half_columns(grads, 1 - core, count, False, send_ref.shape[1])

    else:
        for index, grad in enumerate((grad_cross, grad_cq, grad_attn)):
            keep_ref[:, index * width : (index + 1) * width] = grad


def last_grad_kernel(
    dq_ref, dk_ref, dv_ref, weight_ref, tokens_ref, mod_ref, one_ref, table_ref, text_ref, out_ref, text_out, *, shape
):
    width = tokens_ref.shape[1]
    grad = sum(
        matmul_nt(ref[...], weight_ref[:, part * width : (part + 1) * width])
        for part, ref in enumerate((dq_ref, dk_ref, dv_ref))
    )
    normed, spread = normal(tokens_ref[...].astype(F32))
    back, shift, scale = norm_back(normed, spread, mod_ref[1:2, :], grad)
    out_ref[...] = one_ref[...] + back
    table = [shift, scale] + [table_ref[i : i + 1, :] for i in range(2, 6)]
    dp_count, sp_count = shape
    size = 6 * width // (dp_count * sp_count)

    def flat(low, high):
        pieces = []
        while low < high:
            row, at = divmod(low, width)
            stop = min(high, (row + 1) * width)
            pieces.append(table[row][:, at : at + stop - low])
            low = stop
        return pieces

    step = 2 * width // sp_count
    lines = [[], [], []]
    for place in range(sp_count):
        whole = [piece for i in range(dp_count) for piece in flat((i * sp_count + place) * size, (i * sp_count + place + 1) * size)]
        whole = jnp.concatenate(whole, axis=1)
        for i in range(3):
            lines[i].append(whole[:, i * step : (i + 1) * step])
    rows = [jnp.concatenate(line, axis=1) for line in lines]
    live = text_ref.shape[0]
    rows.append(jnp.zeros((128 - live - 3, 2 * width), F32))
    both = jnp.concatenate([text_ref[...]] + rows, axis=0)
    for low in range(0, 2 * width, 128):
        text_out[low : low + 128, :] = both[:, low : low + 128].T


def caption_kernel(text_ref, caption_ref, out_ref, *, blocks, size):
    live, width = caption_ref.shape
    text = text_ref[...].T
    grad = matmul_tn(caption_ref[...], text[:live].astype(BF)).astype(BF)
    tall = width // blocks
    line = jnp.concatenate([text[live + i : live + i + 1] for i in range(3)], axis=1)
    high = out_ref.shape[0] // blocks
    for block in range(blocks):
        out_ref[block * high : block * high + tall, :] = grad[block * tall : (block + 1) * tall]
        part = side_by_side([line[:, block * size : (block + 1) * size]], out_ref.shape[1])
        out_ref[block * high + tall : (block + 1) * high, :] = jnp.broadcast_to(
            part, (high - tall, out_ref.shape[1])
        ).astype(BF)


def side_by_side(pieces, width):
    missing = width - sum(piece.shape[1] for piece in pieces)
    if missing:
        pieces = [*pieces, jnp.zeros((pieces[0].shape[0], missing), pieces[0].dtype)]
    return pieces[0] if len(pieces) == 1 else jnp.concatenate(pieces, axis=1)


def lanes(width):
    return -(-width // 128) * 128


def slice_parts(size):
    return size // 128 * 128, size % 128


def half_columns(grads, core, count, joined, wide):
    if not joined:
        picked = []
        for grad in grads:
            size = grad.shape[1] // count
            low = [(2 * chip + core) * size for chip in (*range(0, count // 2, 2), *range(1, count // 2, 2))]
            picked.append(
                side_by_side([grad[:, at : at + size] for at in low], wide // len(grads))
            )
        return side_by_side(picked, wide)
    grad = grads[0] if len(grads) == 1 else jnp.concatenate(grads, axis=1)
    size = grad.shape[1] // count
    body, _ = slice_parts(size)
    picked = []
    for parity in (0, 1):
        low = [(2 * chip + core) * size for chip in range(parity, count // 2, 2)]
        picked += [grad[:, at : at + body] for at in low]
        picked.append(side_by_side([grad[:, at + body : at + size] for at in low], 128))
    return side_by_side(picked, wide)


def halves_kernel(core_ref, *refs, count, joined):
    keep_ref, send_ref = refs[-2:]
    for core in (0, 1):

        @pl.when(core_ref[CORE] == core)
        def _(core=core):
            grads = [ref[...] for ref in refs[:-2]]
            keep_ref[...] = half_columns(grads, core, count, joined, keep_ref.shape[1])
            send_ref[...] = half_columns(grads, 1 - core, count, joined, send_ref.shape[1])


def store_halves(flag, stores, pieces):
    for value in (0, 1):

        @pl.when(flag == value)
        def _(value=value):
            for store, piece in zip(stores, (pieces[1 - value], pieces[value])):
                store(piece())


def into(ref):
    def store(value):
        ref[:, : value.shape[1]] = value.astype(ref.dtype)

    return store


def add(*terms):
    return sum(term.astype(F32) for term in terms)


def sending(buffers, sems, out):
    state = {"count": 0}

    def wait(slot):
        pltpu.make_async_copy(buffers.at[slot], out, sems.at[slot]).wait()

    def put(pieces, targets):
        slot = state["count"] % 2
        if state["count"] >= 2:
            wait(slot)
        at = 0
        for piece in pieces:
            buffers[slot, at : at + piece.shape[0], : piece.shape[1]] = piece
            at += piece.shape[0]
        for condition, target in targets:
            copy = pltpu.make_async_copy(buffers.at[slot], target, sems.at[slot])
            if condition is None:
                copy.start()
            else:
                pl.when(condition)(copy.start)
        state["count"] += 1

    def done():
        for slot in range(min(2, state["count"])):
            wait(slot)

    return put, done


def wide_grad_kernel(order_ref, x0_hbm, x1_hbm, g0_hbm, g1_hbm, *refs, mode, first, columns):
    number = 2 if mode == "rows" else 4
    outs, (x_ref, g_ref, turned, buffers, sems, out_sems) = refs[:number], refs[number:]
    rows, width = x0_hbm.shape[0], x_ref.shape[1]
    x0_hbm, x1_hbm, g0_hbm, g1_hbm = (
        hbm if part is None else hbm.at[:, part] for hbm, part in zip((x0_hbm, x1_hbm, g0_hbm, g1_hbm), columns)
    )
    waits = fetch(
        sems,
        (x0_hbm, x_ref.at[0:rows, :]),
        (x1_hbm, x_ref.at[rows : 2 * rows, :]),
        (g0_hbm, g_ref.at[0:rows, :]),
        (g1_hbm, g_ref.at[rows : 2 * rows, :]),
    )
    for part in (0, 1):
        waits[part]()
        for low in range(0, width, 128):
            turned[low : low + 128, part * rows : (part + 1) * rows] = x_ref[
                part * rows : (part + 1) * rows, low : low + 128
            ].T
    waits[2]()
    waits[3]()
    tall = width // 4
    put, done = sending(buffers, out_sems, outs[0].at[0])
    half = g_ref.shape[1] // 2
    for step in range(4):
        here = pl.ds(pl.multiple_of((order_ref[ORDERS + 4 * first + step] if mode == "rows" else step) * tall, 16), tall)
        if mode == "rows":
            total = matmul(turned[here, :], g_ref[...]).astype(BF)
            put([total], [(None, outs[step // 2].at[step % 2])])
        else:
            for p in (0, 1):
                total = matmul(turned[here, :], g_ref[:, p * half : (p + 1) * half]).astype(BF)
                place, second = (step >> p) & 1, (step >> (1 - p)) & 1
                mine = order_ref[ROW + p]
                put(
                    [total],
                    [(mine != place, outs[2 * p].at[second]), (mine == place, outs[2 * p + 1].at[second])],
                )
    done()


def tall_grad_kernel(order_ref, *refs, count, mode, first, columns):
    sources, g0_hbm, g1_hbm = refs[: 2 * count], refs[2 * count], refs[2 * count + 1]
    outs, (x_ref, g_ref, turned, buffers, sems, out_sems) = refs[2 * count + 2 : 2 * count + 4], refs[2 * count + 4 :]
    rows = g0_hbm.shape[0]
    sources = [hbm if part is None else hbm.at[part, :] for hbm, part in zip(sources, columns)]
    pairs = [(g0_hbm, g_ref.at[0:rows, :]), (g1_hbm, g_ref.at[rows : 2 * rows, :])]
    for i, source in enumerate(sources):
        pairs.append((source, x_ref.at[i // 2, i % 2 * rows : (i % 2 + 1) * rows, :]))
    waits = fetch(sems, *pairs)
    wide = g_ref.shape[1]
    for part in (0, 1):
        waits[part]()
        for low in range(0, wide, 128):
            turned[low : low + 128, part * rows : (part + 1) * rows] = g_ref[
                part * rows : (part + 1) * rows, low : low + 128
            ].T
    for wait in waits[2:]:
        wait()
    if mode == "rows":
        high, tall = outs[0].shape[1:]
        put, done = sending(buffers, out_sems, outs[0].at[0])
        for step in range(4):
            here = pl.ds(pl.multiple_of(order_ref[ORDERS + 4 * first + step] * tall, 128), tall)
            total = matmul(turned[0:high, :], x_ref[0, :, here]).astype(BF)
            put([total], [(None, outs[step // 2].at[step % 2])])
    else:
        high = outs[0].shape[0] // count
        put, done = sending(buffers, out_sems, outs[0])
        for p in (0, 1):
            total = [
                matmul(turned[pl.ds(k * (wide // count) + p * high, high), :], x_ref[k]).astype(BF)
                for k in range(count)
            ]
            put(total, [(order_ref[NEAR] != p, outs[0]), (order_ref[NEAR] == p, outs[1])])
    done()


def add_kernel(flag_ref, *refs):
    refs[-1][...] = add(*[ref[...] for ref in refs[:-1]]).astype(BF)


def split_kernel(flag_ref, *refs, parts, axis, bit):
    views = refs[:-2]

    def joined(index):
        def piece():
            sums = [add(*[view[part] for view in views]) for part in parts[index]]
            return sums[0] if len(sums) == 1 else jnp.concatenate(sums, axis=axis)

        return piece

    store_halves(flag_ref[bit], [into(ref) for ref in refs[-2:]], [joined(0), joined(1)])


def split_pair_kernel(flag_ref, *refs):
    def group(p):
        keep, got, more = refs[3 * p : 3 * p + 3]
        return lambda: add(keep[...], got[...], more[...])

    store_halves(flag_ref[NEAR], [into(ref) for ref in refs[-2:]], [group(0), group(1)])


def last_kernel(keep_ref, got_ref, *outs, size):
    if size:
        body, tail = slice_parts(size)
        for part in (slice(0, body), slice(body, size)):
            outs[0][:, part] = add(keep_ref[:, part], got_ref[:, part])
    else:
        high, wide = outs[0].shape
        for index, out in enumerate(outs):
            part = slice(index * high, (index + 1) * high), slice(0, wide)
            out[...] = add(keep_ref[part], got_ref[part])


def prelude_kernel(place_ref, row_ref, len_ref, step_ref, embed_ref, table_ref, info_ref, mod_ref, slab, sem, *, rows):
    slots = len_ref.shape[1]
    width = table_ref.shape[1]

    def image_of(at):
        first = at * rows
        end = begin = length = step = jnp.int32(0)
        for slot in range(slots):
            count = len_ref[0, slot]
            inside = jnp.logical_and(end <= first, first < end + count)
            begin = jnp.where(inside, end, begin)
            length = jnp.where(inside, count, length)
            step = jnp.where(inside, step_ref[0, slot], step)
            end = end + count
        return (first - begin) // rows, length, step

    place = place_ref[0]
    core = place % 2
    blocks = BIG // rows
    within, length, step = image_of(place)
    pair_within = image_of(place + 1 - 2 * core)[0]
    flags = (
        length > rows,
        jnp.where(core == 0, pair_within + 1 < blocks, pair_within + 3 < blocks),
        jnp.where(core == 0, within + 1 < blocks, within >= 1),
        within + 2 < blocks,
        core == 1,
    )
    bits = [(place // 2) & 1, (place // 4) & 1, row_ref[0] & 1, (row_ref[0] >> 1) & 1]
    values = [flag.astype(jnp.int32) for flag in flags] + bits + [1 - bits[2], 1 - bits[3]]
    for first in (0, 1):
        mine = bits[2 + first]
        values += [((1 - mine if s < 2 else mine) << first) + ((s % 2) << (1 - first)) for s in range(4)]
    for index, value in enumerate(values):
        info_ref[index] = value
    copy = pltpu.make_async_copy(embed_ref.at[pl.ds(pl.multiple_of(step // 8 * 8, 8), 8), :], slab, sem)
    copy.start()
    copy.wait()
    row = slab[pl.ds(step % 8, 1), :]
    for index in range(6):
        mod_ref[index : index + 1, :] = (
            row[:, index * width : (index + 1) * width] + table_ref[index : index + 1, :]
        )


class Slot:
    def __init__(self, hbm, ref, sems, out=False):
        self.hbm, self.ref, self.out = hbm, ref, out
        self.sent = False
        self.copies = []
        for i, rows in enumerate(row_chunks(ref.shape, ref.dtype)):
            pair = (hbm.at[rows], ref.at[rows])
            self.copies.append(pltpu.make_async_copy(*(pair[::-1] if out else pair), sems.at[i]))

    def start(self):
        self.sent = True
        for copy in self.copies:
            copy.start()

    send = start

    def wait(self):
        for copy in self.copies:
            copy.wait()


def row_chunks(shape, dtype):
    if len(shape) > 2:
        return [slice(i, i + 1) for i in range(shape[0])]
    size = shape[0] * shape[1] * jnp.dtype(dtype).itemsize
    count = max([n for n in (1, 2, 3, 4, 6) if shape[0] % (16 * n) == 0 and size >= n * 200_000] or [1])
    high = shape[0] // count
    return [slice(i * high, (i + 1) * high) for i in range(count)]


def call(kernel, inputs, outs, flags=None, scratch=(), raw=(), lazy=False, limit=60):
    anywhere = pl.BlockSpec(memory_space=pl.ANY)
    arrays, views = [], []
    for entry in inputs:
        array, part = entry if isinstance(entry, tuple) else (entry, None)
        arrays.append(array)
        views.append(part)

    def view_shape(array, part):
        if part is None:
            return array.shape
        if isinstance(part, slice):
            return (array.shape[0], part.stop - part.start)
        return array.shape[1:]

    in_shapes = [view_shape(array, part) for array, part in zip(arrays, views)]
    slots = [(shape, array.dtype) for shape, array in zip(in_shapes, arrays)] + list(outs)
    held = [i for i in range(len(arrays)) if i not in raw]
    held += [len(arrays) + i for i in range(len(outs)) if "out" not in raw]
    buffers = [pltpu.VMEM(*slots[i]) for i in held]
    sems = [pltpu.SemaphoreType.DMA((len(row_chunks(*slots[i])),)) for i in held]

    def managed(*refs):
        refs = list(refs)
        flag_refs = [refs.pop(0)] if flags is not None else []
        hbm, rest = refs[: len(slots)], refs[len(slots) :]
        own, rest = rest[: len(scratch)], rest[len(scratch) :]
        views_in = []
        for ref, part in zip(hbm, views):
            if isinstance(part, slice):
                ref = ref.at[:, part]
            elif part is not None:
                ref = ref.at[flag_refs[0][part]]
            views_in.append(ref)
        given = views_in + hbm[len(arrays) :]
        for n, i in enumerate(held):
            given[i] = Slot(given[i], rest[n], rest[len(held) + n], i >= len(arrays))
        slots_in = [slot for slot in given if isinstance(slot, Slot) and not slot.out]
        slots_out = [slot for slot in given if isinstance(slot, Slot) and slot.out]
        if not lazy:
            for slot in slots_in:
                slot.start()
            for slot in slots_in:
                slot.wait()
            kernel(*flag_refs, *[getattr(slot, "ref", slot) if isinstance(slot, Slot) else slot for slot in given], *own)
        else:
            kernel(*flag_refs, *given, *own)
        for slot in slots_out:
            if not slot.sent:
                slot.send()
        for slot in slots_out:
            slot.wait()

    return pl.pallas_call(
        managed,
        in_specs=([pl.BlockSpec(memory_space=pltpu.SMEM)] if flags is not None else []) + [anywhere] * len(arrays),
        out_specs=[anywhere] * len(outs),
        out_shape=[jax.ShapeDtypeStruct(shape, dtype) for shape, dtype in outs],
        scratch_shapes=[*scratch, *buffers, *sems],
        compiler_params=pltpu.CompilerParams(vmem_limit_bytes=limit * MIB),
        cost_estimate=pl.CostEstimate(flops=1000, bytes_accessed=1000, transcendentals=0),
    )(*([] if flags is None else [flags]), *arrays)


def prelude(place, row_place, image_len, timestep, time_embed, mod_table, rows):
    smem = pl.BlockSpec(memory_space=pltpu.SMEM)
    return pl.pallas_call(
        functools.partial(prelude_kernel, rows=rows),
        in_specs=[smem] * 4 + [pl.BlockSpec(memory_space=pl.ANY), pl.BlockSpec(memory_space=pltpu.VMEM)],
        out_specs=[smem, pl.BlockSpec(memory_space=pltpu.VMEM)],
        out_shape=[jax.ShapeDtypeStruct((ORDERS + 8,), jnp.int32), jax.ShapeDtypeStruct(mod_table.shape, F32)],
        scratch_shapes=[pltpu.VMEM((8, time_embed.shape[1]), F32), pltpu.SemaphoreType.DMA],
        compiler_params=pltpu.CompilerParams(vmem_limit_bytes=4 * MIB),
    )(place.reshape(1), row_place.reshape(1), image_len, timestep, time_embed, mod_table)


def half_width(grads, count, joined):
    size = (sum(grad.shape[1] for grad in grads) if joined else grads[0].shape[1]) // count
    body, _ = slice_parts(size)
    return 2 * (count // 4 * body + 128) if joined else len(grads) * -(-count // 2 * size // 128) * 128


def halves(core, grads, count, joined):
    out = ((grads[0].shape[0], half_width(grads, count, joined)), BF)
    return call(functools.partial(halves_kernel, count=count, joined=joined), grads, [out] * 2, flags=core, limit=6)


def split(flags, bit, inputs, parts, shape, axis=1):
    return call(
        functools.partial(split_kernel, parts=parts, axis=axis, bit=bit),
        inputs,
        [(shape, BF), (shape, F32)],
        flags=flags,
    )


def add_last(keep, got, size, shapes):
    return call(functools.partial(last_kernel, size=size), [keep, got], [(shape, F32) for shape in shapes])


def wide_grad(order, source, mode, first=0):
    entries = [entry if isinstance(entry, tuple) else (entry, None) for entry in source]
    source = [array for array, _ in entries]
    columns = [part and slice(part.start, part.stop or array.shape[1]) for array, part in entries]
    rows, width = source[0].shape[0], columns[0].stop if columns[0] else source[0].shape[1]
    depth = source[2].shape[1]
    wide, number = (depth, 2) if mode == "rows" else (depth // 2, 4)
    return call(
        functools.partial(wide_grad_kernel, mode=mode, first=first, columns=columns),
        source,
        [((2, width // 4, wide), BF)] * number,
        flags=order,
        raw=(0, 1, 2, 3, "out"),
        scratch=[
            pltpu.VMEM((2 * rows, width), BF),
            pltpu.VMEM((2 * rows, depth), BF),
            pltpu.VMEM((width, 2 * rows), BF),
            pltpu.VMEM((2, width // 4, wide), BF),
            pltpu.SemaphoreType.DMA((4,)),
            pltpu.SemaphoreType.DMA((2,)),
        ],
    )


def tall_grad(order, acts, keep, got, size, mode, first=0):
    count = len(acts)
    entries = [entry if isinstance(entry, tuple) else (entry, None) for pair in acts for entry in pair]
    rows, wide = keep.shape
    width = entries[0][0].shape[1]
    shape = (2, 4 * size, width // 4) if mode == "rows" else (2 * size * count, width)
    return call(
        functools.partial(
            tall_grad_kernel, count=count, mode=mode, first=first, columns=[part for _, part in entries]
        ),
        [array for array, _ in entries] + [keep, got],
        [(shape, BF)] * 2,
        flags=order,
        raw=(*range(2 * count + 2), "out"),
        scratch=[
            pltpu.VMEM((count, 2 * rows, width), BF),
            pltpu.VMEM((2 * rows, wide), BF),
            pltpu.VMEM((wide, 2 * rows), BF),
            pltpu.VMEM((2, *shape[-2:]), BF),
            pltpu.SemaphoreType.DMA((2 * count + 2,)),
            pltpu.SemaphoreType.DMA((2,)),
        ],
    )


def local(
    tokens,
    image_len,
    timestep,
    caption,
    time_embed,
    mod_table,
    w_qkv,
    w_out,
    cross_q,
    cross_kv,
    cross_out,
    w_up,
    w_down,
    cotangent,
):
    sp_count = lax.axis_size("sp")
    dp_count = lax.axis_size("dp")
    place = lax.axis_index("sp")
    row_place = lax.axis_index("dp")
    core = place % 2
    rows, width = tokens.shape[1:]
    factor = 1.0 / math.sqrt(width // HEADS)
    blocks = BIG // rows
    assert blocks == 4

    big, modulation = prelude(place, row_place, image_len, timestep, time_embed, mod_table, rows)
    shift_one, scale_one, gate_one, shift_two, scale_two, gate_two = [modulation[i] for i in range(6)]

    def tie(value, *before):
        return lax.optimization_barrier((value, *[array for array in before if array is not None]))[0]

    pairs = [(i, i ^ 1) for i in range(sp_count)]
    others = [(i, i + 1) for i in range(1, sp_count - 1, 2)] + [(i + 1, i) for i in range(1, sp_count - 1, 2)]
    ahead = [(i, i + 2) for i in range(sp_count - 2)]
    back = [(i + 2, i) for i in range(sp_count - 2)]

    def image_blocks(block, *before):
        from_back = lax.ppermute(block, "sp", ahead)
        from_ahead = lax.ppermute(block, "sp", back)
        from_ahead, from_back = tie(from_ahead, *before), tie(from_back, *before)
        send_pair = jnp.concatenate([jnp.where(big[1] == 1, from_ahead, from_back), block], axis=0)
        send_other = jnp.where(core == 1, from_back, from_ahead)
        both = lax.ppermute(send_pair, "sp", pairs)
        third = lax.ppermute(send_other, "sp", others)
        return [both, third, from_ahead, from_back], (send_pair, send_other)

    def chosen(both, third, from_ahead, from_back):
        high = both.shape[0] // 2
        return [
            both[:high],
            jnp.where(big[2] == 1, both[high:], third),
            jnp.where(big[3] == 1, from_ahead, from_back),
        ]

    def swap(array):
        return lax.ppermute(array, "sp", pairs)

    token_blocks, token_sends = image_blocks(tokens[0])

    def first_norm(block):
        return (normal(block.astype(F32))[0] * (1.0 + scale_one) + shift_one).astype(BF)

    first_in = first_norm(tokens[0])
    other_in = first_norm(jnp.concatenate(chosen(*token_blocks), axis=0))

    chips = sp_count // 2
    square = dp_count == 4 and chips == 4

    def own_half(*grads, joined=True):
        if square:
            return halves(big, grads, sp_count, joined)
        grads = [jnp.concatenate(grads, axis=1)] if joined else grads
        size = grads[0].shape[1] // sp_count
        even, odd = [
            jnp.concatenate(
                [g[:, i * size : (i + 1) * size] for g in grads for i in range(c, sp_count, 2)], axis=1
            )
            for c in (0, 1)
        ]
        return jnp.where(core == 0, even, odd), jnp.where(core == 0, odd, even)

    high = width // 4

    def to_row(array, bit):
        return lax.ppermute(array, "dp", [(i, i ^ (1 << bit)) for i in range(dp_count)])

    def to_chip(array, bit):
        return lax.ppermute(array, "sp", [(i, i ^ (2 << bit)) for i in range(sp_count)])

    def plain_sum(sources, size):
        finals = []
        for item, (x0, x1, g0, g1) in enumerate(sources):
            columns = slice(item * chips * size, (item + 1) * chips * size)
            part = (matmul_tn(x0, g0[:, columns]) + matmul_tn(x1, g1[:, columns])).astype(BF)
            part = part.reshape(dp_count, -1, chips, size).transpose(0, 2, 1, 3)
            bit = dp_count // 2
            while bit:
                mine = (row_place // bit) % 2
                part = part.reshape(2, bit, chips, -1, size)
                got = lax.ppermute(part[1 - mine], "dp", [(i, i ^ bit) for i in range(dp_count)])
                part = add(part[mine], got).astype(BF)
                bit //= 2
            part = part.reshape(chips, -1, size)
            bit = chips // 2
            while bit:
                mine = (place // 2 // bit) % 2
                part = part.reshape(2, bit, -1, size)
                got = lax.ppermute(part[1 - mine], "sp", [(i, i ^ (2 * bit)) for i in range(sp_count)])
                part = add(part[mine], got).astype(BF)
                bit //= 2
            finals.append(part[0].astype(F32))
        return finals

    def add_picked(keep, got, flag):
        return call(add_kernel, [(keep, flag), (got, flag)], [(keep.shape[1:], BF)], flags=big)

    everything = slice(None)

    def cut_slices(size):
        body, tail = slice_parts(size)
        return [
            [
                (everything, slice(h * body, (h + 1) * body)),
                (everything, slice(2 * body + h * tail, 2 * body + (h + 1) * tail)),
            ]
            for h in (0, 1)
        ]

    def sum_wide(source, first, size):
        second = 1 - first
        if size < 256:
            send, keep = tall_grad(big, [source[:2]], *source[2:], size, "rows", first)
        else:
            send, keep = wide_grad(big, source, "rows", first)
        late = yield send
        got = to_row(send, first)
        if size < 256:
            _, tall, wide = keep.shape
            flat = lambda array: array.reshape(2 * tall, wide)
            rows_at = lambda low, high: (slice(low, high),)
            groups = [
                [rows_at(y * tall + h * tall // 2, y * tall + (h + 1) * tall // 2) for y in (0, 1)]
                for h in (0, 1)
            ]
            send, keep = split(big, NEAR, [flat(tie(keep, late)), flat(got)], groups, (tall, wide), 0)
            late = yield send
            groups = [[rows_at(h * tall // 2, (h + 1) * tall // 2)] for h in (0, 1)]
            inputs = [tie(keep, late), to_chip(send, 0)]
            send, keep = split(big, ROW + second, inputs, groups, (tall // 2, wide), 0)
            late = yield send
            groups = [[rows_at(h * tall // 4, (h + 1) * tall // 4)] for h in (0, 1)]
            inputs = [tie(keep, late), to_row(send, second)]
            send, keep = split(big, FAR, inputs, groups, (tall // 4, wide), 0)
            late = yield send
            (final,) = add_last(tie(keep, late), to_chip(send, 1), 0, [(size, wide)])
            yield final.T
        else:
            (send,) = add_picked(tie(keep, late), got, OTHER + second)
            late = yield send
            tall, wide = send.shape
            more = to_row(send, second)
            inputs = [(tie(keep, late), ROW + second), (got, ROW + second), more]
            groups = [[(everything, slice(h * wide // 2, (h + 1) * wide // 2))] for h in (0, 1)]
            send, keep = split(big, NEAR, inputs, groups, (tall, wide // 2))
            late = yield send
            shape = (tall, size // 128 * 128 + 128)
            send, keep = split(big, FAR, [tie(keep, late), to_chip(send, 0)], cut_slices(size), shape)
            late = yield send
            (final,) = add_last(tie(keep, late), to_chip(send, 1), size, [(tall, size)])
            yield final

    def sum_both(source, size):
        outs = wide_grad(big, source, "both")
        late = yield outs[0]
        got = [to_row(outs[0], 0), to_row(outs[2], 1)]
        sends = [
            *add_picked(tie(outs[1], late), got[0], OTHER + 1),
            *add_picked(tie(outs[3], late), got[1], OTHER),
        ]
        late = yield sends[1]
        shape = sends[0].shape
        more = [to_row(sends[0], 1), to_row(sends[1], 0)]
        send, keep = call(
            split_pair_kernel,
            [
                (tie(outs[1], late), ROW + 1), (got[0], ROW + 1), more[0],
                (outs[3], ROW), (got[1], ROW), more[1],
            ],
            [(shape, BF), (shape, F32)],
            flags=big,
        )
        late = yield send
        shape = (shape[0], size // 128 * 128 + 128)
        send, keep = split(big, FAR, [tie(keep, late), to_chip(send, 0)], cut_slices(size), shape)
        late = yield send
        (final,) = add_last(tie(keep, late), to_chip(send, 1), size, [(high, size)])
        yield final

    def sum_chips_first(acts, keep, got, size):
        count = len(acts)
        send, keep = tall_grad(big, acts, keep, got, size, "chips")
        late = yield send
        got = to_chip(send, 0)
        groups = [
            [(everything, slice(i * high, (i + 1) * high)) for i in (h, h + 2)] for h in (0, 1)
        ]
        shape = (2 * count * size, lanes(2 * high))
        send, keep = split(big, ROW, [tie(keep, late), got], groups, shape)
        late = yield send
        got = to_row(send, 0)
        groups = [[(everything, slice(h * high, (h + 1) * high))] for h in (0, 1)]
        shape = (2 * count * size, lanes(high))
        send, keep = split(big, ROW + 1, [tie(keep, late), got], groups, shape)
        late = yield send
        got = to_row(send, 1)
        groups = [
            [(slice((2 * k + h) * size, (2 * k + h + 1) * size),) for k in range(count)] for h in (0, 1)
        ]
        shape = (count * size, lanes(high))
        send, keep = split(big, FAR, [tie(keep, late), got], groups, shape, 0)
        late = yield send
        finals = add_last(tie(keep, late), to_chip(send, 1), 0, [(size, high)] * count)
        yield [final.T for final in finals]

    caption_rows = caption[0]
    live = caption_rows.shape[0]
    padded = -(-live // 128) * 128
    caption_pad = jnp.concatenate([caption_rows, jnp.zeros((padded - live, width), BF)], axis=0)
    text = matmul(caption_pad, cross_kv).astype(BF)
    grad_mlp = (gate_two * cotangent[0].astype(F32)).astype(BF)
    mlp_keep, mlp_send = own_half(grad_mlp, joined=False)
    mlp_got = swap(mlp_send)
    first_pair = swap(first_in)
    own = matmul(tie(first_in, *token_sends), w_qkv).astype(BF)
    far_qkv = matmul(other_in, w_qkv).astype(BF)
    block = ((rows, width), BF)
    stream = ((rows, width), F32)
    stats = ((rows, 128), F32)
    units = w_up.shape[1]
    tile = units // 4
    half = half_width([w_up], sp_count, True) if square else units
    small_width = half_width([grad_mlp] * 3, sp_count, False) if square else 3 * width
    small_out = ((rows, small_width), BF)
    (
        acts, up_pack, hidden, pre_keep,
        stream_three, grad_one, small_keep, small_send, grad_text, pack, stat, table,
    ) = call(
        functools.partial(forward_kernel, factor=factor, live=live, count=sp_count if square else 0),
        [
            own, (tie(far_qkv, mlp_got, first_pair), slice(width, 3 * width)), tokens[0], modulation, text,
            w_out, cross_q, cross_out, grad_mlp, cotangent[0], w_up, w_down,
        ],
        [
            ((3 * rows, width), BF), ((rows, width + (half if square else 0)), BF), ((rows, units), BF),
            ((rows, half), BF),
            stream, stream, small_out, small_out, ((live, 2 * width), F32), ((rows + 16, width), BF), stats,
            (modulation.shape, F32),
        ],
        flags=big,
        raw=(10, 11),
        lazy=True,
        scratch=[
            pltpu.VMEM((3, width, tile), BF),
            pltpu.VMEM((3, tile, width), BF),
            pltpu.SemaphoreType.DMA((3, 4)),
            pltpu.VMEM((rows, tile), BF),
            pltpu.VMEM((rows, tile), BF),
            pltpu.VMEM((rows, 128), F32),
            pltpu.VMEM((rows, width), F32),
            pltpu.VMEM((rows, width), BF),
            *[pltpu.VMEM((rows, width), F32)] * 3,
            *[pltpu.VMEM((rows, width), BF)] * 2,
            *[pltpu.VMEM((padded, width), F32)] * 2,
        ],
        limit=63,
    )

    if not square:
        pre_keep, pre_send = own_half(pre_keep)
        up_pack = jnp.concatenate([up_pack, pre_send], axis=1)
    hidden_pair, up_pair = swap(hidden), swap(up_pack)
    if not square:
        small_keep, small_send = own_half(*jnp.split(small_keep, 3, axis=1), joined=False)
    slice_of = lambda weight: weight.shape[1] // sp_count
    down_source = (hidden, hidden_pair, mlp_keep, mlp_got)
    up_source = ((up_pack, slice(0, width)), (up_pair, slice(0, width)), pre_keep, (up_pair, slice(width, None)))
    send_down = send_up = send_small = None
    if square:
        up_sum = sum_wide((up_source[0], up_source[1], tie(pre_keep, pack), up_source[3]), 1, slice_of(w_up))
        send_up = next(up_sum)
        down_sum = sum_wide((tie(hidden, send_up), *down_source[1:]), 0, slice_of(w_down))
        send_down = next(down_sum)
        small_got = swap(tie(small_send, send_up))
        small_acts = tie(acts, send_up)
        small_acts = [small_acts, swap(small_acts)]
        small_acts = [[(part, slice(i * rows, (i + 1) * rows)) for part in small_acts] for i in range(3)]
        small_sum = sum_chips_first(small_acts, tie(small_keep, send_down), small_got, slice_of(w_out))
        send_small = next(small_sum)
    pack_blocks, pack_sends = image_blocks(pack, send_small)
    (grad_queries,) = call(
        functools.partial(query_grad_kernel, factor=factor),
        [own, (far_qkv, slice(width, 3 * width)), tie(pack, *pack_sends), stat],
        [block],
        flags=big,
    )
    proj_out = ((rows, half_width([w_qkv], sp_count, True) if square else 3 * width), BF)
    grad_keys, grad_values, proj_keep, proj_send = call(
        functools.partial(key_grad_kernel, factor=factor, count=sp_count if square else 0),
        [own, (far_qkv, slice(0, width)), tie(pack, grad_queries), grad_queries, *pack_blocks],
        [block, block, proj_out, proj_out],
        flags=big,
        raw=(4, 5, 6, 7),
        lazy=True,
        scratch=[
            pltpu.VMEM((2 * HEADS, blocks * rows), F32),
            pltpu.VMEM(((blocks - 1) * rows, width), BF),
            pltpu.VMEM((blocks - 1, 16, width), BF),
            pltpu.SemaphoreType.DMA((2 * blocks - 2,)),
        ],
    )
    if not square:
        proj_keep, proj_send = own_half(*jnp.split(proj_keep, 3, axis=1))
    qkv_source = (first_in, first_pair, proj_keep, swap(proj_send))
    grad_tokens, text_part = call(
        functools.partial(last_grad_kernel, shape=(dp_count, sp_count)),
        [
            grad_queries, tie(grad_keys, proj_send), grad_values, w_qkv, tokens[0], modulation, grad_one, table,
            grad_text,
        ],
        [stream, ((2 * width, 128), F32)],
    )
    table = text_part
    text_part = lax.psum_scatter(text_part, "sp", scatter_dimension=0, tiled=True)

    def caption_sum(late):
        part = tie(text_part, late)
        tall, size = width // dp_count, 6 * width // (dp_count * sp_count)
        high = lanes(tall + 16) if dp_count != 4 else tall + 16
        (both,) = call(
            functools.partial(caption_kernel, blocks=dp_count, size=size),
            [part, caption_rows],
            [((dp_count * high, part.shape[0]), BF)],
        )
        total = lax.psum_scatter(both, "dp", scatter_dimension=0, tiled=True).astype(F32)
        return both, total[:tall], total[tall, :size]

    late = None
    if square:
        late = down_sum.send(up_sum.send(table))
        qkv_sum = sum_both((tie(first_in, late), *qkv_source[1:]), slice_of(w_qkv))
        late = next(qkv_sum)
        for step in (small_sum, up_sum, down_sum, qkv_sum):
            late = step.send(late)
        late, final_ckv, final_table = caption_sum(late)
        for step in (up_sum, small_sum, down_sum, qkv_sum):
            late = step.send(late)
        final_up = up_sum.send(late)
        late = small_sum.send(final_up)
        final_down = down_sum.send(late)
        late = qkv_sum.send(tie(final_down, final_ckv))
        final_small = small_sum.send(late)
        final_qkv = qkv_sum.send(final_small[0])
    else:
        _, final_ckv, final_table = caption_sum(table)
        small_pair, small_got = swap(acts), swap(small_send)
        small = [
            (acts[i * rows : (i + 1) * rows], small_pair[i * rows : (i + 1) * rows], small_keep, small_got)
            for i in range(3)
        ]
        up_source = (up_pack[:, :width], up_pair[:, :width], pre_keep, up_pair[:, width:])
        final_small = plain_sum(small, slice_of(w_out))
        (final_down,) = plain_sum([down_source], slice_of(w_down))
        (final_up,) = plain_sum([up_source], slice_of(w_up))
        (final_qkv,) = plain_sum([qkv_source], slice_of(w_qkv))
    return (
        stream_three[None],
        grad_tokens[None],
        final_table,
        final_qkv,
        final_small[2],
        final_small[1],
        final_ckv,
        final_small[0],
        final_up,
        final_down,
    )


def solution(mesh):
    return jax.shard_map(
        local,
        mesh=mesh,
        in_specs=(
            P("dp", "sp", None),
            P("dp", None),
            P("dp", None),
            P("dp", None, None),
            P(),
            P(),
            P(),
            P(),
            P(),
            P(),
            P(),
            P(),
            P(),
            P("dp", "sp", None),
        ),
        out_specs=(
            P("dp", "sp", None),
            P("dp", "sp", None),
            P(("dp", "sp")),
            P("dp", "sp"),
            P("dp", "sp"),
            P("dp", "sp"),
            P("dp", "sp"),
            P("dp", "sp"),
            P("dp", "sp"),
            P("dp", "sp"),
        ),
        check_vma=False,
    )
```

```python
import functools
import math

import jax
import jax.numpy as jnp
from jax import lax
from jax.experimental import pallas as pl
from jax.experimental.pallas import tpu as pltpu
from jax.sharding import PartitionSpec as P

HEADS = 16
BIG = 1024
EPS = 1e-06
BIGNEG = -1e30
LOG2E = 1.4426950408889634
BF = jnp.bfloat16
F32 = jnp.float32
LARGE, CORE, NEAR, FAR, ROW, OTHER, ORDERS = 0, 4, 5, 6, 7, 9, 11
WIN = 256
COST_SCALE = 0.001
MIB = 1024 * 1024


def matmul(left, right):
    return jnp.dot(left, right, preferred_element_type=F32)


def matmul_tn(left, right):
    return lax.dot_general(left, right, (((0,), (0,)), ((), ())), preferred_element_type=F32)


def matmul_nt(left, right):
    return lax.dot_general(left, right, (((1,), (1,)), ((), ())), preferred_element_type=F32)


def head_window(head, width):
    size = width // HEADS
    low = head * size
    start = pl.multiple_of(jnp.minimum(low // 128 * 128, width - WIN), 128)
    lane = lax.broadcasted_iota(jnp.int32, (1, WIN), 1) + start
    return start, jnp.logical_and(lane >= low, lane < low + size)


def pair_window(pair, width):
    size = width // HEADS
    low = 2 * pair * size
    start = pl.multiple_of(low // 128 * 128, 128)
    lane = lax.broadcasted_iota(jnp.int32, (1, WIN), 1) + start
    return start, [
        jnp.logical_and(lane >= low + i * size, lane < low + (i + 1) * size) for i in (0, 1)
    ]


def stacked(block, masks):
    return jnp.concatenate([block * mask.astype(block.dtype) for mask in masks], axis=0)


def keep_pair(ref, start, masks, value):
    rows = ref.shape[0]
    win = pl.ds(start, WIN)
    picked = jnp.where(masks[1], value[rows:], ref[:, win])
    ref[:, win] = jnp.where(masks[0], value[:rows], picked)


def each_pair(body, unroll=2):
    def step(pair, carry):
        body(pair)
        return carry

    lax.fori_loop(0, HEADS // 2, step, 0, unroll=unroll)


def window(ref, start, offset=0):
    return ref[:, pl.ds(pl.multiple_of(start + offset, 128), WIN)]


def keep_columns(ref, start, mask, value):
    win = pl.ds(start, WIN)
    ref[:, win] = jnp.where(mask, value, ref[:, win])


def blockwise(function, arrays, high, wide=None):
    rows, columns = arrays[0].shape
    strips = []
    for low in range(0, rows, high):
        pieces = []
        for left in range(0, columns, wide or columns):
            block = [
                array[
                    slice(low, low + high) if array.shape[0] > 1 else slice(None),
                    slice(left, left + wide) if wide and array.shape[1] > 1 else slice(None),
                ]
                for array in arrays
            ]
            pieces.append(function(*block))
        strips.append([jnp.concatenate(parts, axis=1) if len(parts) > 1 else parts[0] for parts in zip(*pieces)])
    return [jnp.concatenate(parts, axis=0) for parts in zip(*strips)]


def each_head(body, unroll=4):
    def step(head, carry):
        body(head)
        return carry

    lax.fori_loop(0, HEADS, step, 0, unroll=unroll)


def fetch(sems, *pairs):
    copies = [pltpu.make_async_copy(source, target, sems.at[i]) for i, (source, target) in enumerate(pairs)]
    for copy in copies:
        copy.start()
    return [copy.wait for copy in copies]


def attend(big, own_ref, far_ref, out_ref, lse_ref, factor):
    width = out_ref.shape[1]
    scale = factor * LOG2E

    def run(sides):
        def one_pair(pair):
            start, masks = pair_window(pair, width)
            query = stacked(window(own_ref, start), masks)
            scores = [matmul_nt(query, window(side, start, key)) for side, key in sides]
            top = functools.reduce(jnp.maximum, [jnp.max(s, axis=1, keepdims=True) for s in scores])
            raised = [jnp.exp2((s - top) * scale) for s in scores]
            total = sum(jnp.sum(r, axis=1, keepdims=True) for r in raised)
            inverse = 1.0 / total
            result = sum(
                matmul((r * inverse).astype(BF), window(side, start, key + width))
                for r, (side, key) in zip(raised, sides)
            )
            keep_pair(out_ref, start, masks, result.astype(BF))
            lse = top * scale + jnp.log2(total)
            rows = out_ref.shape[0]
            lane = lax.broadcasted_iota(jnp.int32, (1, 128), 1)
            kept = jnp.where(lane == 2 * pair + 1, lse[rows:], lse_ref[...])
            lse_ref[...] = jnp.where(lane == 2 * pair, lse[:rows], kept)

        each_pair(one_pair)

    lse_ref[...] = jnp.zeros_like(lse_ref)

    @pl.when(big)
    def _():
        run([(own_ref, width), (far_ref, 0)])

    @pl.when(jnp.logical_not(big))
    def _():
        run([(own_ref, width)])


def query_grad_kernel(flag_ref, own, far, pack, stat, out, partial, *, factor):
    for slot in (own, pack, stat, far):
        slot.start()
    own_ref, far_ref, pack_ref, stat_ref, out_ref = (slot.ref for slot in (own, far, pack, stat, out))
    rows, width = out_ref.shape
    scale = factor * LOG2E

    def run(side, offset, finish):
        def one_pair(pair):
            start, masks = pair_window(pair, width)
            query = stacked(window(own_ref, start), masks)
            grad = stacked(window(pack_ref.at[0:rows, :], start), masks)
            lane = lax.broadcasted_iota(jnp.int32, (1, 128), 1)
            stats = stat_ref[...]

            def column(low):
                return jnp.concatenate(
                    [
                        jnp.sum(jnp.where(lane == low + 2 * pair + i, stats, 0.0), axis=1, keepdims=True)
                        for i in (0, 1)
                    ],
                    axis=0,
                )

            key = window(side, start, offset)
            prob = jnp.exp2(matmul_nt(query, key) * scale - column(0))
            grad_prob = matmul_nt(grad, window(side, start, offset + width))
            finish(start, masks, matmul((prob * (grad_prob - column(HEADS))).astype(BF), key))

        each_pair(one_pair, 4)

    def first(start, masks, total):
        keep_pair(partial, start, masks, total)

    def second(start, masks, total):
        before = window(partial, start)
        total = total + jnp.concatenate([before, before], axis=0)
        keep_pair(out_ref, start, masks, (total * factor).astype(BF))

    for slot in (own, pack, stat):
        slot.wait()
    run(own_ref, width, first)
    far.wait()

    @pl.when(flag_ref[LARGE] == 1)
    def _():
        run(far_ref, 0, second)

    @pl.when(flag_ref[LARGE] == 0)
    def _():
        out_ref[...] = (partial[...] * factor).astype(BF)


def key_grad_kernel(flag_ref, own, far, pack, dq, both, third, ahead, back, *refs, factor, count):
    dk, dv, keep_out, send_out, stats, grads, tails, part_key, part_value, sems = refs
    own_ref, far_ref, pack_ref, dq_ref = (slot.ref for slot in (own, far, pack, dq))
    dk_ref, dv_ref, keep_ref, send_ref = (slot.ref for slot in (dk, dv, keep_out, send_out))
    rows, width = dk_ref.shape
    tall = rows + 16

    def copies(block, source, low):
        return (
            pltpu.make_async_copy(
                source.at[low : low + rows, :], grads.at[block * rows : (block + 1) * rows, :], sems.at[2 * block]
            ),
            pltpu.make_async_copy(source.at[low + rows : low + tall, :], tails.at[block], sems.at[2 * block + 1]),
        )

    def begin(block, flag, first, second):
        for value, (source, low) in ((1, first), (0, second)):

            @pl.when(flag == value)
            def _(source=source, low=low):
                for copy in copies(block, source, low):
                    copy.start()

    for copy in copies(0, both, 0):
        copy.start()
    begin(1, flag_ref[2], (both, tall), (third, 0))
    begin(2, flag_ref[3], (ahead, 0), (back, 0))
    blocks = 4
    for slot in (own, far, pack, dq):
        slot.start()
    own.wait()
    pack.wait()
    scale = factor * LOG2E

    def unpack(block, both):
        both = both.astype(F32)
        joined = both[:8] + both[8:]
        for group in range(4):
            stats[8 * group : 8 * group + 8, block * rows : block * rows + rows] = joined[
                :, group * rows : group * rows + rows
            ]

    def run(query_ref, grad_ref, low, high, finish):
        def one_pair(pair):
            start, masks = pair_window(pair, width)
            key = stacked(window(own_ref, start, width), masks)
            value = stacked(window(own_ref, start, 2 * width), masks)

            def line(at, low, high):
                return jnp.concatenate(
                    [
                        jnp.broadcast_to(stats[pl.ds(at + 2 * pair + i, 1), low:high], (rows, high - low))
                        for i in (0, 1)
                    ],
                    axis=0,
                )

            query, grad = window(query_ref, start), window(grad_ref.at[0 : high - low, :], start)
            prob = jnp.exp2(matmul_nt(key, query) * scale - line(0, low, high))
            grad_prob = matmul_nt(value, grad)
            grad_score = (prob * (grad_prob - line(HEADS, low, high))).astype(BF)
            finish(start, masks, matmul(grad_score, query), matmul(prob.astype(BF), grad))

        each_pair(one_pair, 4)

    def first(start, masks, *totals):
        for ref, total in zip((part_key, part_value), totals):
            keep_pair(ref, start, masks, total)

    def second(start, masks, *totals):
        for ref, out, total, scaled in zip((part_key, part_value), (dk_ref, dv_ref), totals, (factor, 1.0)):
            before = window(ref, start)
            total = total + jnp.concatenate([before, before], axis=0)
            keep_pair(out, start, masks, (total * scaled).astype(BF))

    unpack(0, pack_ref[rows:, :])
    run(own_ref, pack_ref, 0, rows, first)
    far.wait()
    dq.wait()
    for block in range(blocks - 1):
        for copy in copies(block, both, 0):
            copy.wait()
        unpack(block + 1, tails[block])

    @pl.when(flag_ref[LARGE] == 1)
    def _():
        run(far_ref, grads, rows, blocks * rows, second)

    @pl.when(flag_ref[LARGE] == 0)
    def _():
        dk_ref[...] = (part_key[...] * factor).astype(BF)
        dv_ref[...] = part_value[...].astype(BF)

    dk.send()
    dv.send()
    if count:
        for core in (0, 1):

            @pl.when(flag_ref[CORE] == core)
            def _(core=core):
                grads = [ref[...] for ref in (dq_ref, dk_ref, dv_ref)]
                keep_ref[...] = half_columns(grads, core, count, True, keep_ref.shape[1])
                send_ref[...] = half_columns(grads, 1 - core, count, True, send_ref.shape[1])

    else:
        for index, ref in enumerate((dq_ref, dk_ref, dv_ref)):
            keep_ref[:, index * width : (index + 1) * width] = ref[...]


def text_probs(query, key, scale, live, axis):
    scores = matmul_nt(query, key) if axis else matmul_nt(key, query)
    shape = (1, scores.shape[1]) if axis else (scores.shape[0], 1)
    scores = jnp.where(lax.broadcasted_iota(jnp.int32, shape, axis) < live, scores, BIGNEG)
    raised = jnp.exp2((scores - jnp.max(scores, axis=axis, keepdims=True)) * scale)
    return raised * (1.0 / jnp.sum(raised, axis=axis, keepdims=True))


def normal(stream):
    centred = stream - jnp.mean(stream, axis=-1, keepdims=True)
    spread = lax.rsqrt(jnp.mean(centred * centred, axis=-1, keepdims=True) + EPS)
    return centred * spread, spread


def norm_back(normed, spread, scale, grad):
    scaled = grad * (1.0 + scale)
    back = spread * (
        scaled
        - jnp.mean(scaled, axis=-1, keepdims=True)
        - normed * jnp.mean(scaled * normed, axis=-1, keepdims=True)
    )
    return back, jnp.sum(grad, axis=0, keepdims=True), jnp.sum(grad * normed, axis=0, keepdims=True)


def middle(tokens_ref, mod_ref, att_ref, weights, text_ref, refs, factor, live):
    branch_ref, cross_in_ref, queries_ref, mixed_ref, stream_ref, second_ref = refs
    width = tokens_ref.shape[1]
    out_w_ref, query_w_ref, cross_w_ref = weights
    branch = matmul(att_ref[...], out_w_ref[...])
    branch_ref[...] = branch
    stream = tokens_ref[...].astype(F32) + mod_ref[2:3, :] * branch
    stream_ref[...] = stream
    cross_in = stream.astype(BF)
    cross_in_ref[...] = cross_in
    queries_ref[...] = matmul(cross_in, query_w_ref[...]).astype(BF)

    def one_head(head):
        start, mask = head_window(head, width)
        query = window(queries_ref, start) * mask.astype(BF)
        probs = text_probs(query, window(text_ref, start), factor * LOG2E, live, 1)
        result = matmul(probs.astype(BF), window(text_ref, start, width))
        keep_columns(mixed_ref, start, mask, result.astype(BF))

    each_head(one_head, 8)
    stream = stream_ref[...] + matmul(mixed_ref[...], cross_w_ref[...])
    stream_ref[...] = stream
    scale, shift = 1.0 + mod_ref[4:5, :], mod_ref[3:4, :]
    for low in range(0, stream.shape[0], 16):
        part = stream_ref[low : low + 16, :]
        second_ref[low : low + 16, :] = (normal(part)[0] * scale + shift).astype(BF)


def forward_kernel(
    flag_ref, own, far, tokens, mod, text, out_w, query_w, cross_w, grad, cot, up_hbm, down_hbm,
    acts, up_pack, hidden, keep,
    out, one, small_keep, small_send, text_grad, pack, stat, table,
    up, down, sems, kept0, kept1, lse, branch_ref, queries, stream, mlp_out, back,
    grad_mixed, grad_queries, text_key, text_value, *, factor, live, count
):
    kept = (kept0, kept1)
    rows, width = tokens.ref.shape
    mixed, cross_in, att = (acts.ref.at[i * rows : (i + 1) * rows, :] for i in range(3))
    second = up_pack.ref.at[:, 0:width]
    own.start()
    far.start()
    own.wait()
    far.wait()
    late = (tokens, mod, text, out_w, query_w, cross_w, grad, cot)
    for slot in late:
        slot.start()
    tile = down.shape[1]
    tiles = down_hbm.shape[0] // tile
    ring = down.shape[0]

    def copies(step):
        half = tile // 2
        slot = step % ring
        pairs = []
        for part in (0, 1):
            rows = slice(part * up_hbm.shape[0] // 2, (part + 1) * up_hbm.shape[0] // 2)
            pairs.append((up_hbm.at[rows, step * tile : (step + 1) * tile], up.at[slot, rows, :]))
            rows = slice(part * half, (part + 1) * half)
            pairs.append((down_hbm.at[step * tile + part * half : step * tile + (part + 1) * half, :], down.at[slot, rows, :]))
        return [pltpu.make_async_copy(a, b, sems.at[slot, i]) for i, (a, b) in enumerate(pairs)]

    for step in range(min(ring, tiles)):
        for copy in copies(step):
            copy.start()
    attend(flag_ref[LARGE] == 1, own.ref, far.ref, att, lse, factor)
    for slot in late:
        slot.wait()
    weights = (out_w.ref, query_w.ref, cross_w.ref)
    outs = (branch_ref, cross_in, queries, mixed, stream, second)
    middle(tokens.ref, mod.ref, att, weights, text.ref, outs, factor, live)
    acts.send()

    root = math.sqrt(2.0 / math.pi)

    def both(step):
        if step < tiles:
            for copy in copies(step):
                copy.wait()
            pre = matmul(second[...], up[step % ring])
            slope = matmul_nt(grad.ref[...], down[step % ring])
        if step > 0:
            before = (step - 1) % ring
            ahead = hidden.ref[:, (step - 1) * tile : step * tile]
            behind = kept[(step - 1) % 2][...]
            branch = matmul(ahead, down[before])
            result = matmul_nt(behind, up[before])
        if step < tiles:

            def bent(pre, grad):
                square = pre * pre
                bend = jnp.tanh(pre * (root * 0.044715 * square + root))
                half = 0.5 * bend + 0.5
                rise = (3 * root * 0.044715 * square + root) * pre
                slope = half + 0.5 * rise * (1.0 - bend * bend)
                return (pre * half).astype(BF), (grad * slope).astype(BF)

            ahead, behind = blockwise(bent, [pre, slope], 64, 128)
            kept[step % 2][...] = behind
            hidden.ref[:, step * tile : (step + 1) * tile] = ahead
            if count:
                size = tile // 2
                body, tail = slice_parts(size)
                group = step % 2 * keep.ref.shape[1] // 2
                spots = (
                    (group + step // 2 * body, 0, body),
                    (group + tiles // 2 * body + step // 2 * tail, body, tail),
                )
                for core in (0, 1):

                    @pl.when(flag_ref[CORE] == core)
                    def _(core=core):
                        for at, low, wide in spots:
                            mine, other = core * size + low, (1 - core) * size + low
                            keep.ref[:, at : at + wide] = behind[:, mine : mine + wide]
                            up_pack.ref[:, width + at : width + at + wide] = behind[:, other : other + wide]

            else:
                keep.ref[:, step * tile : (step + 1) * tile] = behind
        if step > 0:
            if step == 1:
                mlp_out[...] = branch
                back[...] = result
            else:
                mlp_out[...] += branch
                back[...] += result
            if step - 1 + ring < tiles:
                for copy in copies(step - 1 + ring):
                    copy.start()

    for step in range(tiles):
        both(step)
    hidden.send()
    keep.send()
    up_pack.send()
    both(tiles)
    middle_grad(
        flag_ref, back, stream, cot.ref, mlp_out, mod.ref, branch_ref, att, lse, queries, text.ref, weights,
        out, one, small_keep, small_send, text_grad, pack, stat, table,
        grad_mixed, grad_queries, text_key, text_value, factor, live, count,
    )


def middle_grad(
    flag_ref, second_grad_ref, stream_ref, cot_ref, mlp_ref, mod_ref, branch_ref, att_ref, lse_ref, queries_ref, text_ref,
    weights, out, one, keep, send, text_grad, pack, stat_out, table,
    mixed, grad_queries, text_key, text_value, factor, live, count
):
    out_w_ref, query_w_ref, cross_w_ref = weights
    one_ref, keep_ref, send_ref, text_grad_ref, pack_ref, stat_ref, table_ref = (
        slot.ref for slot in (one, keep, send, text_grad, pack, stat_out, table)
    )
    rows, width = cot_ref.shape
    gate, scale = mod_ref[5:6, :], 1.0 + mod_ref[4:5, :]
    sums = [0.0] * 3
    for low in range(0, rows, 16):
        part = slice(low, low + 16)
        cot, stream, mlp, grad = cot_ref[part, :].astype(F32), stream_ref[part, :], mlp_ref[part, :], second_grad_ref[part, :]
        out.ref[part, :] = stream + gate * mlp
        normed, spread = normal(stream)
        scaled = grad * scale
        back = spread * (
            scaled
            - jnp.mean(scaled, axis=-1, keepdims=True)
            - normed * jnp.mean(scaled * normed, axis=-1, keepdims=True)
        )
        one_ref[part, :] = cot + back
        sums = [total + term for total, term in zip(sums, (grad, grad * normed, cot * mlp))]
    out.send()
    table_ref[...] = jnp.zeros_like(table_ref)
    for index, total in enumerate(sums):
        table_ref[3 + index : 4 + index, :] = jnp.sum(total, axis=0, keepdims=True)
    grad_cross = one_ref[...].astype(BF)
    mixed[...] = matmul_nt(grad_cross, cross_w_ref[...]).astype(BF)

    def one_head(head):
        start, mask = head_window(head, width)
        keep = mask.astype(BF)
        query = window(queries_ref, start)
        grad = window(mixed, start)
        key = window(text_ref, start) * keep
        probs = text_probs(query, key, factor * LOG2E, live, 0)
        grad_probs = matmul_nt(window(text_ref, start, width) * keep, grad)
        inner = jnp.sum(probs * grad_probs, axis=0, keepdims=True)
        grad_scores = (probs * (grad_probs - inner)).astype(BF)
        keep_columns(grad_queries, start, mask, (matmul_tn(grad_scores, key) * factor).astype(BF))
        keep_columns(text_key, start, mask, matmul(grad_scores, query) * factor)
        keep_columns(text_value, start, mask, matmul(probs.astype(BF), grad))

    each_head(one_head, 8)
    text_grad_ref[:, :width] = text_key[0:live, :]
    text_grad_ref[:, width:] = text_value[0:live, :]
    text_grad.send()
    grad_cq = grad_queries[...]
    grad_one = one_ref[...] + matmul_nt(grad_cq, query_w_ref[...])
    one_ref[...] = grad_one
    table_ref[2:3, :] = jnp.sum(grad_one * branch_ref[...], axis=0, keepdims=True)
    grad_attn = (mod_ref[2:3, :] * grad_one).astype(BF)
    grad_att = matmul_nt(grad_attn, out_w_ref[...]).astype(BF)
    pack_ref[0:rows, :] = grad_att

    product = grad_att.astype(F32) * att_ref[...].astype(F32)
    upper = product.astype(BF)
    lower = (product - upper.astype(F32)).astype(BF)
    size = width // HEADS
    column = lax.broadcasted_iota(jnp.int32, (width, 128), 0)
    low = (lax.broadcasted_iota(jnp.int32, (width, 128), 1) - HEADS) * size
    pick = jnp.logical_and(column >= low, column < low + size).astype(BF)
    stat = lse_ref[...] + matmul(upper, pick) + matmul(lower, pick)
    stat_ref[...] = stat
    turned = stat.T
    upper = [turned[8 * g : 8 * g + 8, :].astype(BF).astype(F32) for g in range(4)]
    lower = [turned[8 * g : 8 * g + 8, :] - part for g, part in enumerate(upper)]
    both = [jnp.concatenate(pair, axis=0) for pair in zip(upper, lower)]
    pack_ref[rows : rows + 16, :] = side_by_side(both, width).astype(BF)
    for slot in (pack, stat_out, one, table):
        slot.send()

    if count:
        for core in (0, 1):

            @pl.when(flag_ref[CORE] == core)
            def _(core=core):
                grads = [grad_cross, grad_cq, grad_attn]
                keep_ref[...] = half_columns(grads, core, count, False, keep_ref.shape[1])
                send_ref[...] = half_columns(grads, 1 - core, count, False, send_ref.shape[1])

    else:
        for index, grad in enumerate((grad_cross, grad_cq, grad_attn)):
            keep_ref[:, index * width : (index + 1) * width] = grad


def last_grad_kernel(
    dq_ref, dk_ref, dv_ref, weight_ref, tokens_ref, mod_ref, one_ref, table_ref, text_ref, out_ref, text_out, *, shape
):
    width = tokens_ref.shape[1]
    grad = sum(
        matmul_nt(ref[...], weight_ref[:, part * width : (part + 1) * width])
        for part, ref in enumerate((dq_ref, dk_ref, dv_ref))
    )
    normed, spread = normal(tokens_ref[...].astype(F32))
    back, shift, scale = norm_back(normed, spread, mod_ref[1:2, :], grad)
    out_ref[...] = one_ref[...] + back
    table = [shift, scale] + [table_ref[i : i + 1, :] for i in range(2, 6)]
    dp_count, sp_count = shape
    size = 6 * width // (dp_count * sp_count)

    def flat(low, high):
        pieces = []
        while low < high:
            row, at = divmod(low, width)
            stop = min(high, (row + 1) * width)
            pieces.append(table[row][:, at : at + stop - low])
            low = stop
        return pieces

    step = 2 * width // sp_count
    lines = [[], [], []]
    for place in range(sp_count):
        whole = [piece for i in range(dp_count) for piece in flat((i * sp_count + place) * size, (i * sp_count + place + 1) * size)]
        whole = jnp.concatenate(whole, axis=1)
        for i in range(3):
            lines[i].append(whole[:, i * step : (i + 1) * step])
    rows = [jnp.concatenate(line, axis=1) for line in lines]
    live = text_ref.shape[0]
    rows.append(jnp.zeros((128 - live - 3, 2 * width), F32))
    both = jnp.concatenate([text_ref[...]] + rows, axis=0)
    for low in range(0, 2 * width, 128):
        text_out[low : low + 128, :] = both[:, low : low + 128].T


def caption_kernel(text_ref, caption_ref, out_ref, *, blocks, size):
    live, width = caption_ref.shape
    text = text_ref[...].T
    grad = matmul_tn(caption_ref[...], text[:live].astype(BF)).astype(BF)
    tall = width // blocks
    line = jnp.concatenate([text[live + i : live + i + 1] for i in range(3)], axis=1)
    high = out_ref.shape[0] // blocks
    for block in range(blocks):
        out_ref[block * high : block * high + tall, :] = grad[block * tall : (block + 1) * tall]
        part = side_by_side([line[:, block * size : (block + 1) * size]], out_ref.shape[1])
        out_ref[block * high + tall : (block + 1) * high, :] = jnp.broadcast_to(
            part, (high - tall, out_ref.shape[1])
        ).astype(BF)


def side_by_side(pieces, width):
    missing = width - sum(piece.shape[1] for piece in pieces)
    if missing:
        pieces = [*pieces, jnp.zeros((pieces[0].shape[0], missing), pieces[0].dtype)]
    return pieces[0] if len(pieces) == 1 else jnp.concatenate(pieces, axis=1)


def lanes(width):
    return -(-width // 128) * 128


def slice_parts(size):
    return size // 128 * 128, size % 128


def half_columns(grads, core, count, joined, wide):
    if not joined:
        picked = []
        for grad in grads:
            size = grad.shape[1] // count
            low = [(2 * chip + core) * size for chip in (*range(0, count // 2, 2), *range(1, count // 2, 2))]
            picked.append(
                side_by_side([grad[:, at : at + size] for at in low], wide // len(grads))
            )
        return side_by_side(picked, wide)
    grad = grads[0] if len(grads) == 1 else jnp.concatenate(grads, axis=1)
    size = grad.shape[1] // count
    body, _ = slice_parts(size)
    picked = []
    for parity in (0, 1):
        low = [(2 * chip + core) * size for chip in range(parity, count // 2, 2)]
        picked += [grad[:, at : at + body] for at in low]
        picked.append(side_by_side([grad[:, at + body : at + size] for at in low], 128))
    return side_by_side(picked, wide)


def halves_kernel(core_ref, *refs, count, joined):
    keep_ref, send_ref = refs[-2:]
    for core in (0, 1):

        @pl.when(core_ref[CORE] == core)
        def _(core=core):
            grads = [ref[...] for ref in refs[:-2]]
            keep_ref[...] = half_columns(grads, core, count, joined, keep_ref.shape[1])
            send_ref[...] = half_columns(grads, 1 - core, count, joined, send_ref.shape[1])


def store_halves(flag, stores, pieces):
    for value in (0, 1):

        @pl.when(flag == value)
        def _(value=value):
            for store, piece in zip(stores, (pieces[1 - value], pieces[value])):
                store(piece())


def into(ref):
    def store(value):
        ref[:, : value.shape[1]] = value.astype(ref.dtype)

    return store


def add(*terms):
    return sum(term.astype(F32) for term in terms)


def sending(buffers, sems, out):
    state = {"count": 0}

    def wait(slot):
        pltpu.make_async_copy(buffers.at[slot], out, sems.at[slot]).wait()

    def put(pieces, targets):
        slot = state["count"] % 2
        if state["count"] >= 2:
            wait(slot)
        at = 0
        for piece in pieces:
            buffers[slot, at : at + piece.shape[0], : piece.shape[1]] = piece
            at += piece.shape[0]
        for condition, target in targets:
            copy = pltpu.make_async_copy(buffers.at[slot], target, sems.at[slot])
            if condition is None:
                copy.start()
            else:
                pl.when(condition)(copy.start)
        state["count"] += 1

    def done():
        for slot in range(min(2, state["count"])):
            wait(slot)

    return put, done


def wide_grad_kernel(order_ref, x0_hbm, x1_hbm, g0_hbm, g1_hbm, *refs, mode, first, columns):
    number = 2 if mode == "rows" else 4
    outs, (x_ref, g_ref, turned, buffers, sems, out_sems) = refs[:number], refs[number:]
    rows, width = x0_hbm.shape[0], x_ref.shape[1]
    x0_hbm, x1_hbm, g0_hbm, g1_hbm = (
        hbm if part is None else hbm.at[:, part] for hbm, part in zip((x0_hbm, x1_hbm, g0_hbm, g1_hbm), columns)
    )
    waits = fetch(
        sems,
        (x0_hbm, x_ref.at[0:rows, :]),
        (x1_hbm, x_ref.at[rows : 2 * rows, :]),
        (g0_hbm, g_ref.at[0:rows, :]),
        (g1_hbm, g_ref.at[rows : 2 * rows, :]),
    )
    for part in (0, 1):
        waits[part]()
        for low in range(0, width, 128):
            turned[low : low + 128, part * rows : (part + 1) * rows] = x_ref[
                part * rows : (part + 1) * rows, low : low + 128
            ].T
    waits[2]()
    waits[3]()
    tall = width // 4
    put, done = sending(buffers, out_sems, outs[0].at[0])
    half = g_ref.shape[1] // 2
    for step in range(4):
        here = pl.ds(pl.multiple_of((order_ref[ORDERS + 4 * first + step] if mode == "rows" else step) * tall, 16), tall)
        if mode == "rows":
            total = matmul(turned[here, :], g_ref[...]).astype(BF)
            put([total], [(None, outs[step // 2].at[step % 2])])
        else:
            for p in (0, 1):
                total = matmul(turned[here, :], g_ref[:, p * half : (p + 1) * half]).astype(BF)
                place, second = (step >> p) & 1, (step >> (1 - p)) & 1
                mine = order_ref[ROW + p]
                put(
                    [total],
                    [(mine != place, outs[2 * p].at[second]), (mine == place, outs[2 * p + 1].at[second])],
                )
    done()


def tall_grad_kernel(order_ref, *refs, count, mode, first, columns):
    sources, g0_hbm, g1_hbm = refs[: 2 * count], refs[2 * count], refs[2 * count + 1]
    outs, (x_ref, g_ref, turned, buffers, sems, out_sems) = refs[2 * count + 2 : 2 * count + 4], refs[2 * count + 4 :]
    rows = g0_hbm.shape[0]
    sources = [hbm if part is None else hbm.at[part, :] for hbm, part in zip(sources, columns)]
    pairs = [(g0_hbm, g_ref.at[0:rows, :]), (g1_hbm, g_ref.at[rows : 2 * rows, :])]
    for i, source in enumerate(sources):
        pairs.append((source, x_ref.at[i // 2, i % 2 * rows : (i % 2 + 1) * rows, :]))
    waits = fetch(sems, *pairs)
    wide = g_ref.shape[1]
    for part in (0, 1):
        waits[part]()
        for low in range(0, wide, 128):
            turned[low : low + 128, part * rows : (part + 1) * rows] = g_ref[
                part * rows : (part + 1) * rows, low : low + 128
            ].T
    for wait in waits[2:]:
        wait()
    if mode == "rows":
        high, tall = outs[0].shape[1:]
        put, done = sending(buffers, out_sems, outs[0].at[0])
        for step in range(4):
            here = pl.ds(pl.multiple_of(order_ref[ORDERS + 4 * first + step] * tall, 128), tall)
            total = matmul(turned[0:high, :], x_ref[0, :, here]).astype(BF)
            put([total], [(None, outs[step // 2].at[step % 2])])
    else:
        high = outs[0].shape[0] // count
        put, done = sending(buffers, out_sems, outs[0])
        for p in (0, 1):
            total = [
                matmul(turned[pl.ds(k * (wide // count) + p * high, high), :], x_ref[k]).astype(BF)
                for k in range(count)
            ]
            put(total, [(order_ref[NEAR] != p, outs[0]), (order_ref[NEAR] == p, outs[1])])
    done()


def add_kernel(flag_ref, *refs):
    refs[-1][...] = add(*[ref[...] for ref in refs[:-1]]).astype(BF)


def split_kernel(flag_ref, *refs, parts, axis, bit):
    views = refs[:-2]

    def joined(index):
        def piece():
            sums = [add(*[view[part] for view in views]) for part in parts[index]]
            return sums[0] if len(sums) == 1 else jnp.concatenate(sums, axis=axis)

        return piece

    store_halves(flag_ref[bit], [into(ref) for ref in refs[-2:]], [joined(0), joined(1)])


def split_pair_kernel(flag_ref, *refs):
    def group(p):
        keep, got, more = refs[3 * p : 3 * p + 3]
        return lambda: add(keep[...], got[...], more[...])

    store_halves(flag_ref[NEAR], [into(ref) for ref in refs[-2:]], [group(0), group(1)])


def last_kernel(keep_ref, got_ref, *outs, size):
    if size:
        body, tail = slice_parts(size)
        for part in (slice(0, body), slice(body, size)):
            outs[0][:, part] = add(keep_ref[:, part], got_ref[:, part])
    else:
        high, wide = outs[0].shape
        for index, out in enumerate(outs):
            part = slice(index * high, (index + 1) * high), slice(0, wide)
            out[...] = add(keep_ref[part], got_ref[part])


def prelude_kernel(place_ref, row_ref, len_ref, step_ref, embed_ref, table_ref, info_ref, mod_ref, slab, sem, *, rows):
    slots = len_ref.shape[1]
    width = table_ref.shape[1]

    def image_of(at):
        first = at * rows
        end = begin = length = step = jnp.int32(0)
        for slot in range(slots):
            count = len_ref[0, slot]
            inside = jnp.logical_and(end <= first, first < end + count)
            begin = jnp.where(inside, end, begin)
            length = jnp.where(inside, count, length)
            step = jnp.where(inside, step_ref[0, slot], step)
            end = end + count
        return (first - begin) // rows, length, step

    place = place_ref[0]
    core = place % 2
    blocks = BIG // rows
    within, length, step = image_of(place)
    pair_within = image_of(place + 1 - 2 * core)[0]
    flags = (
        length > rows,
        jnp.where(core == 0, pair_within + 1 < blocks, pair_within + 3 < blocks),
        jnp.where(core == 0, within + 1 < blocks, within >= 1),
        within + 2 < blocks,
        core == 1,
    )
    bits = [(place // 2) & 1, (place // 4) & 1, row_ref[0] & 1, (row_ref[0] >> 1) & 1]
    values = [flag.astype(jnp.int32) for flag in flags] + bits + [1 - bits[2], 1 - bits[3]]
    for first in (0, 1):
        mine = bits[2 + first]
        values += [((1 - mine if s < 2 else mine) << first) + ((s % 2) << (1 - first)) for s in range(4)]
    for index, value in enumerate(values):
        info_ref[index] = value
    copy = pltpu.make_async_copy(embed_ref.at[pl.ds(pl.multiple_of(step // 8 * 8, 8), 8), :], slab, sem)
    copy.start()
    copy.wait()
    row = slab[pl.ds(step % 8, 1), :]
    for index in range(6):
        mod_ref[index : index + 1, :] = (
            row[:, index * width : (index + 1) * width] + table_ref[index : index + 1, :]
        )


class Slot:
    def __init__(self, hbm, ref, sems, out=False):
        self.hbm, self.ref, self.out = hbm, ref, out
        self.sent = False
        self.copies = []
        for i, rows in enumerate(row_chunks(ref.shape, ref.dtype)):
            pair = (hbm.at[rows], ref.at[rows])
            self.copies.append(pltpu.make_async_copy(*(pair[::-1] if out else pair), sems.at[i]))

    def start(self):
        self.sent = True
        for copy in self.copies:
            copy.start()

    send = start

    def wait(self):
        for copy in self.copies:
            copy.wait()


def row_chunks(shape, dtype):
    if len(shape) > 2:
        return [slice(i, i + 1) for i in range(shape[0])]
    size = shape[0] * shape[1] * jnp.dtype(dtype).itemsize
    count = max([n for n in (1, 2, 3, 4, 6) if shape[0] % (16 * n) == 0 and size >= n * 200_000] or [1])
    high = shape[0] // count
    return [slice(i * high, (i + 1) * high) for i in range(count)]


def call(kernel, inputs, outs, flags=None, scratch=(), raw=(), lazy=False, limit=60):
    anywhere = pl.BlockSpec(memory_space=pl.ANY)
    arrays, views = [], []
    for entry in inputs:
        array, part = entry if isinstance(entry, tuple) else (entry, None)
        arrays.append(array)
        views.append(part)

    def view_shape(array, part):
        if part is None:
            return array.shape
        if isinstance(part, slice):
            return (array.shape[0], part.stop - part.start)
        return array.shape[1:]

    in_shapes = [view_shape(array, part) for array, part in zip(arrays, views)]
    slots = [(shape, array.dtype) for shape, array in zip(in_shapes, arrays)] + list(outs)
    held = [i for i in range(len(arrays)) if i not in raw]
    held += [len(arrays) + i for i in range(len(outs)) if "out" not in raw]
    buffers = [pltpu.VMEM(*slots[i]) for i in held]
    sems = [pltpu.SemaphoreType.DMA((len(row_chunks(*slots[i])),)) for i in held]

    def managed(*refs):
        refs = list(refs)
        flag_refs = [refs.pop(0)] if flags is not None else []
        hbm, rest = refs[: len(slots)], refs[len(slots) :]
        own, rest = rest[: len(scratch)], rest[len(scratch) :]
        views_in = []
        for ref, part in zip(hbm, views):
            if isinstance(part, slice):
                ref = ref.at[:, part]
            elif part is not None:
                ref = ref.at[flag_refs[0][part]]
            views_in.append(ref)
        given = views_in + hbm[len(arrays) :]
        for n, i in enumerate(held):
            given[i] = Slot(given[i], rest[n], rest[len(held) + n], i >= len(arrays))
        slots_in = [slot for slot in given if isinstance(slot, Slot) and not slot.out]
        slots_out = [slot for slot in given if isinstance(slot, Slot) and slot.out]
        if not lazy:
            for slot in slots_in:
                slot.start()
            for slot in slots_in:
                slot.wait()
            kernel(*flag_refs, *[getattr(slot, "ref", slot) if isinstance(slot, Slot) else slot for slot in given], *own)
        else:
            kernel(*flag_refs, *given, *own)
        for slot in slots_out:
            if not slot.sent:
                slot.send()
        for slot in slots_out:
            slot.wait()

    return pl.pallas_call(
        managed,
        in_specs=([pl.BlockSpec(memory_space=pltpu.SMEM)] if flags is not None else []) + [anywhere] * len(arrays),
        out_specs=[anywhere] * len(outs),
        out_shape=[jax.ShapeDtypeStruct(shape, dtype) for shape, dtype in outs],
        scratch_shapes=[*scratch, *buffers, *sems],
        compiler_params=pltpu.CompilerParams(vmem_limit_bytes=limit * MIB),
        cost_estimate=pl.CostEstimate(flops=1000, bytes_accessed=1000, transcendentals=0),
    )(*([] if flags is None else [flags]), *arrays)


def prelude(place, row_place, image_len, timestep, time_embed, mod_table, rows):
    smem = pl.BlockSpec(memory_space=pltpu.SMEM)
    return pl.pallas_call(
        functools.partial(prelude_kernel, rows=rows),
        in_specs=[smem] * 4 + [pl.BlockSpec(memory_space=pl.ANY), pl.BlockSpec(memory_space=pltpu.VMEM)],
        out_specs=[smem, pl.BlockSpec(memory_space=pltpu.VMEM)],
        out_shape=[jax.ShapeDtypeStruct((ORDERS + 8,), jnp.int32), jax.ShapeDtypeStruct(mod_table.shape, F32)],
        scratch_shapes=[pltpu.VMEM((8, time_embed.shape[1]), F32), pltpu.SemaphoreType.DMA],
        compiler_params=pltpu.CompilerParams(vmem_limit_bytes=4 * MIB),
    )(place.reshape(1), row_place.reshape(1), image_len, timestep, time_embed, mod_table)


def half_width(grads, count, joined):
    size = (sum(grad.shape[1] for grad in grads) if joined else grads[0].shape[1]) // count
    body, _ = slice_parts(size)
    return 2 * (count // 4 * body + 128) if joined else len(grads) * -(-count // 2 * size // 128) * 128


def halves(core, grads, count, joined):
    out = ((grads[0].shape[0], half_width(grads, count, joined)), BF)
    return call(functools.partial(halves_kernel, count=count, joined=joined), grads, [out] * 2, flags=core, limit=6)


def split(flags, bit, inputs, parts, shape, axis=1):
    return call(
        functools.partial(split_kernel, parts=parts, axis=axis, bit=bit),
        inputs,
        [(shape, BF), (shape, F32)],
        flags=flags,
    )


def add_last(keep, got, size, shapes):
    return call(functools.partial(last_kernel, size=size), [keep, got], [(shape, F32) for shape in shapes])


def wide_grad(order, source, mode, first=0):
    entries = [entry if isinstance(entry, tuple) else (entry, None) for entry in source]
    source = [array for array, _ in entries]
    columns = [part and slice(part.start, part.stop or array.shape[1]) for array, part in entries]
    rows, width = source[0].shape[0], columns[0].stop if columns[0] else source[0].shape[1]
    depth = source[2].shape[1]
    wide, number = (depth, 2) if mode == "rows" else (depth // 2, 4)
    return call(
        functools.partial(wide_grad_kernel, mode=mode, first=first, columns=columns),
        source,
        [((2, width // 4, wide), BF)] * number,
        flags=order,
        raw=(0, 1, 2, 3, "out"),
        scratch=[
            pltpu.VMEM((2 * rows, width), BF),
            pltpu.VMEM((2 * rows, depth), BF),
            pltpu.VMEM((width, 2 * rows), BF),
            pltpu.VMEM((2, width // 4, wide), BF),
            pltpu.SemaphoreType.DMA((4,)),
            pltpu.SemaphoreType.DMA((2,)),
        ],
    )


def tall_grad(order, acts, keep, got, size, mode, first=0):
    count = len(acts)
    entries = [entry if isinstance(entry, tuple) else (entry, None) for pair in acts for entry in pair]
    rows, wide = keep.shape
    width = entries[0][0].shape[1]
    shape = (2, 4 * size, width // 4) if mode == "rows" else (2 * size * count, width)
    return call(
        functools.partial(
            tall_grad_kernel, count=count, mode=mode, first=first, columns=[part for _, part in entries]
        ),
        [array for array, _ in entries] + [keep, got],
        [(shape, BF)] * 2,
        flags=order,
        raw=(*range(2 * count + 2), "out"),
        scratch=[
            pltpu.VMEM((count, 2 * rows, width), BF),
            pltpu.VMEM((2 * rows, wide), BF),
            pltpu.VMEM((wide, 2 * rows), BF),
            pltpu.VMEM((2, *shape[-2:]), BF),
            pltpu.SemaphoreType.DMA((2 * count + 2,)),
            pltpu.SemaphoreType.DMA((2,)),
        ],
    )


def local(
    tokens,
    image_len,
    timestep,
    caption,
    time_embed,
    mod_table,
    w_qkv,
    w_out,
    cross_q,
    cross_kv,
    cross_out,
    w_up,
    w_down,
    cotangent,
):
    sp_count = lax.axis_size("sp")
    dp_count = lax.axis_size("dp")
    place = lax.axis_index("sp")
    row_place = lax.axis_index("dp")
    core = place % 2
    rows, width = tokens.shape[1:]
    factor = 1.0 / math.sqrt(width // HEADS)
    blocks = BIG // rows
    assert blocks == 4

    big, modulation = prelude(place, row_place, image_len, timestep, time_embed, mod_table, rows)
    shift_one, scale_one, gate_one, shift_two, scale_two, gate_two = [modulation[i] for i in range(6)]

    def tie(value, *before):
        return lax.optimization_barrier((value, *[array for array in before if array is not None]))[0]

    pairs = [(i, i ^ 1) for i in range(sp_count)]
    others = [(i, i + 1) for i in range(1, sp_count - 1, 2)] + [(i + 1, i) for i in range(1, sp_count - 1, 2)]
    ahead = [(i, i + 2) for i in range(sp_count - 2)]
    back = [(i + 2, i) for i in range(sp_count - 2)]

    def image_blocks(block, *before):
        from_back = lax.ppermute(block, "sp", ahead)
        from_ahead = lax.ppermute(block, "sp", back)
        from_ahead, from_back = tie(from_ahead, *before), tie(from_back, *before)
        send_pair = jnp.concatenate([jnp.where(big[1] == 1, from_ahead, from_back), block], axis=0)
        send_other = jnp.where(core == 1, from_back, from_ahead)
        both = lax.ppermute(send_pair, "sp", pairs)
        third = lax.ppermute(send_other, "sp", others)
        return [both, third, from_ahead, from_back], (send_pair, send_other)

    def chosen(both, third, from_ahead, from_back):
        high = both.shape[0] // 2
        return [
            both[:high],
            jnp.where(big[2] == 1, both[high:], third),
            jnp.where(big[3] == 1, from_ahead, from_back),
        ]

    def swap(array):
        return lax.ppermute(array, "sp", pairs)

    token_blocks, token_sends = image_blocks(tokens[0])

    def first_norm(block):
        return (normal(block.astype(F32))[0] * (1.0 + scale_one) + shift_one).astype(BF)

    first_in = first_norm(tokens[0])
    other_in = first_norm(jnp.concatenate(chosen(*token_blocks), axis=0))

    chips = sp_count // 2
    square = dp_count == 4 and chips == 4

    def own_half(*grads, joined=True):
        if square:
            return halves(big, grads, sp_count, joined)
        grads = [jnp.concatenate(grads, axis=1)] if joined else grads
        size = grads[0].shape[1] // sp_count
        even, odd = [
            jnp.concatenate(
                [g[:, i * size : (i + 1) * size] for g in grads for i in range(c, sp_count, 2)], axis=1
            )
            for c in (0, 1)
        ]
        return jnp.where(core == 0, even, odd), jnp.where(core == 0, odd, even)

    high = width // 4

    def to_row(array, bit):
        return lax.ppermute(array, "dp", [(i, i ^ (1 << bit)) for i in range(dp_count)])

    def to_chip(array, bit):
        return lax.ppermute(array, "sp", [(i, i ^ (2 << bit)) for i in range(sp_count)])

    def plain_sum(sources, size):
        finals = []
        for item, (x0, x1, g0, g1) in enumerate(sources):
            columns = slice(item * chips * size, (item + 1) * chips * size)
            part = (matmul_tn(x0, g0[:, columns]) + matmul_tn(x1, g1[:, columns])).astype(BF)
            part = part.reshape(dp_count, -1, chips, size).transpose(0, 2, 1, 3)
            bit = dp_count // 2
            while bit:
                mine = (row_place // bit) % 2
                part = part.reshape(2, bit, chips, -1, size)
                got = lax.ppermute(part[1 - mine], "dp", [(i, i ^ bit) for i in range(dp_count)])
                part = add(part[mine], got).astype(BF)
                bit //= 2
            part = part.reshape(chips, -1, size)
            bit = chips // 2
            while bit:
                mine = (place // 2 // bit) % 2
                part = part.reshape(2, bit, -1, size)
                got = lax.ppermute(part[1 - mine], "sp", [(i, i ^ (2 * bit)) for i in range(sp_count)])
                part = add(part[mine], got).astype(BF)
                bit //= 2
            finals.append(part[0].astype(F32))
        return finals

    def add_picked(keep, got, flag):
        return call(add_kernel, [(keep, flag), (got, flag)], [(keep.shape[1:], BF)], flags=big)

    everything = slice(None)

    def cut_slices(size):
        body, tail = slice_parts(size)
        return [
            [
                (everything, slice(h * body, (h + 1) * body)),
                (everything, slice(2 * body + h * tail, 2 * body + (h + 1) * tail)),
            ]
            for h in (0, 1)
        ]

    def sum_wide(source, first, size):
        second = 1 - first
        if size < 256:
            send, keep = tall_grad(big, [source[:2]], *source[2:], size, "rows", first)
        else:
            send, keep = wide_grad(big, source, "rows", first)
        late = yield send
        got = to_row(send, first)
        if size < 256:
            _, tall, wide = keep.shape
            flat = lambda array: array.reshape(2 * tall, wide)
            rows_at = lambda low, high: (slice(low, high),)
            groups = [
                [rows_at(y * tall + h * tall // 2, y * tall + (h + 1) * tall // 2) for y in (0, 1)]
                for h in (0, 1)
            ]
            send, keep = split(big, NEAR, [flat(tie(keep, late)), flat(got)], groups, (tall, wide), 0)
            late = yield send
            groups = [[rows_at(h * tall // 2, (h + 1) * tall // 2)] for h in (0, 1)]
            inputs = [tie(keep, late), to_chip(send, 0)]
            send, keep = split(big, ROW + second, inputs, groups, (tall // 2, wide), 0)
            late = yield send
            groups = [[rows_at(h * tall // 4, (h + 1) * tall // 4)] for h in (0, 1)]
            inputs = [tie(keep, late), to_row(send, second)]
            send, keep = split(big, FAR, inputs, groups, (tall // 4, wide), 0)
            late = yield send
            (final,) = add_last(tie(keep, late), to_chip(send, 1), 0, [(size, wide)])
            yield final.T
        else:
            (send,) = add_picked(tie(keep, late), got, OTHER + second)
            late = yield send
            tall, wide = send.shape
            more = to_row(send, second)
            inputs = [(tie(keep, late), ROW + second), (got, ROW + second), more]
            groups = [[(everything, slice(h * wide // 2, (h + 1) * wide // 2))] for h in (0, 1)]
            send, keep = split(big, NEAR, inputs, groups, (tall, wide // 2))
            late = yield send
            shape = (tall, size // 128 * 128 + 128)
            send, keep = split(big, FAR, [tie(keep, late), to_chip(send, 0)], cut_slices(size), shape)
            late = yield send
            (final,) = add_last(tie(keep, late), to_chip(send, 1), size, [(tall, size)])
            yield final

    def sum_both(source, size):
        outs = wide_grad(big, source, "both")
        late = yield outs[0]
        got = [to_row(outs[0], 0), to_row(outs[2], 1)]
        sends = [
            *add_picked(tie(outs[1], late), got[0], OTHER + 1),
            *add_picked(tie(outs[3], late), got[1], OTHER),
        ]
        late = yield sends[1]
        shape = sends[0].shape
        more = [to_row(sends[0], 1), to_row(sends[1], 0)]
        send, keep = call(
            split_pair_kernel,
            [
                (tie(outs[1], late), ROW + 1), (got[0], ROW + 1), more[0],
                (outs[3], ROW), (got[1], ROW), more[1],
            ],
            [(shape, BF), (shape, F32)],
            flags=big,
        )
        late = yield send
        shape = (shape[0], size // 128 * 128 + 128)
        send, keep = split(big, FAR, [tie(keep, late), to_chip(send, 0)], cut_slices(size), shape)
        late = yield send
        (final,) = add_last(tie(keep, late), to_chip(send, 1), size, [(high, size)])
        yield final

    def sum_chips_first(acts, keep, got, size):
        count = len(acts)
        send, keep = tall_grad(big, acts, keep, got, size, "chips")
        late = yield send
        got = to_chip(send, 0)
        groups = [[(everything, slice(2 * h * high, 2 * (h + 1) * high))] for h in (0, 1)]
        shape = (2 * count * size, lanes(2 * high))
        send, keep = split(big, ROW + 1, [tie(keep, late), got], groups, shape)
        late = yield send
        got = to_row(send, 1)
        groups = [[(everything, slice(h * high, (h + 1) * high))] for h in (0, 1)]
        shape = (2 * count * size, lanes(high))
        send, keep = split(big, ROW, [tie(keep, late), got], groups, shape)
        late = yield send
        got = to_row(send, 0)
        groups = [
            [(slice((2 * k + h) * size, (2 * k + h + 1) * size),) for k in range(count)] for h in (0, 1)
        ]
        shape = (count * size, lanes(high))
        send, keep = split(big, FAR, [tie(keep, late), got], groups, shape, 0)
        late = yield send
        finals = add_last(tie(keep, late), to_chip(send, 1), 0, [(size, high)] * count)
        yield [final.T for final in finals]

    caption_rows = caption[0]
    live = caption_rows.shape[0]
    padded = -(-live // 128) * 128
    caption_pad = jnp.concatenate([caption_rows, jnp.zeros((padded - live, width), BF)], axis=0)
    text = matmul(caption_pad, cross_kv).astype(BF)
    grad_mlp = (gate_two * cotangent[0].astype(F32)).astype(BF)
    mlp_keep, mlp_send = own_half(grad_mlp, joined=False)
    mlp_got = swap(mlp_send)
    first_pair = swap(first_in)
    own = matmul(tie(first_in, *token_sends), w_qkv).astype(BF)
    far_qkv = matmul(other_in, w_qkv).astype(BF)
    block = ((rows, width), BF)
    stream = ((rows, width), F32)
    stats = ((rows, 128), F32)
    units = w_up.shape[1]
    tile = units // 4
    half = half_width([w_up], sp_count, True) if square else units
    small_width = half_width([grad_mlp] * 3, sp_count, False) if square else 3 * width
    small_out = ((rows, small_width), BF)
    (
        acts, up_pack, hidden, pre_keep,
        stream_three, grad_one, small_keep, small_send, grad_text, pack, stat, table,
    ) = call(
        functools.partial(forward_kernel, factor=factor, live=live, count=sp_count if square else 0),
        [
            own, (tie(far_qkv, mlp_got, first_pair), slice(width, 3 * width)), tokens[0], modulation, text,
            w_out, cross_q, cross_out, grad_mlp, cotangent[0], w_up, w_down,
        ],
        [
            ((3 * rows, width), BF), ((rows, width + (half if square else 0)), BF), ((rows, units), BF),
            ((rows, half), BF),
            stream, stream, small_out, small_out, ((live, 2 * width), F32), ((rows + 16, width), BF), stats,
            (modulation.shape, F32),
        ],
        flags=big,
        raw=(10, 11),
        lazy=True,
        scratch=[
            pltpu.VMEM((3, width, tile), BF),
            pltpu.VMEM((3, tile, width), BF),
            pltpu.SemaphoreType.DMA((3, 4)),
            pltpu.VMEM((rows, tile), BF),
            pltpu.VMEM((rows, tile), BF),
            pltpu.VMEM((rows, 128), F32),
            pltpu.VMEM((rows, width), F32),
            pltpu.VMEM((rows, width), BF),
            *[pltpu.VMEM((rows, width), F32)] * 3,
            *[pltpu.VMEM((rows, width), BF)] * 2,
            *[pltpu.VMEM((padded, width), F32)] * 2,
        ],
        limit=63,
    )

    if not square:
        pre_keep, pre_send = own_half(pre_keep)
        up_pack = jnp.concatenate([up_pack, pre_send], axis=1)
    hidden_pair, up_pair = swap(hidden), swap(up_pack)
    if not square:
        small_keep, small_send = own_half(*jnp.split(small_keep, 3, axis=1), joined=False)
    slice_of = lambda weight: weight.shape[1] // sp_count
    down_source = (hidden, hidden_pair, mlp_keep, mlp_got)
    up_source = ((up_pack, slice(0, width)), (up_pair, slice(0, width)), pre_keep, (up_pair, slice(width, None)))
    send_down = send_up = send_small = None
    if square:
        up_sum = sum_wide((up_source[0], up_source[1], tie(pre_keep, pack), up_source[3]), 1, slice_of(w_up))
        send_up = next(up_sum)
        down_sum = sum_wide((tie(hidden, send_up), *down_source[1:]), 0, slice_of(w_down))
        send_down = next(down_sum)
        small_got = swap(tie(small_send, send_up))
        small_acts = tie(acts, send_up)
        small_acts = [small_acts, swap(small_acts)]
        small_acts = [[(part, slice(i * rows, (i + 1) * rows)) for part in small_acts] for i in range(3)]
        small_sum = sum_chips_first(small_acts, tie(small_keep, send_down), small_got, slice_of(w_out))
        send_small = next(small_sum)
    pack_blocks, pack_sends = image_blocks(pack, send_small)
    (grad_queries,) = call(
        functools.partial(query_grad_kernel, factor=factor),
        [own, (far_qkv, slice(width, 3 * width)), tie(pack, *pack_sends), stat],
        [block],
        flags=big,
        lazy=True,
        scratch=[pltpu.VMEM((rows, width), F32)],
    )
    proj_out = ((rows, half_width([w_qkv], sp_count, True) if square else 3 * width), BF)
    grad_keys, grad_values, proj_keep, proj_send = call(
        functools.partial(key_grad_kernel, factor=factor, count=sp_count if square else 0),
        [own, (far_qkv, slice(0, width)), tie(pack, grad_queries), grad_queries, *pack_blocks],
        [block, block, proj_out, proj_out],
        flags=big,
        raw=(4, 5, 6, 7),
        lazy=True,
        scratch=[
            pltpu.VMEM((2 * HEADS, blocks * rows), F32),
            pltpu.VMEM(((blocks - 1) * rows, width), BF),
            pltpu.VMEM((blocks - 1, 16, width), BF),
            pltpu.VMEM((rows, width), F32),
            pltpu.VMEM((rows, width), F32),
            pltpu.SemaphoreType.DMA((2 * blocks - 2,)),
        ],
    )
    if not square:
        proj_keep, proj_send = own_half(*jnp.split(proj_keep, 3, axis=1))
    qkv_source = (first_in, first_pair, proj_keep, swap(proj_send))
    grad_tokens, text_part = call(
        functools.partial(last_grad_kernel, shape=(dp_count, sp_count)),
        [
            grad_queries, tie(grad_keys, proj_send), grad_values, w_qkv, tokens[0], modulation, grad_one, table,
            grad_text,
        ],
        [stream, ((2 * width, 128), F32)],
    )
    table = text_part
    text_part = lax.psum_scatter(text_part, "sp", scatter_dimension=0, tiled=True)

    def caption_sum(late):
        part = tie(text_part, late)
        tall, size = width // dp_count, 6 * width // (dp_count * sp_count)
        high = lanes(tall + 16) if dp_count != 4 else tall + 16
        (both,) = call(
            functools.partial(caption_kernel, blocks=dp_count, size=size),
            [part, caption_rows],
            [((dp_count * high, part.shape[0]), BF)],
        )
        total = lax.psum_scatter(both, "dp", scatter_dimension=0, tiled=True).astype(F32)
        return both, total[:tall], total[tall, :size]

    late = None
    if square:
        late = down_sum.send(up_sum.send(table))
        qkv_sum = sum_both((tie(first_in, late), *qkv_source[1:]), slice_of(w_qkv))
        late = next(qkv_sum)
        for step in (small_sum, up_sum, down_sum, qkv_sum):
            late = step.send(late)
        late, final_ckv, final_table = caption_sum(late)
        for step in (up_sum, small_sum, down_sum):
            late = step.send(late)
        final_up = up_sum.send(late)
        late = small_sum.send(qkv_sum.send(final_up))
        final_down = down_sum.send(late)
        late = qkv_sum.send(tie(final_down, final_ckv))
        final_small = small_sum.send(late)
        final_qkv = qkv_sum.send(final_small[0])
    else:
        _, final_ckv, final_table = caption_sum(table)
        small_pair, small_got = swap(acts), swap(small_send)
        small = [
            (acts[i * rows : (i + 1) * rows], small_pair[i * rows : (i + 1) * rows], small_keep, small_got)
            for i in range(3)
        ]
        up_source = (up_pack[:, :width], up_pair[:, :width], pre_keep, up_pair[:, width:])
        final_small = plain_sum(small, slice_of(w_out))
        (final_down,) = plain_sum([down_source], slice_of(w_down))
        (final_up,) = plain_sum([up_source], slice_of(w_up))
        (final_qkv,) = plain_sum([qkv_source], slice_of(w_qkv))
    return (
        stream_three[None],
        grad_tokens[None],
        final_table,
        final_qkv,
        final_small[2],
        final_small[1],
        final_ckv,
        final_small[0],
        final_up,
        final_down,
    )


def solution(mesh):
    return jax.shard_map(
        local,
        mesh=mesh,
        in_specs=(
            P("dp", "sp", None),
            P("dp", None),
            P("dp", None),
            P("dp", None, None),
            P(),
            P(),
            P(),
            P(),
            P(),
            P(),
            P(),
            P(),
            P(),
            P("dp", "sp", None),
        ),
        out_specs=(
            P("dp", "sp", None),
            P("dp", "sp", None),
            P(("dp", "sp")),
            P("dp", "sp"),
            P("dp", "sp"),
            P("dp", "sp"),
            P("dp", "sp"),
            P("dp", "sp"),
            P("dp", "sp"),
            P("dp", "sp"),
        ),
        check_vma=False,
    )
```

```python
import functools
import math

import jax
import jax.numpy as jnp
from jax import lax
from jax.experimental import pallas as pl
from jax.experimental.pallas import tpu as pltpu
from jax.sharding import PartitionSpec as P

HEADS = 16
BIG = 1024
EPS = 1e-06
BIGNEG = -1e30
LOG2E = 1.4426950408889634
BF = jnp.bfloat16
F32 = jnp.float32
LARGE, CORE, NEAR, FAR, ROW, OTHER, ORDERS = 0, 4, 5, 6, 7, 9, 11
WIN = 256
COST_SCALE = 0.001
MIB = 1024 * 1024


def matmul(left, right):
    return jnp.dot(left, right, preferred_element_type=F32)


def matmul_tn(left, right):
    return lax.dot_general(left, right, (((0,), (0,)), ((), ())), preferred_element_type=F32)


def matmul_nt(left, right):
    return lax.dot_general(left, right, (((1,), (1,)), ((), ())), preferred_element_type=F32)


def head_window(head, width):
    size = width // HEADS
    low = head * size
    start = pl.multiple_of(jnp.minimum(low // 128 * 128, width - WIN), 128)
    lane = lax.broadcasted_iota(jnp.int32, (1, WIN), 1) + start
    return start, jnp.logical_and(lane >= low, lane < low + size)


def pair_window(pair, width):
    size = width // HEADS
    low = 2 * pair * size
    start = pl.multiple_of(low // 128 * 128, 128)
    lane = lax.broadcasted_iota(jnp.int32, (1, WIN), 1) + start
    return start, [
        jnp.logical_and(lane >= low + i * size, lane < low + (i + 1) * size) for i in (0, 1)
    ]


def stacked(block, masks):
    return jnp.concatenate([block * mask.astype(block.dtype) for mask in masks], axis=0)


def keep_pair(ref, start, masks, value):
    rows = ref.shape[0]
    win = pl.ds(start, WIN)
    picked = jnp.where(masks[1], value[rows:], ref[:, win])
    ref[:, win] = jnp.where(masks[0], value[:rows], picked)


def each_pair(body, unroll=2):
    def step(pair, carry):
        body(pair)
        return carry

    lax.fori_loop(0, HEADS // 2, step, 0, unroll=unroll)


def window(ref, start, offset=0):
    return ref[:, pl.ds(pl.multiple_of(start + offset, 128), WIN)]


def keep_columns(ref, start, mask, value):
    win = pl.ds(start, WIN)
    ref[:, win] = jnp.where(mask, value, ref[:, win])


def blockwise(function, arrays, high, wide=None):
    rows, columns = arrays[0].shape
    strips = []
    for low in range(0, rows, high):
        pieces = []
        for left in range(0, columns, wide or columns):
            block = [
                array[
                    slice(low, low + high) if array.shape[0] > 1 else slice(None),
                    slice(left, left + wide) if wide and array.shape[1] > 1 else slice(None),
                ]
                for array in arrays
            ]
            pieces.append(function(*block))
        strips.append([jnp.concatenate(parts, axis=1) if len(parts) > 1 else parts[0] for parts in zip(*pieces)])
    return [jnp.concatenate(parts, axis=0) for parts in zip(*strips)]


def each_head(body, unroll=4):
    def step(head, carry):
        body(head)
        return carry

    lax.fori_loop(0, HEADS, step, 0, unroll=unroll)


def fetch(sems, *pairs):
    copies = [pltpu.make_async_copy(source, target, sems.at[i]) for i, (source, target) in enumerate(pairs)]
    for copy in copies:
        copy.start()
    return [copy.wait for copy in copies]


def attend(big, own_ref, far_ref, out_ref, lse_ref, factor):
    width = out_ref.shape[1]
    scale = factor * LOG2E

    def run(sides):
        def one_pair(pair):
            start, masks = pair_window(pair, width)
            query = stacked(window(own_ref, start), masks)
            scores = [matmul_nt(query, window(side, start, key)) for side, key in sides]
            top = functools.reduce(jnp.maximum, [jnp.max(s, axis=1, keepdims=True) for s in scores])
            raised = [jnp.exp2((s - top) * scale) for s in scores]
            total = sum(jnp.sum(r, axis=1, keepdims=True) for r in raised)
            inverse = 1.0 / total
            result = sum(
                matmul((r * inverse).astype(BF), window(side, start, key + width))
                for r, (side, key) in zip(raised, sides)
            )
            keep_pair(out_ref, start, masks, result.astype(BF))
            lse = top * scale + jnp.log2(total)
            rows = out_ref.shape[0]
            lane = lax.broadcasted_iota(jnp.int32, (1, 128), 1)
            kept = jnp.where(lane == 2 * pair + 1, lse[rows:], lse_ref[...])
            lse_ref[...] = jnp.where(lane == 2 * pair, lse[:rows], kept)

        each_pair(one_pair)

    lse_ref[...] = jnp.zeros_like(lse_ref)

    @pl.when(big)
    def _():
        run([(own_ref, width), (far_ref, 0)])

    @pl.when(jnp.logical_not(big))
    def _():
        run([(own_ref, width)])


def query_grad_kernel(big_ref, own_ref, far_ref, pack_ref, stat_ref, out_ref, *, factor):
    rows, width = out_ref.shape
    scale = factor * LOG2E

    def run(sides):
        def one_pair(pair):
            start, masks = pair_window(pair, width)
            query = stacked(window(own_ref, start), masks)
            grad = stacked(window(pack_ref.at[0:rows, :], start), masks)
            lane = lax.broadcasted_iota(jnp.int32, (1, 128), 1)
            stat = stat_ref[...]

            def column(low):
                return jnp.concatenate(
                    [
                        jnp.sum(jnp.where(lane == low + 2 * pair + i, stat, 0.0), axis=1, keepdims=True)
                        for i in (0, 1)
                    ],
                    axis=0,
                )

            lse, delta = column(0), column(HEADS)
            total = None
            for side, offset in sides:
                key = window(side, start, offset)
                prob = jnp.exp2(matmul_nt(query, key) * scale - lse)
                grad_prob = matmul_nt(grad, window(side, start, offset + width))
                grad_score = (prob * (grad_prob - delta)).astype(BF)
                part = matmul(grad_score, key)
                total = part if total is None else total + part
            keep_pair(out_ref, start, masks, (total * factor).astype(BF))

        each_pair(one_pair, 4)

    @pl.when(big_ref[0] == 1)
    def _():
        run([(own_ref, width), (far_ref, 0)])

    @pl.when(big_ref[0] == 0)
    def _():
        run([(own_ref, width)])


def key_grad_kernel(flag_ref, own, far, pack, dq, both, third, ahead, back, *refs, factor, count):
    dk, dv, keep_out, send_out, stats, grads, tails, sems = refs
    own_ref, far_ref, pack_ref, dq_ref = (slot.ref for slot in (own, far, pack, dq))
    dk_ref, dv_ref, keep_ref, send_ref = (slot.ref for slot in (dk, dv, keep_out, send_out))
    rows, width = dk_ref.shape
    tall = rows + 16

    def copies(block, source, low):
        return (
            pltpu.make_async_copy(
                source.at[low : low + rows, :], grads.at[block * rows : (block + 1) * rows, :], sems.at[2 * block]
            ),
            pltpu.make_async_copy(source.at[low + rows : low + tall, :], tails.at[block], sems.at[2 * block + 1]),
        )

    def begin(block, flag, first, second):
        for value, (source, low) in ((1, first), (0, second)):

            @pl.when(flag == value)
            def _(source=source, low=low):
                for copy in copies(block, source, low):
                    copy.start()

    for copy in copies(0, both, 0):
        copy.start()
    begin(1, flag_ref[2], (both, tall), (third, 0))
    begin(2, flag_ref[3], (ahead, 0), (back, 0))
    blocks = 4
    for slot in (own, far, pack, dq):
        slot.start()
    for block in range(blocks - 1):
        for copy in copies(block, both, 0):
            copy.wait()
    for slot in (own, far, pack, dq):
        slot.wait()
    scale = factor * LOG2E

    def unpack(block, both):
        both = both.astype(F32)
        joined = both[:8] + both[8:]
        for group in range(4):
            stats[8 * group : 8 * group + 8, block * rows : block * rows + rows] = joined[
                :, group * rows : group * rows + rows
            ]

    unpack(0, pack_ref[rows:, :])
    for block in range(blocks - 1):
        unpack(block + 1, tails[block])

    def run(parts):
        def one_pair(pair):
            start, masks = pair_window(pair, width)
            key = stacked(window(own_ref, start, width), masks)
            value = stacked(window(own_ref, start, 2 * width), masks)

            def line(at, low, high):
                return jnp.concatenate(
                    [
                        jnp.broadcast_to(stats[pl.ds(at + 2 * pair + i, 1), low:high], (rows, high - low))
                        for i in (0, 1)
                    ],
                    axis=0,
                )

            grad_key = grad_value = 0.0
            for query_ref, grad_ref, low, high in parts:
                query, grad = window(query_ref, start), window(grad_ref.at[0 : high - low, :], start)
                prob = jnp.exp2(matmul_nt(key, query) * scale - line(0, low, high))
                grad_prob = matmul_nt(value, grad)
                grad_score = (prob * (grad_prob - line(HEADS, low, high))).astype(BF)
                grad_value = grad_value + matmul(prob.astype(BF), grad)
                grad_key = grad_key + matmul(grad_score, query)
            keep_pair(dk_ref, start, masks, (grad_key * factor).astype(BF))
            keep_pair(dv_ref, start, masks, grad_value.astype(BF))

        each_pair(one_pair, 4)

    local = (own_ref, pack_ref, 0, rows)
    @pl.when(flag_ref[0] == 1)
    def _():
        run([local, (far_ref, grads, rows, blocks * rows)])

    @pl.when(flag_ref[0] == 0)
    def _():
        run([local])

    dk.send()
    dv.send()
    if count:
        for core in (0, 1):

            @pl.when(flag_ref[CORE] == core)
            def _(core=core):
                grads = [ref[...] for ref in (dq_ref, dk_ref, dv_ref)]
                keep_ref[...] = half_columns(grads, core, count, True, keep_ref.shape[1])
                send_ref[...] = half_columns(grads, 1 - core, count, True, send_ref.shape[1])

    else:
        for index, ref in enumerate((dq_ref, dk_ref, dv_ref)):
            keep_ref[:, index * width : (index + 1) * width] = ref[...]


def text_probs(query, key, scale, live, axis):
    scores = matmul_nt(query, key) if axis else matmul_nt(key, query)
    shape = (1, scores.shape[1]) if axis else (scores.shape[0], 1)
    scores = jnp.where(lax.broadcasted_iota(jnp.int32, shape, axis) < live, scores, BIGNEG)
    raised = jnp.exp2((scores - jnp.max(scores, axis=axis, keepdims=True)) * scale)
    return raised * (1.0 / jnp.sum(raised, axis=axis, keepdims=True))


def normal(stream):
    centred = stream - jnp.mean(stream, axis=-1, keepdims=True)
    spread = lax.rsqrt(jnp.mean(centred * centred, axis=-1, keepdims=True) + EPS)
    return centred * spread, spread


def norm_back(normed, spread, scale, grad):
    scaled = grad * (1.0 + scale)
    back = spread * (
        scaled
        - jnp.mean(scaled, axis=-1, keepdims=True)
        - normed * jnp.mean(scaled * normed, axis=-1, keepdims=True)
    )
    return back, jnp.sum(grad, axis=0, keepdims=True), jnp.sum(grad * normed, axis=0, keepdims=True)


def middle(tokens_ref, mod_ref, att_ref, weights, text_ref, refs, factor, live):
    branch_ref, cross_in_ref, queries_ref, mixed_ref, stream_ref, second_ref = refs
    width = tokens_ref.shape[1]
    out_w_ref, query_w_ref, cross_w_ref = weights
    branch = matmul(att_ref[...], out_w_ref[...])
    branch_ref[...] = branch
    stream = tokens_ref[...].astype(F32) + mod_ref[2:3, :] * branch
    stream_ref[...] = stream
    cross_in = stream.astype(BF)
    cross_in_ref[...] = cross_in
    queries_ref[...] = matmul(cross_in, query_w_ref[...]).astype(BF)

    def one_head(head):
        start, mask = head_window(head, width)
        query = window(queries_ref, start) * mask.astype(BF)
        probs = text_probs(query, window(text_ref, start), factor * LOG2E, live, 1)
        result = matmul(probs.astype(BF), window(text_ref, start, width))
        keep_columns(mixed_ref, start, mask, result.astype(BF))

    each_head(one_head, 8)
    stream = stream_ref[...] + matmul(mixed_ref[...], cross_w_ref[...])
    stream_ref[...] = stream
    scale, shift = 1.0 + mod_ref[4:5, :], mod_ref[3:4, :]
    for low in range(0, stream.shape[0], 16):
        part = stream_ref[low : low + 16, :]
        second_ref[low : low + 16, :] = (normal(part)[0] * scale + shift).astype(BF)


def forward_kernel(
    flag_ref, own, far, tokens, mod, text, out_w, query_w, cross_w, grad, cot, up_hbm, down_hbm,
    acts, up_pack, hidden, keep,
    out, one, small_keep, small_send, text_grad, pack, stat, table,
    up, down, sems, kept0, kept1, lse, branch_ref, queries, stream, mlp_out, back,
    grad_mixed, grad_queries, text_key, text_value, *, factor, live, count
):
    kept = (kept0, kept1)
    rows, width = tokens.ref.shape
    mixed, cross_in, att = (acts.ref.at[i * rows : (i + 1) * rows, :] for i in range(3))
    second = up_pack.ref.at[:, 0:width]
    own.start()
    far.start()
    own.wait()
    far.wait()
    late = (tokens, mod, text, out_w, query_w, cross_w, grad, cot)
    for slot in late:
        slot.start()
    tile = down.shape[1]
    tiles = down_hbm.shape[0] // tile
    ring = down.shape[0]

    def copies(step):
        half = tile // 2
        slot = step % ring
        pairs = []
        for part in (0, 1):
            rows = slice(part * up_hbm.shape[0] // 2, (part + 1) * up_hbm.shape[0] // 2)
            pairs.append((up_hbm.at[rows, step * tile : (step + 1) * tile], up.at[slot, rows, :]))
            rows = slice(part * half, (part + 1) * half)
            pairs.append((down_hbm.at[step * tile + part * half : step * tile + (part + 1) * half, :], down.at[slot, rows, :]))
        return [pltpu.make_async_copy(a, b, sems.at[slot, i]) for i, (a, b) in enumerate(pairs)]

    for step in range(min(ring, tiles)):
        for copy in copies(step):
            copy.start()
    attend(flag_ref[LARGE] == 1, own.ref, far.ref, att, lse, factor)
    for slot in late:
        slot.wait()
    weights = (out_w.ref, query_w.ref, cross_w.ref)
    outs = (branch_ref, cross_in, queries, mixed, stream, second)
    middle(tokens.ref, mod.ref, att, weights, text.ref, outs, factor, live)
    acts.send()

    root = math.sqrt(2.0 / math.pi)

    def both(step):
        if step < tiles:
            for copy in copies(step):
                copy.wait()
            pre = matmul(second[...], up[step % ring])
            slope = matmul_nt(grad.ref[...], down[step % ring])
        if step > 0:
            before = (step - 1) % ring
            ahead = hidden.ref[:, (step - 1) * tile : step * tile]
            behind = kept[(step - 1) % 2][...]
            branch = matmul(ahead, down[before])
            result = matmul_nt(behind, up[before])
        if step < tiles:

            def bent(pre, grad):
                square = pre * pre
                bend = jnp.tanh(pre * (root * 0.044715 * square + root))
                half = 0.5 * bend + 0.5
                rise = (3 * root * 0.044715 * square + root) * pre
                slope = half + 0.5 * rise * (1.0 - bend * bend)
                return (pre * half).astype(BF), (grad * slope).astype(BF)

            ahead, behind = blockwise(bent, [pre, slope], 64, 128)
            kept[step % 2][...] = behind
            hidden.ref[:, step * tile : (step + 1) * tile] = ahead
            if count:
                size = tile // 2
                body, tail = slice_parts(size)
                group = step % 2 * keep.ref.shape[1] // 2
                spots = (
                    (group + step // 2 * body, 0, body),
                    (group + tiles // 2 * body + step // 2 * tail, body, tail),
                )
                for core in (0, 1):

                    @pl.when(flag_ref[CORE] == core)
                    def _(core=core):
                        for at, low, wide in spots:
                            mine, other = core * size + low, (1 - core) * size + low
                            keep.ref[:, at : at + wide] = behind[:, mine : mine + wide]
                            up_pack.ref[:, width + at : width + at + wide] = behind[:, other : other + wide]

            else:
                keep.ref[:, step * tile : (step + 1) * tile] = behind
        if step > 0:
            if step == 1:
                mlp_out[...] = branch
                back[...] = result
            else:
                mlp_out[...] += branch
                back[...] += result
            if step - 1 + ring < tiles:
                for copy in copies(step - 1 + ring):
                    copy.start()

    for step in range(tiles):
        both(step)
    hidden.send()
    keep.send()
    up_pack.send()
    both(tiles)
    middle_grad(
        flag_ref, back, stream, cot.ref, mlp_out, mod.ref, branch_ref, att, lse, queries, text.ref, weights,
        out, one, small_keep, small_send, text_grad, pack, stat, table,
        grad_mixed, grad_queries, text_key, text_value, factor, live, count,
    )


def middle_grad(
    flag_ref, second_grad_ref, stream_ref, cot_ref, mlp_ref, mod_ref, branch_ref, att_ref, lse_ref, queries_ref, text_ref,
    weights, out, one, keep, send, text_grad, pack, stat_out, table,
    mixed, grad_queries, text_key, text_value, factor, live, count
):
    out_w_ref, query_w_ref, cross_w_ref = weights
    one_ref, keep_ref, send_ref, text_grad_ref, pack_ref, stat_ref, table_ref = (
        slot.ref for slot in (one, keep, send, text_grad, pack, stat_out, table)
    )
    rows, width = cot_ref.shape
    gate, scale = mod_ref[5:6, :], 1.0 + mod_ref[4:5, :]
    sums = [0.0] * 3
    for low in range(0, rows, 16):
        part = slice(low, low + 16)
        cot, stream, mlp, grad = cot_ref[part, :].astype(F32), stream_ref[part, :], mlp_ref[part, :], second_grad_ref[part, :]
        out.ref[part, :] = stream + gate * mlp
        normed, spread = normal(stream)
        scaled = grad * scale
        back = spread * (
            scaled
            - jnp.mean(scaled, axis=-1, keepdims=True)
            - normed * jnp.mean(scaled * normed, axis=-1, keepdims=True)
        )
        one_ref[part, :] = cot + back
        sums = [total + term for total, term in zip(sums, (grad, grad * normed, cot * mlp))]
    out.send()
    table_ref[...] = jnp.zeros_like(table_ref)
    for index, total in enumerate(sums):
        table_ref[3 + index : 4 + index, :] = jnp.sum(total, axis=0, keepdims=True)
    grad_cross = one_ref[...].astype(BF)
    mixed[...] = matmul_nt(grad_cross, cross_w_ref[...]).astype(BF)

    def one_head(head):
        start, mask = head_window(head, width)
        keep = mask.astype(BF)
        query = window(queries_ref, start)
        grad = window(mixed, start)
        key = window(text_ref, start) * keep
        probs = text_probs(query, key, factor * LOG2E, live, 0)
        grad_probs = matmul_nt(window(text_ref, start, width) * keep, grad)
        inner = jnp.sum(probs * grad_probs, axis=0, keepdims=True)
        grad_scores = (probs * (grad_probs - inner)).astype(BF)
        keep_columns(grad_queries, start, mask, (matmul_tn(grad_scores, key) * factor).astype(BF))
        keep_columns(text_key, start, mask, matmul(grad_scores, query) * factor)
        keep_columns(text_value, start, mask, matmul(probs.astype(BF), grad))

    each_head(one_head, 8)
    text_grad_ref[:, :width] = text_key[0:live, :]
    text_grad_ref[:, width:] = text_value[0:live, :]
    text_grad.send()
    grad_cq = grad_queries[...]
    grad_one = one_ref[...] + matmul_nt(grad_cq, query_w_ref[...])
    one_ref[...] = grad_one
    table_ref[2:3, :] = jnp.sum(grad_one * branch_ref[...], axis=0, keepdims=True)
    grad_attn = (mod_ref[2:3, :] * grad_one).astype(BF)
    grad_att = matmul_nt(grad_attn, out_w_ref[...]).astype(BF)
    pack_ref[0:rows, :] = grad_att

    product = grad_att.astype(F32) * att_ref[...].astype(F32)
    upper = product.astype(BF)
    lower = (product - upper.astype(F32)).astype(BF)
    size = width // HEADS
    column = lax.broadcasted_iota(jnp.int32, (width, 128), 0)
    low = (lax.broadcasted_iota(jnp.int32, (width, 128), 1) - HEADS) * size
    pick = jnp.logical_and(column >= low, column < low + size).astype(BF)
    stat = lse_ref[...] + matmul(upper, pick) + matmul(lower, pick)
    stat_ref[...] = stat
    turned = stat.T
    upper = [turned[8 * g : 8 * g + 8, :].astype(BF).astype(F32) for g in range(4)]
    lower = [turned[8 * g : 8 * g + 8, :] - part for g, part in enumerate(upper)]
    both = [jnp.concatenate(pair, axis=0) for pair in zip(upper, lower)]
    pack_ref[rows : rows + 16, :] = side_by_side(both, width).astype(BF)
    for slot in (pack, stat_out, one, table):
        slot.send()

    if count:
        for core in (0, 1):

            @pl.when(flag_ref[CORE] == core)
            def _(core=core):
                grads = [grad_cross, grad_cq, grad_attn]
                keep_ref[...] = half_columns(grads, core, count, False, keep_ref.shape[1])
                send_ref[...] = half_columns(grads, 1 - core, count, False, send_ref.shape[1])

    else:
        for index, grad in enumerate((grad_cross, grad_cq, grad_attn)):
            keep_ref[:, index * width : (index + 1) * width] = grad


def last_grad_kernel(
    dq_ref, dk_ref, dv_ref, weight_ref, tokens_ref, mod_ref, one_ref, table_ref, text_ref, out_ref, text_out, *, shape
):
    width = tokens_ref.shape[1]
    grad = sum(
        matmul_nt(ref[...], weight_ref[:, part * width : (part + 1) * width])
        for part, ref in enumerate((dq_ref, dk_ref, dv_ref))
    )
    normed, spread = normal(tokens_ref[...].astype(F32))
    back, shift, scale = norm_back(normed, spread, mod_ref[1:2, :], grad)
    out_ref[...] = one_ref[...] + back
    table = [shift, scale] + [table_ref[i : i + 1, :] for i in range(2, 6)]
    dp_count, sp_count = shape
    size = 6 * width // (dp_count * sp_count)

    def flat(low, high):
        pieces = []
        while low < high:
            row, at = divmod(low, width)
            stop = min(high, (row + 1) * width)
            pieces.append(table[row][:, at : at + stop - low])
            low = stop
        return pieces

    step = 2 * width // sp_count
    lines = [[], [], []]
    for place in range(sp_count):
        whole = [piece for i in range(dp_count) for piece in flat((i * sp_count + place) * size, (i * sp_count + place + 1) * size)]
        whole = jnp.concatenate(whole, axis=1)
        for i in range(3):
            lines[i].append(whole[:, i * step : (i + 1) * step])
    rows = [jnp.concatenate(line, axis=1) for line in lines]
    live = text_ref.shape[0]
    rows.append(jnp.zeros((128 - live - 3, 2 * width), F32))
    both = jnp.concatenate([text_ref[...]] + rows, axis=0)
    for low in range(0, 2 * width, 128):
        text_out[low : low + 128, :] = both[:, low : low + 128].T


def caption_kernel(text_ref, caption_ref, out_ref, *, blocks, size):
    live, width = caption_ref.shape
    text = text_ref[...].T
    grad = matmul_tn(caption_ref[...], text[:live].astype(BF)).astype(BF)
    tall = width // blocks
    line = jnp.concatenate([text[live + i : live + i + 1] for i in range(3)], axis=1)
    high = out_ref.shape[0] // blocks
    for block in range(blocks):
        out_ref[block * high : block * high + tall, :] = grad[block * tall : (block + 1) * tall]
        part = side_by_side([line[:, block * size : (block + 1) * size]], out_ref.shape[1])
        out_ref[block * high + tall : (block + 1) * high, :] = jnp.broadcast_to(
            part, (high - tall, out_ref.shape[1])
        ).astype(BF)


def side_by_side(pieces, width):
    missing = width - sum(piece.shape[1] for piece in pieces)
    if missing:
        pieces = [*pieces, jnp.zeros((pieces[0].shape[0], missing), pieces[0].dtype)]
    return pieces[0] if len(pieces) == 1 else jnp.concatenate(pieces, axis=1)


def lanes(width):
    return -(-width // 128) * 128


def slice_parts(size):
    return size // 128 * 128, size % 128


def half_columns(grads, core, count, joined, wide):
    if not joined:
        picked = []
        for grad in grads:
            size = grad.shape[1] // count
            low = [(2 * chip + core) * size for chip in (*range(0, count // 2, 2), *range(1, count // 2, 2))]
            picked.append(
                side_by_side([grad[:, at : at + size] for at in low], wide // len(grads))
            )
        return side_by_side(picked, wide)
    grad = grads[0] if len(grads) == 1 else jnp.concatenate(grads, axis=1)
    size = grad.shape[1] // count
    body, _ = slice_parts(size)
    picked = []
    for parity in (0, 1):
        low = [(2 * chip + core) * size for chip in range(parity, count // 2, 2)]
        picked += [grad[:, at : at + body] for at in low]
        picked.append(side_by_side([grad[:, at + body : at + size] for at in low], 128))
    return side_by_side(picked, wide)


def halves_kernel(core_ref, *refs, count, joined):
    keep_ref, send_ref = refs[-2:]
    for core in (0, 1):

        @pl.when(core_ref[CORE] == core)
        def _(core=core):
            grads = [ref[...] for ref in refs[:-2]]
            keep_ref[...] = half_columns(grads, core, count, joined, keep_ref.shape[1])
            send_ref[...] = half_columns(grads, 1 - core, count, joined, send_ref.shape[1])


def store_halves(flag, stores, pieces):
    for value in (0, 1):

        @pl.when(flag == value)
        def _(value=value):
            for store, piece in zip(stores, (pieces[1 - value], pieces[value])):
                store(piece())


def into(ref):
    def store(value):
        ref[:, : value.shape[1]] = value.astype(ref.dtype)

    return store


def add(*terms):
    return sum(term.astype(F32) for term in terms)


def sending(buffers, sems, out):
    state = {"count": 0}

    def wait(slot):
        pltpu.make_async_copy(buffers.at[slot], out, sems.at[slot]).wait()

    def put(pieces, targets):
        slot = state["count"] % 2
        if state["count"] >= 2:
            wait(slot)
        at = 0
        for piece in pieces:
            buffers[slot, at : at + piece.shape[0], : piece.shape[1]] = piece
            at += piece.shape[0]
        for condition, target in targets:
            copy = pltpu.make_async_copy(buffers.at[slot], target, sems.at[slot])
            if condition is None:
                copy.start()
            else:
                pl.when(condition)(copy.start)
        state["count"] += 1

    def done():
        for slot in range(min(2, state["count"])):
            wait(slot)

    return put, done


def wide_grad_kernel(order_ref, x0_hbm, x1_hbm, g0_hbm, g1_hbm, *refs, mode, first, columns):
    number = 2 if mode == "rows" else 4
    outs, (x_ref, g_ref, turned, buffers, sems, out_sems) = refs[:number], refs[number:]
    rows, width = x0_hbm.shape[0], x_ref.shape[1]
    x0_hbm, x1_hbm, g0_hbm, g1_hbm = (
        hbm if part is None else hbm.at[:, part] for hbm, part in zip((x0_hbm, x1_hbm, g0_hbm, g1_hbm), columns)
    )
    waits = fetch(
        sems,
        (x0_hbm, x_ref.at[0:rows, :]),
        (x1_hbm, x_ref.at[rows : 2 * rows, :]),
        (g0_hbm, g_ref.at[0:rows, :]),
        (g1_hbm, g_ref.at[rows : 2 * rows, :]),
    )
    for part in (0, 1):
        waits[part]()
        for low in range(0, width, 128):
            turned[low : low + 128, part * rows : (part + 1) * rows] = x_ref[
                part * rows : (part + 1) * rows, low : low + 128
            ].T
    waits[2]()
    waits[3]()
    tall = width // 4
    put, done = sending(buffers, out_sems, outs[0].at[0])
    half = g_ref.shape[1] // 2
    for step in range(4):
        here = pl.ds(pl.multiple_of((order_ref[ORDERS + 4 * first + step] if mode == "rows" else step) * tall, 16), tall)
        if mode == "rows":
            total = matmul(turned[here, :], g_ref[...]).astype(BF)
            put([total], [(None, outs[step // 2].at[step % 2])])
        else:
            for p in (0, 1):
                total = matmul(turned[here, :], g_ref[:, p * half : (p + 1) * half]).astype(BF)
                place, second = (step >> p) & 1, (step >> (1 - p)) & 1
                mine = order_ref[ROW + p]
                put(
                    [total],
                    [(mine != place, outs[2 * p].at[second]), (mine == place, outs[2 * p + 1].at[second])],
                )
    done()


def tall_grad_kernel(order_ref, *refs, count, mode, first, columns):
    sources, g0_hbm, g1_hbm = refs[: 2 * count], refs[2 * count], refs[2 * count + 1]
    outs, (x_ref, g_ref, turned, buffers, sems, out_sems) = refs[2 * count + 2 : 2 * count + 4], refs[2 * count + 4 :]
    rows = g0_hbm.shape[0]
    sources = [hbm if part is None else hbm.at[part, :] for hbm, part in zip(sources, columns)]
    pairs = [(g0_hbm, g_ref.at[0:rows, :]), (g1_hbm, g_ref.at[rows : 2 * rows, :])]
    for i, source in enumerate(sources):
        pairs.append((source, x_ref.at[i // 2, i % 2 * rows : (i % 2 + 1) * rows, :]))
    waits = fetch(sems, *pairs)
    wide = g_ref.shape[1]
    for part in (0, 1):
        waits[part]()
        for low in range(0, wide, 128):
            turned[low : low + 128, part * rows : (part + 1) * rows] = g_ref[
                part * rows : (part + 1) * rows, low : low + 128
            ].T
    for wait in waits[2:]:
        wait()
    if mode == "rows":
        high, tall = outs[0].shape[1:]
        put, done = sending(buffers, out_sems, outs[0].at[0])
        for step in range(4):
            here = pl.ds(pl.multiple_of(order_ref[ORDERS + 4 * first + step] * tall, 128), tall)
            total = matmul(turned[0:high, :], x_ref[0, :, here]).astype(BF)
            put([total], [(None, outs[step // 2].at[step % 2])])
    else:
        high = outs[0].shape[0] // count
        put, done = sending(buffers, out_sems, outs[0])
        for p in (0, 1):
            total = [
                matmul(turned[pl.ds(k * (wide // count) + p * high, high), :], x_ref[k]).astype(BF)
                for k in range(count)
            ]
            put(total, [(order_ref[NEAR] != p, outs[0]), (order_ref[NEAR] == p, outs[1])])
    done()


def add_kernel(flag_ref, *refs):
    refs[-1][...] = add(*[ref[...] for ref in refs[:-1]]).astype(BF)


def split_kernel(flag_ref, *refs, parts, axis, bit):
    views = refs[:-2]

    def joined(index):
        def piece():
            sums = [add(*[view[part] for view in views]) for part in parts[index]]
            return sums[0] if len(sums) == 1 else jnp.concatenate(sums, axis=axis)

        return piece

    store_halves(flag_ref[bit], [into(ref) for ref in refs[-2:]], [joined(0), joined(1)])


def split_pair_kernel(flag_ref, *refs):
    def group(p):
        keep, got, more = refs[3 * p : 3 * p + 3]
        return lambda: add(keep[...], got[...], more[...])

    store_halves(flag_ref[NEAR], [into(ref) for ref in refs[-2:]], [group(0), group(1)])


def last_kernel(keep_ref, got_ref, *outs, size):
    if size:
        body, tail = slice_parts(size)
        for part in (slice(0, body), slice(body, size)):
            outs[0][:, part] = add(keep_ref[:, part], got_ref[:, part])
    else:
        high, wide = outs[0].shape
        for index, out in enumerate(outs):
            part = slice(index * high, (index + 1) * high), slice(0, wide)
            out[...] = add(keep_ref[part], got_ref[part])


def prelude_kernel(place_ref, row_ref, len_ref, step_ref, embed_ref, table_ref, info_ref, mod_ref, slab, sem, *, rows):
    slots = len_ref.shape[1]
    width = table_ref.shape[1]

    def image_of(at):
        first = at * rows
        end = begin = length = step = jnp.int32(0)
        for slot in range(slots):
            count = len_ref[0, slot]
            inside = jnp.logical_and(end <= first, first < end + count)
            begin = jnp.where(inside, end, begin)
            length = jnp.where(inside, count, length)
            step = jnp.where(inside, step_ref[0, slot], step)
            end = end + count
        return (first - begin) // rows, length, step

    place = place_ref[0]
    core = place % 2
    blocks = BIG // rows
    within, length, step = image_of(place)
    pair_within = image_of(place + 1 - 2 * core)[0]
    flags = (
        length > rows,
        jnp.where(core == 0, pair_within + 1 < blocks, pair_within + 3 < blocks),
        jnp.where(core == 0, within + 1 < blocks, within >= 1),
        within + 2 < blocks,
        core == 1,
    )
    bits = [(place // 2) & 1, (place // 4) & 1, row_ref[0] & 1, (row_ref[0] >> 1) & 1]
    values = [flag.astype(jnp.int32) for flag in flags] + bits + [1 - bits[2], 1 - bits[3]]
    for first in (0, 1):
        mine = bits[2 + first]
        values += [((1 - mine if s < 2 else mine) << first) + ((s % 2) << (1 - first)) for s in range(4)]
    for index, value in enumerate(values):
        info_ref[index] = value
    copy = pltpu.make_async_copy(embed_ref.at[pl.ds(pl.multiple_of(step // 8 * 8, 8), 8), :], slab, sem)
    copy.start()
    copy.wait()
    row = slab[pl.ds(step % 8, 1), :]
    for index in range(6):
        mod_ref[index : index + 1, :] = (
            row[:, index * width : (index + 1) * width] + table_ref[index : index + 1, :]
        )


class Slot:
    def __init__(self, hbm, ref, sems, out=False):
        self.hbm, self.ref, self.out = hbm, ref, out
        self.sent = False
        self.copies = []
        for i, rows in enumerate(row_chunks(ref.shape, ref.dtype)):
            pair = (hbm.at[rows], ref.at[rows])
            self.copies.append(pltpu.make_async_copy(*(pair[::-1] if out else pair), sems.at[i]))

    def start(self):
        self.sent = True
        for copy in self.copies:
            copy.start()

    send = start

    def wait(self):
        for copy in self.copies:
            copy.wait()


def row_chunks(shape, dtype):
    if len(shape) > 2:
        return [slice(i, i + 1) for i in range(shape[0])]
    size = shape[0] * shape[1] * jnp.dtype(dtype).itemsize
    count = max([n for n in (1, 2, 3, 4, 6) if shape[0] % (16 * n) == 0 and size >= n * 200_000] or [1])
    high = shape[0] // count
    return [slice(i * high, (i + 1) * high) for i in range(count)]


def call(kernel, inputs, outs, flags=None, scratch=(), raw=(), lazy=False, limit=60):
    anywhere = pl.BlockSpec(memory_space=pl.ANY)
    arrays, views = [], []
    for entry in inputs:
        array, part = entry if isinstance(entry, tuple) else (entry, None)
        arrays.append(array)
        views.append(part)

    def view_shape(array, part):
        if part is None:
            return array.shape
        if isinstance(part, slice):
            return (array.shape[0], part.stop - part.start)
        return array.shape[1:]

    in_shapes = [view_shape(array, part) for array, part in zip(arrays, views)]
    slots = [(shape, array.dtype) for shape, array in zip(in_shapes, arrays)] + list(outs)
    held = [i for i in range(len(arrays)) if i not in raw]
    held += [len(arrays) + i for i in range(len(outs)) if "out" not in raw]
    buffers = [pltpu.VMEM(*slots[i]) for i in held]
    sems = [pltpu.SemaphoreType.DMA((len(row_chunks(*slots[i])),)) for i in held]

    def managed(*refs):
        refs = list(refs)
        flag_refs = [refs.pop(0)] if flags is not None else []
        hbm, rest = refs[: len(slots)], refs[len(slots) :]
        own, rest = rest[: len(scratch)], rest[len(scratch) :]
        views_in = []
        for ref, part in zip(hbm, views):
            if isinstance(part, slice):
                ref = ref.at[:, part]
            elif part is not None:
                ref = ref.at[flag_refs[0][part]]
            views_in.append(ref)
        given = views_in + hbm[len(arrays) :]
        for n, i in enumerate(held):
            given[i] = Slot(given[i], rest[n], rest[len(held) + n], i >= len(arrays))
        slots_in = [slot for slot in given if isinstance(slot, Slot) and not slot.out]
        slots_out = [slot for slot in given if isinstance(slot, Slot) and slot.out]
        if not lazy:
            for slot in slots_in:
                slot.start()
            for slot in slots_in:
                slot.wait()
            kernel(*flag_refs, *[getattr(slot, "ref", slot) if isinstance(slot, Slot) else slot for slot in given], *own)
        else:
            kernel(*flag_refs, *given, *own)
        for slot in slots_out:
            if not slot.sent:
                slot.send()
        for slot in slots_out:
            slot.wait()

    return pl.pallas_call(
        managed,
        in_specs=([pl.BlockSpec(memory_space=pltpu.SMEM)] if flags is not None else []) + [anywhere] * len(arrays),
        out_specs=[anywhere] * len(outs),
        out_shape=[jax.ShapeDtypeStruct(shape, dtype) for shape, dtype in outs],
        scratch_shapes=[*scratch, *buffers, *sems],
        compiler_params=pltpu.CompilerParams(vmem_limit_bytes=limit * MIB),
        cost_estimate=pl.CostEstimate(flops=1000, bytes_accessed=1000, transcendentals=0),
    )(*([] if flags is None else [flags]), *arrays)


def prelude(place, row_place, image_len, timestep, time_embed, mod_table, rows):
    smem = pl.BlockSpec(memory_space=pltpu.SMEM)
    return pl.pallas_call(
        functools.partial(prelude_kernel, rows=rows),
        in_specs=[smem] * 4 + [pl.BlockSpec(memory_space=pl.ANY), pl.BlockSpec(memory_space=pltpu.VMEM)],
        out_specs=[smem, pl.BlockSpec(memory_space=pltpu.VMEM)],
        out_shape=[jax.ShapeDtypeStruct((ORDERS + 8,), jnp.int32), jax.ShapeDtypeStruct(mod_table.shape, F32)],
        scratch_shapes=[pltpu.VMEM((8, time_embed.shape[1]), F32), pltpu.SemaphoreType.DMA],
        compiler_params=pltpu.CompilerParams(vmem_limit_bytes=4 * MIB),
    )(place.reshape(1), row_place.reshape(1), image_len, timestep, time_embed, mod_table)


def half_width(grads, count, joined):
    size = (sum(grad.shape[1] for grad in grads) if joined else grads[0].shape[1]) // count
    body, _ = slice_parts(size)
    return 2 * (count // 4 * body + 128) if joined else len(grads) * -(-count // 2 * size // 128) * 128


def halves(core, grads, count, joined):
    out = ((grads[0].shape[0], half_width(grads, count, joined)), BF)
    return call(functools.partial(halves_kernel, count=count, joined=joined), grads, [out] * 2, flags=core, limit=6)


def split(flags, bit, inputs, parts, shape, axis=1):
    return call(
        functools.partial(split_kernel, parts=parts, axis=axis, bit=bit),
        inputs,
        [(shape, BF), (shape, F32)],
        flags=flags,
    )


def add_last(keep, got, size, shapes):
    return call(functools.partial(last_kernel, size=size), [keep, got], [(shape, F32) for shape in shapes])


def wide_grad(order, source, mode, first=0):
    entries = [entry if isinstance(entry, tuple) else (entry, None) for entry in source]
    source = [array for array, _ in entries]
    columns = [part and slice(part.start, part.stop or array.shape[1]) for array, part in entries]
    rows, width = source[0].shape[0], columns[0].stop if columns[0] else source[0].shape[1]
    depth = source[2].shape[1]
    wide, number = (depth, 2) if mode == "rows" else (depth // 2, 4)
    return call(
        functools.partial(wide_grad_kernel, mode=mode, first=first, columns=columns),
        source,
        [((2, width // 4, wide), BF)] * number,
        flags=order,
        raw=(0, 1, 2, 3, "out"),
        scratch=[
            pltpu.VMEM((2 * rows, width), BF),
            pltpu.VMEM((2 * rows, depth), BF),
            pltpu.VMEM((width, 2 * rows), BF),
            pltpu.VMEM((2, width // 4, wide), BF),
            pltpu.SemaphoreType.DMA((4,)),
            pltpu.SemaphoreType.DMA((2,)),
        ],
    )


def tall_grad(order, acts, keep, got, size, mode, first=0):
    count = len(acts)
    entries = [entry if isinstance(entry, tuple) else (entry, None) for pair in acts for entry in pair]
    rows, wide = keep.shape
    width = entries[0][0].shape[1]
    shape = (2, 4 * size, width // 4) if mode == "rows" else (2 * size * count, width)
    return call(
        functools.partial(
            tall_grad_kernel, count=count, mode=mode, first=first, columns=[part for _, part in entries]
        ),
        [array for array, _ in entries] + [keep, got],
        [(shape, BF)] * 2,
        flags=order,
        raw=(*range(2 * count + 2), "out"),
        scratch=[
            pltpu.VMEM((count, 2 * rows, width), BF),
            pltpu.VMEM((2 * rows, wide), BF),
            pltpu.VMEM((wide, 2 * rows), BF),
            pltpu.VMEM((2, *shape[-2:]), BF),
            pltpu.SemaphoreType.DMA((2 * count + 2,)),
            pltpu.SemaphoreType.DMA((2,)),
        ],
    )


def local(
    tokens,
    image_len,
    timestep,
    caption,
    time_embed,
    mod_table,
    w_qkv,
    w_out,
    cross_q,
    cross_kv,
    cross_out,
    w_up,
    w_down,
    cotangent,
):
    sp_count = lax.axis_size("sp")
    dp_count = lax.axis_size("dp")
    place = lax.axis_index("sp")
    row_place = lax.axis_index("dp")
    core = place % 2
    rows, width = tokens.shape[1:]
    factor = 1.0 / math.sqrt(width // HEADS)
    blocks = BIG // rows
    assert blocks == 4

    big, modulation = prelude(place, row_place, image_len, timestep, time_embed, mod_table, rows)
    shift_one, scale_one, gate_one, shift_two, scale_two, gate_two = [modulation[i] for i in range(6)]

    def tie(value, *before):
        before = [array for array in jax.tree.leaves(before) if array is not None]
        return lax.optimization_barrier((value, *before))[0]

    pairs = [(i, i ^ 1) for i in range(sp_count)]
    others = [(i, i + 1) for i in range(1, sp_count - 1, 2)] + [(i + 1, i) for i in range(1, sp_count - 1, 2)]
    ahead = [(i, i + 2) for i in range(sp_count - 2)]
    back = [(i + 2, i) for i in range(sp_count - 2)]

    def image_blocks(block, *before):
        from_back = lax.ppermute(block, "sp", ahead)
        from_ahead = lax.ppermute(block, "sp", back)
        from_ahead, from_back = tie(from_ahead, *before), tie(from_back, *before)
        send_pair = jnp.concatenate([jnp.where(big[1] == 1, from_ahead, from_back), block], axis=0)
        send_other = jnp.where(core == 1, from_back, from_ahead)
        both = lax.ppermute(send_pair, "sp", pairs)
        third = lax.ppermute(send_other, "sp", others)
        return [both, third, from_ahead, from_back], (send_pair, send_other)

    def chosen(both, third, from_ahead, from_back):
        high = both.shape[0] // 2
        return [
            both[:high],
            jnp.where(big[2] == 1, both[high:], third),
            jnp.where(big[3] == 1, from_ahead, from_back),
        ]

    def swap(array):
        return lax.ppermute(array, "sp", pairs)

    token_blocks, token_sends = image_blocks(tokens[0])

    def first_norm(block):
        return (normal(block.astype(F32))[0] * (1.0 + scale_one) + shift_one).astype(BF)

    first_in = first_norm(tokens[0])
    other_in = first_norm(jnp.concatenate(chosen(*token_blocks), axis=0))

    chips = sp_count // 2
    square = dp_count == 4 and chips == 4

    def own_half(*grads, joined=True):
        if square:
            return halves(big, grads, sp_count, joined)
        grads = [jnp.concatenate(grads, axis=1)] if joined else grads
        size = grads[0].shape[1] // sp_count
        even, odd = [
            jnp.concatenate(
                [g[:, i * size : (i + 1) * size] for g in grads for i in range(c, sp_count, 2)], axis=1
            )
            for c in (0, 1)
        ]
        return jnp.where(core == 0, even, odd), jnp.where(core == 0, odd, even)

    high = width // 4

    def to_row(array, bit):
        return lax.ppermute(array, "dp", [(i, i ^ (1 << bit)) for i in range(dp_count)])

    def to_chip(array, bit):
        return lax.ppermute(array, "sp", [(i, i ^ (2 << bit)) for i in range(sp_count)])

    def plain_sum(sources, size):
        finals = []
        for item, (x0, x1, g0, g1) in enumerate(sources):
            columns = slice(item * chips * size, (item + 1) * chips * size)
            part = (matmul_tn(x0, g0[:, columns]) + matmul_tn(x1, g1[:, columns])).astype(BF)
            part = part.reshape(dp_count, -1, chips, size).transpose(0, 2, 1, 3)
            bit = dp_count // 2
            while bit:
                mine = (row_place // bit) % 2
                part = part.reshape(2, bit, chips, -1, size)
                got = lax.ppermute(part[1 - mine], "dp", [(i, i ^ bit) for i in range(dp_count)])
                part = add(part[mine], got).astype(BF)
                bit //= 2
            part = part.reshape(chips, -1, size)
            bit = chips // 2
            while bit:
                mine = (place // 2 // bit) % 2
                part = part.reshape(2, bit, -1, size)
                got = lax.ppermute(part[1 - mine], "sp", [(i, i ^ (2 * bit)) for i in range(sp_count)])
                part = add(part[mine], got).astype(BF)
                bit //= 2
            finals.append(part[0].astype(F32))
        return finals

    def add_picked(keep, got, flag):
        return call(add_kernel, [(keep, flag), (got, flag)], [(keep.shape[1:], BF)], flags=big)

    everything = slice(None)

    def cut_slices(size):
        body, tail = slice_parts(size)
        return [
            [
                (everything, slice(h * body, (h + 1) * body)),
                (everything, slice(2 * body + h * tail, 2 * body + (h + 1) * tail)),
            ]
            for h in (0, 1)
        ]

    def sum_wide(source, first, size):
        second = 1 - first
        if size < 256:
            send, keep = tall_grad(big, [source[:2]], *source[2:], size, "rows", first)
        else:
            send, keep = wide_grad(big, source, "rows", first)
        late = yield send
        got = to_row(send, first)
        if size < 256:
            _, tall, wide = keep.shape
            flat = lambda array: array.reshape(2 * tall, wide)
            rows_at = lambda low, high: (slice(low, high),)
            groups = [
                [rows_at(y * tall + h * tall // 2, y * tall + (h + 1) * tall // 2) for y in (0, 1)]
                for h in (0, 1)
            ]
            send, keep = split(big, NEAR, [flat(tie(keep, late)), flat(got)], groups, (tall, wide), 0)
            late = yield send
            groups = [[rows_at(h * tall // 2, (h + 1) * tall // 2)] for h in (0, 1)]
            inputs = [tie(keep, late), to_chip(send, 0)]
            send, keep = split(big, ROW + second, inputs, groups, (tall // 2, wide), 0)
            late = yield send
            groups = [[rows_at(h * tall // 4, (h + 1) * tall // 4)] for h in (0, 1)]
            inputs = [tie(keep, late), to_row(send, second)]
            send, keep = split(big, FAR, inputs, groups, (tall // 4, wide), 0)
            late = yield send
            (final,) = add_last(tie(keep, late), to_chip(send, 1), 0, [(size, wide)])
            yield final.T
        else:
            (send,) = add_picked(tie(keep, late), got, OTHER + second)
            late = yield send
            tall, wide = send.shape
            more = to_row(send, second)
            inputs = [(tie(keep, late), ROW + second), (got, ROW + second), more]
            groups = [[(everything, slice(h * wide // 2, (h + 1) * wide // 2))] for h in (0, 1)]
            send, keep = split(big, NEAR, inputs, groups, (tall, wide // 2))
            late = yield send
            shape = (tall, size // 128 * 128 + 128)
            send, keep = split(big, FAR, [tie(keep, late), to_chip(send, 0)], cut_slices(size), shape)
            late = yield send
            (final,) = add_last(tie(keep, late), to_chip(send, 1), size, [(tall, size)])
            yield final

    def sum_both(source, size):
        outs = wide_grad(big, source, "both")
        late = yield outs[0]
        got = [to_row(outs[0], 0), to_row(outs[2], 1)]
        sends = [
            *add_picked(tie(outs[1], late), got[0], OTHER + 1),
            *add_picked(tie(outs[3], late), got[1], OTHER),
        ]
        late = yield sends[1]
        shape = sends[0].shape
        more = [to_row(sends[0], 1), to_row(sends[1], 0)]
        send, keep = call(
            split_pair_kernel,
            [
                (tie(outs[1], late), ROW + 1), (got[0], ROW + 1), more[0],
                (outs[3], ROW), (got[1], ROW), more[1],
            ],
            [(shape, BF), (shape, F32)],
            flags=big,
        )
        late = yield send
        shape = (shape[0], size // 128 * 128 + 128)
        send, keep = split(big, FAR, [tie(keep, late), to_chip(send, 0)], cut_slices(size), shape)
        late = yield send
        (final,) = add_last(tie(keep, late), to_chip(send, 1), size, [(high, size)])
        yield final

    def sum_chips_first(acts, keep, got, size):
        count = len(acts)
        send, keep = tall_grad(big, acts, keep, got, size, "chips")
        late = yield send
        got = to_chip(send, 0)
        groups = [[(everything, slice(2 * h * high, 2 * (h + 1) * high))] for h in (0, 1)]
        shape = (2 * count * size, lanes(2 * high))
        send, keep = split(big, ROW + 1, [tie(keep, late), got], groups, shape)
        late = yield send
        got = to_row(send, 1)
        groups = [[(everything, slice(h * high, (h + 1) * high))] for h in (0, 1)]
        shape = (2 * count * size, lanes(high))
        send, keep = split(big, ROW, [tie(keep, late), got], groups, shape)
        late = yield send
        got = to_row(send, 0)
        groups = [
            [(slice((2 * k + h) * size, (2 * k + h + 1) * size),) for k in range(count)] for h in (0, 1)
        ]
        shape = (count * size, lanes(high))
        send, keep = split(big, FAR, [tie(keep, late), got], groups, shape, 0)
        late = yield send
        finals = add_last(tie(keep, late), to_chip(send, 1), 0, [(size, high)] * count)
        yield [final.T for final in finals]

    caption_rows = caption[0]
    live = caption_rows.shape[0]
    padded = -(-live // 128) * 128
    caption_pad = jnp.concatenate([caption_rows, jnp.zeros((padded - live, width), BF)], axis=0)
    text = matmul(caption_pad, cross_kv).astype(BF)
    grad_mlp = (gate_two * cotangent[0].astype(F32)).astype(BF)
    mlp_keep, mlp_send = own_half(grad_mlp, joined=False)
    mlp_got = swap(mlp_send)
    first_pair = swap(first_in)
    own = matmul(tie(first_in, *token_sends), w_qkv).astype(BF)
    far_qkv = matmul(other_in, w_qkv).astype(BF)
    block = ((rows, width), BF)
    stream = ((rows, width), F32)
    stats = ((rows, 128), F32)
    units = w_up.shape[1]
    tile = units // 4
    half = half_width([w_up], sp_count, True) if square else units
    small_width = half_width([grad_mlp] * 3, sp_count, False) if square else 3 * width
    small_out = ((rows, small_width), BF)
    (
        acts, up_pack, hidden, pre_keep,
        stream_three, grad_one, small_keep, small_send, grad_text, pack, stat, table,
    ) = call(
        functools.partial(forward_kernel, factor=factor, live=live, count=sp_count if square else 0),
        [
            own, (tie(far_qkv, mlp_got, first_pair), slice(width, 3 * width)), tokens[0], modulation, text,
            w_out, cross_q, cross_out, grad_mlp, cotangent[0], w_up, w_down,
        ],
        [
            ((3 * rows, width), BF), ((rows, width + (half if square else 0)), BF), ((rows, units), BF),
            ((rows, half), BF),
            stream, stream, small_out, small_out, ((live, 2 * width), F32), ((rows + 16, width), BF), stats,
            (modulation.shape, F32),
        ],
        flags=big,
        raw=(10, 11),
        lazy=True,
        scratch=[
            pltpu.VMEM((3, width, tile), BF),
            pltpu.VMEM((3, tile, width), BF),
            pltpu.SemaphoreType.DMA((3, 4)),
            pltpu.VMEM((rows, tile), BF),
            pltpu.VMEM((rows, tile), BF),
            pltpu.VMEM((rows, 128), F32),
            pltpu.VMEM((rows, width), F32),
            pltpu.VMEM((rows, width), BF),
            *[pltpu.VMEM((rows, width), F32)] * 3,
            *[pltpu.VMEM((rows, width), BF)] * 2,
            *[pltpu.VMEM((padded, width), F32)] * 2,
        ],
        limit=63,
    )

    if not square:
        pre_keep, pre_send = own_half(pre_keep)
        up_pack = jnp.concatenate([up_pack, pre_send], axis=1)
    hidden_pair, up_pair = swap(hidden), swap(up_pack)
    if not square:
        small_keep, small_send = own_half(*jnp.split(small_keep, 3, axis=1), joined=False)
    slice_of = lambda weight: weight.shape[1] // sp_count
    down_source = (hidden, hidden_pair, mlp_keep, mlp_got)
    up_source = ((up_pack, slice(0, width)), (up_pair, slice(0, width)), pre_keep, (up_pair, slice(width, None)))
    send_down = send_up = send_small = None
    if square:
        up_sum = sum_wide((up_source[0], up_source[1], tie(pre_keep, pack), up_source[3]), 1, slice_of(w_up))
        send_up = next(up_sum)
        down_sum = sum_wide((tie(hidden, send_up), *down_source[1:]), 0, slice_of(w_down))
        send_down = next(down_sum)
        small_got = swap(tie(small_send, send_up))
        small_acts = tie(acts, send_up)
        small_acts = [small_acts, swap(small_acts)]
        small_acts = [[(part, slice(i * rows, (i + 1) * rows)) for part in small_acts] for i in range(3)]
        small_sum = sum_chips_first(small_acts, tie(small_keep, send_down), small_got, slice_of(w_out))
        send_small = next(small_sum)
    pack_blocks, pack_sends = image_blocks(pack, send_small)
    (grad_queries,) = call(
        functools.partial(query_grad_kernel, factor=factor),
        [own, (far_qkv, slice(width, 3 * width)), tie(pack, *pack_sends), stat],
        [block],
        flags=big,
    )
    proj_out = ((rows, half_width([w_qkv], sp_count, True) if square else 3 * width), BF)
    grad_keys, grad_values, proj_keep, proj_send = call(
        functools.partial(key_grad_kernel, factor=factor, count=sp_count if square else 0),
        [own, (far_qkv, slice(0, width)), tie(pack, grad_queries), grad_queries, *pack_blocks],
        [block, block, proj_out, proj_out],
        flags=big,
        raw=(4, 5, 6, 7),
        lazy=True,
        scratch=[
            pltpu.VMEM((2 * HEADS, blocks * rows), F32),
            pltpu.VMEM(((blocks - 1) * rows, width), BF),
            pltpu.VMEM((blocks - 1, 16, width), BF),
            pltpu.SemaphoreType.DMA((2 * blocks - 2,)),
        ],
    )
    if not square:
        proj_keep, proj_send = own_half(*jnp.split(proj_keep, 3, axis=1))
    qkv_source = (first_in, first_pair, proj_keep, swap(proj_send))
    grad_tokens, text_part = call(
        functools.partial(last_grad_kernel, shape=(dp_count, sp_count)),
        [
            grad_queries, tie(grad_keys, proj_send), grad_values, w_qkv, tokens[0], modulation, grad_one, table,
            grad_text,
        ],
        [stream, ((2 * width, 128), F32)],
    )
    table = text_part
    text_part = lax.psum_scatter(text_part, "sp", scatter_dimension=0, tiled=True)

    def caption_sum(late):
        part = tie(text_part, late)
        tall, size = width // dp_count, 6 * width // (dp_count * sp_count)
        high = lanes(tall + 16) if dp_count != 4 else tall + 16
        (both,) = call(
            functools.partial(caption_kernel, blocks=dp_count, size=size),
            [part, caption_rows],
            [((dp_count * high, part.shape[0]), BF)],
        )
        total = lax.psum_scatter(both, "dp", scatter_dimension=0, tiled=True).astype(F32)
        return both, total[:tall], total[tall, :size]

    late = None
    if square:
        late = down_sum.send(small_sum.send(up_sum.send(table)))
        qkv_sum = sum_both((tie(first_in, late), *qkv_source[1:]), slice_of(w_qkv))
        late = next(qkv_sum)
        for step in (small_sum, up_sum, down_sum, qkv_sum):
            late = step.send(late)
        late, final_ckv, final_table = caption_sum(late)
        for step in (up_sum, down_sum, small_sum):
            late = step.send(late)
        final_up = up_sum.send(late)
        late = qkv_sum.send(final_up)
        final_down = down_sum.send(late)
        late = qkv_sum.send(tie(final_down, final_ckv))
        final_small = small_sum.send(late)
        final_qkv = qkv_sum.send((final_small[0], final_ckv, final_table))
    else:
        _, final_ckv, final_table = caption_sum(table)
        small_pair, small_got = swap(acts), swap(small_send)
        small = [
            (acts[i * rows : (i + 1) * rows], small_pair[i * rows : (i + 1) * rows], small_keep, small_got)
            for i in range(3)
        ]
        up_source = (up_pack[:, :width], up_pair[:, :width], pre_keep, up_pair[:, width:])
        final_small = plain_sum(small, slice_of(w_out))
        (final_down,) = plain_sum([down_source], slice_of(w_down))
        (final_up,) = plain_sum([up_source], slice_of(w_up))
        (final_qkv,) = plain_sum([qkv_source], slice_of(w_qkv))
    return (
        stream_three[None],
        grad_tokens[None],
        final_table,
        final_qkv,
        final_small[2],
        final_small[1],
        final_ckv,
        final_small[0],
        final_up,
        final_down,
    )


def solution(mesh):
    return jax.shard_map(
        local,
        mesh=mesh,
        in_specs=(
            P("dp", "sp", None),
            P("dp", None),
            P("dp", None),
            P("dp", None, None),
            P(),
            P(),
            P(),
            P(),
            P(),
            P(),
            P(),
            P(),
            P(),
            P("dp", "sp", None),
        ),
        out_specs=(
            P("dp", "sp", None),
            P("dp", "sp", None),
            P(("dp", "sp")),
            P("dp", "sp"),
            P("dp", "sp"),
            P("dp", "sp"),
            P("dp", "sp"),
            P("dp", "sp"),
            P("dp", "sp"),
            P("dp", "sp"),
        ),
        check_vma=False,
    )
```
